32 devices in a mesh: ctx: 8 (over z, y), fsdp: 4 (over x, core).
Axes of the slice: x: 2, y: 2, z: 4, core: 2. Of those that a mesh axis runs over, the one named last changes fastest.
Arguments:
- tokens: bfloat16 [4, 1024, 768], P('fsdp', 'ctx'), may hold values from -6 to 6
- memory: bfloat16 [4, 5120, 768], P('fsdp', 'ctx'), may hold values from -6 to 6
- piece_order: int32 [16], replicated, may hold values from 0 to 15, as said below
- bucket_table: int32 [2047], replicated, may hold values from 0 to 31, as said below
- passage_lengths: int32 [4, 20], P('fsdp'), may hold values from 32 to 256, as said below
- self_gain: bfloat16 [768], P('fsdp'), may hold values from 0.5 to 1.5
- cross_gain: bfloat16 [768], P('fsdp'), may hold values from 0.5 to 1.5
- hidden_gain: bfloat16 [768], P('fsdp'), may hold values from 0.5 to 1.5
- position_bias: bfloat16 [32, 12], P('fsdp'), may hold values from -3 to 3
- self_query: bfloat16 [768, 768], P('fsdp'), may hold values from -0.09375 to 0.09375
- self_attention_key: bfloat16 [768, 768], P('fsdp'), may hold values from -0.09375 to 0.09375
- self_value: bfloat16 [768, 768], P('fsdp'), may hold values from -0.21875 to 0.21875
- self_output: bfloat16 [768, 768], P('fsdp'), may hold values from -2 to 2
- cross_query: bfloat16 [768, 768], P('fsdp'), may hold values from -0.09375 to 0.09375
- cross_key: bfloat16 [768, 768], P('fsdp'), may hold values from -0.09375 to 0.09375
- cross_value: bfloat16 [768, 768], P('fsdp'), may hold values from -0.21875 to 0.21875
- cross_output: bfloat16 [768, 768], P('fsdp'), may hold values from -2 to 2
- hidden_in: bfloat16 [768, 3072], P('fsdp'), may hold values from -0.21875 to 0.21875
- hidden_out: bfloat16 [3072, 768], P('fsdp'), may hold values from -0.15625 to 0.15625
- grad_output: bfloat16 [4, 1024, 768], P('fsdp', 'ctx'), may hold values from -6 to 6
Outputs:
- layer_output: bfloat16 [4, 1024, 768], P('fsdp', 'ctx')
- grad_tokens: bfloat16 [4, 1024, 768], P('fsdp', 'ctx')
- grad_memory: bfloat16 [4, 5120, 768], P('fsdp', 'ctx')
- grad_self_gain: float32 [768], P('fsdp')
- grad_cross_gain: float32 [768], P('fsdp')
- grad_hidden_gain: float32 [768], P('fsdp')
- grad_position_bias: float32 [32, 12], P('fsdp')
- grad_self_query: float32 [768, 768], P('fsdp')
- grad_self_key: float32 [768, 768], P('fsdp')
- grad_self_value: float32 [768, 768], P('fsdp')
- grad_self_output: float32 [768, 768], P('fsdp')
- grad_cross_query: float32 [768, 768], P('fsdp')
- grad_cross_key: float32 [768, 768], P('fsdp')
- grad_cross_value: float32 [768, 768], P('fsdp')
- grad_cross_output: float32 [768, 768], P('fsdp')
- grad_hidden_in: float32 [768, 3072], P('fsdp')
- grad_hidden_out: float32 [3072, 768], P('fsdp')
The draws below stay inside these ranges and needn't reach their ends.
Inputs may be any that keep to these rules, and one draw needn't show every extreme that they name: `piece_order`: slots 2i and 2i + 1 hold two pieces whose numbers add up to 15; every piece appears once. `bucket_table`: entry 1023 + r is the bucket of r = key place minus query place; buckets below 16 serve r <= 0, the others r > 0, and on either side the bucket never falls as the distance grows. `passage_lengths`: in every sequence one passage fills all 256 slots.
All inputs are finite; a program needn't handle non-finite values.
Results may differ from the reference program's by a relative error of at most 0.03.
Values may be sent and summed in bfloat16 or wider, within the bound.
A program may use at most 320 MiB of HBM per device.

```python
import jax
import jax.numpy as jnp
from jax import lax

D = 768
HEADS = 12
HEAD_DIM = 64
FF = 3072
BUCKETS = 32
PIECE = 64
BLOCK = 256
KBLK = 512
PSG = 20
PLEN = 256
LEN = 1024
MEM = 5120
SEQ_ALL = 4
N_CTX = 8


def draw_piece_order(key, part):
    order_key, flip_key = jax.random.split(key)
    order = jax.random.permutation(order_key, N_CTX).astype(jnp.int32)
    flips = jax.random.randint(flip_key, (N_CTX,), 0, 2, dtype=jnp.int32)
    front = jnp.where(flips == 1, 2 * N_CTX - 1 - order, order)
    behind = 2 * N_CTX - 1 - front
    return jnp.stack([front, behind], axis=1).reshape(2 * N_CTX).astype(jnp.int32)


def draw_bucket_table(key, part):
    half_count = BUCKETS // 2
    exact_count = BUCKETS // 4
    gaps = jax.random.randint(key, (half_count - exact_count - 1,), 1, BLOCK // 4 + 1, dtype=jnp.int32)
    bounds = exact_count + jnp.cumsum(gaps)
    relative = jnp.arange(2 * LEN - 1, dtype=jnp.int32) - (LEN - 1)
    distance = jnp.abs(relative)
    farther = exact_count + jnp.sum((bounds[None, :] <= distance[:, None]).astype(jnp.int32), axis=1)
    relative_bucket_index = jnp.where(distance < exact_count, distance, farther)
    return (relative_bucket_index + jnp.where(relative > 0, half_count, 0)).astype(jnp.int32)


def draw_passage_lengths(key, part):
    base_key, full_key, short_key = jax.random.split(key, 3)
    lengths = jax.random.randint(base_key, (SEQ_ALL, PSG), PLEN // 8, PLEN + 1, dtype=jnp.int32)
    full_at = jax.random.randint(full_key, (SEQ_ALL, 1), 0, PSG, dtype=jnp.int32)
    short_at = (full_at + jax.random.randint(short_key, (SEQ_ALL, 1), 1, PSG, dtype=jnp.int32)) % PSG
    column = jnp.arange(PSG, dtype=jnp.int32)[None, :]
    lengths = jnp.where(column == full_at, PLEN, lengths)
    return jnp.where(column == short_at, PLEN // 8, lengths).astype(jnp.int32)


def block_levels(own_key, shape, pieces, least, top_value):
    loudness, own = 1.0, jax.random.fold_in(own_key, 6)
    for dim, parts in pieces:
        draws = jnp.exp(jax.random.uniform(jax.random.fold_in(own, dim), (parts,), jnp.float32, least / len(pieces), top_value / len(pieces)))
        loudness = loudness * jnp.repeat(draws, shape[dim] // parts).reshape([-1 if axis == dim else 1 for axis in range(len(shape))])
    return loudness


def gaussian(stream_key, shape, scale, limit, pieces=(), kind=jnp.bfloat16):
    result = scale * jax.random.normal(stream_key, shape, jnp.float32)
    if pieces:
        result = result * block_levels(stream_key, shape, pieces, -0.22, 0.18)
    return jnp.clip(result, -limit, limit).astype(kind)


def setup_inputs(seed: int = 0) -> dict:
    key_list = jax.random.split(jax.random.key(seed), 21)
    return {
        "tokens": gaussian(key_list[0], (SEQ_ALL, LEN, D), 1.0, 6.0, ((0, 4), (1, 8))),
        "memory": gaussian(key_list[1], (SEQ_ALL, MEM, D), 1.0, 6.0, ((0, 4), (1, 8))),
        "piece_order": draw_piece_order(jax.random.fold_in(key_list[20], 71), 0),
        "bucket_table": draw_bucket_table(jax.random.fold_in(key_list[20], 71), 0),
        "passage_lengths": draw_passage_lengths(jax.random.fold_in(key_list[20], 71), 0),
        "self_gain": jnp.clip(1.0 + 0.1 * jax.random.normal(key_list[5], (D,), jnp.float32), 0.5, 1.5).astype(jnp.bfloat16),
        "cross_gain": jnp.clip(1.0 + 0.1 * jax.random.normal(key_list[6], (D,), jnp.float32), 0.5, 1.5).astype(jnp.bfloat16),
        "hidden_gain": jnp.clip(1.0 + 0.1 * jax.random.normal(key_list[7], (D,), jnp.float32), 0.5, 1.5).astype(jnp.bfloat16),
        "position_bias": gaussian(key_list[8], (BUCKETS, HEADS), 0.5, 3.0, ((0, 4),)),
        "self_query": gaussian(key_list[9], (D, D), (16 * D // 3) ** -0.5, 0.09375, ((0, 4),)),
        "self_attention_key": gaussian(key_list[10], (D, D), (16 * D // 3) ** -0.5, 0.09375, ((0, 4),)),
        "self_value": gaussian(key_list[11], (D, D), D ** -0.5, 0.21875, ((0, 4),)),
        "self_output": gaussian(key_list[12], (D, D), (max(D // 96, 1)) ** -0.5, 2.0, ((0, 4),)),
        "cross_query": gaussian(key_list[13], (D, D), (16 * D // 3) ** -0.5, 0.09375, ((0, 4),)),
        "cross_key": gaussian(key_list[14], (D, D), (16 * D // 3) ** -0.5, 0.09375, ((0, 4),)),
        "cross_value": gaussian(key_list[15], (D, D), D ** -0.5, 0.21875, ((0, 4),)),
        "cross_output": gaussian(key_list[16], (D, D), (max(D // 96, 1)) ** -0.5, 2.0, ((0, 4),)),
        "hidden_in": gaussian(key_list[17], (D, FF), D ** -0.5, 0.21875, ((0, 4),)),
        "hidden_out": gaussian(key_list[18], (FF, D), (FF // 2) ** -0.5, 0.15625, ((0, 4),)),
        "grad_output": gaussian(key_list[19], (SEQ_ALL, LEN, D), 1.0, 6.0, ((0, 4), (1, 8))),
    }


EPSILON = 1e-06
NEGATIVE = -1e+30
HIGHEST = lax.Precision.HIGHEST

@jax.custom_vjp
def low(v):
    return lax.optimization_barrier(v.astype(jnp.bfloat16)).astype(jnp.float32)

@jax.custom_vjp
def low_back(v):
    return v

def low_keep(v):
    return (low(v), None)

def low_pass(kept, grad):
    return (grad,)

def back_keep(v):
    return (v, None)

def back_low(kept, grad):
    return (low(grad),)
low.defvjp(low_keep, low_pass)
low_back.defvjp(back_keep, back_low)

def norm_scale(values, gain_vector):
    return values * lax.rsqrt(lax.optimization_barrier(jnp.mean(values * values, axis=-1, keepdims=True)) + EPSILON) * gain_vector

def smooth_gate(values):
    return jax.nn.gelu(values, approximate=True)

def product(operand, matrix):
    return jnp.dot(operand, matrix, precision=HIGHEST, preferred_element_type=jnp.float32)

def attention(queries, keys_all, values_all, extras):
    block_count = keys_all.shape[0] // KBLK

    def single_block_tile(block_index):
        offset = block_index * KBLK
        key_block = lax.dynamic_slice_in_dim(keys_all, offset, KBLK, 0)
        value_block = lax.dynamic_slice_in_dim(values_all, offset, KBLK, 0)
        added_bias, visible = extras(offset)
        scores = low_back(jnp.einsum('qhd,khd->hqk', queries, key_block, precision=HIGHEST, preferred_element_type=jnp.float32)) + added_bias
        block_maximum = lax.optimization_barrier(jnp.max(jnp.where(visible, scores, NEGATIVE), axis=-1))
        weights = jnp.exp(jnp.where(visible, scores - block_maximum[..., None], NEGATIVE))
        numerator = low_back(jnp.einsum('hqk,khd->hqd', low(weights), value_block, precision=HIGHEST, preferred_element_type=jnp.float32))
        return (block_maximum, lax.optimization_barrier(jnp.sum(weights, axis=-1)), numerator)
    block_maximum, block_sum, numerator = lax.map(jax.checkpoint(single_block_tile), jnp.arange(block_count, dtype=jnp.int32))
    row_maximum = lax.optimization_barrier(jnp.max(block_maximum, axis=0))
    rescale = jnp.exp(block_maximum - row_maximum)
    row_total = lax.optimization_barrier(jnp.sum(rescale * block_sum, axis=0))
    return lax.optimization_barrier(jnp.sum(rescale[..., None] * numerator, axis=0)) / row_total[..., None]

def join_heads(tensor):
    return jnp.transpose(tensor, (1, 0, 2)).reshape(tensor.shape[1], HEADS * HEAD_DIM)

def layer(inputs, memory_rows, lengths, params, key_position, bucket_table):
    gain_one, gain_two, gain_three, position_bias_lookup, query_weight, key_weight, value_weight, output_weight, cross_query_weight, cross_key_weight, cross_value_weight, cross_output_weight, inner_weight, outer_weight = params
    normed_one = low(norm_scale(inputs, gain_one))
    queries_one = low(low_back(product(normed_one, query_weight))).reshape(LEN, HEADS, HEAD_DIM)
    keys_one = low(low_back(product(normed_one, key_weight))).reshape(LEN, HEADS, HEAD_DIM)
    values_one = low(low_back(product(normed_one, value_weight))).reshape(LEN, HEADS, HEAD_DIM)

    def self_extras(offset):
        key_block_position = lax.dynamic_slice_in_dim(key_position, offset, KBLK)
        relative_bucket_index = jnp.take(bucket_table, key_block_position[None, :] - key_position[:, None] + LEN - 1)
        added_bias = jnp.transpose(jnp.take(position_bias_lookup, relative_bucket_index, axis=0), (2, 0, 1))
        visible = key_block_position[None, :] // BLOCK <= key_position[:, None] // BLOCK
        return (added_bias, visible)
    attended_one = low(low_back(join_heads(attention(queries_one, keys_one, values_one, self_extras))))
    hidden_one = inputs + low_back(product(attended_one, output_weight))
    normed_two = low(norm_scale(hidden_one, gain_two))
    queries_two = low(low_back(product(normed_two, cross_query_weight))).reshape(LEN, HEADS, HEAD_DIM)
    keys_two = low(low_back(product(memory_rows, cross_key_weight))).reshape(MEM, HEADS, HEAD_DIM)
    values_two = low(low_back(product(memory_rows, cross_value_weight))).reshape(MEM, HEADS, HEAD_DIM)
    memory_valid = (lengths[:, None] > jnp.arange(PLEN, dtype=jnp.int32)[None, :]).reshape(MEM)

    def cross_extras(offset):
        return (0.0, lax.dynamic_slice_in_dim(memory_valid, offset, KBLK)[None, None, :])
    attended_two = low(low_back(join_heads(attention(queries_two, keys_two, values_two, cross_extras))))
    hidden_two = hidden_one + low_back(product(attended_two, cross_output_weight))
    normed_three = low(norm_scale(hidden_two, gain_three))
    activated = low(smooth_gate(low_back(product(normed_three, inner_weight))))
    return hidden_two + low_back(product(activated, outer_weight))

def reference(tokens, memory, piece_order, bucket_table, passage_lengths, self_gain, cross_gain, hidden_gain, position_bias, self_query, self_attention_key, self_value, self_output, cross_query, cross_key, cross_value, cross_output, hidden_in, hidden_out, grad_output):
    key_position = (piece_order[:, None] * PIECE + jnp.arange(PIECE, dtype=jnp.int32)[None, :]).reshape(LEN)
    params = tuple((member.astype(jnp.float32) for member in (self_gain, cross_gain, hidden_gain, position_bias, self_query, self_attention_key, self_value, self_output, cross_query, cross_key, cross_value, cross_output, hidden_in, hidden_out)))

    def forward(inputs_all, memory_all, weights):

        def one_sequence(sequence_items):
            return layer(sequence_items[0], sequence_items[1], sequence_items[2], weights, key_position, bucket_table)
        return lax.map(one_sequence, (inputs_all, memory_all, passage_lengths))
    outputs, pullback = jax.vjp(forward, tokens.astype(jnp.float32), memory.astype(jnp.float32), params)
    grad_inputs, grad_memory, grad_params = pullback(grad_output.astype(jnp.float32))
    return (outputs.astype(jnp.bfloat16), grad_inputs.astype(jnp.bfloat16), grad_memory.astype(jnp.bfloat16), grad_params[0], grad_params[1], grad_params[2], grad_params[3], grad_params[4], grad_params[5], grad_params[6], grad_params[7], grad_params[8], grad_params[9], grad_params[10], grad_params[11], grad_params[12], grad_params[13])
```

```python
import jax
import jax.numpy as jnp
from jax import lax
from jax.experimental import pallas as pl
from jax.experimental.pallas import tpu as pltpu
from jax.sharding import PartitionSpec as P

D = 768
HEADS = 12
PAIRS = HEADS // 2
HEAD_DIM = 64
PIECE = 64
BLOCK = 256
PLEN = 256
KBLK = 512
PSG = 20
BUCKETS = 32
RESIDENT_ROWS = 1024
LANES = 128
EPSILON = 1e-06
NEGATIVE = -1e30
F32 = jnp.float32
BF16 = jnp.bfloat16
VMEM_LIMIT = 60 * 2**20

def nn(a, b):
    return lax.dot_general(a, b, (((1,), (0,)), ((), ())), preferred_element_type=F32)
def nt(a, b):
    return lax.dot_general(a, b, (((1,), (1,)), ((), ())), preferred_element_type=F32)
def tn(a, b):
    return lax.dot_general(a, b, (((0,), (0,)), ((), ())), preferred_element_type=F32)

def normed(x, gain):
    return x * lax.rsqrt(jnp.mean(x * x, axis=-1, keepdims=True) + EPSILON) * gain

def half_mask(x, half):
    lane = lax.broadcasted_iota(jnp.int32, x.shape, 1) // HEAD_DIM
    return jnp.where(lane == half, x, jnp.zeros_like(x))

def lanes_of(pair):
    return pl.ds(pl.multiple_of(pair * LANES, LANES), LANES)

def shear(x, sign):
    row = lax.broadcasted_iota(jnp.int32, x.shape, 0)
    for bit in (1, 2, 4):
        x = jnp.where(row & bit != 0, pltpu.roll(x, (sign * bit) % x.shape[1], 1), x)
    return x

def bias_tables_kernel(table, back_table, ahead, behind):
    full = table.shape[1]
    def head(h, c):
        for src, out in ((table, ahead), (back_table, behind)):
            base = shear(pltpu.roll(jnp.broadcast_to(src[pl.ds(h, 1), :], (8, full)), 1, 1), 1)
            for parity in range(2):
                for i in range(PIECE // 16):
                    both = [pltpu.roll(base, (8 * g - 64 * parity) % full, 1) if (8 * g - 64 * parity) % full else base
                            for g in (2 * i, 2 * i + 1)]
                    out[parity, h, 16 * i:16 * i + 16, :] = jnp.concatenate(both, 0).astype(BF16)
        return c
    lax.fori_loop(0, HEADS, head, 0)

def bias_tables(table, back_table):
    full = table.shape[1]
    return pl.pallas_call(
        bias_tables_kernel,
        name="bias_tables",
        out_shape=[sds((2, HEADS, PIECE, full), BF16)] * 2,
        in_specs=[full_spec()] * 2,
        out_specs=[full_spec()] * 2,
        compiler_params=pltpu.CompilerParams(vmem_limit_bytes=VMEM_LIMIT),
    )(table, back_table)

def piece_bias(tables, h, piece, length):
    start = pl.multiple_of(length - (piece + piece % 2) * PIECE, LANES)
    return tables[piece % 2, h, :, pl.ds(start, length)].astype(F32)

def bias_rows(tables, h, own, count, length):
    return jnp.concatenate([piece_bias(tables, h, own[i], length) for i in range(count)], 0)

def add_diagonals(acc, block, piece):
    rows, length = block.shape
    wide = jnp.concatenate([block, jnp.zeros((rows, LANES), F32)], axis=1)
    total = pltpu.roll(wide[0:8], LANES, 1)
    for g in range(1, rows // 8):
        total += pltpu.roll(wide[8 * g:8 * g + 8], LANES - 8 * g, 1)
    start = pl.multiple_of(length - (piece - piece % 2) * PIECE - LANES, LANES)
    where = (piece % 2, slice(None), pl.ds(start, length + LANES))
    acc[where] += total

def self_forward_kernel(order, own, tok_all, tok, w, gains, table, wo, wq2,
                        q_nat, k_nat, v_nat, o1, h1, a1, a2, q2, lse, inv, q_own):
    length = tok_all.shape[0]
    rows = tok.shape[0]
    slots, mine = length // PIECE, rows // PIECE
    for s in range(slots):
        inv[order[s]] = s
    per = BLOCK // PIECE

    def tile(t, c):
        parts = [tok_all[pl.ds(pl.multiple_of(inv[t * per + i] * PIECE, PIECE), PIECE), :] for i in range(per)]
        a = normed(jnp.concatenate(parts, 0).astype(F32), gains[0:1, :]).astype(BF16)
        dst = pl.ds(pl.multiple_of(t * BLOCK, BLOCK), BLOCK)
        for j, out in enumerate((q_nat, k_nat, v_nat)):
            out[dst, :] = nn(a, w[:, j * D:(j + 1) * D]).astype(BF16)
        return c

    lax.fori_loop(0, length // BLOCK, tile, 0)
    for i in range(mine):
        q_own[i * PIECE:(i + 1) * PIECE, :] = q_nat[pl.ds(pl.multiple_of(own[i] * PIECE, PIECE), PIECE), :]
    a1[...] = normed(tok[...].astype(F32), gains[0:1, :]).astype(BF16)
    lane = lax.broadcasted_iota(jnp.int32, (rows, length), 1)
    limit = jnp.concatenate([jnp.full((PIECE, 1), (own[i] // per + 1) * BLOCK, jnp.int32) for i in range(mine)], 0)
    visible = lane < limit
    stat_lane = lax.broadcasted_iota(jnp.int32, (rows, LANES), 1)

    def pair(p, stats):
        sl = lanes_of(p)
        q, k, v = q_own[:, sl], k_nat[:, sl], v_nat[:, sl]
        total = jnp.zeros((rows, LANES), F32)
        for half in range(2):
            h = 2 * p + half
            s = jnp.where(visible, nt(q, half_mask(k, half)) + bias_rows(table, h, own, mine, length), NEGATIVE)
            m = jnp.max(s, axis=1, keepdims=True)
            e = jnp.exp(s - m)
            l = jnp.sum(e, axis=1, keepdims=True)
            total += nn(e.astype(BF16), half_mask(v, half)) / l
            stats = jnp.where(stat_lane == h, m + jnp.log(l), stats)
        o1[:, sl] = total.astype(BF16)
        return stats

    lse[...] = lax.fori_loop(0, PAIRS, pair, jnp.zeros((rows, LANES), F32))
    h = tok[...].astype(F32) + nn(o1[...], wo[...])
    h1[...] = h
    a = normed(h, gains[1:2, :]).astype(BF16)
    a2[...] = a
    q2[...] = nn(a, wq2[...]).astype(BF16)

def full_spec():
    return pl.BlockSpec(memory_space=pltpu.VMEM)
def smem_spec():
    return pl.BlockSpec(memory_space=pltpu.SMEM)
def sds(shape, dtype):
    return jax.ShapeDtypeStruct(shape, dtype)

def self_forward(order, own, tok_all, tok, w, gains, table, wo, wq2):
    length, rows = tok_all.shape[0], tok.shape[0]
    return pl.pallas_call(
        self_forward_kernel,
        name="self_forward",
        out_shape=[sds((length, D), BF16)] * 3 + [sds((rows, D), BF16), sds((rows, D), F32), sds((rows, D), BF16),
                   sds((rows, D), BF16), sds((rows, D), BF16), sds((rows, LANES), F32)],
        in_specs=[smem_spec()] * 2 + [full_spec()] * 7,
        out_specs=[full_spec()] * 9,
        scratch_shapes=[pltpu.SMEM((length // PIECE,), jnp.int32), pltpu.VMEM((rows, D), BF16)],
        compiler_params=pltpu.CompilerParams(vmem_limit_bytes=VMEM_LIMIT),
    )(order, own, tok_all, tok, w, gains, table, wo, wq2)

def cross_forward_kernel(q_all, k2, v2, mask, o, lse):
    rows = q_all.shape[0]
    step = BLOCK
    stat_lane = lax.broadcasted_iota(jnp.int32, (step, LANES), 1)

    def tile(t, c):
        rs = pl.ds(pl.multiple_of(t * step, step), step)
        def pair(p, stats):
            sl = lanes_of(p)
            q, k, v = q_all[rs, sl], k2[:, sl], v2[:, sl]
            total = jnp.zeros((step, LANES), F32)
            for half in range(2):
                s = nt(q, half_mask(k, half)) + mask[...]
                m = jnp.max(s, axis=1, keepdims=True)
                e = jnp.exp(s - m)
                l = jnp.sum(e, axis=1, keepdims=True)
                total += nn(e.astype(BF16), half_mask(v, half)) / l
                stats = jnp.where(stat_lane == 2 * p + half, m + jnp.log(l), stats)
            o[rs, sl] = total.astype(BF16)
            return stats
        lse[rs, :] = lax.fori_loop(0, PAIRS, pair, jnp.zeros((step, LANES), F32))
        return c
    lax.fori_loop(0, rows // step, tile, 0)

def cross_forward(q_all, k2, v2, mask):
    rows = q_all.shape[0]
    return pl.pallas_call(
        cross_forward_kernel,
        name="cross_forward",
        out_shape=[sds((rows, D), BF16), sds((rows, LANES), F32)],
        in_specs=[full_spec()] * 4,
        out_specs=[full_spec()] * 2,
        compiler_params=pltpu.CompilerParams(vmem_limit_bytes=VMEM_LIMIT),
    )(q_all, k2, v2, mask)

def cross_backward_kernel(q_all, do_all, stats, k2, v2, mask, dq, dk, dv):
    rows = q_all.shape[0]
    slots = k2.shape[0]
    step = BLOCK

    def pair(p, c):
        sl = lanes_of(p)
        ks = [half_mask(k2[:, sl], i) for i in range(2)]
        vs = [half_mask(v2[:, sl], i) for i in range(2)]
        def tile(t, carry):
            dkp, dvp = carry
            rs = pl.ds(pl.multiple_of(t * step, step), step)
            q, do = q_all[rs, sl], do_all[rs, sl]
            dqp = jnp.zeros((step, LANES), F32)
            for half in range(2):
                h = 2 * p + half
                qm, dom = half_mask(q, half), half_mask(do, half)
                s = nt(ks[half], q) + mask[...]
                e = jnp.exp(s - stats[pl.ds(h, 1), rs])
                dvp = dvp + nn(e.astype(BF16), dom)
                ds = (e * (nt(vs[half], do) - stats[pl.ds(16 + h, 1), rs])).astype(BF16)
                dkp = dkp + nn(ds, qm)
                dqp = dqp + tn(ds, ks[half])
            dq[rs, sl] = dqp.astype(dq.dtype)
            return dkp, dvp
        zero = jnp.zeros((slots, LANES), F32)
        dkp, dvp = lax.fori_loop(0, rows // step, tile, (zero, zero))
        dk[:, sl] = dkp.astype(BF16)
        dv[:, sl] = dvp.astype(BF16)
        return c
    lax.fori_loop(0, PAIRS, pair, 0)

def cross_backward(q_all, do_all, stats, k2, v2, mask):
    rows, slots = q_all.shape[0], k2.shape[0]
    return pl.pallas_call(
        cross_backward_kernel,
        name="cross_backward",
        out_shape=[sds((rows, D), F32), sds((slots, D), BF16), sds((slots, D), BF16)],
        in_specs=[full_spec()] * 6,
        out_specs=[full_spec()] * 3,
        compiler_params=pltpu.CompilerParams(vmem_limit_bytes=VMEM_LIMIT),
    )(q_all, do_all, stats, k2, v2, mask)

def self_backward_kernel(order, own, q_nat, k_nat, v_nat, do_slot, do_own, stat_slot, stat_own, delta_own, table, back_table,
                         dq, dk, dv, diag, inv, q_own, k_own, v_own, do_nat, stat_nat, stat_t, acc):
    length = q_nat.shape[0]
    rows = do_own.shape[0]
    full = 2 * length
    slots, mine = length // PIECE, rows // PIECE
    per = BLOCK // PIECE
    for s in range(slots):
        inv[order[s]] = s
    def move(i, c):
        src = pl.ds(pl.multiple_of(inv[i] * PIECE, PIECE), PIECE)
        dst = pl.ds(pl.multiple_of(i * PIECE, PIECE), PIECE)
        do_nat[dst, :] = do_slot[src, :]
        stat_nat[dst, :] = stat_slot[src, :]
        return c
    lax.fori_loop(0, slots, move, 0)
    for i in range(length // LANES):
        stat_t[:, i * LANES:(i + 1) * LANES] = stat_nat[i * LANES:(i + 1) * LANES, :].T
    for i in range(mine):
        src = pl.ds(pl.multiple_of(own[i] * PIECE, PIECE), PIECE)
        dst = slice(i * PIECE, (i + 1) * PIECE)
        q_own[dst, :] = q_nat[src, :]
        k_own[dst, :] = k_nat[src, :]
        v_own[dst, :] = v_nat[src, :]
    lane = lax.broadcasted_iota(jnp.int32, (rows, length), 1)
    limit = jnp.concatenate([jnp.full((PIECE, 1), (own[i] // per + 1) * BLOCK, jnp.int32) for i in range(mine)], 0)
    first = jnp.concatenate([jnp.full((PIECE, 1), (own[i] // per) * BLOCK, jnp.int32) for i in range(mine)], 0)
    visible, seen = lane < limit, lane >= first
    stat_lane = lax.broadcasted_iota(jnp.int32, (rows, LANES), 1)

    def column(h):
        return jnp.sum(jnp.where(stat_lane == h, stat_own[...], 0.0), axis=1, keepdims=True)

    diag[...] = jnp.zeros_like(diag)
    def pair(p, c):
        sl = lanes_of(p)
        q, k, v, do = q_own[:, sl], k_nat[:, sl], v_nat[:, sl], do_own[:, sl]
        kq, vq, qa, da = k_own[:, sl], v_own[:, sl], q_nat[:, sl], do_nat[:, sl]
        dqp = jnp.zeros((rows, LANES), F32)
        dkp = jnp.zeros((rows, LANES), F32)
        dvp = jnp.zeros((rows, LANES), F32)
        for half in range(2):
            h = 2 * p + half
            bias = bias_rows(table, h, own, mine, length)
            km, vm = half_mask(k, half), half_mask(v, half)
            s = jnp.where(visible, nt(q, km) + bias, NEGATIVE)
            e = jnp.exp(s - column(h))
            ds = e * (nt(do, vm) - column(16 + h))
            dqp += nn(ds.astype(BF16), km)
            acc[...] = jnp.zeros_like(acc)
            for i in range(mine):
                add_diagonals(acc, ds[i * PIECE:(i + 1) * PIECE, :], own[i])
            joined = shear(acc[0] + pltpu.roll(acc[1], full - PIECE, 1), -1)
            diag[pl.ds(h, 1), :] = jnp.sum(pltpu.roll(joined, full - 1, 1), axis=0, keepdims=True)
            bias = bias_rows(back_table, h, own, mine, length)
            s = jnp.where(seen, nt(half_mask(kq, half), qa) + bias, NEGATIVE)
            e = jnp.exp(s - stat_t[pl.ds(h, 1), :])
            dvp += nn(e.astype(BF16), half_mask(da, half))
            ds = e * (nt(half_mask(vq, half), da) - stat_t[pl.ds(16 + h, 1), :])
            dkp += nn(ds.astype(BF16), half_mask(qa, half))
        dq[:, sl] = dqp.astype(BF16)
        dk[:, sl] = dkp.astype(BF16)
        dv[:, sl] = dvp.astype(BF16)
        return c
    lax.fori_loop(0, PAIRS, pair, 0)

def self_backward(order, own, q_nat, k_nat, v_nat, do_slot, do_own, stat_slot, stat_own, table, back_table):
    length, rows = q_nat.shape[0], do_own.shape[0]
    def kern(order, own, q_nat, k_nat, v_nat, do_slot, do_own, stat_slot, stat_own, table, back_table, *rest):
        self_backward_kernel(order, own, q_nat, k_nat, v_nat, do_slot, do_own, stat_slot, stat_own, None, table, back_table, *rest)
    return pl.pallas_call(
        kern,
        name="self_backward",
        out_shape=[sds((rows, D), BF16)] * 3 + [sds((16, 2 * length), F32)],
        in_specs=[smem_spec()] * 2 + [full_spec()] * 9,
        out_specs=[full_spec()] * 4,
        scratch_shapes=[pltpu.SMEM((length // PIECE,), jnp.int32)] + [pltpu.VMEM((rows, D), BF16)] * 3
        + [pltpu.VMEM((length, D), BF16), pltpu.VMEM((length, LANES), F32), pltpu.VMEM((LANES, length), F32), pltpu.VMEM((2, 8, 2 * length), F32)],
        compiler_params=pltpu.CompilerParams(vmem_limit_bytes=VMEM_LIMIT),
    )(order, own, q_nat, k_nat, v_nat, do_slot, do_own, stat_slot, stat_own, table, back_table)


def norm_scale(values, gain_vector):
    return (
        values
        * lax.rsqrt(jnp.mean(values * values, axis=-1, keepdims=True) + EPSILON)
        * gain_vector
    )


def smooth_gate(values):
    return jax.nn.gelu(values, approximate=True)


def project(operand, matrix):
    return jnp.dot(operand, matrix, preferred_element_type=jnp.float32)


def project_back(operand, matrix):
    return jnp.einsum("sra,ba->srb", operand, matrix, preferred_element_type=jnp.float32)


def weight_grad(inputs, upstream):
    return jnp.einsum("sra,srb->ab", inputs, upstream, preferred_element_type=jnp.float32)


def to_heads(matrix):
    return matrix.reshape(matrix.shape[0], matrix.shape[1], HEADS, HEAD_DIM)


def heads_first(matrix):
    return jnp.transpose(to_heads(matrix), (0, 2, 1, 3))


def from_heads(tensor):
    return jnp.transpose(tensor, (0, 2, 1, 3)).reshape(
        tensor.shape[0], tensor.shape[2], HEADS * HEAD_DIM
    )


def block_scores(queries, keys_all, values_all, extras, offset):
    key_block = lax.dynamic_slice_in_dim(keys_all, offset, KBLK, 1)
    value_block = lax.dynamic_slice_in_dim(values_all, offset, KBLK, 1)
    added_bias, visible, bucket_indicator = extras(offset)
    scores = (
        jnp.einsum("sqhd,skhd->shqk", queries, key_block, preferred_element_type=jnp.float32)
        + added_bias
    )
    block_maximum = jnp.max(jnp.where(visible, scores, NEGATIVE), axis=-1)
    weights = jnp.exp(jnp.where(visible, scores - block_maximum[..., None], NEGATIVE))
    return (key_block, value_block, bucket_indicator, block_maximum, weights)


def attend_forward(queries, keys_all, values_all, extras):
    block_count = keys_all.shape[1] // KBLK

    def single_block_tile(carried, block_index):
        key_block, value_block, bucket_indicator, block_maximum, weights = block_scores(
            queries, keys_all, values_all, extras, block_index * KBLK
        )
        numerator = jnp.einsum(
            "shqk,skhd->shqd",
            weights.astype(jnp.bfloat16),
            value_block,
            preferred_element_type=jnp.float32,
        )
        return (carried, (block_maximum, jnp.sum(weights, axis=-1), numerator))

    ignored, stacked = lax.scan(
        single_block_tile, jnp.zeros((), jnp.float32), jnp.arange(block_count, dtype=jnp.int32)
    )
    block_maximum, block_sum, numerator = stacked
    row_maximum = jnp.max(block_maximum, axis=0)
    rescale = jnp.exp(block_maximum - row_maximum)
    row_total = jnp.sum(rescale * block_sum, axis=0)
    output = jnp.sum(rescale[..., None] * numerator, axis=0) / row_total[..., None]
    return (output, row_maximum, row_total)


def attend_backward(
    queries, keys_all, values_all, extras, grad_out, output, row_maximum, row_total
):
    block_count = keys_all.shape[1] // KBLK
    grad_wide = grad_out.astype(jnp.float32)
    row_dot = jnp.sum(grad_wide * output, axis=-1)
    scaled = grad_wide / row_total[..., None]
    sum_weight = -row_dot / row_total
    initial = (
        jnp.zeros(queries.shape, jnp.float32),
        jnp.zeros(keys_all.shape, jnp.float32),
        jnp.zeros(values_all.shape, jnp.float32),
        jnp.zeros((BUCKETS, HEADS), jnp.float32),
    )

    def single_block_tile(carried, block_index):
        grad_query, grad_keys, grad_values, grad_bias = carried
        offset = block_index * KBLK
        key_block, value_block, bucket_indicator, block_maximum, weights = block_scores(
            queries, keys_all, values_all, extras, offset
        )
        rescale = jnp.exp(block_maximum - row_maximum)
        grad_numerator = (scaled * rescale[..., None]).astype(jnp.bfloat16)
        grad_weights = (
            jnp.einsum(
                "shqd,skhd->shqk", grad_numerator, value_block, preferred_element_type=jnp.float32
            )
            + (sum_weight * rescale)[..., None]
        )
        grad_scores = weights * grad_weights
        gradient_bfloat_cast = grad_scores.astype(jnp.bfloat16)
        grad_query = grad_query + jnp.einsum(
            "shqk,skhd->sqhd", gradient_bfloat_cast, key_block, preferred_element_type=jnp.float32
        )
        key_part = jnp.einsum(
            "shqk,sqhd->skhd", gradient_bfloat_cast, queries, preferred_element_type=jnp.float32
        )
        value_part = jnp.einsum(
            "shqk,shqd->skhd",
            weights.astype(jnp.bfloat16),
            grad_numerator,
            preferred_element_type=jnp.float32,
        )
        grad_keys = lax.dynamic_update_slice_in_dim(grad_keys, key_part, offset, 1)
        grad_values = lax.dynamic_update_slice_in_dim(grad_values, value_part, offset, 1)
        if bucket_indicator is not None:
            remainder_portion = (grad_scores - gradient_bfloat_cast.astype(jnp.float32)).astype(
                jnp.bfloat16
            )
            grad_bias = (
                grad_bias
                + jnp.einsum(
                    "uljf,pjf->pl",
                    gradient_bfloat_cast,
                    bucket_indicator,
                    preferred_element_type=jnp.float32,
                )
                + jnp.einsum(
                    "uljf,pjf->pl",
                    remainder_portion,
                    bucket_indicator,
                    preferred_element_type=jnp.float32,
                )
            )
        return ((grad_query, grad_keys, grad_values, grad_bias), None)

    result, ignored = lax.scan(single_block_tile, initial, jnp.arange(block_count, dtype=jnp.int32))
    return result


def streamed_shards(
    tokens,
    memory,
    piece_order,
    bucket_table,
    passage_lengths,
    self_gain,
    cross_gain,
    hidden_gain,
    position_bias,
    self_query,
    self_attention_key,
    self_value,
    self_output,
    cross_query,
    cross_key,
    cross_value,
    cross_output,
    hidden_in,
    hidden_out,
    grad_output,
):
    (
        gain_one,
        gain_two,
        gain_three,
        position_bias_lookup,
        query_full,
        key_full,
        value_full,
        output_full,
        cross_query_full,
        cross_key_full,
        cross_value_full,
        cross_output_full,
        inner_full,
        outer_full,
    ) = (
        lax.all_gather(self_gain, "fsdp", axis=0, tiled=True),
        lax.all_gather(cross_gain, "fsdp", axis=0, tiled=True),
        lax.all_gather(hidden_gain, "fsdp", axis=0, tiled=True),
        lax.all_gather(position_bias, "fsdp", axis=0, tiled=True),
        lax.all_gather(self_query, "fsdp", axis=0, tiled=True),
        lax.all_gather(self_attention_key, "fsdp", axis=0, tiled=True),
        lax.all_gather(self_value, "fsdp", axis=0, tiled=True),
        lax.all_gather(self_output, "fsdp", axis=0, tiled=True),
        lax.all_gather(cross_query, "fsdp", axis=0, tiled=True),
        lax.all_gather(cross_key, "fsdp", axis=0, tiled=True),
        lax.all_gather(cross_value, "fsdp", axis=0, tiled=True),
        lax.all_gather(cross_output, "fsdp", axis=0, tiled=True),
        lax.all_gather(hidden_in, "fsdp", axis=0, tiled=True),
        lax.all_gather(hidden_out, "fsdp", axis=0, tiled=True),
    )
    gain_one = gain_one.astype(jnp.float32)
    gain_two = gain_two.astype(jnp.float32)
    gain_three = gain_three.astype(jnp.float32)
    sequence_count = tokens.shape[0]
    local_rows = tokens.shape[1]
    sequence_length = (bucket_table.shape[0] + 1) // 2
    memory_length = PSG * PLEN
    piece_offsets = jnp.arange(PIECE, dtype=jnp.int32)
    local_pieces = lax.dynamic_slice_in_dim(
        piece_order, lax.axis_index("ctx") * (local_rows // PIECE), local_rows // PIECE
    )
    query_position = (local_pieces[:, None] * PIECE + piece_offsets[None, :]).reshape(local_rows)
    key_position = (piece_order[:, None] * PIECE + piece_offsets[None, :]).reshape(sequence_length)
    bucket_numbers = jnp.arange(BUCKETS, dtype=jnp.int32)

    def self_extras(offset):
        key_block_position = lax.dynamic_slice_in_dim(key_position, offset, KBLK)
        relative_bucket_index = jnp.take(
            bucket_table,
            key_block_position[None, :] - query_position[:, None] + sequence_length - 1,
        )
        bucket_indicator = (
            relative_bucket_index[None, :, :] == bucket_numbers[:, None, None]
        ).astype(jnp.bfloat16)
        added_bias = jnp.einsum(
            "lvj,lf->fvj",
            bucket_indicator,
            position_bias_lookup,
            preferred_element_type=jnp.float32,
        )
        visible = key_block_position[None, :] // BLOCK <= query_position[:, None] // BLOCK
        return (added_bias, visible, bucket_indicator)

    slot_numbers = jnp.arange(PLEN, dtype=jnp.int32)
    memory_valid = (passage_lengths[:, :, None] > slot_numbers[None, None, :]).reshape(
        sequence_count, memory_length
    )

    def cross_extras(offset):
        visible = lax.dynamic_slice_in_dim(memory_valid, offset, KBLK, 1)[:, None, None, :]
        return (0.0, visible, None)

    inputs_wide = tokens.astype(jnp.float32)
    normed_one = norm_scale(inputs_wide, gain_one).astype(jnp.bfloat16)
    queries_one = project(normed_one, query_full).astype(jnp.bfloat16)
    keys_local = project(normed_one, key_full).astype(jnp.bfloat16)
    values_local = project(normed_one, value_full).astype(jnp.bfloat16)
    memory_keys = project(memory, cross_key_full).astype(jnp.bfloat16)
    memory_values = project(memory, cross_value_full).astype(jnp.bfloat16)
    keys_all, values_all, memory_keys_all, memory_values_all = (
        lax.all_gather(keys_local, "ctx", axis=1, tiled=True),
        lax.all_gather(values_local, "ctx", axis=1, tiled=True),
        lax.all_gather(memory_keys, "ctx", axis=1, tiled=True),
        lax.all_gather(memory_values, "ctx", axis=1, tiled=True),
    )
    output_one, maximum_one, total_one = attend_forward(
        to_heads(queries_one), to_heads(keys_all), to_heads(values_all), self_extras
    )
    attended_one = from_heads(output_one).astype(jnp.bfloat16)
    hidden_one = inputs_wide + project(attended_one, output_full)
    normed_two = norm_scale(hidden_one, gain_two).astype(jnp.bfloat16)
    queries_two = project(normed_two, cross_query_full).astype(jnp.bfloat16)
    output_two, maximum_two, total_two = attend_forward(
        to_heads(queries_two), to_heads(memory_keys_all), to_heads(memory_values_all), cross_extras
    )
    attended_two = from_heads(output_two).astype(jnp.bfloat16)
    hidden_two = hidden_one + project(attended_two, cross_output_full)
    normed_three = norm_scale(hidden_two, gain_three).astype(jnp.bfloat16)
    before_gate = project(normed_three, inner_full)
    gated_wide, gate_pullback = jax.vjp(smooth_gate, before_gate)
    activated = gated_wide.astype(jnp.bfloat16)
    layer_output = (hidden_two + project(activated, outer_full)).astype(jnp.bfloat16)
    grad_wide = grad_output.astype(jnp.float32)
    grad_outer = weight_grad(activated, grad_output)
    grad_activated = project_back(grad_output, outer_full)
    grad_before = gate_pullback(grad_activated)[0].astype(jnp.bfloat16)
    grad_inner = weight_grad(normed_three, grad_before)
    ignored, norm_pullback = jax.vjp(norm_scale, hidden_two, gain_three)
    grad_hidden_part, grad_gain_three = norm_pullback(project_back(grad_before, inner_full))
    grad_hidden_two = grad_wide + grad_hidden_part
    branch_two = grad_hidden_two.astype(jnp.bfloat16)
    grad_cross_output = weight_grad(attended_two, branch_two)
    grad_attended_two = project_back(branch_two, cross_output_full).astype(jnp.bfloat16)
    keys_back, values_back, memory_keys_back, memory_values_back = (
        keys_all,
        values_all,
        memory_keys_all,
        memory_values_all,
    )
    grad_query_two, grad_memory_keys, grad_memory_values, unused_bias = attend_backward(
        to_heads(queries_two),
        to_heads(memory_keys_back),
        to_heads(memory_values_back),
        cross_extras,
        heads_first(grad_attended_two),
        output_two,
        maximum_two,
        total_two,
    )
    memory_key_sum, memory_value_sum = (
        lax.psum_scatter(
            grad_memory_keys.reshape(sequence_count, memory_length, D),
            "ctx",
            scatter_dimension=1,
            tiled=True,
        ),
        lax.psum_scatter(
            grad_memory_values.reshape(sequence_count, memory_length, D),
            "ctx",
            scatter_dimension=1,
            tiled=True,
        ),
    )
    memory_key_rounded = memory_key_sum.astype(jnp.bfloat16)
    memory_value_rounded = memory_value_sum.astype(jnp.bfloat16)
    query_two_rounded = grad_query_two.reshape(sequence_count, local_rows, D).astype(jnp.bfloat16)
    grad_cross_query = weight_grad(normed_two, query_two_rounded)
    grad_cross_key = weight_grad(memory, memory_key_rounded)
    grad_cross_value = weight_grad(memory, memory_value_rounded)
    grad_memory = (
        project_back(memory_key_rounded, cross_key_full)
        + project_back(memory_value_rounded, cross_value_full)
    ).astype(jnp.bfloat16)
    ignored, norm_pullback = jax.vjp(norm_scale, hidden_one, gain_two)
    grad_hidden_part, grad_gain_two = norm_pullback(
        project_back(query_two_rounded, cross_query_full)
    )
    grad_hidden_one = grad_hidden_two + grad_hidden_part
    branch_one = grad_hidden_one.astype(jnp.bfloat16)
    grad_self_output = weight_grad(attended_one, branch_one)
    grad_attended_one = project_back(branch_one, output_full).astype(jnp.bfloat16)
    grad_query_one, grad_keys_all, grad_values_all, grad_bias = attend_backward(
        to_heads(queries_one),
        to_heads(keys_back),
        to_heads(values_back),
        self_extras,
        heads_first(grad_attended_one),
        output_one,
        maximum_one,
        total_one,
    )
    key_sum, value_sum = (
        lax.psum_scatter(
            grad_keys_all.reshape(sequence_count, sequence_length, D),
            "ctx",
            scatter_dimension=1,
            tiled=True,
        ),
        lax.psum_scatter(
            grad_values_all.reshape(sequence_count, sequence_length, D),
            "ctx",
            scatter_dimension=1,
            tiled=True,
        ),
    )
    query_one_rounded = grad_query_one.reshape(sequence_count, local_rows, D).astype(jnp.bfloat16)
    first_key_bfloat_cast = key_sum.astype(jnp.bfloat16)
    value_one_rounded = value_sum.astype(jnp.bfloat16)
    grad_self_query = weight_grad(normed_one, query_one_rounded)
    grad_self_key = weight_grad(normed_one, first_key_bfloat_cast)
    grad_self_value = weight_grad(normed_one, value_one_rounded)
    grad_normed_one = (
        project_back(query_one_rounded, query_full)
        + project_back(first_key_bfloat_cast, key_full)
        + project_back(value_one_rounded, value_full)
    )
    ignored, norm_pullback = jax.vjp(norm_scale, inputs_wide, gain_one)
    grad_input_part, grad_gain_one = norm_pullback(grad_normed_one)
    grad_tokens = (grad_hidden_one + grad_input_part).astype(jnp.bfloat16)
    (
        shard_gain_one,
        shard_gain_two,
        shard_gain_three,
        shard_bias,
        shard_query,
        shard_key,
        shard_value,
        shard_output,
        shard_cross_query,
        shard_cross_key,
        shard_cross_value,
        shard_cross_output,
        shard_inner,
        shard_outer,
    ) = (
        lax.psum_scatter(
            grad_gain_one.astype(jnp.bfloat16), "fsdp", scatter_dimension=0, tiled=True
        ).astype(jnp.float32),
        lax.psum_scatter(
            grad_gain_two.astype(jnp.bfloat16), "fsdp", scatter_dimension=0, tiled=True
        ).astype(jnp.float32),
        lax.psum_scatter(
            grad_gain_three.astype(jnp.bfloat16), "fsdp", scatter_dimension=0, tiled=True
        ).astype(jnp.float32),
        lax.psum_scatter(
            grad_bias.astype(jnp.bfloat16), "fsdp", scatter_dimension=0, tiled=True
        ).astype(jnp.float32),
        lax.psum_scatter(
            grad_self_query.astype(jnp.bfloat16), "fsdp", scatter_dimension=0, tiled=True
        ).astype(jnp.float32),
        lax.psum_scatter(
            grad_self_key.astype(jnp.bfloat16), "fsdp", scatter_dimension=0, tiled=True
        ).astype(jnp.float32),
        lax.psum_scatter(
            grad_self_value.astype(jnp.bfloat16), "fsdp", scatter_dimension=0, tiled=True
        ).astype(jnp.float32),
        lax.psum_scatter(
            grad_self_output.astype(jnp.bfloat16), "fsdp", scatter_dimension=0, tiled=True
        ).astype(jnp.float32),
        lax.psum_scatter(
            grad_cross_query.astype(jnp.bfloat16), "fsdp", scatter_dimension=0, tiled=True
        ).astype(jnp.float32),
        lax.psum_scatter(
            grad_cross_key.astype(jnp.bfloat16), "fsdp", scatter_dimension=0, tiled=True
        ).astype(jnp.float32),
        lax.psum_scatter(
            grad_cross_value.astype(jnp.bfloat16), "fsdp", scatter_dimension=0, tiled=True
        ).astype(jnp.float32),
        lax.psum_scatter(
            grad_cross_output.astype(jnp.bfloat16), "fsdp", scatter_dimension=0, tiled=True
        ).astype(jnp.float32),
        lax.psum_scatter(
            grad_inner.astype(jnp.bfloat16), "fsdp", scatter_dimension=0, tiled=True
        ).astype(jnp.float32),
        lax.psum_scatter(
            grad_outer.astype(jnp.bfloat16), "fsdp", scatter_dimension=0, tiled=True
        ).astype(jnp.float32),
    )
    (
        total_gain_one,
        total_gain_two,
        total_gain_three,
        total_bias,
        total_query,
        total_key,
        total_value,
        total_output,
        total_cross_query,
        total_cross_key,
        total_cross_value,
        total_cross_output,
        total_inner,
        total_outer,
    ) = lax.psum(
        (
            shard_gain_one,
            shard_gain_two,
            shard_gain_three,
            shard_bias,
            shard_query,
            shard_key,
            shard_value,
            shard_output,
            shard_cross_query,
            shard_cross_key,
            shard_cross_value,
            shard_cross_output,
            shard_inner,
            shard_outer,
        ),
        "ctx",
    )
    return (
        layer_output,
        grad_tokens,
        grad_memory,
        total_gain_one,
        total_gain_two,
        total_gain_three,
        total_bias,
        total_query,
        total_key,
        total_value,
        total_output,
        total_cross_query,
        total_cross_key,
        total_cross_value,
        total_cross_output,
        total_inner,
        total_outer,
    )


def norm_back(x, gain, dy):
    r = lax.rsqrt(jnp.mean(x * x, axis=-1, keepdims=True) + EPSILON)
    gdy = gain * dy
    dx = r * gdy - x * (r * r * r) * jnp.mean(x * gdy, axis=-1, keepdims=True)
    return dx, jnp.sum(dy * x * r, axis=0)


def gather(x, axis_name, axis=0):
    return lax.all_gather(x, axis_name, axis=axis, tiled=True)


def scatter(x, axis_name, axis=0):
    return lax.psum_scatter(x, axis_name, scatter_dimension=axis, tiled=True)


def shards(
    tokens,
    memory,
    piece_order,
    bucket_table,
    passage_lengths,
    self_gain,
    cross_gain,
    hidden_gain,
    position_bias,
    self_query,
    self_attention_key,
    self_value,
    self_output,
    cross_query,
    cross_key,
    cross_value,
    cross_output,
    hidden_in,
    hidden_out,
    grad_output,
):
    tok, mem, grad = tokens[0], memory[0], grad_output[0]
    rows, slots = tok.shape[0], mem.shape[0]
    length = (bucket_table.shape[0] + 1) // 2
    peers = length // rows
    index = lax.axis_index("ctx")
    own = lax.dynamic_slice_in_dim(piece_order, index * (rows // PIECE), rows // PIECE)
    tok_all = gather(tok, "ctx")
    w_self = gather(jnp.concatenate([self_query, self_attention_key, self_value], 1), "fsdp")
    w_mid = gather(jnp.concatenate([self_output, cross_query], 1), "fsdp")
    w_mem = gather(jnp.concatenate([cross_key, cross_value], 1), "fsdp")
    w_co = gather(cross_output, "fsdp")
    gains = gather(jnp.stack([self_gain, cross_gain, hidden_gain]), "fsdp", 1).astype(F32)
    bias_rows_all = gather(position_bias, "fsdp")
    w_in = lax.all_to_all(hidden_in, "fsdp", split_axis=1, concat_axis=0, tiled=True)
    wo, wq2 = w_mid[:, :D], w_mid[:, D:]
    buckets = jnp.arange(BUCKETS, dtype=jnp.int32)[:, None]
    hot = (bucket_table[None, :] == buckets).astype(BF16)
    hot = jnp.pad(hot, ((0, 0), (0, 1)))
    hot_back = jnp.pad(hot[:, -2::-1], ((0, 0), (0, 1)))
    spread = lambda x: jnp.pad(jnp.einsum("lr,lh->hr", x, bias_rows_all, preferred_element_type=F32), ((0, 4), (0, 0)))
    ahead, behind = bias_tables(spread(hot), spread(hot_back))
    q1_nat, k1_nat, v1_nat, o1, h1, a1, a2, q2, lse1 = self_forward(
        piece_order, own, tok_all, tok, w_self, jnp.pad(gains, ((0, 5), (0, 0))), ahead, wo, wq2
    )
    kv2 = project(mem, w_mem).astype(BF16)
    k2, v2 = kv2[:, :D], kv2[:, D:]
    slot = index * slots + jnp.arange(slots, dtype=jnp.int32)
    hidden = jnp.where(slot % PLEN < jnp.take(passage_lengths[0], slot // PLEN), 0.0, NEGATIVE)
    q2_all = gather(q2, "ctx")
    part, part_lse = cross_forward(q2_all, k2, v2, hidden[None, :])
    swap = lambda x: lax.all_to_all(x.reshape(peers, rows, x.shape[-1]), "ctx", 0, 0)
    part, part_lse = swap(part), swap(part_lse)[:, :, :HEADS]
    top = jnp.max(part_lse, axis=0)
    share = jnp.exp(part_lse - top)
    lse2 = top + jnp.log(jnp.sum(share, axis=0))
    share = share / jnp.sum(share, axis=0)
    out2 = jnp.sum(jnp.repeat(share, HEAD_DIM, axis=2) * part.astype(F32), axis=0)
    o2 = out2.astype(BF16)
    h2 = h1 + project(o2, w_co)
    a3 = norm_scale(h2, gains[2]).astype(BF16)
    a3_all, g_all = gather(a3, "fsdp"), gather(grad, "fsdp")
    pre = project(a3_all, w_in)
    act, pullback = jax.vjp(smooth_gate, pre)
    act = act.astype(BF16)
    out_part = project(act, hidden_out)
    dpre = pullback(nt(g_all, hidden_out))[0].astype(BF16)
    da3_part = nt(dpre, w_in)
    da3 = scatter(da3_part.astype(BF16), "fsdp").astype(F32)
    layer_output = (h2 + scatter(out_part.astype(BF16), "fsdp").astype(F32)).astype(BF16)
    g_out = tn(act, g_all)
    g_in = lax.all_to_all(tn(a3_all, dpre).astype(BF16), "fsdp", split_axis=0, concat_axis=1, tiled=True)
    dx, gg3 = norm_back(h2, gains[2], da3)
    dh2 = grad.astype(F32) + dx
    branch2 = dh2.astype(BF16)
    do2 = nt(branch2, w_co).astype(BF16)
    delta = lambda d, o: jnp.sum((d.astype(F32) * o).reshape(rows, HEADS, HEAD_DIM), axis=2)
    pad4 = lambda x: jnp.pad(x, ((0, 0), (0, 4)))
    stat2 = jnp.concatenate([pad4(lse2), pad4(delta(do2, out2))], 1)
    do2_all = gather(do2, "ctx")
    stat2_all = gather(stat2.T, "ctx", 1)
    dq2_part, dk2, dv2 = cross_backward(q2_all, do2_all, stat2_all, k2, v2, hidden[:, None])
    dq2 = scatter(dq2_part, "ctx").astype(BF16)
    dx, gg2 = norm_back(h1, gains[1], nt(dq2, wq2))
    dh1 = dh2 + dx
    branch1 = dh1.astype(BF16)
    do1 = nt(branch1, wo).astype(BF16)
    stat1 = jnp.pad(jnp.concatenate([lse1[:, :16], pad4(delta(do1, o1.astype(F32)))], 1), ((0, 0), (0, LANES - 32)))
    do1_all = gather(do1, "ctx")
    stat1_all = gather(stat1, "ctx")
    dq1, dk1, dv1, diag = self_backward(
        piece_order, own, q1_nat, k1_nat, v1_nat, do1_all, do1, stat1_all, stat1, ahead, behind
    )
    g_bias = jnp.einsum(
        "hr,lr->lh", diag[:HEADS], hot.astype(F32), precision=lax.Precision.HIGHEST, preferred_element_type=F32
    )
    da1 = nt(dq1, w_self[:, :D]) + nt(dk1, w_self[:, D : 2 * D]) + nt(dv1, w_self[:, 2 * D :])
    tok_wide = tok.astype(F32)
    dx, gg1 = norm_back(tok_wide, gains[0], da1)
    grad_tokens = (dh1 + dx).astype(BF16)
    grad_memory = (nt(dk2, w_mem[:, :D]) + nt(dv2, w_mem[:, D:])).astype(BF16)
    full = jnp.concatenate(
        [
            tn(a1, dq1),
            tn(a1, dk1),
            tn(a1, dv1),
            tn(o1, branch1),
            tn(a2, dq2),
            tn(mem, dk2),
            tn(mem, dv2),
            tn(o2, branch2),
        ],
        1,
    ).astype(BF16)
    mine = scatter(full, "fsdp")
    quarter = mine.shape[0]
    mine = jnp.concatenate([mine, g_in, g_out.astype(BF16).reshape(quarter, -1)], 1)
    total = lax.psum(mine, "ctx").astype(F32)
    cut = lambda i: total[:, i * D : (i + 1) * D]
    small = jnp.concatenate([jnp.stack([gg1, gg2, gg3]), jnp.pad(g_bias.T, ((0, 0), (0, D - BUCKETS)))], 0)
    small = lax.psum(small, ("ctx", "fsdp"))
    f = lax.axis_index("fsdp")
    gain = lambda i: lax.dynamic_slice_in_dim(small[i], f * quarter, quarter)
    eighth = position_bias.shape[0]
    bias_out = lax.dynamic_slice_in_dim(small[3:].T, f * eighth, eighth)
    return (
        layer_output[None],
        grad_tokens[None],
        grad_memory[None],
        gain(0),
        gain(1),
        gain(2),
        bias_out,
        *[cut(i) for i in range(8)],
        total[:, 8 * D : 12 * D],
        total[:, 12 * D :].reshape(-1, D),
    )


def pick(*arrays):
    resident = (arrays[3].shape[0] + 1) // 2 <= RESIDENT_ROWS
    return (shards if resident else streamed_shards)(*arrays)


def solution(mesh):
    return jax.shard_map(
        pick,
        mesh=mesh,
        in_specs=(
            P("fsdp", "ctx", None),
            P("fsdp", "ctx", None),
            P(),
            P(),
            P("fsdp", None),
            P("fsdp"),
            P("fsdp"),
            P("fsdp"),
            P("fsdp", None),
            P("fsdp", None),
            P("fsdp", None),
            P("fsdp", None),
            P("fsdp", None),
            P("fsdp", None),
            P("fsdp", None),
            P("fsdp", None),
            P("fsdp", None),
            P("fsdp", None),
            P("fsdp", None),
            P("fsdp", "ctx", None),
        ),
        out_specs=(
            P("fsdp", "ctx", None),
            P("fsdp", "ctx", None),
            P("fsdp", "ctx", None),
            P("fsdp"),
            P("fsdp"),
            P("fsdp"),
            P("fsdp", None),
            P("fsdp", None),
            P("fsdp", None),
            P("fsdp", None),
            P("fsdp", None),
            P("fsdp", None),
            P("fsdp", None),
            P("fsdp", None),
            P("fsdp", None),
            P("fsdp", None),
            P("fsdp", None),
        ),
        check_vma=False,
    )
```

```python
import functools

import jax
import jax.numpy as jnp
from jax import lax
from jax.experimental import pallas as pl
from jax.experimental.pallas import tpu as pltpu
from jax.sharding import PartitionSpec as P

D = 768
HEADS = 12
PAIRS = HEADS // 2
HEAD_DIM = 64
PIECE = 64
BLOCK = 256
PLEN = 256
KBLK = 512
PSG = 20
BUCKETS = 32
RESIDENT_ROWS = 1024
LANES = 128
EPSILON = 1e-06
NEGATIVE = -1e30
F32 = jnp.float32
BF16 = jnp.bfloat16
VMEM_LIMIT = 60 * 2**20

def nn(a, b):
    return lax.dot_general(a, b, (((1,), (0,)), ((), ())), preferred_element_type=F32)
def nt(a, b):
    return lax.dot_general(a, b, (((1,), (1,)), ((), ())), preferred_element_type=F32)
def tn(a, b):
    return lax.dot_general(a, b, (((0,), (0,)), ((), ())), preferred_element_type=F32)

def normed(x, gain):
    return x * lax.rsqrt(jnp.mean(x * x, axis=-1, keepdims=True) + EPSILON) * gain

def half_mask(x, half):
    lane = lax.broadcasted_iota(jnp.int32, x.shape, 1) // HEAD_DIM
    return jnp.where(lane == half, x, jnp.zeros_like(x))

def lanes_of(pair):
    return pl.ds(pl.multiple_of(pair * LANES, LANES), LANES)

def shear(x, sign):
    row = lax.broadcasted_iota(jnp.int32, x.shape, 0)
    for bit in (1, 2, 4):
        x = jnp.where(row & bit != 0, pltpu.roll(x, (sign * bit) % x.shape[1], 1), x)
    return x

def bias_tables_kernel(table, back_table, ahead, behind):
    full = table.shape[1]
    def head(h, c):
        for src, out in ((table, ahead), (back_table, behind)):
            base = shear(pltpu.roll(jnp.broadcast_to(src[pl.ds(h, 1), :], (8, full)), 1, 1), 1)
            for parity in range(2):
                for i in range(PIECE // 16):
                    both = [pltpu.roll(base, (8 * g - 64 * parity) % full, 1) if (8 * g - 64 * parity) % full else base
                            for g in (2 * i, 2 * i + 1)]
                    out[parity, h, 16 * i:16 * i + 16, :] = jnp.concatenate(both, 0).astype(BF16)
        return c
    lax.fori_loop(0, HEADS, head, 0)

def bias_tables(table, back_table):
    full = table.shape[1]
    return pl.pallas_call(
        bias_tables_kernel,
        name="bias_tables",
        out_shape=[sds((2, HEADS, PIECE, full), BF16)] * 2,
        in_specs=[full_spec()] * 2,
        out_specs=[full_spec()] * 2,
        compiler_params=pltpu.CompilerParams(vmem_limit_bytes=VMEM_LIMIT),
    )(table, back_table)

def piece_bias(tables, h, piece, length):
    start = pl.multiple_of(length - (piece + piece % 2) * PIECE, LANES)
    return tables[piece % 2, h, :, pl.ds(start, length)].astype(F32)

def bias_rows(tables, h, own, count, length):
    return jnp.concatenate([piece_bias(tables, h, own[i], length) for i in range(count)], 0)

def add_diagonals(acc, block, piece):
    rows, length = block.shape
    wide = jnp.concatenate([block, jnp.zeros((rows, LANES), F32)], axis=1)
    total = pltpu.roll(wide[0:8], LANES, 1)
    for g in range(1, rows // 8):
        total += pltpu.roll(wide[8 * g:8 * g + 8], LANES - 8 * g, 1)
    start = pl.multiple_of(length - (piece - piece % 2) * PIECE - LANES, LANES)
    where = (piece % 2, slice(None), pl.ds(start, length + LANES))
    acc[where] += total

def self_forward_kernel(order, own, tok_all, tok, w, gains, table, wo, wq2,
                        q_nat, k_nat, v_nat, o1, h1, a1, a2, q2, lse, inv, q_own):
    length = tok_all.shape[0]
    rows = tok.shape[0]
    slots, mine = length // PIECE, rows // PIECE
    for s in range(slots):
        inv[order[s]] = s
    per = BLOCK // PIECE

    def tile(t, c):
        parts = [tok_all[pl.ds(pl.multiple_of(inv[t * per + i] * PIECE, PIECE), PIECE), :] for i in range(per)]
        a = normed(jnp.concatenate(parts, 0).astype(F32), gains[0:1, :]).astype(BF16)
        dst = pl.ds(pl.multiple_of(t * BLOCK, BLOCK), BLOCK)
        for j, out in enumerate((q_nat, k_nat, v_nat)):
            out[dst, :] = nn(a, w[:, j * D:(j + 1) * D]).astype(BF16)
        return c

    lax.fori_loop(0, length // BLOCK, tile, 0)
    for i in range(mine):
        q_own[i * PIECE:(i + 1) * PIECE, :] = q_nat[pl.ds(pl.multiple_of(own[i] * PIECE, PIECE), PIECE), :]
    a1[...] = normed(tok[...].astype(F32), gains[0:1, :]).astype(BF16)
    lane = lax.broadcasted_iota(jnp.int32, (rows, length), 1)
    limit = jnp.concatenate([jnp.full((PIECE, 1), (own[i] // per + 1) * BLOCK, jnp.int32) for i in range(mine)], 0)
    visible = lane < limit
    stat_lane = lax.broadcasted_iota(jnp.int32, (rows, LANES), 1)

    def pair(p, stats):
        sl = lanes_of(p)
        q, k, v = q_own[:, sl], k_nat[:, sl], v_nat[:, sl]
        total = jnp.zeros((rows, LANES), F32)
        for half in range(2):
            h = 2 * p + half
            s = jnp.where(visible, nt(q, half_mask(k, half)) + bias_rows(table, h, own, mine, length), NEGATIVE)
            m = jnp.max(s, axis=1, keepdims=True)
            e = jnp.exp(s - m)
            l = jnp.sum(e, axis=1, keepdims=True)
            total += nn(e.astype(BF16), half_mask(v, half)) / l
            stats = jnp.where(stat_lane == h, m + jnp.log(l), stats)
        o1[:, sl] = total.astype(BF16)
        return stats

    lse[...] = lax.fori_loop(0, PAIRS, pair, jnp.zeros((rows, LANES), F32))
    h = tok[...].astype(F32) + nn(o1[...], wo[...])
    h1[...] = h
    a = normed(h, gains[1:2, :]).astype(BF16)
    a2[...] = a
    q2[...] = nn(a, wq2[...]).astype(BF16)

def full_spec():
    return pl.BlockSpec(memory_space=pltpu.VMEM)
def smem_spec():
    return pl.BlockSpec(memory_space=pltpu.SMEM)
def sds(shape, dtype):
    return jax.ShapeDtypeStruct(shape, dtype)

def self_forward(order, own, tok_all, tok, w, gains, table, wo, wq2):
    length, rows = tok_all.shape[0], tok.shape[0]
    return pl.pallas_call(
        self_forward_kernel,
        name="self_forward",
        out_shape=[sds((length, D), BF16)] * 3 + [sds((rows, D), BF16), sds((rows, D), F32), sds((rows, D), BF16),
                   sds((rows, D), BF16), sds((rows, D), BF16), sds((rows, LANES), F32)],
        in_specs=[smem_spec()] * 2 + [full_spec()] * 7,
        out_specs=[full_spec()] * 9,
        scratch_shapes=[pltpu.SMEM((length // PIECE,), jnp.int32), pltpu.VMEM((rows, D), BF16)],
        compiler_params=pltpu.CompilerParams(vmem_limit_bytes=VMEM_LIMIT),
    )(order, own, tok_all, tok, w, gains, table, wo, wq2)

def cross_forward_kernel(q_all, k2, v2, mask, o, lse):
    rows = q_all.shape[0]
    step = BLOCK
    stat_lane = lax.broadcasted_iota(jnp.int32, (step, LANES), 1)

    def tile(t, c):
        rs = pl.ds(pl.multiple_of(t * step, step), step)
        def pair(p, stats):
            sl = lanes_of(p)
            q, k, v = q_all[rs, sl], k2[:, sl], v2[:, sl]
            total = jnp.zeros((step, LANES), F32)
            for half in range(2):
                s = nt(q, half_mask(k, half)) + mask[...]
                m = jnp.max(s, axis=1, keepdims=True)
                e = jnp.exp(s - m)
                l = jnp.sum(e, axis=1, keepdims=True)
                total += nn(e.astype(BF16), half_mask(v, half)) / l
                stats = jnp.where(stat_lane == 2 * p + half, m + jnp.log(l), stats)
            o[rs, sl] = total.astype(BF16)
            return stats
        lse[rs, :] = lax.fori_loop(0, PAIRS, pair, jnp.zeros((step, LANES), F32))
        return c
    lax.fori_loop(0, rows // step, tile, 0)

def cross_forward(q_all, k2, v2, mask):
    rows = q_all.shape[0]
    return pl.pallas_call(
        cross_forward_kernel,
        name="cross_forward",
        out_shape=[sds((rows, D), BF16), sds((rows, LANES), F32)],
        in_specs=[full_spec()] * 4,
        out_specs=[full_spec()] * 2,
        compiler_params=pltpu.CompilerParams(vmem_limit_bytes=VMEM_LIMIT),
    )(q_all, k2, v2, mask)

def cross_backward_kernel(q_all, do_all, stats, k2, v2, mask, dq, dk, dv):
    rows = q_all.shape[0]
    slots = k2.shape[0]
    step = BLOCK

    def pair(p, c):
        sl = lanes_of(p)
        ks = [half_mask(k2[:, sl], i) for i in range(2)]
        vs = [half_mask(v2[:, sl], i) for i in range(2)]
        def tile(t, carry):
            dkp, dvp = carry
            rs = pl.ds(pl.multiple_of(t * step, step), step)
            q, do = q_all[rs, sl], do_all[rs, sl]
            dqp = jnp.zeros((step, LANES), F32)
            for half in range(2):
                h = 2 * p + half
                qm, dom = half_mask(q, half), half_mask(do, half)
                s = nt(ks[half], q) + mask[...]
                e = jnp.exp(s - stats[pl.ds(h, 1), rs])
                dvp = dvp + nn(e.astype(BF16), dom)
                ds = (e * (nt(vs[half], do) - stats[pl.ds(16 + h, 1), rs])).astype(BF16)
                dkp = dkp + nn(ds, qm)
                dqp = dqp + tn(ds, ks[half])
            dq[rs, sl] = dqp.astype(dq.dtype)
            return dkp, dvp
        zero = jnp.zeros((slots, LANES), F32)
        dkp, dvp = lax.fori_loop(0, rows // step, tile, (zero, zero))
        dk[:, sl] = dkp.astype(BF16)
        dv[:, sl] = dvp.astype(BF16)
        return c
    lax.fori_loop(0, PAIRS, pair, 0)

def cross_backward(q_all, do_all, stats, k2, v2, mask):
    rows, slots = q_all.shape[0], k2.shape[0]
    return pl.pallas_call(
        cross_backward_kernel,
        name="cross_backward",
        out_shape=[sds((rows, D), F32), sds((slots, D), BF16), sds((slots, D), BF16)],
        in_specs=[full_spec()] * 6,
        out_specs=[full_spec()] * 3,
        compiler_params=pltpu.CompilerParams(vmem_limit_bytes=VMEM_LIMIT),
    )(q_all, do_all, stats, k2, v2, mask)

def self_backward_kernel(order, own, q_nat, k_nat, v_nat, do_slot, do_own, stat_slot, stat_own, delta_own, table, back_table,
                         dq, dk, dv, diag, inv, q_own, k_own, v_own, do_nat, stat_nat, stat_t, acc):
    length = q_nat.shape[0]
    rows = do_own.shape[0]
    full = 2 * length
    slots, mine = length // PIECE, rows // PIECE
    per = BLOCK // PIECE
    for s in range(slots):
        inv[order[s]] = s
    def move(i, c):
        src = pl.ds(pl.multiple_of(inv[i] * PIECE, PIECE), PIECE)
        dst = pl.ds(pl.multiple_of(i * PIECE, PIECE), PIECE)
        do_nat[dst, :] = do_slot[src, :]
        stat_nat[dst, :] = stat_slot[src, :]
        return c
    lax.fori_loop(0, slots, move, 0)
    for i in range(length // LANES):
        stat_t[:, i * LANES:(i + 1) * LANES] = stat_nat[i * LANES:(i + 1) * LANES, :].T
    for i in range(mine):
        src = pl.ds(pl.multiple_of(own[i] * PIECE, PIECE), PIECE)
        dst = slice(i * PIECE, (i + 1) * PIECE)
        q_own[dst, :] = q_nat[src, :]
        k_own[dst, :] = k_nat[src, :]
        v_own[dst, :] = v_nat[src, :]
    lane = lax.broadcasted_iota(jnp.int32, (rows, length), 1)
    limit = jnp.concatenate([jnp.full((PIECE, 1), (own[i] // per + 1) * BLOCK, jnp.int32) for i in range(mine)], 0)
    first = jnp.concatenate([jnp.full((PIECE, 1), (own[i] // per) * BLOCK, jnp.int32) for i in range(mine)], 0)
    visible, seen = lane < limit, lane >= first
    stat_lane = lax.broadcasted_iota(jnp.int32, (rows, LANES), 1)

    def column(h):
        return jnp.sum(jnp.where(stat_lane == h, stat_own[...], 0.0), axis=1, keepdims=True)

    diag[...] = jnp.zeros_like(diag)
    def pair(p, c):
        sl = lanes_of(p)
        q, k, v, do = q_own[:, sl], k_nat[:, sl], v_nat[:, sl], do_own[:, sl]
        kq, vq, qa, da = k_own[:, sl], v_own[:, sl], q_nat[:, sl], do_nat[:, sl]
        dqp = jnp.zeros((rows, LANES), F32)
        dkp = jnp.zeros((rows, LANES), F32)
        dvp = jnp.zeros((rows, LANES), F32)
        for half in range(2):
            h = 2 * p + half
            bias = bias_rows(table, h, own, mine, length)
            km, vm = half_mask(k, half), half_mask(v, half)
            s = jnp.where(visible, nt(q, km) + bias, NEGATIVE)
            e = jnp.exp(s - column(h))
            ds = e * (nt(do, vm) - column(16 + h))
            dqp += nn(ds.astype(BF16), km)
            acc[...] = jnp.zeros_like(acc)
            for i in range(mine):
                add_diagonals(acc, ds[i * PIECE:(i + 1) * PIECE, :], own[i])
            joined = shear(acc[0] + pltpu.roll(acc[1], full - PIECE, 1), -1)
            diag[pl.ds(h, 1), :] = jnp.sum(pltpu.roll(joined, full - 1, 1), axis=0, keepdims=True)
            bias = bias_rows(back_table, h, own, mine, length)
            s = jnp.where(seen, nt(half_mask(kq, half), qa) + bias, NEGATIVE)
            e = jnp.exp(s - stat_t[pl.ds(h, 1), :])
            dvp += nn(e.astype(BF16), half_mask(da, half))
            ds = e * (nt(half_mask(vq, half), da) - stat_t[pl.ds(16 + h, 1), :])
            dkp += nn(ds.astype(BF16), half_mask(qa, half))
        dq[:, sl] = dqp.astype(BF16)
        dk[:, sl] = dkp.astype(BF16)
        dv[:, sl] = dvp.astype(BF16)
        return c
    lax.fori_loop(0, PAIRS, pair, 0)

def self_backward(order, own, q_nat, k_nat, v_nat, do_slot, do_own, stat_slot, stat_own, table, back_table):
    length, rows = q_nat.shape[0], do_own.shape[0]
    def kern(order, own, q_nat, k_nat, v_nat, do_slot, do_own, stat_slot, stat_own, table, back_table, *rest):
        self_backward_kernel(order, own, q_nat, k_nat, v_nat, do_slot, do_own, stat_slot, stat_own, None, table, back_table, *rest)
    return pl.pallas_call(
        kern,
        name="self_backward",
        out_shape=[sds((rows, D), BF16)] * 3 + [sds((16, 2 * length), F32)],
        in_specs=[smem_spec()] * 2 + [full_spec()] * 9,
        out_specs=[full_spec()] * 4,
        scratch_shapes=[pltpu.SMEM((length // PIECE,), jnp.int32)] + [pltpu.VMEM((rows, D), BF16)] * 3
        + [pltpu.VMEM((length, D), BF16), pltpu.VMEM((length, LANES), F32), pltpu.VMEM((LANES, length), F32), pltpu.VMEM((2, 8, 2 * length), F32)],
        compiler_params=pltpu.CompilerParams(vmem_limit_bytes=VMEM_LIMIT),
    )(order, own, q_nat, k_nat, v_nat, do_slot, do_own, stat_slot, stat_own, table, back_table)


def norm_scale(values, gain_vector):
    return (
        values
        * lax.rsqrt(jnp.mean(values * values, axis=-1, keepdims=True) + EPSILON)
        * gain_vector
    )


def smooth_gate(values):
    return jax.nn.gelu(values, approximate=True)


def project(operand, matrix):
    return jnp.dot(operand, matrix, preferred_element_type=jnp.float32)


def project_back(operand, matrix):
    return jnp.einsum("sra,ba->srb", operand, matrix, preferred_element_type=jnp.float32)


def weight_grad(inputs, upstream):
    return jnp.einsum("sra,srb->ab", inputs, upstream, preferred_element_type=jnp.float32)


def to_heads(matrix):
    return matrix.reshape(matrix.shape[0], matrix.shape[1], HEADS, HEAD_DIM)


def heads_first(matrix):
    return jnp.transpose(to_heads(matrix), (0, 2, 1, 3))


def from_heads(tensor):
    return jnp.transpose(tensor, (0, 2, 1, 3)).reshape(
        tensor.shape[0], tensor.shape[2], HEADS * HEAD_DIM
    )


def block_scores(queries, keys_all, values_all, extras, offset):
    key_block = lax.dynamic_slice_in_dim(keys_all, offset, KBLK, 1)
    value_block = lax.dynamic_slice_in_dim(values_all, offset, KBLK, 1)
    added_bias, visible, bucket_indicator = extras(offset)
    scores = (
        jnp.einsum("sqhd,skhd->shqk", queries, key_block, preferred_element_type=jnp.float32)
        + added_bias
    )
    block_maximum = jnp.max(jnp.where(visible, scores, NEGATIVE), axis=-1)
    weights = jnp.exp(jnp.where(visible, scores - block_maximum[..., None], NEGATIVE))
    return (key_block, value_block, bucket_indicator, block_maximum, weights)


def attend_forward(queries, keys_all, values_all, extras):
    block_count = keys_all.shape[1] // KBLK

    def single_block_tile(carried, block_index):
        key_block, value_block, bucket_indicator, block_maximum, weights = block_scores(
            queries, keys_all, values_all, extras, block_index * KBLK
        )
        numerator = jnp.einsum(
            "shqk,skhd->shqd",
            weights.astype(jnp.bfloat16),
            value_block,
            preferred_element_type=jnp.float32,
        )
        return (carried, (block_maximum, jnp.sum(weights, axis=-1), numerator))

    ignored, stacked = lax.scan(
        single_block_tile, jnp.zeros((), jnp.float32), jnp.arange(block_count, dtype=jnp.int32)
    )
    block_maximum, block_sum, numerator = stacked
    row_maximum = jnp.max(block_maximum, axis=0)
    rescale = jnp.exp(block_maximum - row_maximum)
    row_total = jnp.sum(rescale * block_sum, axis=0)
    output = jnp.sum(rescale[..., None] * numerator, axis=0) / row_total[..., None]
    return (output, row_maximum, row_total)


def attend_backward(
    queries, keys_all, values_all, extras, grad_out, output, row_maximum, row_total
):
    block_count = keys_all.shape[1] // KBLK
    grad_wide = grad_out.astype(jnp.float32)
    row_dot = jnp.sum(grad_wide * output, axis=-1)
    scaled = grad_wide / row_total[..., None]
    sum_weight = -row_dot / row_total
    initial = (
        jnp.zeros(queries.shape, jnp.float32),
        jnp.zeros(keys_all.shape, jnp.float32),
        jnp.zeros(values_all.shape, jnp.float32),
        jnp.zeros((BUCKETS, HEADS), jnp.float32),
    )

    def single_block_tile(carried, block_index):
        grad_query, grad_keys, grad_values, grad_bias = carried
        offset = block_index * KBLK
        key_block, value_block, bucket_indicator, block_maximum, weights = block_scores(
            queries, keys_all, values_all, extras, offset
        )
        rescale = jnp.exp(block_maximum - row_maximum)
        grad_numerator = (scaled * rescale[..., None]).astype(jnp.bfloat16)
        grad_weights = (
            jnp.einsum(
                "shqd,skhd->shqk", grad_numerator, value_block, preferred_element_type=jnp.float32
            )
            + (sum_weight * rescale)[..., None]
        )
        grad_scores = weights * grad_weights
        gradient_bfloat_cast = grad_scores.astype(jnp.bfloat16)
        grad_query = grad_query + jnp.einsum(
            "shqk,skhd->sqhd", gradient_bfloat_cast, key_block, preferred_element_type=jnp.float32
        )
        key_part = jnp.einsum(
            "shqk,sqhd->skhd", gradient_bfloat_cast, queries, preferred_element_type=jnp.float32
        )
        value_part = jnp.einsum(
            "shqk,shqd->skhd",
            weights.astype(jnp.bfloat16),
            grad_numerator,
            preferred_element_type=jnp.float32,
        )
        grad_keys = lax.dynamic_update_slice_in_dim(grad_keys, key_part, offset, 1)
        grad_values = lax.dynamic_update_slice_in_dim(grad_values, value_part, offset, 1)
        if bucket_indicator is not None:
            remainder_portion = (grad_scores - gradient_bfloat_cast.astype(jnp.float32)).astype(
                jnp.bfloat16
            )
            grad_bias = (
                grad_bias
                + jnp.einsum(
                    "uljf,pjf->pl",
                    gradient_bfloat_cast,
                    bucket_indicator,
                    preferred_element_type=jnp.float32,
                )
                + jnp.einsum(
                    "uljf,pjf->pl",
                    remainder_portion,
                    bucket_indicator,
                    preferred_element_type=jnp.float32,
                )
            )
        return ((grad_query, grad_keys, grad_values, grad_bias), None)

    result, ignored = lax.scan(single_block_tile, initial, jnp.arange(block_count, dtype=jnp.int32))
    return result


def streamed_shards(
    tokens,
    memory,
    piece_order,
    bucket_table,
    passage_lengths,
    self_gain,
    cross_gain,
    hidden_gain,
    position_bias,
    self_query,
    self_attention_key,
    self_value,
    self_output,
    cross_query,
    cross_key,
    cross_value,
    cross_output,
    hidden_in,
    hidden_out,
    grad_output,
):
    (
        gain_one,
        gain_two,
        gain_three,
        position_bias_lookup,
        query_full,
        key_full,
        value_full,
        output_full,
        cross_query_full,
        cross_key_full,
        cross_value_full,
        cross_output_full,
        inner_full,
        outer_full,
    ) = (
        lax.all_gather(self_gain, "fsdp", axis=0, tiled=True),
        lax.all_gather(cross_gain, "fsdp", axis=0, tiled=True),
        lax.all_gather(hidden_gain, "fsdp", axis=0, tiled=True),
        lax.all_gather(position_bias, "fsdp", axis=0, tiled=True),
        lax.all_gather(self_query, "fsdp", axis=0, tiled=True),
        lax.all_gather(self_attention_key, "fsdp", axis=0, tiled=True),
        lax.all_gather(self_value, "fsdp", axis=0, tiled=True),
        lax.all_gather(self_output, "fsdp", axis=0, tiled=True),
        lax.all_gather(cross_query, "fsdp", axis=0, tiled=True),
        lax.all_gather(cross_key, "fsdp", axis=0, tiled=True),
        lax.all_gather(cross_value, "fsdp", axis=0, tiled=True),
        lax.all_gather(cross_output, "fsdp", axis=0, tiled=True),
        lax.all_gather(hidden_in, "fsdp", axis=0, tiled=True),
        lax.all_gather(hidden_out, "fsdp", axis=0, tiled=True),
    )
    gain_one = gain_one.astype(jnp.float32)
    gain_two = gain_two.astype(jnp.float32)
    gain_three = gain_three.astype(jnp.float32)
    sequence_count = tokens.shape[0]
    local_rows = tokens.shape[1]
    sequence_length = (bucket_table.shape[0] + 1) // 2
    memory_length = PSG * PLEN
    piece_offsets = jnp.arange(PIECE, dtype=jnp.int32)
    local_pieces = lax.dynamic_slice_in_dim(
        piece_order, lax.axis_index("ctx") * (local_rows // PIECE), local_rows // PIECE
    )
    query_position = (local_pieces[:, None] * PIECE + piece_offsets[None, :]).reshape(local_rows)
    key_position = (piece_order[:, None] * PIECE + piece_offsets[None, :]).reshape(sequence_length)
    bucket_numbers = jnp.arange(BUCKETS, dtype=jnp.int32)

    def self_extras(offset):
        key_block_position = lax.dynamic_slice_in_dim(key_position, offset, KBLK)
        relative_bucket_index = jnp.take(
            bucket_table,
            key_block_position[None, :] - query_position[:, None] + sequence_length - 1,
        )
        bucket_indicator = (
            relative_bucket_index[None, :, :] == bucket_numbers[:, None, None]
        ).astype(jnp.bfloat16)
        added_bias = jnp.einsum(
            "lvj,lf->fvj",
            bucket_indicator,
            position_bias_lookup,
            preferred_element_type=jnp.float32,
        )
        visible = key_block_position[None, :] // BLOCK <= query_position[:, None] // BLOCK
        return (added_bias, visible, bucket_indicator)

    slot_numbers = jnp.arange(PLEN, dtype=jnp.int32)
    memory_valid = (passage_lengths[:, :, None] > slot_numbers[None, None, :]).reshape(
        sequence_count, memory_length
    )

    def cross_extras(offset):
        visible = lax.dynamic_slice_in_dim(memory_valid, offset, KBLK, 1)[:, None, None, :]
        return (0.0, visible, None)

    inputs_wide = tokens.astype(jnp.float32)
    normed_one = norm_scale(inputs_wide, gain_one).astype(jnp.bfloat16)
    queries_one = project(normed_one, query_full).astype(jnp.bfloat16)
    keys_local = project(normed_one, key_full).astype(jnp.bfloat16)
    values_local = project(normed_one, value_full).astype(jnp.bfloat16)
    memory_keys = project(memory, cross_key_full).astype(jnp.bfloat16)
    memory_values = project(memory, cross_value_full).astype(jnp.bfloat16)
    keys_all, values_all, memory_keys_all, memory_values_all = (
        lax.all_gather(keys_local, "ctx", axis=1, tiled=True),
        lax.all_gather(values_local, "ctx", axis=1, tiled=True),
        lax.all_gather(memory_keys, "ctx", axis=1, tiled=True),
        lax.all_gather(memory_values, "ctx", axis=1, tiled=True),
    )
    output_one, maximum_one, total_one = attend_forward(
        to_heads(queries_one), to_heads(keys_all), to_heads(values_all), self_extras
    )
    attended_one = from_heads(output_one).astype(jnp.bfloat16)
    hidden_one = inputs_wide + project(attended_one, output_full)
    normed_two = norm_scale(hidden_one, gain_two).astype(jnp.bfloat16)
    queries_two = project(normed_two, cross_query_full).astype(jnp.bfloat16)
    output_two, maximum_two, total_two = attend_forward(
        to_heads(queries_two), to_heads(memory_keys_all), to_heads(memory_values_all), cross_extras
    )
    attended_two = from_heads(output_two).astype(jnp.bfloat16)
    hidden_two = hidden_one + project(attended_two, cross_output_full)
    normed_three = norm_scale(hidden_two, gain_three).astype(jnp.bfloat16)
    before_gate = project(normed_three, inner_full)
    gated_wide, gate_pullback = jax.vjp(smooth_gate, before_gate)
    activated = gated_wide.astype(jnp.bfloat16)
    layer_output = (hidden_two + project(activated, outer_full)).astype(jnp.bfloat16)
    grad_wide = grad_output.astype(jnp.float32)
    grad_outer = weight_grad(activated, grad_output)
    grad_activated = project_back(grad_output, outer_full)
    grad_before = gate_pullback(grad_activated)[0].astype(jnp.bfloat16)
    grad_inner = weight_grad(normed_three, grad_before)
    ignored, norm_pullback = jax.vjp(norm_scale, hidden_two, gain_three)
    grad_hidden_part, grad_gain_three = norm_pullback(project_back(grad_before, inner_full))
    grad_hidden_two = grad_wide + grad_hidden_part
    branch_two = grad_hidden_two.astype(jnp.bfloat16)
    grad_cross_output = weight_grad(attended_two, branch_two)
    grad_attended_two = project_back(branch_two, cross_output_full).astype(jnp.bfloat16)
    keys_back, values_back, memory_keys_back, memory_values_back = (
        keys_all,
        values_all,
        memory_keys_all,
        memory_values_all,
    )
    grad_query_two, grad_memory_keys, grad_memory_values, unused_bias = attend_backward(
        to_heads(queries_two),
        to_heads(memory_keys_back),
        to_heads(memory_values_back),
        cross_extras,
        heads_first(grad_attended_two),
        output_two,
        maximum_two,
        total_two,
    )
    memory_key_sum, memory_value_sum = (
        lax.psum_scatter(
            grad_memory_keys.reshape(sequence_count, memory_length, D),
            "ctx",
            scatter_dimension=1,
            tiled=True,
        ),
        lax.psum_scatter(
            grad_memory_values.reshape(sequence_count, memory_length, D),
            "ctx",
            scatter_dimension=1,
            tiled=True,
        ),
    )
    memory_key_rounded = memory_key_sum.astype(jnp.bfloat16)
    memory_value_rounded = memory_value_sum.astype(jnp.bfloat16)
    query_two_rounded = grad_query_two.reshape(sequence_count, local_rows, D).astype(jnp.bfloat16)
    grad_cross_query = weight_grad(normed_two, query_two_rounded)
    grad_cross_key = weight_grad(memory, memory_key_rounded)
    grad_cross_value = weight_grad(memory, memory_value_rounded)
    grad_memory = (
        project_back(memory_key_rounded, cross_key_full)
        + project_back(memory_value_rounded, cross_value_full)
    ).astype(jnp.bfloat16)
    ignored, norm_pullback = jax.vjp(norm_scale, hidden_one, gain_two)
    grad_hidden_part, grad_gain_two = norm_pullback(
        project_back(query_two_rounded, cross_query_full)
    )
    grad_hidden_one = grad_hidden_two + grad_hidden_part
    branch_one = grad_hidden_one.astype(jnp.bfloat16)
    grad_self_output = weight_grad(attended_one, branch_one)
    grad_attended_one = project_back(branch_one, output_full).astype(jnp.bfloat16)
    grad_query_one, grad_keys_all, grad_values_all, grad_bias = attend_backward(
        to_heads(queries_one),
        to_heads(keys_back),
        to_heads(values_back),
        self_extras,
        heads_first(grad_attended_one),
        output_one,
        maximum_one,
        total_one,
    )
    key_sum, value_sum = (
        lax.psum_scatter(
            grad_keys_all.reshape(sequence_count, sequence_length, D),
            "ctx",
            scatter_dimension=1,
            tiled=True,
        ),
        lax.psum_scatter(
            grad_values_all.reshape(sequence_count, sequence_length, D),
            "ctx",
            scatter_dimension=1,
            tiled=True,
        ),
    )
    query_one_rounded = grad_query_one.reshape(sequence_count, local_rows, D).astype(jnp.bfloat16)
    first_key_bfloat_cast = key_sum.astype(jnp.bfloat16)
    value_one_rounded = value_sum.astype(jnp.bfloat16)
    grad_self_query = weight_grad(normed_one, query_one_rounded)
    grad_self_key = weight_grad(normed_one, first_key_bfloat_cast)
    grad_self_value = weight_grad(normed_one, value_one_rounded)
    grad_normed_one = (
        project_back(query_one_rounded, query_full)
        + project_back(first_key_bfloat_cast, key_full)
        + project_back(value_one_rounded, value_full)
    )
    ignored, norm_pullback = jax.vjp(norm_scale, inputs_wide, gain_one)
    grad_input_part, grad_gain_one = norm_pullback(grad_normed_one)
    grad_tokens = (grad_hidden_one + grad_input_part).astype(jnp.bfloat16)
    (
        shard_gain_one,
        shard_gain_two,
        shard_gain_three,
        shard_bias,
        shard_query,
        shard_key,
        shard_value,
        shard_output,
        shard_cross_query,
        shard_cross_key,
        shard_cross_value,
        shard_cross_output,
        shard_inner,
        shard_outer,
    ) = (
        lax.psum_scatter(
            grad_gain_one.astype(jnp.bfloat16), "fsdp", scatter_dimension=0, tiled=True
        ).astype(jnp.float32),
        lax.psum_scatter(
            grad_gain_two.astype(jnp.bfloat16), "fsdp", scatter_dimension=0, tiled=True
        ).astype(jnp.float32),
        lax.psum_scatter(
            grad_gain_three.astype(jnp.bfloat16), "fsdp", scatter_dimension=0, tiled=True
        ).astype(jnp.float32),
        lax.psum_scatter(
            grad_bias.astype(jnp.bfloat16), "fsdp", scatter_dimension=0, tiled=True
        ).astype(jnp.float32),
        lax.psum_scatter(
            grad_self_query.astype(jnp.bfloat16), "fsdp", scatter_dimension=0, tiled=True
        ).astype(jnp.float32),
        lax.psum_scatter(
            grad_self_key.astype(jnp.bfloat16), "fsdp", scatter_dimension=0, tiled=True
        ).astype(jnp.float32),
        lax.psum_scatter(
            grad_self_value.astype(jnp.bfloat16), "fsdp", scatter_dimension=0, tiled=True
        ).astype(jnp.float32),
        lax.psum_scatter(
            grad_self_output.astype(jnp.bfloat16), "fsdp", scatter_dimension=0, tiled=True
        ).astype(jnp.float32),
        lax.psum_scatter(
            grad_cross_query.astype(jnp.bfloat16), "fsdp", scatter_dimension=0, tiled=True
        ).astype(jnp.float32),
        lax.psum_scatter(
            grad_cross_key.astype(jnp.bfloat16), "fsdp", scatter_dimension=0, tiled=True
        ).astype(jnp.float32),
        lax.psum_scatter(
            grad_cross_value.astype(jnp.bfloat16), "fsdp", scatter_dimension=0, tiled=True
        ).astype(jnp.float32),
        lax.psum_scatter(
            grad_cross_output.astype(jnp.bfloat16), "fsdp", scatter_dimension=0, tiled=True
        ).astype(jnp.float32),
        lax.psum_scatter(
            grad_inner.astype(jnp.bfloat16), "fsdp", scatter_dimension=0, tiled=True
        ).astype(jnp.float32),
        lax.psum_scatter(
            grad_outer.astype(jnp.bfloat16), "fsdp", scatter_dimension=0, tiled=True
        ).astype(jnp.float32),
    )
    (
        total_gain_one,
        total_gain_two,
        total_gain_three,
        total_bias,
        total_query,
        total_key,
        total_value,
        total_output,
        total_cross_query,
        total_cross_key,
        total_cross_value,
        total_cross_output,
        total_inner,
        total_outer,
    ) = lax.psum(
        (
            shard_gain_one,
            shard_gain_two,
            shard_gain_three,
            shard_bias,
            shard_query,
            shard_key,
            shard_value,
            shard_output,
            shard_cross_query,
            shard_cross_key,
            shard_cross_value,
            shard_cross_output,
            shard_inner,
            shard_outer,
        ),
        "ctx",
    )
    return (
        layer_output,
        grad_tokens,
        grad_memory,
        total_gain_one,
        total_gain_two,
        total_gain_three,
        total_bias,
        total_query,
        total_key,
        total_value,
        total_output,
        total_cross_query,
        total_cross_key,
        total_cross_value,
        total_cross_output,
        total_inner,
        total_outer,
    )


MESH = pl.DeviceIdType.MESH
WAYS = 4


class Place:
    def __init__(self, peers):
        self.depth = peers // 2
        c, f = lax.axis_index("ctx"), lax.axis_index("fsdp")
        self.c, self.f = c, f
        self.a, self.b, self.x, self.k = c // 2, c % 2, f // 2, f % 2
        self.core = (c, self.x * 2 + 1 - self.k)
        self.across = (c, (1 - self.x) * 2 + self.k)
        self.beside = (self.a * 2 + 1 - self.b, f)

    def ahead(self, d):
        return lax.rem(self.a + d, self.depth)

    def behind(self, d):
        return lax.rem(self.a + self.depth - d, self.depth)

    def column(self, a):
        return (a * 2 + self.b, self.f)

    def group(self, d):
        return (self.c, lax.rem(self.f + d, WAYS))


def greet(targets):
    barrier = pltpu.get_barrier_semaphore()
    for target in targets:
        pl.semaphore_signal(barrier, inc=1, device_id=target, device_id_type=MESH)
    pl.semaphore_wait(barrier, len(targets))


def remote(src, dst, sems, index, target):
    return pltpu.make_async_remote_copy(
        src_ref=src,
        dst_ref=dst,
        send_sem=sems[0].at[index],
        recv_sem=sems[1].at[index],
        device_id=target,
        device_id_type=MESH,
    )


def sems(count):
    return [pltpu.SemaphoreType.DMA((count,)), pltpu.SemaphoreType.DMA((count,))]


def reduce_kernel(peers, left_index, *refs):
    n_left = len(set(left_index))
    n_mats = len(left_index)
    lefts, rights = refs[:n_left], refs[n_left : n_left + n_mats]
    g_in, g_out, small, out, small_out = refs[n_left + n_mats : n_left + n_mats + 5]
    (prod, own, sa, ra, sb, rb, sc, rc, sd, rd, tiny, tiny_in, *sem) = refs[n_left + n_mats + 5 :]
    sem_a, sem_b, sem_c, sem_d, sem_e, sem_f, sem_g, sem_t = [sem[2 * i : 2 * i + 2] for i in range(8)]
    at = Place(peers)
    depth = at.depth
    quarter, wide = out.shape[1], out.shape[2]
    half, part = wide // 2, quarter // depth
    total = out.shape[0]
    sent = []

    def go(copy):
        copy.start()
        sent.append(copy)
        return copy

    columns = lambda b: pl.ds(pl.multiple_of(b * half, LANES), half)
    shard_rows = lambda f: pl.ds(pl.multiple_of(f * quarter, quarter), quarter)
    part_rows = lambda a: pl.ds(pl.multiple_of(a * part, part), part)
    mine, theirs = columns(at.b), columns(1 - at.b)

    greet(
        [at.core, at.across, at.beside]
        + [at.column(at.ahead(d)) for d in range(1, depth)]
        + [(at.c, (1 - at.x) * 2 + 1 - at.k)]
    )

    def stage_a(i):
        prod[...] = tn(lefts[left_index[i]][...], rights[i][...])
        for x in range(2):
            own[i, x] = prod[shard_rows(x * 2 + at.k), :]
            sa[i, x] = prod[shard_rows(x * 2 + 1 - at.k), :].astype(BF16)
        go(remote(sa.at[i], ra.at[i], sem_a, i, at.core))

    def stage_b(i):
        remote(sa.at[i], ra.at[i], sem_a, i, at.core).wait_recv()
        sb[i] = (own[i, 1 - at.x] + ra[i, 1 - at.x].astype(F32)).astype(BF16)
        go(remote(sb.at[i], rb.at[i], sem_b, i, at.across))

    def stage_c(j):
        if j < n_mats:
            remote(sb.at[j], rb.at[j], sem_b, j, at.across).wait_recv()
            value = own[j, at.x] + ra[j, at.x].astype(F32) + rb[j].astype(F32)
            sc[j] = value.astype(BF16)
        go(remote(sc.at[j, :, theirs], rc.at[j], sem_c, j, at.beside))

    def stage_d(j):
        remote(sc.at[j, :, mine], rc.at[j], sem_c, j, at.beside).wait_recv()
        value = sc[j, :, mine].astype(F32) + rc[j].astype(F32)
        sd[j] = value.astype(BF16)
        for d in range(1, depth):
            go(remote(sd.at[j, part_rows(at.ahead(d))], rd.at[j, part_rows(at.a)], sem_d, j * depth + d, at.column(at.ahead(d))))

    def stage_e(j):
        value = sd[j, part_rows(at.a), :].astype(F32)
        for d in range(1, depth):
            slot = rd.at[j, part_rows(at.behind(d))]
            remote(slot, slot, sem_d, j * depth + d, at.column(at.behind(d))).wait_recv()
            value += slot[...].astype(F32)
        spot = out.at[j, part_rows(at.a), mine]
        spot[...] = value.astype(BF16)
        for d in range(1, depth):
            go(remote(spot, spot, sem_e, j * depth + d, at.column(at.ahead(d))))

    def stage_f(j):
        for d in range(1, depth):
            spot = out.at[j, part_rows(at.behind(d)), mine]
            remote(spot, spot, sem_e, j * depth + d, at.column(at.behind(d))).wait_recv()
        go(remote(out.at[j, :, mine], out.at[j, :, mine], sem_f, j, at.beside))

    def stage_g(j):
        remote(out.at[j, :, theirs], out.at[j, :, theirs], sem_f, j, at.beside).wait_recv()

    order = list(range(n_mats + WAYS, n_mats + 2 * WAYS)) + list(range(n_mats)) + list(range(n_mats, n_mats + WAYS))
    for q in range(WAYS):
        sc[n_mats + WAYS + q] = g_out[q * quarter : (q + 1) * quarter, :]
    tiny[0] = small[...]
    hops = [at.core, at.across, at.beside]
    for t in range(total + 4):
        if 4 <= t:
            stage_g(order[t - 4])
        if 3 <= t < total + 3:
            stage_f(order[t - 3])
        if 2 <= t < total + 2:
            stage_e(order[t - 2])
        if 1 <= t < total + 1:
            stage_d(order[t - 1])
        if t == total - WAYS:
            for d in range(1, WAYS):
                slot = sc.at[n_mats + lax.rem(at.f + WAYS - d, WAYS)]
                remote(slot, slot, sem_g, d, at.group(WAYS - d)).wait_recv()
        if t < total:
            stage_c(order[t])
        if 1 <= t <= n_mats:
            stage_b(t - 1)
        if t < n_mats:
            stage_a(t)
        if t == n_mats:
            sc[n_mats + at.f] = g_in[shard_rows(at.f), :]
            for d in range(1, WAYS):
                f = lax.rem(at.f + d, WAYS)
                go(remote(g_in.at[shard_rows(f)], sc.at[n_mats + at.f], sem_g, d, at.group(d)))
        if t < 4:
            if t:
                remote(tiny.at[t - 1], tiny_in.at[t - 1], sem_t, t - 1, hops[t - 1]).wait_recv()
                tiny[t] = tiny[t - 1] + tiny_in[t - 1]
            if t < 3:
                go(remote(tiny.at[t], tiny_in.at[t], sem_t, t, hops[t]))
            else:
                for d in range(1, depth):
                    go(remote(tiny.at[3], tiny_in.at[2 + d], sem_t, 2 + d, at.column(at.ahead(d))))
        if t == 4:
            value = tiny[3]
            for d in range(1, depth):
                remote(tiny.at[3], tiny_in.at[2 + d], sem_t, 2 + d, at.column(at.behind(d))).wait_recv()
                value += tiny_in[2 + d]
            small_out[...] = value
    for copy in sent:
        copy.wait_send()


def reduce_grads(peers, pairs, g_in, g_out, small):
    lefts, left_index = [], []
    for left, _ in pairs:
        for i, seen in enumerate(lefts):
            if seen is left:
                break
        else:
            lefts.append(left)
            i = len(lefts) - 1
        left_index.append(i)
    rights = [right for _, right in pairs]
    n, total = len(pairs), len(pairs) + 2 * WAYS
    width = g_in.shape[1]
    quarter, half, depth = width // WAYS, width // 2, peers // 2
    return pl.pallas_call(
        functools.partial(reduce_kernel, peers, left_index),
        name="reduce_grads",
        out_shape=[sds((total, quarter, width), BF16), sds(small.shape, F32)],
        in_specs=[full_spec()] * (len(lefts) + n + 3),
        out_specs=[full_spec()] * 2,
        scratch_shapes=[
            pltpu.VMEM((width, width), F32),
            pltpu.VMEM((n, 2, quarter, width), F32),
            pltpu.VMEM((n, 2, quarter, width), BF16),
            pltpu.VMEM((n, 2, quarter, width), BF16),
            pltpu.VMEM((n, quarter, width), BF16),
            pltpu.VMEM((n, quarter, width), BF16),
            pltpu.VMEM((total, quarter, width), BF16),
            pltpu.VMEM((total, quarter, half), BF16),
            pltpu.VMEM((total, quarter, half), BF16),
            pltpu.VMEM((total, quarter, half), BF16),
            pltpu.VMEM((4,) + small.shape, F32),
            pltpu.VMEM((3 + depth,) + small.shape, F32),
        ]
        + sems(n) + sems(n) + sems(total) + sems(total * depth) + sems(total * depth) + sems(total) + sems(WAYS) + sems(3 + depth),
        compiler_params=pltpu.CompilerParams(collective_id=0, has_side_effects=True, vmem_limit_bytes=VMEM_LIMIT),
    )(*lefts, *rights, g_in, g_out, small)


def norm_back(x, gain, dy):
    r = lax.rsqrt(jnp.mean(x * x, axis=-1, keepdims=True) + EPSILON)
    gdy = gain * dy
    dx = r * gdy - x * (r * r * r) * jnp.mean(x * gdy, axis=-1, keepdims=True)
    return dx, jnp.sum(dy * x * r, axis=0)


def gather(x, axis_name, axis=0):
    return lax.all_gather(x, axis_name, axis=axis, tiled=True)


def scatter(x, axis_name, axis=0):
    return lax.psum_scatter(x, axis_name, scatter_dimension=axis, tiled=True)


def shards(
    tokens,
    memory,
    piece_order,
    bucket_table,
    passage_lengths,
    self_gain,
    cross_gain,
    hidden_gain,
    position_bias,
    self_query,
    self_attention_key,
    self_value,
    self_output,
    cross_query,
    cross_key,
    cross_value,
    cross_output,
    hidden_in,
    hidden_out,
    grad_output,
):
    tok, mem, grad = tokens[0], memory[0], grad_output[0]
    rows, slots = tok.shape[0], mem.shape[0]
    length = (bucket_table.shape[0] + 1) // 2
    peers = length // rows
    index = lax.axis_index("ctx")
    own = lax.dynamic_slice_in_dim(piece_order, index * (rows // PIECE), rows // PIECE)
    tok_all = gather(tok, "ctx")
    w_self = gather(jnp.concatenate([self_query, self_attention_key, self_value], 1), "fsdp")
    w_mid = gather(jnp.concatenate([self_output, cross_query], 1), "fsdp")
    w_mem = gather(jnp.concatenate([cross_key, cross_value], 1), "fsdp")
    w_co = gather(cross_output, "fsdp")
    gains = gather(jnp.stack([self_gain, cross_gain, hidden_gain]), "fsdp", 1).astype(F32)
    bias_rows_all = gather(position_bias, "fsdp")
    w_in = lax.all_to_all(hidden_in, "fsdp", split_axis=1, concat_axis=0, tiled=True)
    wo, wq2 = w_mid[:, :D], w_mid[:, D:]
    buckets = jnp.arange(BUCKETS, dtype=jnp.int32)[:, None]
    hot = (bucket_table[None, :] == buckets).astype(BF16)
    hot = jnp.pad(hot, ((0, 0), (0, 1)))
    hot_back = jnp.pad(hot[:, -2::-1], ((0, 0), (0, 1)))
    spread = lambda x: jnp.pad(jnp.einsum("lr,lh->hr", x, bias_rows_all, preferred_element_type=F32), ((0, 4), (0, 0)))
    ahead, behind = bias_tables(spread(hot), spread(hot_back))
    q1_nat, k1_nat, v1_nat, o1, h1, a1, a2, q2, lse1 = self_forward(
        piece_order, own, tok_all, tok, w_self, jnp.pad(gains, ((0, 5), (0, 0))), ahead, wo, wq2
    )
    kv2 = project(mem, w_mem).astype(BF16)
    k2, v2 = kv2[:, :D], kv2[:, D:]
    slot = index * slots + jnp.arange(slots, dtype=jnp.int32)
    hidden = jnp.where(slot % PLEN < jnp.take(passage_lengths[0], slot // PLEN), 0.0, NEGATIVE)
    q2_all = gather(q2, "ctx")
    part, part_lse = cross_forward(q2_all, k2, v2, hidden[None, :])
    swap = lambda x: lax.all_to_all(x.reshape(peers, rows, x.shape[-1]), "ctx", 0, 0)
    part, part_lse = swap(part), swap(part_lse)[:, :, :HEADS]
    top = jnp.max(part_lse, axis=0)
    share = jnp.exp(part_lse - top)
    lse2 = top + jnp.log(jnp.sum(share, axis=0))
    share = share / jnp.sum(share, axis=0)
    out2 = jnp.sum(jnp.repeat(share, HEAD_DIM, axis=2) * part.astype(F32), axis=0)
    o2 = out2.astype(BF16)
    h2 = h1 + project(o2, w_co)
    a3 = norm_scale(h2, gains[2]).astype(BF16)
    a3_all, g_all = gather(a3, "fsdp"), gather(grad, "fsdp")
    pre = project(a3_all, w_in)
    act, pullback = jax.vjp(smooth_gate, pre)
    act = act.astype(BF16)
    out_part = project(act, hidden_out)
    dpre = pullback(nt(g_all, hidden_out))[0].astype(BF16)
    da3_part = nt(dpre, w_in)
    da3 = scatter(da3_part.astype(BF16), "fsdp").astype(F32)
    layer_output = (h2 + scatter(out_part.astype(BF16), "fsdp").astype(F32)).astype(BF16)
    g_out = tn(act, g_all).astype(BF16)
    g_in = tn(a3_all, dpre).astype(BF16)
    dx, gg3 = norm_back(h2, gains[2], da3)
    dh2 = grad.astype(F32) + dx
    branch2 = dh2.astype(BF16)
    do2 = nt(branch2, w_co).astype(BF16)
    delta = lambda d, o: jnp.sum((d.astype(F32) * o).reshape(rows, HEADS, HEAD_DIM), axis=2)
    pad4 = lambda x: jnp.pad(x, ((0, 0), (0, 4)))
    stat2 = jnp.concatenate([pad4(lse2), pad4(delta(do2, out2))], 1)
    do2_all = gather(do2, "ctx")
    stat2_all = gather(stat2.T, "ctx", 1)
    dq2_part, dk2, dv2 = cross_backward(q2_all, do2_all, stat2_all, k2, v2, hidden[:, None])
    dq2 = scatter(dq2_part, "ctx").astype(BF16)
    dx, gg2 = norm_back(h1, gains[1], nt(dq2, wq2))
    dh1 = dh2 + dx
    branch1 = dh1.astype(BF16)
    do1 = nt(branch1, wo).astype(BF16)
    stat1 = jnp.pad(jnp.concatenate([lse1[:, :16], pad4(delta(do1, o1.astype(F32)))], 1), ((0, 0), (0, LANES - 32)))
    do1_all = gather(do1, "ctx")
    stat1_all = gather(stat1, "ctx")
    dq1, dk1, dv1, diag = self_backward(
        piece_order, own, q1_nat, k1_nat, v1_nat, do1_all, do1, stat1_all, stat1, ahead, behind
    )
    g_bias = jnp.einsum(
        "hr,lr->lh", diag[:HEADS], hot.astype(F32), precision=lax.Precision.HIGHEST, preferred_element_type=F32
    )
    da1 = nt(dq1, w_self[:, :D]) + nt(dk1, w_self[:, D : 2 * D]) + nt(dv1, w_self[:, 2 * D :])
    tok_wide = tok.astype(F32)
    dx, gg1 = norm_back(tok_wide, gains[0], da1)
    grad_tokens = (dh1 + dx).astype(BF16)
    grad_memory = (nt(dk2, w_mem[:, :D]) + nt(dv2, w_mem[:, D:])).astype(BF16)
    quarter, eighth = self_query.shape[0], position_bias.shape[0]
    small = jnp.concatenate(
        [jnp.stack([gg1, gg2, gg3]), jnp.pad(g_bias, ((0, 0), (0, D - HEADS)))], 0
    )
    small = jnp.pad(small, ((0, -small.shape[0] % 8), (0, 0)))
    pairs = [
        (a1, dq1),
        (a1, dk1),
        (a1, dv1),
        (o1, branch1),
        (a2, dq2),
        (mem, dk2),
        (mem, dv2),
        (o2, branch2),
    ]
    total, small = reduce_grads(peers, pairs, g_in, g_out, small)
    total = total.astype(F32)
    f = lax.axis_index("fsdp")
    gain = lambda i: lax.dynamic_slice_in_dim(small[i], f * quarter, quarter)
    bias_out = lax.dynamic_slice_in_dim(small[3:], f * eighth, eighth)[:, :HEADS]
    count = len(pairs)
    return (
        layer_output[None],
        grad_tokens[None],
        grad_memory[None],
        gain(0),
        gain(1),
        gain(2),
        bias_out,
        *[total[i] for i in range(count)],
        jnp.concatenate([total[count + i] for i in range(WAYS)], 1),
        total[count + WAYS :].reshape(-1, D),
    )


def pick(*arrays):
    resident = (arrays[3].shape[0] + 1) // 2 <= RESIDENT_ROWS
    return (shards if resident else streamed_shards)(*arrays)


def solution(mesh):
    return jax.shard_map(
        pick,
        mesh=mesh,
        in_specs=(
            P("fsdp", "ctx", None),
            P("fsdp", "ctx", None),
            P(),
            P(),
            P("fsdp", None),
            P("fsdp"),
            P("fsdp"),
            P("fsdp"),
            P("fsdp", None),
            P("fsdp", None),
            P("fsdp", None),
            P("fsdp", None),
            P("fsdp", None),
            P("fsdp", None),
            P("fsdp", None),
            P("fsdp", None),
            P("fsdp", None),
            P("fsdp", None),
            P("fsdp", None),
            P("fsdp", "ctx", None),
        ),
        out_specs=(
            P("fsdp", "ctx", None),
            P("fsdp", "ctx", None),
            P("fsdp", "ctx", None),
            P("fsdp"),
            P("fsdp"),
            P("fsdp"),
            P("fsdp", None),
            P("fsdp", None),
            P("fsdp", None),
            P("fsdp", None),
            P("fsdp", None),
            P("fsdp", None),
            P("fsdp", None),
            P("fsdp", None),
            P("fsdp", None),
            P("fsdp", None),
            P("fsdp", None),
        ),
        check_vma=False,
    )
```

```python
import functools

import jax
import jax.numpy as jnp
from jax import lax
from jax.experimental import pallas as pl
from jax.experimental.pallas import tpu as pltpu
from jax.sharding import PartitionSpec as P

D = 768
HEADS = 12
PAIRS = HEADS // 2
HEAD_DIM = 64
PIECE = 64
BLOCK = 256
PLEN = 256
KBLK = 512
PSG = 20
BUCKETS = 32
RESIDENT_ROWS = 1024
LANES = 128
EPSILON = 1e-06
NEGATIVE = -1e30
F32 = jnp.float32
BF16 = jnp.bfloat16
VMEM_LIMIT = 60 * 2**20

def nn(a, b):
    return lax.dot_general(a, b, (((1,), (0,)), ((), ())), preferred_element_type=F32)
def nt(a, b):
    return lax.dot_general(a, b, (((1,), (1,)), ((), ())), preferred_element_type=F32)
def tn(a, b):
    return lax.dot_general(a, b, (((0,), (0,)), ((), ())), preferred_element_type=F32)

def normed(x, gain):
    return x * lax.rsqrt(jnp.mean(x * x, axis=-1, keepdims=True) + EPSILON) * gain

def half_mask(x, half):
    lane = lax.broadcasted_iota(jnp.int32, x.shape, 1) // HEAD_DIM
    return jnp.where(lane == half, x, jnp.zeros_like(x))

def lanes_of(pair):
    return pl.ds(pl.multiple_of(pair * LANES, LANES), LANES)

def shear(x, sign):
    row = lax.broadcasted_iota(jnp.int32, x.shape, 0)
    for bit in (1, 2, 4):
        x = jnp.where(row & bit != 0, pltpu.roll(x, (sign * bit) % x.shape[1], 1), x)
    return x

def piece_bias(tables, h, piece, length):
    start = pl.multiple_of(length - (piece + piece % 2) * PIECE, LANES)
    return tables[piece % 2, h, :, pl.ds(start, length)].astype(F32)

def bias_rows(tables, h, own, count, length):
    return jnp.concatenate([piece_bias(tables, h, own[i], length) for i in range(count)], 0)

def bias_at(tables, h, own, count, length):
    parts = []
    for i in range(count):
        parts.append(tables[own[i, 1], h, :, pl.ds(own[i, 2] * LANES, length)].astype(F32))
    return jnp.concatenate(parts, 0)


def add_diagonals(acc, block, piece):
    rows, length = block.shape
    wide = jnp.concatenate([block, jnp.zeros((rows, LANES), F32)], axis=1)
    total = pltpu.roll(wide[0:8], LANES, 1)
    for g in range(1, rows // 8):
        total += pltpu.roll(wide[8 * g:8 * g + 8], LANES - 8 * g, 1)
    start = pl.multiple_of(length - (piece - piece % 2) * PIECE - LANES, LANES)
    where = (piece % 2, slice(None), pl.ds(start, length + LANES))
    acc[where] += total

def full_spec():
    return pl.BlockSpec(memory_space=pltpu.VMEM)
def smem_spec():
    return pl.BlockSpec(memory_space=pltpu.SMEM)
def sds(shape, dtype):
    return jax.ShapeDtypeStruct(shape, dtype)

def cross_forward_kernel(q_all, k2, v2, mask, o, lse):
    rows = q_all.shape[0]
    step = BLOCK
    stat_lane = lax.broadcasted_iota(jnp.int32, (step, LANES), 1)

    def tile(t, c):
        rs = pl.ds(pl.multiple_of(t * step, step), step)
        def pair(p, stats):
            sl = lanes_of(p)
            q, k, v = q_all[rs, sl], k2[:, sl], v2[:, sl]
            total = jnp.zeros((step, LANES), F32)
            for half in range(2):
                s = nt(q, half_mask(k, half)) + mask[...]
                m = jnp.max(s, axis=1, keepdims=True)
                e = jnp.exp(s - m)
                l = jnp.sum(e, axis=1, keepdims=True)
                total += nn(e.astype(BF16), half_mask(v, half)) / l
                stats = jnp.where(stat_lane == 2 * p + half, m + jnp.log(l), stats)
            o[rs, sl] = total.astype(BF16)
            return stats
        lse[rs, :] = lax.fori_loop(0, PAIRS, pair, jnp.zeros((step, LANES), F32))
        return c
    lax.fori_loop(0, rows // step, tile, 0)

def cross_forward(q_all, k2, v2, mask):
    rows = q_all.shape[0]
    return pl.pallas_call(
        cross_forward_kernel,
        name="cross_forward",
        out_shape=[sds((rows, D), BF16), sds((rows, LANES), F32)],
        in_specs=[full_spec()] * 4,
        out_specs=[full_spec()] * 2,
        compiler_params=pltpu.CompilerParams(vmem_limit_bytes=VMEM_LIMIT),
    )(q_all, k2, v2, mask)

def cross_backward_kernel(q_all, do_all, stats, k2, v2, mask, dq, dk, dv):
    rows = q_all.shape[0]
    slots = k2.shape[0]
    step = BLOCK

    def pair(p, c):
        sl = lanes_of(p)
        ks = [half_mask(k2[:, sl], i) for i in range(2)]
        vs = [half_mask(v2[:, sl], i) for i in range(2)]
        def tile(t, carry):
            dkp, dvp = carry
            rs = pl.ds(pl.multiple_of(t * step, step), step)
            q, do = q_all[rs, sl], do_all[rs, sl]
            dqp = jnp.zeros((step, LANES), F32)
            for half in range(2):
                h = 2 * p + half
                qm, dom = half_mask(q, half), half_mask(do, half)
                s = nt(ks[half], q) + mask[...]
                e = jnp.exp(s - stats[pl.ds(h, 1), rs])
                dvp = dvp + nn(e.astype(BF16), dom)
                ds = (e * (nt(vs[half], do) - stats[pl.ds(16 + h, 1), rs])).astype(BF16)
                dkp = dkp + nn(ds, qm)
                dqp = dqp + tn(ds, ks[half])
            dq[rs, sl] = dqp.astype(dq.dtype)
            return dkp, dvp
        zero = jnp.zeros((slots, LANES), F32)
        dkp, dvp = lax.fori_loop(0, rows // step, tile, (zero, zero))
        dk[:, sl] = dkp.astype(BF16)
        dv[:, sl] = dvp.astype(BF16)
        return c
    lax.fori_loop(0, PAIRS, pair, 0)

def cross_backward(q_all, do_all, stats, k2, v2, mask):
    rows, slots = q_all.shape[0], k2.shape[0]
    return pl.pallas_call(
        cross_backward_kernel,
        name="cross_backward",
        out_shape=[sds((rows, D), F32), sds((slots, D), BF16), sds((slots, D), BF16)],
        in_specs=[full_spec()] * 6,
        out_specs=[full_spec()] * 3,
        compiler_params=pltpu.CompilerParams(vmem_limit_bytes=VMEM_LIMIT),
    )(q_all, do_all, stats, k2, v2, mask)

def self_backward_kernel(order, own, q_nat, k_nat, v_nat, do_slot, do_own, stat_slot, stat_own, delta_own, table, back_table,
                         dq, dk, dv, diag, inv, q_own, k_own, v_own, do_nat, stat_nat, stat_t, acc):
    length = q_nat.shape[0]
    rows = do_own.shape[0]
    full = 2 * length
    slots, mine = length // PIECE, rows // PIECE
    per = BLOCK // PIECE
    for s in range(slots):
        inv[order[s]] = s
    def move(i, c):
        src = pl.ds(pl.multiple_of(inv[i] * PIECE, PIECE), PIECE)
        dst = pl.ds(pl.multiple_of(i * PIECE, PIECE), PIECE)
        do_nat[dst, :] = do_slot[src, :]
        stat_nat[dst, :] = stat_slot[src, :]
        return c
    lax.fori_loop(0, slots, move, 0)
    for i in range(length // LANES):
        stat_t[:, i * LANES:(i + 1) * LANES] = stat_nat[i * LANES:(i + 1) * LANES, :].T
    for i in range(mine):
        src = pl.ds(pl.multiple_of(own[i] * PIECE, PIECE), PIECE)
        dst = slice(i * PIECE, (i + 1) * PIECE)
        q_own[dst, :] = q_nat[src, :]
        k_own[dst, :] = k_nat[src, :]
        v_own[dst, :] = v_nat[src, :]
    lane = lax.broadcasted_iota(jnp.int32, (rows, length), 1)
    limit = jnp.concatenate([jnp.full((PIECE, 1), (own[i] // per + 1) * BLOCK, jnp.int32) for i in range(mine)], 0)
    first = jnp.concatenate([jnp.full((PIECE, 1), (own[i] // per) * BLOCK, jnp.int32) for i in range(mine)], 0)
    visible, seen = lane < limit, lane >= first
    stat_lane = lax.broadcasted_iota(jnp.int32, (rows, LANES), 1)

    def column(h):
        return jnp.sum(jnp.where(stat_lane == h, stat_own[...], 0.0), axis=1, keepdims=True)

    diag[...] = jnp.zeros_like(diag)
    def pair(p, c):
        sl = lanes_of(p)
        q, k, v, do = q_own[:, sl], k_nat[:, sl], v_nat[:, sl], do_own[:, sl]
        kq, vq, qa, da = k_own[:, sl], v_own[:, sl], q_nat[:, sl], do_nat[:, sl]
        dqp = jnp.zeros((rows, LANES), F32)
        dkp = jnp.zeros((rows, LANES), F32)
        dvp = jnp.zeros((rows, LANES), F32)
        for half in range(2):
            h = 2 * p + half
            bias = bias_rows(table, h, own, mine, length)
            km, vm = half_mask(k, half), half_mask(v, half)
            s = jnp.where(visible, nt(q, km) + bias, NEGATIVE)
            e = jnp.exp(s - column(h))
            ds = e * (nt(do, vm) - column(16 + h))
            dqp += nn(ds.astype(BF16), km)
            acc[...] = jnp.zeros_like(acc)
            for i in range(mine):
                add_diagonals(acc, ds[i * PIECE:(i + 1) * PIECE, :], own[i])
            joined = shear(acc[0] + pltpu.roll(acc[1], full - PIECE, 1), -1)
            diag[pl.ds(h, 1), :] = jnp.sum(pltpu.roll(joined, full - 1, 1), axis=0, keepdims=True)
            bias = bias_rows(back_table, h, own, mine, length)
            s = jnp.where(seen, nt(half_mask(kq, half), qa) + bias, NEGATIVE)
            e = jnp.exp(s - stat_t[pl.ds(h, 1), :])
            dvp += nn(e.astype(BF16), half_mask(da, half))
            ds = e * (nt(half_mask(vq, half), da) - stat_t[pl.ds(16 + h, 1), :])
            dkp += nn(ds.astype(BF16), half_mask(qa, half))
        dq[:, sl] = dqp.astype(BF16)
        dk[:, sl] = dkp.astype(BF16)
        dv[:, sl] = dvp.astype(BF16)
        return c
    lax.fori_loop(0, PAIRS, pair, 0)

def self_backward(order, own, q_nat, k_nat, v_nat, do_slot, do_own, stat_slot, stat_own, table, back_table):
    length, rows = q_nat.shape[0], do_own.shape[0]
    def kern(order, own, q_nat, k_nat, v_nat, do_slot, do_own, stat_slot, stat_own, table, back_table, *rest):
        self_backward_kernel(order, own, q_nat, k_nat, v_nat, do_slot, do_own, stat_slot, stat_own, None, table, back_table, *rest)
    return pl.pallas_call(
        kern,
        name="self_backward",
        out_shape=[sds((rows, D), BF16)] * 3 + [sds((16, 2 * length), F32)],
        in_specs=[smem_spec()] * 2 + [full_spec()] * 9,
        out_specs=[full_spec()] * 4,
        scratch_shapes=[pltpu.SMEM((length // PIECE,), jnp.int32)] + [pltpu.VMEM((rows, D), BF16)] * 3
        + [pltpu.VMEM((length, D), BF16), pltpu.VMEM((length, LANES), F32), pltpu.VMEM((LANES, length), F32), pltpu.VMEM((2, 8, 2 * length), F32)],
        compiler_params=pltpu.CompilerParams(vmem_limit_bytes=VMEM_LIMIT),
    )(order, own, q_nat, k_nat, v_nat, do_slot, do_own, stat_slot, stat_own, table, back_table)


def norm_scale(values, gain_vector):
    return (
        values
        * lax.rsqrt(jnp.mean(values * values, axis=-1, keepdims=True) + EPSILON)
        * gain_vector
    )


def smooth_gate(values):
    return jax.nn.gelu(values, approximate=True)


def project(operand, matrix):
    return jnp.dot(operand, matrix, preferred_element_type=jnp.float32)


def project_back(operand, matrix):
    return jnp.einsum("sra,ba->srb", operand, matrix, preferred_element_type=jnp.float32)


def weight_grad(inputs, upstream):
    return jnp.einsum("sra,srb->ab", inputs, upstream, preferred_element_type=jnp.float32)


def to_heads(matrix):
    return matrix.reshape(matrix.shape[0], matrix.shape[1], HEADS, HEAD_DIM)


def heads_first(matrix):
    return jnp.transpose(to_heads(matrix), (0, 2, 1, 3))


def from_heads(tensor):
    return jnp.transpose(tensor, (0, 2, 1, 3)).reshape(
        tensor.shape[0], tensor.shape[2], HEADS * HEAD_DIM
    )


def block_scores(queries, keys_all, values_all, extras, offset):
    key_block = lax.dynamic_slice_in_dim(keys_all, offset, KBLK, 1)
    value_block = lax.dynamic_slice_in_dim(values_all, offset, KBLK, 1)
    added_bias, visible, bucket_indicator = extras(offset)
    scores = (
        jnp.einsum("sqhd,skhd->shqk", queries, key_block, preferred_element_type=jnp.float32)
        + added_bias
    )
    block_maximum = jnp.max(jnp.where(visible, scores, NEGATIVE), axis=-1)
    weights = jnp.exp(jnp.where(visible, scores - block_maximum[..., None], NEGATIVE))
    return (key_block, value_block, bucket_indicator, block_maximum, weights)


def attend_forward(queries, keys_all, values_all, extras):
    block_count = keys_all.shape[1] // KBLK

    def single_block_tile(carried, block_index):
        key_block, value_block, bucket_indicator, block_maximum, weights = block_scores(
            queries, keys_all, values_all, extras, block_index * KBLK
        )
        numerator = jnp.einsum(
            "shqk,skhd->shqd",
            weights.astype(jnp.bfloat16),
            value_block,
            preferred_element_type=jnp.float32,
        )
        return (carried, (block_maximum, jnp.sum(weights, axis=-1), numerator))

    ignored, stacked = lax.scan(
        single_block_tile, jnp.zeros((), jnp.float32), jnp.arange(block_count, dtype=jnp.int32)
    )
    block_maximum, block_sum, numerator = stacked
    row_maximum = jnp.max(block_maximum, axis=0)
    rescale = jnp.exp(block_maximum - row_maximum)
    row_total = jnp.sum(rescale * block_sum, axis=0)
    output = jnp.sum(rescale[..., None] * numerator, axis=0) / row_total[..., None]
    return (output, row_maximum, row_total)


def attend_backward(
    queries, keys_all, values_all, extras, grad_out, output, row_maximum, row_total
):
    block_count = keys_all.shape[1] // KBLK
    grad_wide = grad_out.astype(jnp.float32)
    row_dot = jnp.sum(grad_wide * output, axis=-1)
    scaled = grad_wide / row_total[..., None]
    sum_weight = -row_dot / row_total
    initial = (
        jnp.zeros(queries.shape, jnp.float32),
        jnp.zeros(keys_all.shape, jnp.float32),
        jnp.zeros(values_all.shape, jnp.float32),
        jnp.zeros((BUCKETS, HEADS), jnp.float32),
    )

    def single_block_tile(carried, block_index):
        grad_query, grad_keys, grad_values, grad_bias = carried
        offset = block_index * KBLK
        key_block, value_block, bucket_indicator, block_maximum, weights = block_scores(
            queries, keys_all, values_all, extras, offset
        )
        rescale = jnp.exp(block_maximum - row_maximum)
        grad_numerator = (scaled * rescale[..., None]).astype(jnp.bfloat16)
        grad_weights = (
            jnp.einsum(
                "shqd,skhd->shqk", grad_numerator, value_block, preferred_element_type=jnp.float32
            )
            + (sum_weight * rescale)[..., None]
        )
        grad_scores = weights * grad_weights
        gradient_bfloat_cast = grad_scores.astype(jnp.bfloat16)
        grad_query = grad_query + jnp.einsum(
            "shqk,skhd->sqhd", gradient_bfloat_cast, key_block, preferred_element_type=jnp.float32
        )
        key_part = jnp.einsum(
            "shqk,sqhd->skhd", gradient_bfloat_cast, queries, preferred_element_type=jnp.float32
        )
        value_part = jnp.einsum(
            "shqk,shqd->skhd",
            weights.astype(jnp.bfloat16),
            grad_numerator,
            preferred_element_type=jnp.float32,
        )
        grad_keys = lax.dynamic_update_slice_in_dim(grad_keys, key_part, offset, 1)
        grad_values = lax.dynamic_update_slice_in_dim(grad_values, value_part, offset, 1)
        if bucket_indicator is not None:
            remainder_portion = (grad_scores - gradient_bfloat_cast.astype(jnp.float32)).astype(
                jnp.bfloat16
            )
            grad_bias = (
                grad_bias
                + jnp.einsum(
                    "uljf,pjf->pl",
                    gradient_bfloat_cast,
                    bucket_indicator,
                    preferred_element_type=jnp.float32,
                )
                + jnp.einsum(
                    "uljf,pjf->pl",
                    remainder_portion,
                    bucket_indicator,
                    preferred_element_type=jnp.float32,
                )
            )
        return ((grad_query, grad_keys, grad_values, grad_bias), None)

    result, ignored = lax.scan(single_block_tile, initial, jnp.arange(block_count, dtype=jnp.int32))
    return result


def streamed_shards(
    tokens,
    memory,
    piece_order,
    bucket_table,
    passage_lengths,
    self_gain,
    cross_gain,
    hidden_gain,
    position_bias,
    self_query,
    self_attention_key,
    self_value,
    self_output,
    cross_query,
    cross_key,
    cross_value,
    cross_output,
    hidden_in,
    hidden_out,
    grad_output,
):
    (
        gain_one,
        gain_two,
        gain_three,
        position_bias_lookup,
        query_full,
        key_full,
        value_full,
        output_full,
        cross_query_full,
        cross_key_full,
        cross_value_full,
        cross_output_full,
        inner_full,
        outer_full,
    ) = (
        lax.all_gather(self_gain, "fsdp", axis=0, tiled=True),
        lax.all_gather(cross_gain, "fsdp", axis=0, tiled=True),
        lax.all_gather(hidden_gain, "fsdp", axis=0, tiled=True),
        lax.all_gather(position_bias, "fsdp", axis=0, tiled=True),
        lax.all_gather(self_query, "fsdp", axis=0, tiled=True),
        lax.all_gather(self_attention_key, "fsdp", axis=0, tiled=True),
        lax.all_gather(self_value, "fsdp", axis=0, tiled=True),
        lax.all_gather(self_output, "fsdp", axis=0, tiled=True),
        lax.all_gather(cross_query, "fsdp", axis=0, tiled=True),
        lax.all_gather(cross_key, "fsdp", axis=0, tiled=True),
        lax.all_gather(cross_value, "fsdp", axis=0, tiled=True),
        lax.all_gather(cross_output, "fsdp", axis=0, tiled=True),
        lax.all_gather(hidden_in, "fsdp", axis=0, tiled=True),
        lax.all_gather(hidden_out, "fsdp", axis=0, tiled=True),
    )
    gain_one = gain_one.astype(jnp.float32)
    gain_two = gain_two.astype(jnp.float32)
    gain_three = gain_three.astype(jnp.float32)
    sequence_count = tokens.shape[0]
    local_rows = tokens.shape[1]
    sequence_length = (bucket_table.shape[0] + 1) // 2
    memory_length = PSG * PLEN
    piece_offsets = jnp.arange(PIECE, dtype=jnp.int32)
    local_pieces = lax.dynamic_slice_in_dim(
        piece_order, lax.axis_index("ctx") * (local_rows // PIECE), local_rows // PIECE
    )
    query_position = (local_pieces[:, None] * PIECE + piece_offsets[None, :]).reshape(local_rows)
    key_position = (piece_order[:, None] * PIECE + piece_offsets[None, :]).reshape(sequence_length)
    bucket_numbers = jnp.arange(BUCKETS, dtype=jnp.int32)

    def self_extras(offset):
        key_block_position = lax.dynamic_slice_in_dim(key_position, offset, KBLK)
        relative_bucket_index = jnp.take(
            bucket_table,
            key_block_position[None, :] - query_position[:, None] + sequence_length - 1,
        )
        bucket_indicator = (
            relative_bucket_index[None, :, :] == bucket_numbers[:, None, None]
        ).astype(jnp.bfloat16)
        added_bias = jnp.einsum(
            "lvj,lf->fvj",
            bucket_indicator,
            position_bias_lookup,
            preferred_element_type=jnp.float32,
        )
        visible = key_block_position[None, :] // BLOCK <= query_position[:, None] // BLOCK
        return (added_bias, visible, bucket_indicator)

    slot_numbers = jnp.arange(PLEN, dtype=jnp.int32)
    memory_valid = (passage_lengths[:, :, None] > slot_numbers[None, None, :]).reshape(
        sequence_count, memory_length
    )

    def cross_extras(offset):
        visible = lax.dynamic_slice_in_dim(memory_valid, offset, KBLK, 1)[:, None, None, :]
        return (0.0, visible, None)

    inputs_wide = tokens.astype(jnp.float32)
    normed_one = norm_scale(inputs_wide, gain_one).astype(jnp.bfloat16)
    queries_one = project(normed_one, query_full).astype(jnp.bfloat16)
    keys_local = project(normed_one, key_full).astype(jnp.bfloat16)
    values_local = project(normed_one, value_full).astype(jnp.bfloat16)
    memory_keys = project(memory, cross_key_full).astype(jnp.bfloat16)
    memory_values = project(memory, cross_value_full).astype(jnp.bfloat16)
    keys_all, values_all, memory_keys_all, memory_values_all = (
        lax.all_gather(keys_local, "ctx", axis=1, tiled=True),
        lax.all_gather(values_local, "ctx", axis=1, tiled=True),
        lax.all_gather(memory_keys, "ctx", axis=1, tiled=True),
        lax.all_gather(memory_values, "ctx", axis=1, tiled=True),
    )
    output_one, maximum_one, total_one = attend_forward(
        to_heads(queries_one), to_heads(keys_all), to_heads(values_all), self_extras
    )
    attended_one = from_heads(output_one).astype(jnp.bfloat16)
    hidden_one = inputs_wide + project(attended_one, output_full)
    normed_two = norm_scale(hidden_one, gain_two).astype(jnp.bfloat16)
    queries_two = project(normed_two, cross_query_full).astype(jnp.bfloat16)
    output_two, maximum_two, total_two = attend_forward(
        to_heads(queries_two), to_heads(memory_keys_all), to_heads(memory_values_all), cross_extras
    )
    attended_two = from_heads(output_two).astype(jnp.bfloat16)
    hidden_two = hidden_one + project(attended_two, cross_output_full)
    normed_three = norm_scale(hidden_two, gain_three).astype(jnp.bfloat16)
    before_gate = project(normed_three, inner_full)
    gated_wide, gate_pullback = jax.vjp(smooth_gate, before_gate)
    activated = gated_wide.astype(jnp.bfloat16)
    layer_output = (hidden_two + project(activated, outer_full)).astype(jnp.bfloat16)
    grad_wide = grad_output.astype(jnp.float32)
    grad_outer = weight_grad(activated, grad_output)
    grad_activated = project_back(grad_output, outer_full)
    grad_before = gate_pullback(grad_activated)[0].astype(jnp.bfloat16)
    grad_inner = weight_grad(normed_three, grad_before)
    ignored, norm_pullback = jax.vjp(norm_scale, hidden_two, gain_three)
    grad_hidden_part, grad_gain_three = norm_pullback(project_back(grad_before, inner_full))
    grad_hidden_two = grad_wide + grad_hidden_part
    branch_two = grad_hidden_two.astype(jnp.bfloat16)
    grad_cross_output = weight_grad(attended_two, branch_two)
    grad_attended_two = project_back(branch_two, cross_output_full).astype(jnp.bfloat16)
    keys_back, values_back, memory_keys_back, memory_values_back = (
        keys_all,
        values_all,
        memory_keys_all,
        memory_values_all,
    )
    grad_query_two, grad_memory_keys, grad_memory_values, unused_bias = attend_backward(
        to_heads(queries_two),
        to_heads(memory_keys_back),
        to_heads(memory_values_back),
        cross_extras,
        heads_first(grad_attended_two),
        output_two,
        maximum_two,
        total_two,
    )
    memory_key_sum, memory_value_sum = (
        lax.psum_scatter(
            grad_memory_keys.reshape(sequence_count, memory_length, D),
            "ctx",
            scatter_dimension=1,
            tiled=True,
        ),
        lax.psum_scatter(
            grad_memory_values.reshape(sequence_count, memory_length, D),
            "ctx",
            scatter_dimension=1,
            tiled=True,
        ),
    )
    memory_key_rounded = memory_key_sum.astype(jnp.bfloat16)
    memory_value_rounded = memory_value_sum.astype(jnp.bfloat16)
    query_two_rounded = grad_query_two.reshape(sequence_count, local_rows, D).astype(jnp.bfloat16)
    grad_cross_query = weight_grad(normed_two, query_two_rounded)
    grad_cross_key = weight_grad(memory, memory_key_rounded)
    grad_cross_value = weight_grad(memory, memory_value_rounded)
    grad_memory = (
        project_back(memory_key_rounded, cross_key_full)
        + project_back(memory_value_rounded, cross_value_full)
    ).astype(jnp.bfloat16)
    ignored, norm_pullback = jax.vjp(norm_scale, hidden_one, gain_two)
    grad_hidden_part, grad_gain_two = norm_pullback(
        project_back(query_two_rounded, cross_query_full)
    )
    grad_hidden_one = grad_hidden_two + grad_hidden_part
    branch_one = grad_hidden_one.astype(jnp.bfloat16)
    grad_self_output = weight_grad(attended_one, branch_one)
    grad_attended_one = project_back(branch_one, output_full).astype(jnp.bfloat16)
    grad_query_one, grad_keys_all, grad_values_all, grad_bias = attend_backward(
        to_heads(queries_one),
        to_heads(keys_back),
        to_heads(values_back),
        self_extras,
        heads_first(grad_attended_one),
        output_one,
        maximum_one,
        total_one,
    )
    key_sum, value_sum = (
        lax.psum_scatter(
            grad_keys_all.reshape(sequence_count, sequence_length, D),
            "ctx",
            scatter_dimension=1,
            tiled=True,
        ),
        lax.psum_scatter(
            grad_values_all.reshape(sequence_count, sequence_length, D),
            "ctx",
            scatter_dimension=1,
            tiled=True,
        ),
    )
    query_one_rounded = grad_query_one.reshape(sequence_count, local_rows, D).astype(jnp.bfloat16)
    first_key_bfloat_cast = key_sum.astype(jnp.bfloat16)
    value_one_rounded = value_sum.astype(jnp.bfloat16)
    grad_self_query = weight_grad(normed_one, query_one_rounded)
    grad_self_key = weight_grad(normed_one, first_key_bfloat_cast)
    grad_self_value = weight_grad(normed_one, value_one_rounded)
    grad_normed_one = (
        project_back(query_one_rounded, query_full)
        + project_back(first_key_bfloat_cast, key_full)
        + project_back(value_one_rounded, value_full)
    )
    ignored, norm_pullback = jax.vjp(norm_scale, inputs_wide, gain_one)
    grad_input_part, grad_gain_one = norm_pullback(grad_normed_one)
    grad_tokens = (grad_hidden_one + grad_input_part).astype(jnp.bfloat16)
    (
        shard_gain_one,
        shard_gain_two,
        shard_gain_three,
        shard_bias,
        shard_query,
        shard_key,
        shard_value,
        shard_output,
        shard_cross_query,
        shard_cross_key,
        shard_cross_value,
        shard_cross_output,
        shard_inner,
        shard_outer,
    ) = (
        lax.psum_scatter(
            grad_gain_one.astype(jnp.bfloat16), "fsdp", scatter_dimension=0, tiled=True
        ).astype(jnp.float32),
        lax.psum_scatter(
            grad_gain_two.astype(jnp.bfloat16), "fsdp", scatter_dimension=0, tiled=True
        ).astype(jnp.float32),
        lax.psum_scatter(
            grad_gain_three.astype(jnp.bfloat16), "fsdp", scatter_dimension=0, tiled=True
        ).astype(jnp.float32),
        lax.psum_scatter(
            grad_bias.astype(jnp.bfloat16), "fsdp", scatter_dimension=0, tiled=True
        ).astype(jnp.float32),
        lax.psum_scatter(
            grad_self_query.astype(jnp.bfloat16), "fsdp", scatter_dimension=0, tiled=True
        ).astype(jnp.float32),
        lax.psum_scatter(
            grad_self_key.astype(jnp.bfloat16), "fsdp", scatter_dimension=0, tiled=True
        ).astype(jnp.float32),
        lax.psum_scatter(
            grad_self_value.astype(jnp.bfloat16), "fsdp", scatter_dimension=0, tiled=True
        ).astype(jnp.float32),
        lax.psum_scatter(
            grad_self_output.astype(jnp.bfloat16), "fsdp", scatter_dimension=0, tiled=True
        ).astype(jnp.float32),
        lax.psum_scatter(
            grad_cross_query.astype(jnp.bfloat16), "fsdp", scatter_dimension=0, tiled=True
        ).astype(jnp.float32),
        lax.psum_scatter(
            grad_cross_key.astype(jnp.bfloat16), "fsdp", scatter_dimension=0, tiled=True
        ).astype(jnp.float32),
        lax.psum_scatter(
            grad_cross_value.astype(jnp.bfloat16), "fsdp", scatter_dimension=0, tiled=True
        ).astype(jnp.float32),
        lax.psum_scatter(
            grad_cross_output.astype(jnp.bfloat16), "fsdp", scatter_dimension=0, tiled=True
        ).astype(jnp.float32),
        lax.psum_scatter(
            grad_inner.astype(jnp.bfloat16), "fsdp", scatter_dimension=0, tiled=True
        ).astype(jnp.float32),
        lax.psum_scatter(
            grad_outer.astype(jnp.bfloat16), "fsdp", scatter_dimension=0, tiled=True
        ).astype(jnp.float32),
    )
    (
        total_gain_one,
        total_gain_two,
        total_gain_three,
        total_bias,
        total_query,
        total_key,
        total_value,
        total_output,
        total_cross_query,
        total_cross_key,
        total_cross_value,
        total_cross_output,
        total_inner,
        total_outer,
    ) = lax.psum(
        (
            shard_gain_one,
            shard_gain_two,
            shard_gain_three,
            shard_bias,
            shard_query,
            shard_key,
            shard_value,
            shard_output,
            shard_cross_query,
            shard_cross_key,
            shard_cross_value,
            shard_cross_output,
            shard_inner,
            shard_outer,
        ),
        "ctx",
    )
    return (
        layer_output,
        grad_tokens,
        grad_memory,
        total_gain_one,
        total_gain_two,
        total_gain_three,
        total_bias,
        total_query,
        total_key,
        total_value,
        total_output,
        total_cross_query,
        total_cross_key,
        total_cross_value,
        total_cross_output,
        total_inner,
        total_outer,
    )


MESH = pl.DeviceIdType.MESH
WAYS = 4


class Place:
    def __init__(self, peers):
        self.depth = peers // 2
        c, f = lax.axis_index("ctx"), lax.axis_index("fsdp")
        self.c, self.f = c, f
        self.a, self.b, self.x, self.k = c // 2, c % 2, f // 2, f % 2
        self.core = (c, self.x * 2 + 1 - self.k)
        self.across = (c, (1 - self.x) * 2 + self.k)
        self.beside = (self.a * 2 + 1 - self.b, f)

    def ahead(self, d):
        return lax.rem(self.a + d, self.depth)

    def behind(self, d):
        return lax.rem(self.a + self.depth - d, self.depth)

    def column(self, a):
        return (a * 2 + self.b, self.f)

    def group(self, d):
        return (self.c, lax.rem(self.f + d, WAYS))


def greet(targets):
    barrier = pltpu.get_barrier_semaphore()
    for target in targets:
        pl.semaphore_signal(barrier, inc=1, device_id=target, device_id_type=MESH)
    pl.semaphore_wait(barrier, len(targets))


def remote(src, dst, sems, index, target):
    return pltpu.make_async_remote_copy(
        src_ref=src,
        dst_ref=dst,
        send_sem=sems[0].at[index],
        recv_sem=sems[1].at[index],
        device_id=target,
        device_id_type=MESH,
    )


def sems(count):
    return [pltpu.SemaphoreType.DMA((count,)), pltpu.SemaphoreType.DMA((count,))]


class Wire:
    def __init__(self, peers):
        self.at = Place(peers)
        self.depth = self.at.depth
        self.sent = []

    def go(self, copy):
        copy.start()
        self.sent.append(copy)

    def drain(self):
        for copy in self.sent:
            copy.wait_send()

    def partners(self):
        at = self.at
        return (
            [at.group(d) for d in range(1, WAYS)]
            + [at.beside]
            + [at.column(at.ahead(d)) for d in range(1, self.depth)]
        )

    def near(self, step):
        a, last = self.at.a, self.depth - 1
        low = jnp.where(step - 1 < a, step - 1, step)
        mirrored = jnp.where(step - 1 < last - a, step - 1, step)
        return jnp.where(2 * a < last, low, last - mirrored)

    def slot(self, buf, c):
        if len(buf.shape) == 3:
            return buf.at[c]
        rows = buf.shape[0] // (2 * self.depth)
        return buf.at[pl.ds(pl.multiple_of(c * rows, rows), rows)]

    def spread(self, src, buf, sem):
        at = self.at
        slot = self.slot(buf, at.c)
        self.go(remote(src, slot, sem, at.a, at.beside))
        for step in range(1, self.depth):
            self.go(remote(src, slot, sem, self.depth + at.a, at.column(self.near(step))))

    def relay(self, buf, sem, step):
        a = self.near(step)
        slot = self.slot(buf, a * 2 + self.at.b)
        remote(slot, slot, sem, self.depth + a, self.at.beside).wait_recv()
        self.go(remote(slot, slot, sem, a, self.at.beside))

    def from_beside(self, buf, sem, a):
        slot = self.slot(buf, a * 2 + 1 - self.at.b)
        remote(slot, slot, sem, a, self.at.beside).wait_recv()

    def shard(self, full, f):
        quarter = full.shape[0] // WAYS
        return full.at[pl.ds(pl.multiple_of(f * quarter, quarter), quarter)]

    def weight_start(self, src, full, sem, i):
        at = self.at
        slot = self.shard(full, at.f)
        slot[...] = src[...]
        self.go(remote(src, slot, sem, 3 * i, at.across))
        self.go(remote(src, slot, sem, 3 * i + 1, at.core))

    def weight_relay(self, full, sem, i):
        at = self.at
        slot = self.shard(full, (1 - at.x) * 2 + at.k)
        remote(slot, slot, sem, 3 * i, at.across).wait_recv()
        self.go(remote(slot, slot, sem, 3 * i + 2, at.core))

    def weight_ready(self, full, sem, i):
        at = self.at
        slot = self.shard(full, at.x * 2 + 1 - at.k)
        remote(slot, slot, sem, 3 * i + 1, at.core).wait_recv()
        slot = self.shard(full, (1 - at.x) * 2 + 1 - at.k)
        remote(slot, slot, sem, 3 * i + 2, at.core).wait_recv()


def fill_tables(table, out):
    full = table.shape[1]

    def head(h, c):
        base = shear(pltpu.roll(jnp.broadcast_to(table[pl.ds(h, 1), :], (8, full)), 1, 1), 1)
        for parity in range(2):
            for i in range(PIECE // 16):
                shifts = [(8 * g - 64 * parity) % full for g in (2 * i, 2 * i + 1)]
                both = [pltpu.roll(base, s, 1) if s else base for s in shifts]
                out[parity, h, 16 * i : 16 * i + 16, :] = jnp.concatenate(both, 0).astype(BF16)
        return c

    lax.fori_loop(0, HEADS, head, 0)


N_FRONT = 7
N_GAINS = 16


def front_kernel(peers, *refs):
    inv, own, tok, pack, buckets, buckets_back = refs[:6]
    shards_in = refs[6 : 6 + N_FRONT]
    (weights, gains, ahead, behind, q_nat, k_nat, v_nat, a1, o1, h1, a2, q2, lse) = refs[6 + N_FRONT : 19 + N_FRONT]
    (tok_all, pack_all, table, q_own, *sem) = refs[19 + N_FRONT :]
    sem_t, sem_w, sem_p = sem[0:2], sem[2:4], sem[4:6]
    wire = Wire(peers)
    at, depth = wire.at, wire.depth
    rows = tok.shape[0]
    length = peers * rows
    mine, per = rows // PIECE, BLOCK // PIECE
    greet(wire.partners())
    for d in range(1, WAYS):
        wire.go(remote(pack, pack_all.at[at.f], sem_p, d, at.group(d)))
    wire.spread(tok, tok_all, sem_t)
    for i in range(3):
        wire.weight_start(shards_in[i], weights.at[i], sem_w, i)
    wire.slot(tok_all, at.c)[...] = tok[...]
    pack_all[at.f] = pack[...]
    for d in range(1, WAYS):
        slot = pack_all.at[lax.rem(at.f + WAYS - d, WAYS)]
        remote(slot, slot, sem_p, d, at.group(WAYS - d)).wait_recv()
    everything = pack_all[0].astype(F32) + pack_all[1].astype(F32) + pack_all[2].astype(F32) + pack_all[3].astype(F32)
    gains[...] = everything[0:8, :]
    bias = everything[N_GAINS:, 0:LANES].astype(BF16)
    bucket = lax.broadcasted_iota(jnp.int32, (bias.shape[0], 2 * length), 0)
    for line, out in ((buckets, ahead), (buckets_back, behind)):
        hot = jnp.where(line[...] == bucket, 1.0, 0.0).astype(BF16)
        table[...] = tn(bias, hot)[0:16, :]
        fill_tables(table, out)
    for step in range(1, depth):
        wire.relay(tok_all, sem_t, step)
    for i in range(3):
        wire.weight_relay(weights.at[i], sem_w, i)
    for i in range(3, N_FRONT):
        wire.weight_start(shards_in[i], weights.at[i], sem_w, i)
    first = gains[0:1, :]
    a1[...] = normed(tok[...].astype(F32), first).astype(BF16)
    for i in range(3):
        wire.weight_ready(weights.at[i], sem_w, i)
    for step in range(depth):
        wire.from_beside(tok_all, sem_t, step)

    def tile(t, c):
        parts = []
        for i in range(per):
            parts.append(tok_all[pl.ds(inv[t * per + i] * PIECE, PIECE), :])
        a = normed(jnp.concatenate(parts, 0).astype(F32), first).astype(BF16)
        dst = pl.ds(pl.multiple_of(t * BLOCK, BLOCK), BLOCK)
        for j, out in enumerate((q_nat, k_nat, v_nat)):
            out[dst, :] = nn(a, weights[j]).astype(BF16)
        return c

    lax.fori_loop(0, length // BLOCK, tile, 0)
    for i in range(mine):
        q_own[i * PIECE : (i + 1) * PIECE, :] = q_nat[pl.ds(own[i, 0] * PIECE, PIECE), :]
    wire.weight_relay(weights.at[3], sem_w, 3)
    lane = lax.broadcasted_iota(jnp.int32, (rows, length), 1)
    limit = jnp.concatenate([jnp.full((PIECE, 1), own[i, 3], jnp.int32) for i in range(mine)], 0)
    visible = lane < limit
    stat_lane = lax.broadcasted_iota(jnp.int32, (rows, LANES), 1)

    def pair(p, stats):
        sl = lanes_of(p)
        q, k, v = q_own[:, sl], k_nat[:, sl], v_nat[:, sl]
        total = jnp.zeros((rows, LANES), F32)
        for half in range(2):
            h = 2 * p + half
            s = jnp.where(visible, nt(q, half_mask(k, half)) + bias_at(ahead, h, own, mine, length), NEGATIVE)
            m = jnp.max(s, axis=1, keepdims=True)
            e = jnp.exp(s - m)
            l = jnp.sum(e, axis=1, keepdims=True)
            total += nn(e.astype(BF16), half_mask(v, half)) / l
            stats = jnp.where(stat_lane == h, m + jnp.log(l), stats)
        o1[:, sl] = total.astype(BF16)
        return stats

    stats = lax.fori_loop(0, PAIRS // 2, pair, jnp.zeros((rows, LANES), F32))
    wire.weight_relay(weights.at[4], sem_w, 4)
    lse[...] = lax.fori_loop(PAIRS // 2, PAIRS, pair, stats)
    wire.weight_relay(weights.at[5], sem_w, 5)
    wire.weight_ready(weights.at[3], sem_w, 3)
    h = tok[...].astype(F32) + nn(o1[...], weights[3])
    h1[...] = h
    a = normed(h, gains[1:2, :]).astype(BF16)
    a2[...] = a
    wire.weight_ready(weights.at[4], sem_w, 4)
    q2[...] = nn(a, weights[4]).astype(BF16)
    wire.weight_relay(weights.at[6], sem_w, 6)
    for i in (5, 6):
        wire.weight_ready(weights.at[i], sem_w, i)
    wire.drain()


def front(peers, inv, own, tok, pack, buckets, buckets_back, weight_shards):
    rows = tok.shape[0]
    length, depth = peers * rows, peers // 2
    block = lambda dtype: sds((rows, D), dtype)
    return pl.pallas_call(
        functools.partial(front_kernel, peers),
        name="front",
        out_shape=[sds((N_FRONT, D, D), BF16), sds((8, D), F32)]
        + [sds((2, HEADS, PIECE, 2 * length), BF16)] * 2
        + [sds((length, D), BF16)] * 3
        + [block(BF16), block(BF16), block(F32), block(BF16), block(BF16), sds((rows, LANES), F32)],
        in_specs=[smem_spec()] * 2 + [full_spec()] * (4 + N_FRONT),
        out_specs=[full_spec()] * 13,
        scratch_shapes=[
            pltpu.VMEM((length, D), BF16),
            pltpu.VMEM((WAYS,) + pack.shape, BF16),
            pltpu.VMEM((16, 2 * length), F32),
            pltpu.VMEM((rows, D), BF16),
        ]
        + sems(2 * depth) + sems(3 * N_FRONT) + sems(WAYS),
        compiler_params=pltpu.CompilerParams(collective_id=1, has_side_effects=True, vmem_limit_bytes=VMEM_LIMIT),
    )(inv, own, tok, pack, buckets, buckets_back, *weight_shards)


def reduce_kernel(peers, left_index, *refs):
    n_left = len(set(left_index))
    n_mats = len(left_index)
    lefts, rights = refs[:n_left], refs[n_left : n_left + n_mats]
    g_in, g_out, small, out, small_out = refs[n_left + n_mats : n_left + n_mats + 5]
    (prod, own, sa, ra, sb, rb, sc, rc, sd, rd, tiny, tiny_in, *sem) = refs[n_left + n_mats + 5 :]
    sem_a, sem_b, sem_c, sem_d, sem_e, sem_f, sem_g, sem_t = [sem[2 * i : 2 * i + 2] for i in range(8)]
    at = Place(peers)
    depth = at.depth
    quarter, wide = out.shape[1], out.shape[2]
    half, part = wide // 2, quarter // depth
    total = out.shape[0]
    sent = []

    def go(copy):
        copy.start()
        sent.append(copy)
        return copy

    columns = lambda b: pl.ds(pl.multiple_of(b * half, LANES), half)
    shard_rows = lambda f: pl.ds(pl.multiple_of(f * quarter, quarter), quarter)
    part_rows = lambda a: pl.ds(pl.multiple_of(a * part, part), part)
    mine, theirs = columns(at.b), columns(1 - at.b)

    greet(
        [at.core, at.across, at.beside]
        + [at.column(at.ahead(d)) for d in range(1, depth)]
        + [(at.c, (1 - at.x) * 2 + 1 - at.k)]
    )

    def stage_a(i):
        prod[...] = tn(lefts[left_index[i]][...], rights[i][...])
        for x in range(2):
            own[i, x] = prod[shard_rows(x * 2 + at.k), :]
            sa[i, x] = prod[shard_rows(x * 2 + 1 - at.k), :].astype(BF16)
        go(remote(sa.at[i], ra.at[i], sem_a, i, at.core))

    def stage_b(i):
        remote(sa.at[i], ra.at[i], sem_a, i, at.core).wait_recv()
        sb[i] = (own[i, 1 - at.x] + ra[i, 1 - at.x].astype(F32)).astype(BF16)
        go(remote(sb.at[i], rb.at[i], sem_b, i, at.across))

    def stage_c(j):
        if j < n_mats:
            remote(sb.at[j], rb.at[j], sem_b, j, at.across).wait_recv()
            value = own[j, at.x] + ra[j, at.x].astype(F32) + rb[j].astype(F32)
            sc[j] = value.astype(BF16)
        go(remote(sc.at[j, :, theirs], rc.at[j], sem_c, j, at.beside))

    def stage_d(j):
        remote(sc.at[j, :, mine], rc.at[j], sem_c, j, at.beside).wait_recv()
        value = sc[j, :, mine].astype(F32) + rc[j].astype(F32)
        sd[j] = value.astype(BF16)
        for d in range(1, depth):
            go(remote(sd.at[j, part_rows(at.ahead(d))], rd.at[j, part_rows(at.a)], sem_d, j * depth + d, at.column(at.ahead(d))))

    def stage_e(j):
        value = sd[j, part_rows(at.a), :].astype(F32)
        for d in range(1, depth):
            slot = rd.at[j, part_rows(at.behind(d))]
            remote(slot, slot, sem_d, j * depth + d, at.column(at.behind(d))).wait_recv()
            value += slot[...].astype(F32)
        spot = out.at[j, part_rows(at.a), mine]
        spot[...] = value.astype(BF16)
        for d in range(1, depth):
            go(remote(spot, spot, sem_e, j * depth + d, at.column(at.ahead(d))))

    def stage_f(j):
        for d in range(1, depth):
            spot = out.at[j, part_rows(at.behind(d)), mine]
            remote(spot, spot, sem_e, j * depth + d, at.column(at.behind(d))).wait_recv()
        go(remote(out.at[j, :, mine], out.at[j, :, mine], sem_f, j, at.beside))

    def stage_g(j):
        remote(out.at[j, :, theirs], out.at[j, :, theirs], sem_f, j, at.beside).wait_recv()

    order = list(range(n_mats + WAYS, n_mats + 2 * WAYS)) + list(range(n_mats)) + list(range(n_mats, n_mats + WAYS))
    for q in range(WAYS):
        sc[n_mats + WAYS + q] = g_out[q * quarter : (q + 1) * quarter, :]
    tiny[0] = small[...]
    hops = [at.core, at.across, at.beside]
    for t in range(total + 4):
        if 4 <= t:
            stage_g(order[t - 4])
        if 3 <= t < total + 3:
            stage_f(order[t - 3])
        if 2 <= t < total + 2:
            stage_e(order[t - 2])
        if 1 <= t < total + 1:
            stage_d(order[t - 1])
        if t == total - WAYS:
            for d in range(1, WAYS):
                slot = sc.at[n_mats + lax.rem(at.f + WAYS - d, WAYS)]
                remote(slot, slot, sem_g, d, at.group(WAYS - d)).wait_recv()
        if t < total:
            stage_c(order[t])
        if 1 <= t <= n_mats:
            stage_b(t - 1)
        if t < n_mats:
            stage_a(t)
        if t == n_mats:
            sc[n_mats + at.f] = g_in[shard_rows(at.f), :]
            for d in range(1, WAYS):
                f = lax.rem(at.f + d, WAYS)
                go(remote(g_in.at[shard_rows(f)], sc.at[n_mats + at.f], sem_g, d, at.group(d)))
        if t < 4:
            if t:
                remote(tiny.at[t - 1], tiny_in.at[t - 1], sem_t, t - 1, hops[t - 1]).wait_recv()
                tiny[t] = tiny[t - 1] + tiny_in[t - 1]
            if t < 3:
                go(remote(tiny.at[t], tiny_in.at[t], sem_t, t, hops[t]))
            else:
                for d in range(1, depth):
                    go(remote(tiny.at[3], tiny_in.at[2 + d], sem_t, 2 + d, at.column(at.ahead(d))))
        if t == 4:
            value = tiny[3]
            for d in range(1, depth):
                remote(tiny.at[3], tiny_in.at[2 + d], sem_t, 2 + d, at.column(at.behind(d))).wait_recv()
                value += tiny_in[2 + d]
            small_out[...] = value
    for copy in sent:
        copy.wait_send()


def reduce_grads(peers, pairs, g_in, g_out, small):
    lefts, left_index = [], []
    for left, _ in pairs:
        for i, seen in enumerate(lefts):
            if seen is left:
                break
        else:
            lefts.append(left)
            i = len(lefts) - 1
        left_index.append(i)
    rights = [right for _, right in pairs]
    n, total = len(pairs), len(pairs) + 2 * WAYS
    width = g_in.shape[1]
    quarter, half, depth = width // WAYS, width // 2, peers // 2
    return pl.pallas_call(
        functools.partial(reduce_kernel, peers, left_index),
        name="reduce_grads",
        out_shape=[sds((total, quarter, width), BF16), sds(small.shape, F32)],
        in_specs=[full_spec()] * (len(lefts) + n + 3),
        out_specs=[full_spec()] * 2,
        scratch_shapes=[
            pltpu.VMEM((width, width), F32),
            pltpu.VMEM((n, 2, quarter, width), F32),
            pltpu.VMEM((n, 2, quarter, width), BF16),
            pltpu.VMEM((n, 2, quarter, width), BF16),
            pltpu.VMEM((n, quarter, width), BF16),
            pltpu.VMEM((n, quarter, width), BF16),
            pltpu.VMEM((total, quarter, width), BF16),
            pltpu.VMEM((total, quarter, half), BF16),
            pltpu.VMEM((total, quarter, half), BF16),
            pltpu.VMEM((total, quarter, half), BF16),
            pltpu.VMEM((4,) + small.shape, F32),
            pltpu.VMEM((3 + depth,) + small.shape, F32),
        ]
        + sems(n) + sems(n) + sems(total) + sems(total * depth) + sems(total * depth) + sems(total) + sems(WAYS) + sems(3 + depth),
        compiler_params=pltpu.CompilerParams(collective_id=0, has_side_effects=True, vmem_limit_bytes=VMEM_LIMIT),
    )(*lefts, *rights, g_in, g_out, small)


def norm_back(x, gain, dy):
    r = lax.rsqrt(jnp.mean(x * x, axis=-1, keepdims=True) + EPSILON)
    gdy = gain * dy
    dx = r * gdy - x * (r * r * r) * jnp.mean(x * gdy, axis=-1, keepdims=True)
    return dx, jnp.sum(dy * x * r, axis=0)


def gather(x, axis_name, axis=0):
    return lax.all_gather(x, axis_name, axis=axis, tiled=True)


def scatter(x, axis_name, axis=0):
    return lax.psum_scatter(x, axis_name, scatter_dimension=axis, tiled=True)


def shards(
    tokens,
    memory,
    piece_order,
    bucket_table,
    passage_lengths,
    self_gain,
    cross_gain,
    hidden_gain,
    position_bias,
    self_query,
    self_attention_key,
    self_value,
    self_output,
    cross_query,
    cross_key,
    cross_value,
    cross_output,
    hidden_in,
    hidden_out,
    grad_output,
):
    tok, mem, grad = tokens[0], memory[0], grad_output[0]
    rows, slots = tok.shape[0], mem.shape[0]
    length = (bucket_table.shape[0] + 1) // 2
    peers = length // rows
    index = lax.axis_index("ctx")
    own = lax.dynamic_slice_in_dim(piece_order, index * (rows // PIECE), rows // PIECE)
    f = lax.axis_index("fsdp")
    quarter, eighth = self_query.shape[0], position_bias.shape[0]
    slots_all = jnp.arange(piece_order.shape[0], dtype=jnp.int32)
    inv = jnp.sum(jnp.where(piece_order[None, :] == slots_all[:, None], slots_all[None, :], 0), axis=1)
    own_facts = jnp.stack(
        [own, own % 2, (length - (own + own % 2) * PIECE) // LANES, (own * PIECE // BLOCK + 1) * BLOCK], axis=1
    )
    pack = jnp.zeros((N_GAINS + BUCKETS, D), BF16)
    pack = lax.dynamic_update_slice(pack, jnp.stack([self_gain, cross_gain, hidden_gain]), (0, f * quarter))
    pack = lax.dynamic_update_slice(pack, position_bias, (N_GAINS + f * eighth, 0))
    buckets = jnp.pad(bucket_table, (0, 1), constant_values=-1)[None]
    buckets_back = jnp.pad(bucket_table[::-1], (0, 1), constant_values=-1)[None]
    hot = (buckets == jnp.arange(BUCKETS, dtype=jnp.int32)[:, None]).astype(F32)
    weights, gains, ahead, behind, q1_nat, k1_nat, v1_nat, a1, o1, h1, a2, q2, lse1 = front(
        peers,
        inv,
        own_facts,
        tok,
        pack,
        buckets,
        buckets_back,
        [self_query, self_attention_key, self_value, self_output, cross_query, cross_key, cross_value],
    )
    wq1, wk1, wv1, wo, wq2, wk2, wv2 = [weights[i] for i in range(N_FRONT)]
    w_co = gather(cross_output, "fsdp")
    w_in = lax.all_to_all(hidden_in, "fsdp", split_axis=1, concat_axis=0, tiled=True)
    k2, v2 = project(mem, wk2).astype(BF16), project(mem, wv2).astype(BF16)
    slot = index * slots + jnp.arange(slots, dtype=jnp.int32)
    hidden = jnp.where(slot % PLEN < jnp.take(passage_lengths[0], slot // PLEN), 0.0, NEGATIVE)
    q2_all = gather(q2, "ctx")
    part, part_lse = cross_forward(q2_all, k2, v2, hidden[None, :])
    swap = lambda x: lax.all_to_all(x.reshape(peers, rows, x.shape[-1]), "ctx", 0, 0)
    part, part_lse = swap(part), swap(part_lse)[:, :, :HEADS]
    top = jnp.max(part_lse, axis=0)
    share = jnp.exp(part_lse - top)
    lse2 = top + jnp.log(jnp.sum(share, axis=0))
    share = share / jnp.sum(share, axis=0)
    out2 = jnp.sum(jnp.repeat(share, HEAD_DIM, axis=2) * part.astype(F32), axis=0)
    o2 = out2.astype(BF16)
    h2 = h1 + project(o2, w_co)
    a3 = norm_scale(h2, gains[2]).astype(BF16)
    a3_all, g_all = gather(a3, "fsdp"), gather(grad, "fsdp")
    pre = project(a3_all, w_in)
    act, pullback = jax.vjp(smooth_gate, pre)
    act = act.astype(BF16)
    out_part = project(act, hidden_out)
    dpre = pullback(nt(g_all, hidden_out))[0].astype(BF16)
    da3_part = nt(dpre, w_in)
    da3 = scatter(da3_part.astype(BF16), "fsdp").astype(F32)
    layer_output = (h2 + scatter(out_part.astype(BF16), "fsdp").astype(F32)).astype(BF16)
    g_out = tn(act, g_all).astype(BF16)
    g_in = tn(a3_all, dpre).astype(BF16)
    dx, gg3 = norm_back(h2, gains[2], da3)
    dh2 = grad.astype(F32) + dx
    branch2 = dh2.astype(BF16)
    do2 = nt(branch2, w_co).astype(BF16)
    delta = lambda d, o: jnp.sum((d.astype(F32) * o).reshape(rows, HEADS, HEAD_DIM), axis=2)
    pad4 = lambda x: jnp.pad(x, ((0, 0), (0, 4)))
    stat2 = jnp.concatenate([pad4(lse2), pad4(delta(do2, out2))], 1)
    do2_all = gather(do2, "ctx")
    stat2_all = gather(stat2.T, "ctx", 1)
    dq2_part, dk2, dv2 = cross_backward(q2_all, do2_all, stat2_all, k2, v2, hidden[:, None])
    dq2 = scatter(dq2_part, "ctx").astype(BF16)
    dx, gg2 = norm_back(h1, gains[1], nt(dq2, wq2))
    dh1 = dh2 + dx
    branch1 = dh1.astype(BF16)
    do1 = nt(branch1, wo).astype(BF16)
    stat1 = jnp.pad(jnp.concatenate([lse1[:, :16], pad4(delta(do1, o1.astype(F32)))], 1), ((0, 0), (0, LANES - 32)))
    do1_all = gather(do1, "ctx")
    stat1_all = gather(stat1, "ctx")
    dq1, dk1, dv1, diag = self_backward(
        piece_order, own, q1_nat, k1_nat, v1_nat, do1_all, do1, stat1_all, stat1, ahead, behind
    )
    g_bias = jnp.einsum(
        "hr,lr->lh", diag[:HEADS], hot, precision=lax.Precision.HIGHEST, preferred_element_type=F32
    )
    da1 = nt(dq1, wq1) + nt(dk1, wk1) + nt(dv1, wv1)
    tok_wide = tok.astype(F32)
    dx, gg1 = norm_back(tok_wide, gains[0], da1)
    grad_tokens = (dh1 + dx).astype(BF16)
    grad_memory = (nt(dk2, wk2) + nt(dv2, wv2)).astype(BF16)
    small = jnp.concatenate(
        [jnp.stack([gg1, gg2, gg3]), jnp.pad(g_bias, ((0, 0), (0, D - HEADS)))], 0
    )
    small = jnp.pad(small, ((0, -small.shape[0] % 8), (0, 0)))
    pairs = [
        (a1, dq1),
        (a1, dk1),
        (a1, dv1),
        (o1, branch1),
        (a2, dq2),
        (mem, dk2),
        (mem, dv2),
        (o2, branch2),
    ]
    total, small = reduce_grads(peers, pairs, g_in, g_out, small)
    total = total.astype(F32)
    gain = lambda i: lax.dynamic_slice_in_dim(small[i], f * quarter, quarter)
    bias_out = lax.dynamic_slice_in_dim(small[3:], f * eighth, eighth)[:, :HEADS]
    count = len(pairs)
    return (
        layer_output[None],
        grad_tokens[None],
        grad_memory[None],
        gain(0),
        gain(1),
        gain(2),
        bias_out,
        *[total[i] for i in range(count)],
        jnp.concatenate([total[count + i] for i in range(WAYS)], 1),
        total[count + WAYS :].reshape(-1, D),
    )


def pick(*arrays):
    resident = (arrays[3].shape[0] + 1) // 2 <= RESIDENT_ROWS
    return (shards if resident else streamed_shards)(*arrays)


def solution(mesh):
    return jax.shard_map(
        pick,
        mesh=mesh,
        in_specs=(
            P("fsdp", "ctx", None),
            P("fsdp", "ctx", None),
            P(),
            P(),
            P("fsdp", None),
            P("fsdp"),
            P("fsdp"),
            P("fsdp"),
            P("fsdp", None),
            P("fsdp", None),
            P("fsdp", None),
            P("fsdp", None),
            P("fsdp", None),
            P("fsdp", None),
            P("fsdp", None),
            P("fsdp", None),
            P("fsdp", None),
            P("fsdp", None),
            P("fsdp", None),
            P("fsdp", "ctx", None),
        ),
        out_specs=(
            P("fsdp", "ctx", None),
            P("fsdp", "ctx", None),
            P("fsdp", "ctx", None),
            P("fsdp"),
            P("fsdp"),
            P("fsdp"),
            P("fsdp", None),
            P("fsdp", None),
            P("fsdp", None),
            P("fsdp", None),
            P("fsdp", None),
            P("fsdp", None),
            P("fsdp", None),
            P("fsdp", None),
            P("fsdp", None),
            P("fsdp", None),
            P("fsdp", None),
        ),
        check_vma=False,
    )
```

```python
import functools

import jax
import jax.numpy as jnp
from jax import lax
from jax.experimental import pallas as pl
from jax.experimental.pallas import tpu as pltpu
from jax.sharding import PartitionSpec as P

D = 768
HEADS = 12
PAIRS = HEADS // 2
HEAD_DIM = 64
PIECE = 64
BLOCK = 256
PLEN = 256
KBLK = 512
PSG = 20
BUCKETS = 32
RESIDENT_ROWS = 1024
LANES = 128
EPSILON = 1e-06
NEGATIVE = -1e30
F32 = jnp.float32
BF16 = jnp.bfloat16
VMEM_LIMIT = 60 * 2**20

def nn(a, b):
    return lax.dot_general(a, b, (((1,), (0,)), ((), ())), preferred_element_type=F32)
def nt(a, b):
    return lax.dot_general(a, b, (((1,), (1,)), ((), ())), preferred_element_type=F32)
def tn(a, b):
    return lax.dot_general(a, b, (((0,), (0,)), ((), ())), preferred_element_type=F32)

def normed(x, gain):
    return x * lax.rsqrt(jnp.mean(x * x, axis=-1, keepdims=True) + EPSILON) * gain

def half_mask(x, half):
    lane = lax.broadcasted_iota(jnp.int32, x.shape, 1) // HEAD_DIM
    return jnp.where(lane == half, x, jnp.zeros_like(x))

def lanes_of(pair):
    return pl.ds(pl.multiple_of(pair * LANES, LANES), LANES)

def shear(x, sign):
    row = lax.broadcasted_iota(jnp.int32, x.shape, 0)
    for bit in (1, 2, 4):
        x = jnp.where(row & bit != 0, pltpu.roll(x, (sign * bit) % x.shape[1], 1), x)
    return x

def piece_bias(tables, h, piece, length):
    start = pl.multiple_of(length - (piece + piece % 2) * PIECE, LANES)
    return tables[piece % 2, h, :, pl.ds(start, length)].astype(F32)

def bias_rows(tables, h, own, count, length):
    return jnp.concatenate([piece_bias(tables, h, own[i], length) for i in range(count)], 0)

def bias_at(tables, h, own, count, length):
    parts = []
    for i in range(count):
        parts.append(tables[own[i, 1], h, :, pl.ds(own[i, 2] * LANES, length)].astype(F32))
    return jnp.concatenate(parts, 0)


def add_diagonals(acc, block, piece):
    rows, length = block.shape
    wide = jnp.concatenate([block, jnp.zeros((rows, LANES), F32)], axis=1)
    total = pltpu.roll(wide[0:8], LANES, 1)
    for g in range(1, rows // 8):
        total += pltpu.roll(wide[8 * g:8 * g + 8], LANES - 8 * g, 1)
    start = pl.multiple_of(length - (piece - piece % 2) * PIECE - LANES, LANES)
    where = (piece % 2, slice(None), pl.ds(start, length + LANES))
    acc[where] += total

def full_spec():
    return pl.BlockSpec(memory_space=pltpu.VMEM)
def smem_spec():
    return pl.BlockSpec(memory_space=pltpu.SMEM)
def sds(shape, dtype):
    return jax.ShapeDtypeStruct(shape, dtype)

def self_backward_kernel(order, own, q_nat, k_nat, v_nat, do_slot, do_own, stat_slot, stat_own, delta_own, table, back_table,
                         dq, dk, dv, diag, inv, q_own, k_own, v_own, do_nat, stat_nat, stat_t, acc):
    length = q_nat.shape[0]
    rows = do_own.shape[0]
    full = 2 * length
    slots, mine = length // PIECE, rows // PIECE
    per = BLOCK // PIECE
    for s in range(slots):
        inv[order[s]] = s
    def move(i, c):
        src = pl.ds(pl.multiple_of(inv[i] * PIECE, PIECE), PIECE)
        dst = pl.ds(pl.multiple_of(i * PIECE, PIECE), PIECE)
        do_nat[dst, :] = do_slot[src, :]
        stat_nat[dst, :] = stat_slot[src, :]
        return c
    lax.fori_loop(0, slots, move, 0)
    for i in range(length // LANES):
        stat_t[:, i * LANES:(i + 1) * LANES] = stat_nat[i * LANES:(i + 1) * LANES, :].T
    for i in range(mine):
        src = pl.ds(pl.multiple_of(own[i] * PIECE, PIECE), PIECE)
        dst = slice(i * PIECE, (i + 1) * PIECE)
        q_own[dst, :] = q_nat[src, :]
        k_own[dst, :] = k_nat[src, :]
        v_own[dst, :] = v_nat[src, :]
    lane = lax.broadcasted_iota(jnp.int32, (rows, length), 1)
    limit = jnp.concatenate([jnp.full((PIECE, 1), (own[i] // per + 1) * BLOCK, jnp.int32) for i in range(mine)], 0)
    first = jnp.concatenate([jnp.full((PIECE, 1), (own[i] // per) * BLOCK, jnp.int32) for i in range(mine)], 0)
    visible, seen = lane < limit, lane >= first
    stat_lane = lax.broadcasted_iota(jnp.int32, (rows, LANES), 1)

    def column(h):
        return jnp.sum(jnp.where(stat_lane == h, stat_own[...], 0.0), axis=1, keepdims=True)

    diag[...] = jnp.zeros_like(diag)
    def pair(p, c):
        sl = lanes_of(p)
        q, k, v, do = q_own[:, sl], k_nat[:, sl], v_nat[:, sl], do_own[:, sl]
        kq, vq, qa, da = k_own[:, sl], v_own[:, sl], q_nat[:, sl], do_nat[:, sl]
        dqp = jnp.zeros((rows, LANES), F32)
        dkp = jnp.zeros((rows, LANES), F32)
        dvp = jnp.zeros((rows, LANES), F32)
        for half in range(2):
            h = 2 * p + half
            bias = bias_rows(table, h, own, mine, length)
            km, vm = half_mask(k, half), half_mask(v, half)
            s = jnp.where(visible, nt(q, km) + bias, NEGATIVE)
            e = jnp.exp(s - column(h))
            ds = e * (nt(do, vm) - column(16 + h))
            dqp += nn(ds.astype(BF16), km)
            acc[...] = jnp.zeros_like(acc)
            for i in range(mine):
                add_diagonals(acc, ds[i * PIECE:(i + 1) * PIECE, :], own[i])
            joined = shear(acc[0] + pltpu.roll(acc[1], full - PIECE, 1), -1)
            diag[pl.ds(h, 1), :] = jnp.sum(pltpu.roll(joined, full - 1, 1), axis=0, keepdims=True)
            bias = bias_rows(back_table, h, own, mine, length)
            s = jnp.where(seen, nt(half_mask(kq, half), qa) + bias, NEGATIVE)
            e = jnp.exp(s - stat_t[pl.ds(h, 1), :])
            dvp += nn(e.astype(BF16), half_mask(da, half))
            ds = e * (nt(half_mask(vq, half), da) - stat_t[pl.ds(16 + h, 1), :])
            dkp += nn(ds.astype(BF16), half_mask(qa, half))
        dq[:, sl] = dqp.astype(BF16)
        dk[:, sl] = dkp.astype(BF16)
        dv[:, sl] = dvp.astype(BF16)
        return c
    lax.fori_loop(0, PAIRS, pair, 0)

def self_backward(order, own, q_nat, k_nat, v_nat, do_slot, do_own, stat_slot, stat_own, table, back_table):
    length, rows = q_nat.shape[0], do_own.shape[0]
    def kern(order, own, q_nat, k_nat, v_nat, do_slot, do_own, stat_slot, stat_own, table, back_table, *rest):
        self_backward_kernel(order, own, q_nat, k_nat, v_nat, do_slot, do_own, stat_slot, stat_own, None, table, back_table, *rest)
    return pl.pallas_call(
        kern,
        name="self_backward",
        out_shape=[sds((rows, D), BF16)] * 3 + [sds((16, 2 * length), F32)],
        in_specs=[smem_spec()] * 2 + [full_spec()] * 9,
        out_specs=[full_spec()] * 4,
        scratch_shapes=[pltpu.SMEM((length // PIECE,), jnp.int32)] + [pltpu.VMEM((rows, D), BF16)] * 3
        + [pltpu.VMEM((length, D), BF16), pltpu.VMEM((length, LANES), F32), pltpu.VMEM((LANES, length), F32), pltpu.VMEM((2, 8, 2 * length), F32)],
        compiler_params=pltpu.CompilerParams(vmem_limit_bytes=VMEM_LIMIT),
    )(order, own, q_nat, k_nat, v_nat, do_slot, do_own, stat_slot, stat_own, table, back_table)


def norm_scale(values, gain_vector):
    return (
        values
        * lax.rsqrt(jnp.mean(values * values, axis=-1, keepdims=True) + EPSILON)
        * gain_vector
    )


def smooth_gate(values):
    return jax.nn.gelu(values, approximate=True)


def project(operand, matrix):
    return jnp.dot(operand, matrix, preferred_element_type=jnp.float32)


def project_back(operand, matrix):
    return jnp.einsum("sra,ba->srb", operand, matrix, preferred_element_type=jnp.float32)


def weight_grad(inputs, upstream):
    return jnp.einsum("sra,srb->ab", inputs, upstream, preferred_element_type=jnp.float32)


def to_heads(matrix):
    return matrix.reshape(matrix.shape[0], matrix.shape[1], HEADS, HEAD_DIM)


def heads_first(matrix):
    return jnp.transpose(to_heads(matrix), (0, 2, 1, 3))


def from_heads(tensor):
    return jnp.transpose(tensor, (0, 2, 1, 3)).reshape(
        tensor.shape[0], tensor.shape[2], HEADS * HEAD_DIM
    )


def block_scores(queries, keys_all, values_all, extras, offset):
    key_block = lax.dynamic_slice_in_dim(keys_all, offset, KBLK, 1)
    value_block = lax.dynamic_slice_in_dim(values_all, offset, KBLK, 1)
    added_bias, visible, bucket_indicator = extras(offset)
    scores = (
        jnp.einsum("sqhd,skhd->shqk", queries, key_block, preferred_element_type=jnp.float32)
        + added_bias
    )
    block_maximum = jnp.max(jnp.where(visible, scores, NEGATIVE), axis=-1)
    weights = jnp.exp(jnp.where(visible, scores - block_maximum[..., None], NEGATIVE))
    return (key_block, value_block, bucket_indicator, block_maximum, weights)


def attend_forward(queries, keys_all, values_all, extras):
    block_count = keys_all.shape[1] // KBLK

    def single_block_tile(carried, block_index):
        key_block, value_block, bucket_indicator, block_maximum, weights = block_scores(
            queries, keys_all, values_all, extras, block_index * KBLK
        )
        numerator = jnp.einsum(
            "shqk,skhd->shqd",
            weights.astype(jnp.bfloat16),
            value_block,
            preferred_element_type=jnp.float32,
        )
        return (carried, (block_maximum, jnp.sum(weights, axis=-1), numerator))

    ignored, stacked = lax.scan(
        single_block_tile, jnp.zeros((), jnp.float32), jnp.arange(block_count, dtype=jnp.int32)
    )
    block_maximum, block_sum, numerator = stacked
    row_maximum = jnp.max(block_maximum, axis=0)
    rescale = jnp.exp(block_maximum - row_maximum)
    row_total = jnp.sum(rescale * block_sum, axis=0)
    output = jnp.sum(rescale[..., None] * numerator, axis=0) / row_total[..., None]
    return (output, row_maximum, row_total)


def attend_backward(
    queries, keys_all, values_all, extras, grad_out, output, row_maximum, row_total
):
    block_count = keys_all.shape[1] // KBLK
    grad_wide = grad_out.astype(jnp.float32)
    row_dot = jnp.sum(grad_wide * output, axis=-1)
    scaled = grad_wide / row_total[..., None]
    sum_weight = -row_dot / row_total
    initial = (
        jnp.zeros(queries.shape, jnp.float32),
        jnp.zeros(keys_all.shape, jnp.float32),
        jnp.zeros(values_all.shape, jnp.float32),
        jnp.zeros((BUCKETS, HEADS), jnp.float32),
    )

    def single_block_tile(carried, block_index):
        grad_query, grad_keys, grad_values, grad_bias = carried
        offset = block_index * KBLK
        key_block, value_block, bucket_indicator, block_maximum, weights = block_scores(
            queries, keys_all, values_all, extras, offset
        )
        rescale = jnp.exp(block_maximum - row_maximum)
        grad_numerator = (scaled * rescale[..., None]).astype(jnp.bfloat16)
        grad_weights = (
            jnp.einsum(
                "shqd,skhd->shqk", grad_numerator, value_block, preferred_element_type=jnp.float32
            )
            + (sum_weight * rescale)[..., None]
        )
        grad_scores = weights * grad_weights
        gradient_bfloat_cast = grad_scores.astype(jnp.bfloat16)
        grad_query = grad_query + jnp.einsum(
            "shqk,skhd->sqhd", gradient_bfloat_cast, key_block, preferred_element_type=jnp.float32
        )
        key_part = jnp.einsum(
            "shqk,sqhd->skhd", gradient_bfloat_cast, queries, preferred_element_type=jnp.float32
        )
        value_part = jnp.einsum(
            "shqk,shqd->skhd",
            weights.astype(jnp.bfloat16),
            grad_numerator,
            preferred_element_type=jnp.float32,
        )
        grad_keys = lax.dynamic_update_slice_in_dim(grad_keys, key_part, offset, 1)
        grad_values = lax.dynamic_update_slice_in_dim(grad_values, value_part, offset, 1)
        if bucket_indicator is not None:
            remainder_portion = (grad_scores - gradient_bfloat_cast.astype(jnp.float32)).astype(
                jnp.bfloat16
            )
            grad_bias = (
                grad_bias
                + jnp.einsum(
                    "uljf,pjf->pl",
                    gradient_bfloat_cast,
                    bucket_indicator,
                    preferred_element_type=jnp.float32,
                )
                + jnp.einsum(
                    "uljf,pjf->pl",
                    remainder_portion,
                    bucket_indicator,
                    preferred_element_type=jnp.float32,
                )
            )
        return ((grad_query, grad_keys, grad_values, grad_bias), None)

    result, ignored = lax.scan(single_block_tile, initial, jnp.arange(block_count, dtype=jnp.int32))
    return result


def streamed_shards(
    tokens,
    memory,
    piece_order,
    bucket_table,
    passage_lengths,
    self_gain,
    cross_gain,
    hidden_gain,
    position_bias,
    self_query,
    self_attention_key,
    self_value,
    self_output,
    cross_query,
    cross_key,
    cross_value,
    cross_output,
    hidden_in,
    hidden_out,
    grad_output,
):
    (
        gain_one,
        gain_two,
        gain_three,
        position_bias_lookup,
        query_full,
        key_full,
        value_full,
        output_full,
        cross_query_full,
        cross_key_full,
        cross_value_full,
        cross_output_full,
        inner_full,
        outer_full,
    ) = (
        lax.all_gather(self_gain, "fsdp", axis=0, tiled=True),
        lax.all_gather(cross_gain, "fsdp", axis=0, tiled=True),
        lax.all_gather(hidden_gain, "fsdp", axis=0, tiled=True),
        lax.all_gather(position_bias, "fsdp", axis=0, tiled=True),
        lax.all_gather(self_query, "fsdp", axis=0, tiled=True),
        lax.all_gather(self_attention_key, "fsdp", axis=0, tiled=True),
        lax.all_gather(self_value, "fsdp", axis=0, tiled=True),
        lax.all_gather(self_output, "fsdp", axis=0, tiled=True),
        lax.all_gather(cross_query, "fsdp", axis=0, tiled=True),
        lax.all_gather(cross_key, "fsdp", axis=0, tiled=True),
        lax.all_gather(cross_value, "fsdp", axis=0, tiled=True),
        lax.all_gather(cross_output, "fsdp", axis=0, tiled=True),
        lax.all_gather(hidden_in, "fsdp", axis=0, tiled=True),
        lax.all_gather(hidden_out, "fsdp", axis=0, tiled=True),
    )
    gain_one = gain_one.astype(jnp.float32)
    gain_two = gain_two.astype(jnp.float32)
    gain_three = gain_three.astype(jnp.float32)
    sequence_count = tokens.shape[0]
    local_rows = tokens.shape[1]
    sequence_length = (bucket_table.shape[0] + 1) // 2
    memory_length = PSG * PLEN
    piece_offsets = jnp.arange(PIECE, dtype=jnp.int32)
    local_pieces = lax.dynamic_slice_in_dim(
        piece_order, lax.axis_index("ctx") * (local_rows // PIECE), local_rows // PIECE
    )
    query_position = (local_pieces[:, None] * PIECE + piece_offsets[None, :]).reshape(local_rows)
    key_position = (piece_order[:, None] * PIECE + piece_offsets[None, :]).reshape(sequence_length)
    bucket_numbers = jnp.arange(BUCKETS, dtype=jnp.int32)

    def self_extras(offset):
        key_block_position = lax.dynamic_slice_in_dim(key_position, offset, KBLK)
        relative_bucket_index = jnp.take(
            bucket_table,
            key_block_position[None, :] - query_position[:, None] + sequence_length - 1,
        )
        bucket_indicator = (
            relative_bucket_index[None, :, :] == bucket_numbers[:, None, None]
        ).astype(jnp.bfloat16)
        added_bias = jnp.einsum(
            "lvj,lf->fvj",
            bucket_indicator,
            position_bias_lookup,
            preferred_element_type=jnp.float32,
        )
        visible = key_block_position[None, :] // BLOCK <= query_position[:, None] // BLOCK
        return (added_bias, visible, bucket_indicator)

    slot_numbers = jnp.arange(PLEN, dtype=jnp.int32)
    memory_valid = (passage_lengths[:, :, None] > slot_numbers[None, None, :]).reshape(
        sequence_count, memory_length
    )

    def cross_extras(offset):
        visible = lax.dynamic_slice_in_dim(memory_valid, offset, KBLK, 1)[:, None, None, :]
        return (0.0, visible, None)

    inputs_wide = tokens.astype(jnp.float32)
    normed_one = norm_scale(inputs_wide, gain_one).astype(jnp.bfloat16)
    queries_one = project(normed_one, query_full).astype(jnp.bfloat16)
    keys_local = project(normed_one, key_full).astype(jnp.bfloat16)
    values_local = project(normed_one, value_full).astype(jnp.bfloat16)
    memory_keys = project(memory, cross_key_full).astype(jnp.bfloat16)
    memory_values = project(memory, cross_value_full).astype(jnp.bfloat16)
    keys_all, values_all, memory_keys_all, memory_values_all = (
        lax.all_gather(keys_local, "ctx", axis=1, tiled=True),
        lax.all_gather(values_local, "ctx", axis=1, tiled=True),
        lax.all_gather(memory_keys, "ctx", axis=1, tiled=True),
        lax.all_gather(memory_values, "ctx", axis=1, tiled=True),
    )
    output_one, maximum_one, total_one = attend_forward(
        to_heads(queries_one), to_heads(keys_all), to_heads(values_all), self_extras
    )
    attended_one = from_heads(output_one).astype(jnp.bfloat16)
    hidden_one = inputs_wide + project(attended_one, output_full)
    normed_two = norm_scale(hidden_one, gain_two).astype(jnp.bfloat16)
    queries_two = project(normed_two, cross_query_full).astype(jnp.bfloat16)
    output_two, maximum_two, total_two = attend_forward(
        to_heads(queries_two), to_heads(memory_keys_all), to_heads(memory_values_all), cross_extras
    )
    attended_two = from_heads(output_two).astype(jnp.bfloat16)
    hidden_two = hidden_one + project(attended_two, cross_output_full)
    normed_three = norm_scale(hidden_two, gain_three).astype(jnp.bfloat16)
    before_gate = project(normed_three, inner_full)
    gated_wide, gate_pullback = jax.vjp(smooth_gate, before_gate)
    activated = gated_wide.astype(jnp.bfloat16)
    layer_output = (hidden_two + project(activated, outer_full)).astype(jnp.bfloat16)
    grad_wide = grad_output.astype(jnp.float32)
    grad_outer = weight_grad(activated, grad_output)
    grad_activated = project_back(grad_output, outer_full)
    grad_before = gate_pullback(grad_activated)[0].astype(jnp.bfloat16)
    grad_inner = weight_grad(normed_three, grad_before)
    ignored, norm_pullback = jax.vjp(norm_scale, hidden_two, gain_three)
    grad_hidden_part, grad_gain_three = norm_pullback(project_back(grad_before, inner_full))
    grad_hidden_two = grad_wide + grad_hidden_part
    branch_two = grad_hidden_two.astype(jnp.bfloat16)
    grad_cross_output = weight_grad(attended_two, branch_two)
    grad_attended_two = project_back(branch_two, cross_output_full).astype(jnp.bfloat16)
    keys_back, values_back, memory_keys_back, memory_values_back = (
        keys_all,
        values_all,
        memory_keys_all,
        memory_values_all,
    )
    grad_query_two, grad_memory_keys, grad_memory_values, unused_bias = attend_backward(
        to_heads(queries_two),
        to_heads(memory_keys_back),
        to_heads(memory_values_back),
        cross_extras,
        heads_first(grad_attended_two),
        output_two,
        maximum_two,
        total_two,
    )
    memory_key_sum, memory_value_sum = (
        lax.psum_scatter(
            grad_memory_keys.reshape(sequence_count, memory_length, D),
            "ctx",
            scatter_dimension=1,
            tiled=True,
        ),
        lax.psum_scatter(
            grad_memory_values.reshape(sequence_count, memory_length, D),
            "ctx",
            scatter_dimension=1,
            tiled=True,
        ),
    )
    memory_key_rounded = memory_key_sum.astype(jnp.bfloat16)
    memory_value_rounded = memory_value_sum.astype(jnp.bfloat16)
    query_two_rounded = grad_query_two.reshape(sequence_count, local_rows, D).astype(jnp.bfloat16)
    grad_cross_query = weight_grad(normed_two, query_two_rounded)
    grad_cross_key = weight_grad(memory, memory_key_rounded)
    grad_cross_value = weight_grad(memory, memory_value_rounded)
    grad_memory = (
        project_back(memory_key_rounded, cross_key_full)
        + project_back(memory_value_rounded, cross_value_full)
    ).astype(jnp.bfloat16)
    ignored, norm_pullback = jax.vjp(norm_scale, hidden_one, gain_two)
    grad_hidden_part, grad_gain_two = norm_pullback(
        project_back(query_two_rounded, cross_query_full)
    )
    grad_hidden_one = grad_hidden_two + grad_hidden_part
    branch_one = grad_hidden_one.astype(jnp.bfloat16)
    grad_self_output = weight_grad(attended_one, branch_one)
    grad_attended_one = project_back(branch_one, output_full).astype(jnp.bfloat16)
    grad_query_one, grad_keys_all, grad_values_all, grad_bias = attend_backward(
        to_heads(queries_one),
        to_heads(keys_back),
        to_heads(values_back),
        self_extras,
        heads_first(grad_attended_one),
        output_one,
        maximum_one,
        total_one,
    )
    key_sum, value_sum = (
        lax.psum_scatter(
            grad_keys_all.reshape(sequence_count, sequence_length, D),
            "ctx",
            scatter_dimension=1,
            tiled=True,
        ),
        lax.psum_scatter(
            grad_values_all.reshape(sequence_count, sequence_length, D),
            "ctx",
            scatter_dimension=1,
            tiled=True,
        ),
    )
    query_one_rounded = grad_query_one.reshape(sequence_count, local_rows, D).astype(jnp.bfloat16)
    first_key_bfloat_cast = key_sum.astype(jnp.bfloat16)
    value_one_rounded = value_sum.astype(jnp.bfloat16)
    grad_self_query = weight_grad(normed_one, query_one_rounded)
    grad_self_key = weight_grad(normed_one, first_key_bfloat_cast)
    grad_self_value = weight_grad(normed_one, value_one_rounded)
    grad_normed_one = (
        project_back(query_one_rounded, query_full)
        + project_back(first_key_bfloat_cast, key_full)
        + project_back(value_one_rounded, value_full)
    )
    ignored, norm_pullback = jax.vjp(norm_scale, inputs_wide, gain_one)
    grad_input_part, grad_gain_one = norm_pullback(grad_normed_one)
    grad_tokens = (grad_hidden_one + grad_input_part).astype(jnp.bfloat16)
    (
        shard_gain_one,
        shard_gain_two,
        shard_gain_three,
        shard_bias,
        shard_query,
        shard_key,
        shard_value,
        shard_output,
        shard_cross_query,
        shard_cross_key,
        shard_cross_value,
        shard_cross_output,
        shard_inner,
        shard_outer,
    ) = (
        lax.psum_scatter(
            grad_gain_one.astype(jnp.bfloat16), "fsdp", scatter_dimension=0, tiled=True
        ).astype(jnp.float32),
        lax.psum_scatter(
            grad_gain_two.astype(jnp.bfloat16), "fsdp", scatter_dimension=0, tiled=True
        ).astype(jnp.float32),
        lax.psum_scatter(
            grad_gain_three.astype(jnp.bfloat16), "fsdp", scatter_dimension=0, tiled=True
        ).astype(jnp.float32),
        lax.psum_scatter(
            grad_bias.astype(jnp.bfloat16), "fsdp", scatter_dimension=0, tiled=True
        ).astype(jnp.float32),
        lax.psum_scatter(
            grad_self_query.astype(jnp.bfloat16), "fsdp", scatter_dimension=0, tiled=True
        ).astype(jnp.float32),
        lax.psum_scatter(
            grad_self_key.astype(jnp.bfloat16), "fsdp", scatter_dimension=0, tiled=True
        ).astype(jnp.float32),
        lax.psum_scatter(
            grad_self_value.astype(jnp.bfloat16), "fsdp", scatter_dimension=0, tiled=True
        ).astype(jnp.float32),
        lax.psum_scatter(
            grad_self_output.astype(jnp.bfloat16), "fsdp", scatter_dimension=0, tiled=True
        ).astype(jnp.float32),
        lax.psum_scatter(
            grad_cross_query.astype(jnp.bfloat16), "fsdp", scatter_dimension=0, tiled=True
        ).astype(jnp.float32),
        lax.psum_scatter(
            grad_cross_key.astype(jnp.bfloat16), "fsdp", scatter_dimension=0, tiled=True
        ).astype(jnp.float32),
        lax.psum_scatter(
            grad_cross_value.astype(jnp.bfloat16), "fsdp", scatter_dimension=0, tiled=True
        ).astype(jnp.float32),
        lax.psum_scatter(
            grad_cross_output.astype(jnp.bfloat16), "fsdp", scatter_dimension=0, tiled=True
        ).astype(jnp.float32),
        lax.psum_scatter(
            grad_inner.astype(jnp.bfloat16), "fsdp", scatter_dimension=0, tiled=True
        ).astype(jnp.float32),
        lax.psum_scatter(
            grad_outer.astype(jnp.bfloat16), "fsdp", scatter_dimension=0, tiled=True
        ).astype(jnp.float32),
    )
    (
        total_gain_one,
        total_gain_two,
        total_gain_three,
        total_bias,
        total_query,
        total_key,
        total_value,
        total_output,
        total_cross_query,
        total_cross_key,
        total_cross_value,
        total_cross_output,
        total_inner,
        total_outer,
    ) = lax.psum(
        (
            shard_gain_one,
            shard_gain_two,
            shard_gain_three,
            shard_bias,
            shard_query,
            shard_key,
            shard_value,
            shard_output,
            shard_cross_query,
            shard_cross_key,
            shard_cross_value,
            shard_cross_output,
            shard_inner,
            shard_outer,
        ),
        "ctx",
    )
    return (
        layer_output,
        grad_tokens,
        grad_memory,
        total_gain_one,
        total_gain_two,
        total_gain_three,
        total_bias,
        total_query,
        total_key,
        total_value,
        total_output,
        total_cross_query,
        total_cross_key,
        total_cross_value,
        total_cross_output,
        total_inner,
        total_outer,
    )


MESH = pl.DeviceIdType.MESH
WAYS = 4


class Place:
    def __init__(self, peers):
        self.depth = peers // 2
        c, f = lax.axis_index("ctx"), lax.axis_index("fsdp")
        self.c, self.f = c, f
        self.a, self.b, self.x, self.k = c // 2, c % 2, f // 2, f % 2
        self.core = (c, self.x * 2 + 1 - self.k)
        self.across = (c, (1 - self.x) * 2 + self.k)
        self.beside = (self.a * 2 + 1 - self.b, f)

    def ahead(self, d):
        return lax.rem(self.a + d, self.depth)

    def behind(self, d):
        return lax.rem(self.a + self.depth - d, self.depth)

    def column(self, a):
        return (a * 2 + self.b, self.f)

    def group(self, d):
        return (self.c, lax.rem(self.f + d, WAYS))


def greet(targets):
    barrier = pltpu.get_barrier_semaphore()
    for target in targets:
        pl.semaphore_signal(barrier, inc=1, device_id=target, device_id_type=MESH)
    pl.semaphore_wait(barrier, len(targets))


def remote(src, dst, sems, index, target):
    return pltpu.make_async_remote_copy(
        src_ref=src,
        dst_ref=dst,
        send_sem=sems[0].at[index],
        recv_sem=sems[1].at[index],
        device_id=target,
        device_id_type=MESH,
    )


def sems(count):
    return [pltpu.SemaphoreType.DMA((count,)), pltpu.SemaphoreType.DMA((count,))]


class Wire:
    def __init__(self, peers):
        self.at = Place(peers)
        self.depth = self.at.depth
        self.sent = []

    def go(self, copy):
        copy.start()
        self.sent.append(copy)

    def drain(self):
        for copy in self.sent:
            copy.wait_send()

    def partners(self):
        at = self.at
        return (
            [at.group(d) for d in range(1, WAYS)]
            + [at.beside]
            + [at.column(at.ahead(d)) for d in range(1, self.depth)]
        )

    def near(self, step):
        a, last = self.at.a, self.depth - 1
        low = jnp.where(step - 1 < a, step - 1, step)
        mirrored = jnp.where(step - 1 < last - a, step - 1, step)
        return jnp.where(2 * a < last, low, last - mirrored)

    def slot(self, buf, c):
        if len(buf.shape) == 3:
            return buf.at[c]
        rows = buf.shape[0] // (2 * self.depth)
        return buf.at[pl.ds(pl.multiple_of(c * rows, rows), rows)]

    def spread(self, src, buf, sem):
        at = self.at
        slot = self.slot(buf, at.c)
        self.go(remote(src, slot, sem, at.a, at.beside))
        for step in range(1, self.depth):
            self.go(remote(src, slot, sem, self.depth + at.a, at.column(self.near(step))))

    def relay(self, buf, sem, step):
        a = self.near(step)
        slot = self.slot(buf, a * 2 + self.at.b)
        remote(slot, slot, sem, self.depth + a, self.at.beside).wait_recv()
        self.go(remote(slot, slot, sem, a, self.at.beside))

    def from_beside(self, buf, sem, a):
        slot = self.slot(buf, a * 2 + 1 - self.at.b)
        remote(slot, slot, sem, a, self.at.beside).wait_recv()

    def shard(self, full, f):
        quarter = full.shape[0] // WAYS
        return full.at[pl.ds(pl.multiple_of(f * quarter, quarter), quarter)]

    def weight_start(self, src, full, sem, i):
        at = self.at
        slot = self.shard(full, at.f)
        slot[...] = src[...]
        self.go(remote(src, slot, sem, 3 * i, at.across))
        self.go(remote(src, slot, sem, 3 * i + 1, at.core))

    def weight_relay(self, full, sem, i):
        at = self.at
        slot = self.shard(full, (1 - at.x) * 2 + at.k)
        remote(slot, slot, sem, 3 * i, at.across).wait_recv()
        self.go(remote(slot, slot, sem, 3 * i + 2, at.core))

    def weight_ready(self, full, sem, i):
        at = self.at
        slot = self.shard(full, at.x * 2 + 1 - at.k)
        remote(slot, slot, sem, 3 * i + 1, at.core).wait_recv()
        slot = self.shard(full, (1 - at.x) * 2 + 1 - at.k)
        remote(slot, slot, sem, 3 * i + 2, at.core).wait_recv()


def fill_tables(table, out):
    full = table.shape[1]

    def head(h, c):
        base = shear(pltpu.roll(jnp.broadcast_to(table[pl.ds(h, 1), :], (8, full)), 1, 1), 1)
        for parity in range(2):
            for i in range(PIECE // 16):
                shifts = [(8 * g - 64 * parity) % full for g in (2 * i, 2 * i + 1)]
                both = [pltpu.roll(base, s, 1) if s else base for s in shifts]
                out[parity, h, 16 * i : 16 * i + 16, :] = jnp.concatenate(both, 0).astype(BF16)
        return c

    lax.fori_loop(0, HEADS, head, 0)


N_FRONT = 7
N_GAINS = 16


def front_kernel(peers, *refs):
    inv, own, tok, pack, buckets, buckets_back = refs[:6]
    shards_in = refs[6 : 6 + N_FRONT]
    (w_self, w_rest, gains, ahead, behind, q_nat, k_nat, v_nat, a1, o1, h1, a2, q2, lse) = refs[6 + N_FRONT : 20 + N_FRONT]
    (tok_all, pack_all, table, q_own, *sem) = refs[20 + N_FRONT :]
    weights = [w_self.at[i] for i in range(3)] + [w_rest.at[i] for i in range(N_FRONT - 3)]
    sem_t, sem_w, sem_p = sem[0:2], sem[2:4], sem[4:6]
    wire = Wire(peers)
    at, depth = wire.at, wire.depth
    rows = tok.shape[0]
    length = peers * rows
    mine, per = rows // PIECE, BLOCK // PIECE
    greet(wire.partners())
    for d in range(1, WAYS):
        wire.go(remote(pack, pack_all.at[at.f], sem_p, d, at.group(d)))
    wire.spread(tok, tok_all, sem_t)
    for i in range(3):
        wire.weight_start(shards_in[i], weights[i], sem_w, i)
    wire.slot(tok_all, at.c)[...] = tok[...]
    pack_all[at.f] = pack[...]
    for d in range(1, WAYS):
        slot = pack_all.at[lax.rem(at.f + WAYS - d, WAYS)]
        remote(slot, slot, sem_p, d, at.group(WAYS - d)).wait_recv()
    everything = pack_all[0].astype(F32) + pack_all[1].astype(F32) + pack_all[2].astype(F32) + pack_all[3].astype(F32)
    gains[...] = everything[0:8, :]
    bias = everything[N_GAINS:, 0:LANES].astype(BF16)
    bucket = lax.broadcasted_iota(jnp.int32, (bias.shape[0], 2 * length), 0)
    for line, out in ((buckets, ahead), (buckets_back, behind)):
        hot = jnp.where(line[...] == bucket, 1.0, 0.0).astype(BF16)
        table[...] = tn(bias, hot)[0:16, :]
        fill_tables(table, out)
    for step in range(1, depth):
        wire.relay(tok_all, sem_t, step)
    for i in range(3):
        wire.weight_relay(weights[i], sem_w, i)
    for i in range(3, N_FRONT):
        wire.weight_start(shards_in[i], weights[i], sem_w, i)
    first = gains[0:1, :]
    a1[...] = normed(tok[...].astype(F32), first).astype(BF16)
    for i in range(3):
        wire.weight_ready(weights[i], sem_w, i)
    for step in range(depth):
        wire.from_beside(tok_all, sem_t, step)

    def tile(t, c):
        parts = []
        for i in range(per):
            parts.append(tok_all[pl.ds(inv[t * per + i] * PIECE, PIECE), :])
        a = normed(jnp.concatenate(parts, 0).astype(F32), first).astype(BF16)
        dst = pl.ds(pl.multiple_of(t * BLOCK, BLOCK), BLOCK)
        for j, out in enumerate((q_nat, k_nat, v_nat)):
            out[dst, :] = nn(a, weights[j][...]).astype(BF16)
        return c

    lax.fori_loop(0, length // BLOCK, tile, 0)
    for i in range(mine):
        q_own[i * PIECE : (i + 1) * PIECE, :] = q_nat[pl.ds(own[i, 0] * PIECE, PIECE), :]
    wire.weight_relay(weights[3], sem_w, 3)
    lane = lax.broadcasted_iota(jnp.int32, (rows, length), 1)
    limit = jnp.concatenate([jnp.full((PIECE, 1), own[i, 3], jnp.int32) for i in range(mine)], 0)
    visible = lane < limit
    stat_lane = lax.broadcasted_iota(jnp.int32, (rows, LANES), 1)

    def pair(p, stats):
        sl = lanes_of(p)
        q, k, v = q_own[:, sl], k_nat[:, sl], v_nat[:, sl]
        total = jnp.zeros((rows, LANES), F32)
        for half in range(2):
            h = 2 * p + half
            s = jnp.where(visible, nt(q, half_mask(k, half)) + bias_at(ahead, h, own, mine, length), NEGATIVE)
            m = jnp.max(s, axis=1, keepdims=True)
            e = jnp.exp(s - m)
            l = jnp.sum(e, axis=1, keepdims=True)
            total += nn(e.astype(BF16), half_mask(v, half)) / l
            stats = jnp.where(stat_lane == h, m + jnp.log(l), stats)
        o1[:, sl] = total.astype(BF16)
        return stats

    stats = lax.fori_loop(0, PAIRS // 2, pair, jnp.zeros((rows, LANES), F32))
    wire.weight_relay(weights[4], sem_w, 4)
    lse[...] = lax.fori_loop(PAIRS // 2, PAIRS, pair, stats)
    wire.weight_relay(weights[5], sem_w, 5)
    wire.weight_ready(weights[3], sem_w, 3)
    h = tok[...].astype(F32) + nn(o1[...], weights[3][...])
    h1[...] = h
    a = normed(h, gains[1:2, :]).astype(BF16)
    a2[...] = a
    wire.weight_ready(weights[4], sem_w, 4)
    q2[...] = nn(a, weights[4][...]).astype(BF16)
    wire.weight_relay(weights[6], sem_w, 6)
    for i in (5, 6):
        wire.weight_ready(weights[i], sem_w, i)
    wire.drain()


def front(peers, inv, own, tok, pack, buckets, buckets_back, weight_shards):
    rows = tok.shape[0]
    length, depth = peers * rows, peers // 2
    block = lambda dtype: sds((rows, D), dtype)
    return pl.pallas_call(
        functools.partial(front_kernel, peers),
        name="front",
        out_shape=[sds((3, D, D), BF16), sds((N_FRONT - 3, D, D), BF16), sds((8, D), F32)]
        + [sds((2, HEADS, PIECE, 2 * length), BF16)] * 2
        + [sds((length, D), BF16)] * 3
        + [block(BF16), block(BF16), block(F32), block(BF16), block(BF16), sds((rows, LANES), F32)],
        in_specs=[smem_spec()] * 2 + [full_spec()] * (4 + N_FRONT),
        out_specs=[full_spec()] * 14,
        scratch_shapes=[
            pltpu.VMEM((length, D), BF16),
            pltpu.VMEM((WAYS,) + pack.shape, BF16),
            pltpu.VMEM((16, 2 * length), F32),
            pltpu.VMEM((rows, D), BF16),
        ]
        + sems(2 * depth) + sems(3 * N_FRONT) + sems(WAYS),
        compiler_params=pltpu.CompilerParams(collective_id=1, has_side_effects=True, vmem_limit_bytes=VMEM_LIMIT),
    )(inv, own, tok, pack, buckets, buckets_back, *weight_shards)


STAT = 16


def split(x):
    high = x.astype(BF16)
    return high, (x - high.astype(F32)).astype(BF16)


def head_matrix(rows):
    row = lax.broadcasted_iota(jnp.int32, (rows, D), 0)
    lane = lax.broadcasted_iota(jnp.int32, (rows, D), 1)
    return jnp.where(lane // HEAD_DIM == row, 1.0, 0.0).astype(BF16)


def per_head_sums(x, heads):
    high, low = split(x)
    return nt(heads, high) + nt(heads, low)


def blend(parts, stats, heads):
    top = functools.reduce(jnp.maximum, stats)
    shares = [jnp.exp(s - top) for s in stats]
    total = functools.reduce(jnp.add, shares)
    value = 0.0
    for part, share in zip(parts, shares):
        high, low = split(share / total)
        value = value + (tn(high, heads) + tn(low, heads)) * part.astype(F32)
    return value, top + jnp.log(total)


def norm_back_rows(x, gain, dy):
    r = lax.rsqrt(jnp.mean(x * x, axis=-1, keepdims=True) + EPSILON)
    gdy = gain * dy
    dx = r * gdy - x * (r * r * r) * jnp.mean(x * gdy, axis=-1, keepdims=True)
    return dx, jnp.sum(dy * x * r, axis=0, keepdims=True)


def round_trip(wire, gathered, filler, compute, ship, fold):
    at = wire.at
    b = at.b
    first, second, third = [wire.near(step) for step in (1, 2, 3)]

    def relay(step):
        for buf, sem in gathered:
            wire.relay(buf, sem, step)

    def ready(a):
        for buf, sem in gathered:
            wire.from_beside(buf, sem, a)

    filler()
    relay(1)
    ready(at.a)
    compute(at.c, at.a * 2 + 1 - b)
    ship(at.a)
    relay(2)
    relay(3)
    compute(first * 2 + b, second * 2 + b)
    ready(third)
    ready(second)
    compute(third * 2 + 1 - b, second * 2 + 1 - b)
    ship(third)
    ship(second)
    ready(first)
    compute(third * 2 + b, first * 2 + 1 - b)
    ship(first)
    fold(third)
    fold(second)
    fold(first)


def middle_kernel(peers, *refs):
    (q2, h1, o1, lse1, w_rest, gains, mem, mask_row, mask_col, grad, co_shard, in_shard, w_out) = refs[:13]
    (o2_out, branch2_out, dq2_out, dk2_out, dv2_out, branch1_out, dh1_out, do1_out, do1_all, stat1_all, g_in, g_out, layer_out, gmem_out, small) = refs[13:28]
    (q_all, k2, v2, part, part_lse, from_b, from_b_lse, joined, joined_lse, from_z, from_z_lse,
     w_co, w_in, g_all, a3_all, dact, act, dpre, da3_send, da3_in, out_send, out_in,
     do_all, stat_all, stat_own, dk_acc, dv_acc, dqp, dq_b, dq_j, dq_z, *sem) = refs[28:]
    sem = [sem[2 * i : 2 * i + 2] for i in range(len(sem) // 2)]
    (s_q, s_w, s_in, s_g, s_y, s_yl, s_z, s_zl, s_a3, s_da3, s_out, s_do, s_st, s_dy, s_dz, s_do1, s_st1) = sem
    wire = Wire(peers)
    at, depth = wire.at, wire.depth
    rows = q2.shape[0]
    heads = head_matrix(STAT)
    quarter = co_shard.shape[0]
    units = w_out.shape[0]
    block = lambda f: pl.ds(pl.multiple_of(f * rows, rows), rows)
    greet(wire.partners())
    wire.spread(q2, q_all, s_q)
    q_all[at.c] = q2[...]
    wire.weight_start(co_shard, w_co, s_w, 0)
    for d in range(1, WAYS):
        f = lax.rem(at.f + d, WAYS)
        wire.go(remote(grad, g_all.at[block(at.f)], s_g, d, at.group(d)))
        wire.go(remote(in_shard.at[:, pl.ds(pl.multiple_of(f * units, LANES), units)], wire.shard(w_in, at.f), s_in, d, at.group(d)))
    g_all[block(at.f), :] = grad[...]
    wire.shard(w_in, at.f)[...] = in_shard[:, pl.ds(pl.multiple_of(at.f * units, LANES), units)]

    def project_memory():
        k2[...] = nn(mem[...], w_rest[2]).astype(BF16)
        v2[...] = nn(mem[...], w_rest[3]).astype(BF16)

    stat_lane = lax.broadcasted_iota(jnp.int32, (2 * rows, LANES), 1)

    def attend(c1, c2):
        def pair(p, stats):
            sl = lanes_of(p)
            q = jnp.concatenate([q_all[c1, :, sl], q_all[c2, :, sl]], 0)
            k, v = k2[:, sl], v2[:, sl]
            total = jnp.zeros((2 * rows, LANES), F32)
            for half in range(2):
                s = nt(q, half_mask(k, half)) + mask_row[...]
                m = jnp.max(s, axis=1, keepdims=True)
                e = jnp.exp(s - m)
                l = jnp.sum(e, axis=1, keepdims=True)
                total += nn(e.astype(BF16), half_mask(v, half)) / l
                stats = jnp.where(stat_lane == 2 * p + half, m + jnp.log(l), stats)
            part[c1, :, sl] = total[:rows].astype(BF16)
            part[c2, :, sl] = total[rows:].astype(BF16)
            return stats

        stats = lax.fori_loop(0, PAIRS, pair, jnp.zeros((2 * rows, LANES), F32))
        part_lse[c1] = stats[:rows].T[:STAT]
        part_lse[c2] = stats[rows:].T[:STAT]

    def ship_part(a):
        other = a * 2 + 1 - at.b
        wire.go(remote(part.at[other], from_b.at[a], s_y, a, at.beside))
        wire.go(remote(part_lse.at[other], from_b_lse.at[a], s_yl, a, at.beside))

    def blend_column(a):
        remote(from_b.at[a], from_b.at[a], s_y, a, at.beside).wait_recv()
        remote(from_b_lse.at[a], from_b_lse.at[a], s_yl, a, at.beside).wait_recv()
        c = a * 2 + at.b
        return blend([part[c], from_b[a]], [part_lse[c], from_b_lse[a]], heads)

    def fold_part(a):
        value, stat = blend_column(a)
        joined[a] = value.astype(BF16)
        joined_lse[a] = stat
        wire.go(remote(joined.at[a], from_z.at[at.a], s_z, at.a, at.column(a)))
        wire.go(remote(joined_lse.at[a], from_z_lse.at[at.a], s_zl, at.a, at.column(a)))

    round_trip(wire, [(q_all, s_q)], project_memory, attend, ship_part, fold_part)
    wire.weight_relay(w_co, s_w, 0)
    value, stat = blend_column(at.a)
    parts, stats = [value], [stat]
    for step in range(1, depth):
        a = wire.near(step)
        remote(from_z.at[a], from_z.at[a], s_z, a, at.column(a)).wait_recv()
        remote(from_z_lse.at[a], from_z_lse.at[a], s_zl, a, at.column(a)).wait_recv()
        parts.append(from_z[a])
        stats.append(from_z_lse[a])
    out2, lse2 = blend(parts, stats, heads)
    o2 = out2.astype(BF16)
    o2_out[...] = o2
    wire.weight_ready(w_co, s_w, 0)
    h2 = h1[...] + nn(o2, w_co[...])
    a3 = normed(h2, gains[2:3, :]).astype(BF16)
    a3_all[block(at.f), :] = a3
    for d in range(1, WAYS):
        spot = a3_all.at[block(at.f)]
        wire.go(remote(spot, spot, s_a3, d, at.group(d)))

    def arrive(buf, sem, size):
        for d in range(1, WAYS):
            f = lax.rem(at.f + WAYS - d, WAYS)
            spot = buf.at[pl.ds(pl.multiple_of(f * size, size), size)]
            remote(spot, spot, sem, d, at.group(WAYS - d)).wait_recv()

    arrive(g_all, s_g, rows)
    tiles = [slice(2 * rows * t, 2 * rows * (t + 1)) for t in range(WAYS // 2)]
    for rs in tiles:
        dact[rs, :] = nt(g_all[rs, :], w_out[...])
    arrive(w_in, s_in, quarter)
    arrive(a3_all, s_a3, rows)
    for rs in tiles:
        pre = nn(a3_all[rs, :], w_in[...])
        square = pre * pre
        t = jnp.tanh(0.7978845608028654 * (pre + 0.044715 * pre * square))
        act[rs, :] = (0.5 * pre * (1.0 + t)).astype(BF16)
        slope = 0.5 * (1.0 + t) + 0.5 * pre * (1.0 - t * t) * (0.7978845608028654 * (1.0 + 3 * 0.044715 * square))
        d = (dact[rs, :] * slope).astype(BF16)
        dpre[rs, :] = d
        da3_send[rs, :] = nt(d, w_in[...]).astype(BF16)

    def exchange(src, dst, sem):
        for d in range(1, WAYS):
            f = lax.rem(at.f + d, WAYS)
            wire.go(remote(src.at[block(f)], dst.at[block(at.f)], sem, d, at.group(d)))

    def collect(src, dst, sem):
        arrive(dst, sem, rows)
        value = src[block(at.f), :].astype(F32)
        for d in range(1, WAYS):
            value += dst[block(lax.rem(at.f + WAYS - d, WAYS)), :].astype(F32)
        return value

    exchange(da3_send, da3_in, s_da3)
    for rs in tiles:
        out_send[rs, :] = nn(act[rs, :], w_out[...]).astype(BF16)
    exchange(out_send, out_in, s_out)
    da3 = collect(da3_send, da3_in, s_da3)
    dx, dgain = norm_back_rows(h2, gains[2:3, :], da3)
    small[...] = jnp.zeros_like(small)
    small[1:2, :] = dgain
    dh2 = grad[...].astype(F32) + dx
    branch2 = dh2.astype(BF16)
    branch2_out[...] = branch2
    do2 = nt(branch2, w_co[...]).astype(BF16)
    do_all[at.c] = do2
    stat_own[0] = jnp.concatenate([lse2, per_head_sums(do2.astype(F32) * out2, heads)], 0)
    stat_all[at.c] = stat_own[0]
    wire.spread(do_all.at[at.c], do_all, s_do)
    wire.spread(stat_own.at[0], stat_all, s_st)

    def feed_forward_grads():
        layer_out[...] = (h2 + collect(out_send, out_in, s_out)).astype(BF16)
        g_out[...] = tn(act[...], g_all[...]).astype(BF16)
        g_in[...] = tn(a3_all[...], dpre[...]).astype(BF16)
        dk_acc[...] = jnp.zeros_like(dk_acc)
        dv_acc[...] = jnp.zeros_like(dv_acc)

    def attend_back(c1, c2):
        def pair(p, carry):
            sl = lanes_of(p)
            q = jnp.concatenate([q_all[c1, :, sl], q_all[c2, :, sl]], 0)
            do = jnp.concatenate([do_all[c1, :, sl], do_all[c2, :, sl]], 0)
            k, v = k2[:, sl], v2[:, sl]
            dkp, dvp = dk_acc[:, sl], dv_acc[:, sl]
            dq = jnp.zeros((2 * rows, LANES), F32)
            for half in range(2):
                line = lambda i: jnp.concatenate([stat_all[c1, pl.ds(i, 1), :], stat_all[c2, pl.ds(i, 1), :]], 1)
                h = 2 * p + half
                km = half_mask(k, half)
                s = nt(km, q) + mask_col[...]
                e = jnp.exp(s - line(h))
                dvp = dvp + nn(e.astype(BF16), half_mask(do, half))
                ds = (e * (nt(half_mask(v, half), do) - line(STAT + h))).astype(BF16)
                dkp = dkp + nn(ds, half_mask(q, half))
                dq = dq + tn(ds, km)
            dk_acc[:, sl] = dkp
            dv_acc[:, sl] = dvp
            dqp[c1, :, sl] = dq[:rows].astype(BF16)
            dqp[c2, :, sl] = dq[rows:].astype(BF16)
            return carry

        lax.fori_loop(0, PAIRS, pair, 0)

    def ship_dq(a):
        wire.go(remote(dqp.at[a * 2 + 1 - at.b], dq_b.at[a], s_dy, a, at.beside))

    def column_dq(a):
        remote(dq_b.at[a], dq_b.at[a], s_dy, a, at.beside).wait_recv()
        return dqp[a * 2 + at.b].astype(F32) + dq_b[a].astype(F32)

    def fold_dq(a):
        dq_j[a] = column_dq(a).astype(BF16)
        wire.go(remote(dq_j.at[a], dq_z.at[at.a], s_dz, at.a, at.column(a)))

    round_trip(wire, [(do_all, s_do), (stat_all, s_st)], feed_forward_grads, attend_back, ship_dq, fold_dq)
    dk2_out[...] = dk_acc[...].astype(BF16)
    dv2_out[...] = dv_acc[...].astype(BF16)
    value = column_dq(at.a)
    for step in range(1, depth):
        a = wire.near(step)
        remote(dq_z.at[a], dq_z.at[a], s_dz, a, at.column(a)).wait_recv()
        value += dq_z[a].astype(F32)
    dq2 = value.astype(BF16)
    dq2_out[...] = dq2
    dx, dgain = norm_back_rows(h1[...], gains[1:2, :], nt(dq2, w_rest[1]))
    small[0:1, :] = dgain
    dh1 = dh2 + dx
    dh1_out[...] = dh1
    branch1 = dh1.astype(BF16)
    branch1_out[...] = branch1
    do1 = nt(branch1, w_rest[0]).astype(BF16)
    do1_out[...] = do1
    stat_own[1] = jnp.concatenate([lse1[...].T[:STAT], per_head_sums(do1.astype(F32) * o1[...].astype(F32), heads)], 0)
    wire.slot(do1_all, at.c)[...] = do1
    stat1_all[at.c] = stat_own[1]
    wire.spread(do1_out, do1_all, s_do1)
    wire.spread(stat_own.at[1], stat1_all, s_st1)
    gmem_out[...] = (nt(dk2_out[...], w_rest[2]) + nt(dv2_out[...], w_rest[3])).astype(BF16)
    both = [(do1_all, s_do1), (stat1_all, s_st1)]
    for step in range(1, depth):
        for buf, s in both:
            wire.relay(buf, s, step)
    for a in range(depth):
        for buf, s in both:
            wire.from_beside(buf, s, a)
    wire.drain()


def middle(peers, q2, h1, o1, lse1, w_rest, gains, mem, mask_row, mask_col, grad, co_shard, in_shard, w_out):
    rows, slots = q2.shape[0], mem.shape[0]
    length, depth = peers * rows, peers // 2
    units = w_out.shape[0]
    row = lambda dtype: sds((rows, D), dtype)
    store = lambda n, dtype=BF16: pltpu.VMEM((n, rows, D), dtype)
    stat = lambda n, k=STAT: pltpu.VMEM((n, k, rows), F32)
    group = lambda width, dtype=BF16: pltpu.VMEM((WAYS * rows, width), dtype)
    return pl.pallas_call(
        functools.partial(middle_kernel, peers),
        name="middle",
        out_shape=[
            row(BF16),
            row(BF16),
            row(BF16),
            sds((slots, D), BF16),
            sds((slots, D), BF16),
            row(BF16),
            row(F32),
            row(BF16),
            sds((length, D), BF16),
            sds((peers, 2 * STAT, rows), F32),
            sds((D, units), BF16),
            sds((units, D), BF16),
            row(BF16),
            sds((slots, D), BF16),
            sds((8, D), F32),
        ],
        in_specs=[full_spec()] * 13,
        out_specs=[full_spec()] * 15,
        scratch_shapes=[
            store(peers), pltpu.VMEM((slots, D), BF16), pltpu.VMEM((slots, D), BF16),
            store(peers), stat(peers), store(depth), stat(depth), store(depth), stat(depth), store(depth), stat(depth),
            pltpu.VMEM((D, D), BF16), pltpu.VMEM((D, units), BF16),
            group(D), group(D), group(units, F32), group(units), group(units), group(D), group(D), group(D), group(D),
            store(peers), stat(peers, 2 * STAT), stat(2, 2 * STAT),
            pltpu.VMEM((slots, D), F32), pltpu.VMEM((slots, D), F32),
            store(peers), store(depth), store(depth), store(depth),
        ]
        + sems(2 * depth) + sems(3) + sems(WAYS) + sems(WAYS)
        + sems(depth) * 4
        + sems(WAYS) * 3
        + sems(2 * depth) * 2
        + sems(depth) * 2
        + sems(2 * depth) * 2,
        compiler_params=pltpu.CompilerParams(collective_id=2, has_side_effects=True, vmem_limit_bytes=VMEM_LIMIT),
    )(q2, h1, o1, lse1, w_rest, gains, mem, mask_row, mask_col, grad, co_shard, in_shard, w_out)


def reduce_kernel(peers, left_index, *refs):
    n_left = len(set(left_index))
    n_mats = len(left_index)
    lefts, rights = refs[:n_left], refs[n_left : n_left + n_mats]
    g_in, g_out, small, out, small_out = refs[n_left + n_mats : n_left + n_mats + 5]
    (prod, own, sa, ra, sb, rb, sc, rc, sd, rd, tiny, tiny_in, *sem) = refs[n_left + n_mats + 5 :]
    sem_a, sem_b, sem_c, sem_d, sem_e, sem_f, sem_g, sem_t = [sem[2 * i : 2 * i + 2] for i in range(8)]
    at = Place(peers)
    depth = at.depth
    quarter, wide = out.shape[1], out.shape[2]
    half, part = wide // 2, quarter // depth
    total = out.shape[0]
    sent = []

    def go(copy):
        copy.start()
        sent.append(copy)
        return copy

    columns = lambda b: pl.ds(pl.multiple_of(b * half, LANES), half)
    shard_rows = lambda f: pl.ds(pl.multiple_of(f * quarter, quarter), quarter)
    part_rows = lambda a: pl.ds(pl.multiple_of(a * part, part), part)
    mine, theirs = columns(at.b), columns(1 - at.b)

    greet(
        [at.core, at.across, at.beside]
        + [at.column(at.ahead(d)) for d in range(1, depth)]
        + [(at.c, (1 - at.x) * 2 + 1 - at.k)]
    )

    def stage_a(i):
        prod[...] = tn(lefts[left_index[i]][...], rights[i][...])
        for x in range(2):
            own[i, x] = prod[shard_rows(x * 2 + at.k), :]
            sa[i, x] = prod[shard_rows(x * 2 + 1 - at.k), :].astype(BF16)
        go(remote(sa.at[i], ra.at[i], sem_a, i, at.core))

    def stage_b(i):
        remote(sa.at[i], ra.at[i], sem_a, i, at.core).wait_recv()
        sb[i] = (own[i, 1 - at.x] + ra[i, 1 - at.x].astype(F32)).astype(BF16)
        go(remote(sb.at[i], rb.at[i], sem_b, i, at.across))

    def stage_c(j):
        if j < n_mats:
            remote(sb.at[j], rb.at[j], sem_b, j, at.across).wait_recv()
            value = own[j, at.x] + ra[j, at.x].astype(F32) + rb[j].astype(F32)
            sc[j] = value.astype(BF16)
        go(remote(sc.at[j, :, theirs], rc.at[j], sem_c, j, at.beside))

    def stage_d(j):
        remote(sc.at[j, :, mine], rc.at[j], sem_c, j, at.beside).wait_recv()
        value = sc[j, :, mine].astype(F32) + rc[j].astype(F32)
        sd[j] = value.astype(BF16)
        for d in range(1, depth):
            go(remote(sd.at[j, part_rows(at.ahead(d))], rd.at[j, part_rows(at.a)], sem_d, j * depth + d, at.column(at.ahead(d))))

    def stage_e(j):
        value = sd[j, part_rows(at.a), :].astype(F32)
        for d in range(1, depth):
            slot = rd.at[j, part_rows(at.behind(d))]
            remote(slot, slot, sem_d, j * depth + d, at.column(at.behind(d))).wait_recv()
            value += slot[...].astype(F32)
        spot = out.at[j, part_rows(at.a), mine]
        spot[...] = value.astype(BF16)
        for d in range(1, depth):
            go(remote(spot, spot, sem_e, j * depth + d, at.column(at.ahead(d))))

    def stage_f(j):
        for d in range(1, depth):
            spot = out.at[j, part_rows(at.behind(d)), mine]
            remote(spot, spot, sem_e, j * depth + d, at.column(at.behind(d))).wait_recv()
        go(remote(out.at[j, :, mine], out.at[j, :, mine], sem_f, j, at.beside))

    def stage_g(j):
        remote(out.at[j, :, theirs], out.at[j, :, theirs], sem_f, j, at.beside).wait_recv()

    order = list(range(n_mats + WAYS, n_mats + 2 * WAYS)) + list(range(n_mats)) + list(range(n_mats, n_mats + WAYS))
    for q in range(WAYS):
        sc[n_mats + WAYS + q] = g_out[q * quarter : (q + 1) * quarter, :]
    tiny[0] = small[...]
    hops = [at.core, at.across, at.beside]
    for t in range(total + 4):
        if 4 <= t:
            stage_g(order[t - 4])
        if 3 <= t < total + 3:
            stage_f(order[t - 3])
        if 2 <= t < total + 2:
            stage_e(order[t - 2])
        if 1 <= t < total + 1:
            stage_d(order[t - 1])
        if t == total - WAYS:
            for d in range(1, WAYS):
                slot = sc.at[n_mats + lax.rem(at.f + WAYS - d, WAYS)]
                remote(slot, slot, sem_g, d, at.group(WAYS - d)).wait_recv()
        if t < total:
            stage_c(order[t])
        if 1 <= t <= n_mats:
            stage_b(t - 1)
        if t < n_mats:
            stage_a(t)
        if t == n_mats:
            sc[n_mats + at.f] = g_in[shard_rows(at.f), :]
            for d in range(1, WAYS):
                f = lax.rem(at.f + d, WAYS)
                go(remote(g_in.at[shard_rows(f)], sc.at[n_mats + at.f], sem_g, d, at.group(d)))
        if t < 4:
            if t:
                remote(tiny.at[t - 1], tiny_in.at[t - 1], sem_t, t - 1, hops[t - 1]).wait_recv()
                tiny[t] = tiny[t - 1] + tiny_in[t - 1]
            if t < 3:
                go(remote(tiny.at[t], tiny_in.at[t], sem_t, t, hops[t]))
            else:
                for d in range(1, depth):
                    go(remote(tiny.at[3], tiny_in.at[2 + d], sem_t, 2 + d, at.column(at.ahead(d))))
        if t == 4:
            value = tiny[3]
            for d in range(1, depth):
                remote(tiny.at[3], tiny_in.at[2 + d], sem_t, 2 + d, at.column(at.behind(d))).wait_recv()
                value += tiny_in[2 + d]
            small_out[...] = value
    for copy in sent:
        copy.wait_send()


def reduce_grads(peers, pairs, g_in, g_out, small):
    lefts, left_index = [], []
    for left, _ in pairs:
        for i, seen in enumerate(lefts):
            if seen is left:
                break
        else:
            lefts.append(left)
            i = len(lefts) - 1
        left_index.append(i)
    rights = [right for _, right in pairs]
    n, total = len(pairs), len(pairs) + 2 * WAYS
    width = g_in.shape[1]
    quarter, half, depth = width // WAYS, width // 2, peers // 2
    return pl.pallas_call(
        functools.partial(reduce_kernel, peers, left_index),
        name="reduce_grads",
        out_shape=[sds((total, quarter, width), BF16), sds(small.shape, F32)],
        in_specs=[full_spec()] * (len(lefts) + n + 3),
        out_specs=[full_spec()] * 2,
        scratch_shapes=[
            pltpu.VMEM((width, width), F32),
            pltpu.VMEM((n, 2, quarter, width), F32),
            pltpu.VMEM((n, 2, quarter, width), BF16),
            pltpu.VMEM((n, 2, quarter, width), BF16),
            pltpu.VMEM((n, quarter, width), BF16),
            pltpu.VMEM((n, quarter, width), BF16),
            pltpu.VMEM((total, quarter, width), BF16),
            pltpu.VMEM((total, quarter, half), BF16),
            pltpu.VMEM((total, quarter, half), BF16),
            pltpu.VMEM((total, quarter, half), BF16),
            pltpu.VMEM((4,) + small.shape, F32),
            pltpu.VMEM((3 + depth,) + small.shape, F32),
        ]
        + sems(n) + sems(n) + sems(total) + sems(total * depth) + sems(total * depth) + sems(total) + sems(WAYS) + sems(3 + depth),
        compiler_params=pltpu.CompilerParams(collective_id=0, has_side_effects=True, vmem_limit_bytes=VMEM_LIMIT),
    )(*lefts, *rights, g_in, g_out, small)


def norm_back(x, gain, dy):
    r = lax.rsqrt(jnp.mean(x * x, axis=-1, keepdims=True) + EPSILON)
    gdy = gain * dy
    dx = r * gdy - x * (r * r * r) * jnp.mean(x * gdy, axis=-1, keepdims=True)
    return dx, jnp.sum(dy * x * r, axis=0)


def shards(
    tokens,
    memory,
    piece_order,
    bucket_table,
    passage_lengths,
    self_gain,
    cross_gain,
    hidden_gain,
    position_bias,
    self_query,
    self_attention_key,
    self_value,
    self_output,
    cross_query,
    cross_key,
    cross_value,
    cross_output,
    hidden_in,
    hidden_out,
    grad_output,
):
    tok, mem, grad = tokens[0], memory[0], grad_output[0]
    rows, slots = tok.shape[0], mem.shape[0]
    length = (bucket_table.shape[0] + 1) // 2
    peers = length // rows
    index = lax.axis_index("ctx")
    own = lax.dynamic_slice_in_dim(piece_order, index * (rows // PIECE), rows // PIECE)
    f = lax.axis_index("fsdp")
    quarter, eighth = self_query.shape[0], position_bias.shape[0]
    slots_all = jnp.arange(piece_order.shape[0], dtype=jnp.int32)
    inv = jnp.sum(jnp.where(piece_order[None, :] == slots_all[:, None], slots_all[None, :], 0), axis=1)
    own_facts = jnp.stack(
        [own, own % 2, (length - (own + own % 2) * PIECE) // LANES, (own * PIECE // BLOCK + 1) * BLOCK], axis=1
    )
    pack = jnp.zeros((N_GAINS + BUCKETS, D), BF16)
    pack = lax.dynamic_update_slice(pack, jnp.stack([self_gain, cross_gain, hidden_gain]), (0, f * quarter))
    pack = lax.dynamic_update_slice(pack, position_bias, (N_GAINS + f * eighth, 0))
    buckets = jnp.pad(bucket_table, (0, 1), constant_values=-1)[None]
    buckets_back = jnp.pad(bucket_table[::-1], (0, 1), constant_values=-1)[None]
    hot = (buckets == jnp.arange(BUCKETS, dtype=jnp.int32)[:, None]).astype(F32)
    w_self, w_rest, gains, ahead, behind, q1_nat, k1_nat, v1_nat, a1, o1, h1, a2, q2, lse1 = front(
        peers,
        inv,
        own_facts,
        tok,
        pack,
        buckets,
        buckets_back,
        [self_query, self_attention_key, self_value, self_output, cross_query, cross_key, cross_value],
    )
    slot = index * slots + jnp.arange(slots, dtype=jnp.int32)
    hidden = jnp.where(slot % PLEN < jnp.take(passage_lengths[0], slot // PLEN), 0.0, NEGATIVE)
    (
        o2,
        branch2,
        dq2,
        dk2,
        dv2,
        branch1,
        dh1,
        do1,
        do1_all,
        stat1_all,
        g_in,
        g_out,
        layer_output,
        grad_memory,
        small_mid,
    ) = middle(
        peers,
        q2,
        h1,
        o1,
        lse1,
        w_rest,
        gains,
        mem,
        hidden[None, :],
        hidden[:, None],
        grad,
        cross_output,
        hidden_in,
        hidden_out,
    )
    stat1_all = jnp.pad(jnp.transpose(stat1_all, (0, 2, 1)).reshape(length, 2 * STAT), ((0, 0), (0, LANES - 2 * STAT)))
    stat1 = lax.dynamic_slice_in_dim(stat1_all, index * rows, rows)
    dq1, dk1, dv1, diag = self_backward(
        piece_order, own, q1_nat, k1_nat, v1_nat, do1_all, do1, stat1_all, stat1, ahead, behind
    )
    g_bias = jnp.einsum(
        "hr,lr->lh", diag[:HEADS], hot, precision=lax.Precision.HIGHEST, preferred_element_type=F32
    )
    da1 = nt(dq1, w_self[0]) + nt(dk1, w_self[1]) + nt(dv1, w_self[2])
    tok_wide = tok.astype(F32)
    dx, gg1 = norm_back(tok_wide, gains[0], da1)
    grad_tokens = (dh1 + dx).astype(BF16)
    small = jnp.concatenate(
        [gg1[None], small_mid[:2], jnp.pad(g_bias, ((0, 0), (0, D - HEADS)))], 0
    )
    small = jnp.pad(small, ((0, -small.shape[0] % 8), (0, 0)))
    pairs = [
        (a1, dq1),
        (a1, dk1),
        (a1, dv1),
        (o1, branch1),
        (a2, dq2),
        (mem, dk2),
        (mem, dv2),
        (o2, branch2),
    ]
    total, small = reduce_grads(peers, pairs, g_in, g_out, small)
    total = total.astype(F32)
    gain = lambda i: lax.dynamic_slice_in_dim(small[i], f * quarter, quarter)
    bias_out = lax.dynamic_slice_in_dim(small[3:], f * eighth, eighth)[:, :HEADS]
    count = len(pairs)
    return (
        layer_output[None],
        grad_tokens[None],
        grad_memory[None],
        gain(0),
        gain(1),
        gain(2),
        bias_out,
        *[total[i] for i in range(count)],
        jnp.concatenate([total[count + i] for i in range(WAYS)], 1),
        total[count + WAYS :].reshape(-1, D),
    )


def pick(*arrays):
    resident = (arrays[3].shape[0] + 1) // 2 <= RESIDENT_ROWS
    return (shards if resident else streamed_shards)(*arrays)


def solution(mesh):
    return jax.shard_map(
        pick,
        mesh=mesh,
        in_specs=(
            P("fsdp", "ctx", None),
            P("fsdp", "ctx", None),
            P(),
            P(),
            P("fsdp", None),
            P("fsdp"),
            P("fsdp"),
            P("fsdp"),
            P("fsdp", None),
            P("fsdp", None),
            P("fsdp", None),
            P("fsdp", None),
            P("fsdp", None),
            P("fsdp", None),
            P("fsdp", None),
            P("fsdp", None),
            P("fsdp", None),
            P("fsdp", None),
            P("fsdp", None),
            P("fsdp", "ctx", None),
        ),
        out_specs=(
            P("fsdp", "ctx", None),
            P("fsdp", "ctx", None),
            P("fsdp", "ctx", None),
            P("fsdp"),
            P("fsdp"),
            P("fsdp"),
            P("fsdp", None),
            P("fsdp", None),
            P("fsdp", None),
            P("fsdp", None),
            P("fsdp", None),
            P("fsdp", None),
            P("fsdp", None),
            P("fsdp", None),
            P("fsdp", None),
            P("fsdp", None),
            P("fsdp", None),
        ),
        check_vma=False,
    )
```

```python
import functools

import jax
import jax.numpy as jnp
from jax import lax
from jax.experimental import pallas as pl
from jax.experimental.pallas import tpu as pltpu
from jax.sharding import PartitionSpec as P

D = 768
HEADS = 12
PAIRS = HEADS // 2
HEAD_DIM = 64
PIECE = 64
BLOCK = 256
PLEN = 256
KBLK = 512
PSG = 20
BUCKETS = 32
RESIDENT_ROWS = 1024
LANES = 128
EPSILON = 1e-06
NEGATIVE = -1e30
F32 = jnp.float32
BF16 = jnp.bfloat16
VMEM_LIMIT = 60 * 2**20
TAIL_VMEM = 63 * 2**20

def nn(a, b):
    return lax.dot_general(a, b, (((1,), (0,)), ((), ())), preferred_element_type=F32)
def nt(a, b):
    return lax.dot_general(a, b, (((1,), (1,)), ((), ())), preferred_element_type=F32)
def tn(a, b):
    return lax.dot_general(a, b, (((0,), (0,)), ((), ())), preferred_element_type=F32)

def normed(x, gain):
    return x * lax.rsqrt(jnp.mean(x * x, axis=-1, keepdims=True) + EPSILON) * gain

def half_mask(x, half):
    lane = lax.broadcasted_iota(jnp.int32, x.shape, 1) // HEAD_DIM
    return jnp.where(lane == half, x, jnp.zeros_like(x))

def lanes_of(pair):
    return pl.ds(pl.multiple_of(pair * LANES, LANES), LANES)

def shear(x, sign):
    row = lax.broadcasted_iota(jnp.int32, x.shape, 0)
    for bit in (1, 2, 4):
        x = jnp.where(row & bit != 0, pltpu.roll(x, (sign * bit) % x.shape[1], 1), x)
    return x

def full_spec():
    return pl.BlockSpec(memory_space=pltpu.VMEM)
def smem_spec():
    return pl.BlockSpec(memory_space=pltpu.SMEM)
def sds(shape, dtype):
    return jax.ShapeDtypeStruct(shape, dtype)

def norm_scale(values, gain_vector):
    return (
        values
        * lax.rsqrt(jnp.mean(values * values, axis=-1, keepdims=True) + EPSILON)
        * gain_vector
    )


def smooth_gate(values):
    return jax.nn.gelu(values, approximate=True)


def project(operand, matrix):
    return jnp.dot(operand, matrix, preferred_element_type=jnp.float32)


def project_back(operand, matrix):
    return jnp.einsum("sra,ba->srb", operand, matrix, preferred_element_type=jnp.float32)


def weight_grad(inputs, upstream):
    return jnp.einsum("sra,srb->ab", inputs, upstream, preferred_element_type=jnp.float32)


def to_heads(matrix):
    return matrix.reshape(matrix.shape[0], matrix.shape[1], HEADS, HEAD_DIM)


def heads_first(matrix):
    return jnp.transpose(to_heads(matrix), (0, 2, 1, 3))


def from_heads(tensor):
    return jnp.transpose(tensor, (0, 2, 1, 3)).reshape(
        tensor.shape[0], tensor.shape[2], HEADS * HEAD_DIM
    )


def block_scores(queries, keys_all, values_all, extras, offset):
    key_block = lax.dynamic_slice_in_dim(keys_all, offset, KBLK, 1)
    value_block = lax.dynamic_slice_in_dim(values_all, offset, KBLK, 1)
    added_bias, visible, bucket_indicator = extras(offset)
    scores = (
        jnp.einsum("sqhd,skhd->shqk", queries, key_block, preferred_element_type=jnp.float32)
        + added_bias
    )
    block_maximum = jnp.max(jnp.where(visible, scores, NEGATIVE), axis=-1)
    weights = jnp.exp(jnp.where(visible, scores - block_maximum[..., None], NEGATIVE))
    return (key_block, value_block, bucket_indicator, block_maximum, weights)


def attend_forward(queries, keys_all, values_all, extras):
    block_count = keys_all.shape[1] // KBLK

    def single_block_tile(carried, block_index):
        key_block, value_block, bucket_indicator, block_maximum, weights = block_scores(
            queries, keys_all, values_all, extras, block_index * KBLK
        )
        numerator = jnp.einsum(
            "shqk,skhd->shqd",
            weights.astype(jnp.bfloat16),
            value_block,
            preferred_element_type=jnp.float32,
        )
        return (carried, (block_maximum, jnp.sum(weights, axis=-1), numerator))

    ignored, stacked = lax.scan(
        single_block_tile, jnp.zeros((), jnp.float32), jnp.arange(block_count, dtype=jnp.int32)
    )
    block_maximum, block_sum, numerator = stacked
    row_maximum = jnp.max(block_maximum, axis=0)
    rescale = jnp.exp(block_maximum - row_maximum)
    row_total = jnp.sum(rescale * block_sum, axis=0)
    output = jnp.sum(rescale[..., None] * numerator, axis=0) / row_total[..., None]
    return (output, row_maximum, row_total)


def attend_backward(
    queries, keys_all, values_all, extras, grad_out, output, row_maximum, row_total
):
    block_count = keys_all.shape[1] // KBLK
    grad_wide = grad_out.astype(jnp.float32)
    row_dot = jnp.sum(grad_wide * output, axis=-1)
    scaled = grad_wide / row_total[..., None]
    sum_weight = -row_dot / row_total
    initial = (
        jnp.zeros(queries.shape, jnp.float32),
        jnp.zeros(keys_all.shape, jnp.float32),
        jnp.zeros(values_all.shape, jnp.float32),
        jnp.zeros((BUCKETS, HEADS), jnp.float32),
    )

    def single_block_tile(carried, block_index):
        grad_query, grad_keys, grad_values, grad_bias = carried
        offset = block_index * KBLK
        key_block, value_block, bucket_indicator, block_maximum, weights = block_scores(
            queries, keys_all, values_all, extras, offset
        )
        rescale = jnp.exp(block_maximum - row_maximum)
        grad_numerator = (scaled * rescale[..., None]).astype(jnp.bfloat16)
        grad_weights = (
            jnp.einsum(
                "shqd,skhd->shqk", grad_numerator, value_block, preferred_element_type=jnp.float32
            )
            + (sum_weight * rescale)[..., None]
        )
        grad_scores = weights * grad_weights
        gradient_bfloat_cast = grad_scores.astype(jnp.bfloat16)
        grad_query = grad_query + jnp.einsum(
            "shqk,skhd->sqhd", gradient_bfloat_cast, key_block, preferred_element_type=jnp.float32
        )
        key_part = jnp.einsum(
            "shqk,sqhd->skhd", gradient_bfloat_cast, queries, preferred_element_type=jnp.float32
        )
        value_part = jnp.einsum(
            "shqk,shqd->skhd",
            weights.astype(jnp.bfloat16),
            grad_numerator,
            preferred_element_type=jnp.float32,
        )
        grad_keys = lax.dynamic_update_slice_in_dim(grad_keys, key_part, offset, 1)
        grad_values = lax.dynamic_update_slice_in_dim(grad_values, value_part, offset, 1)
        if bucket_indicator is not None:
            remainder_portion = (grad_scores - gradient_bfloat_cast.astype(jnp.float32)).astype(
                jnp.bfloat16
            )
            grad_bias = (
                grad_bias
                + jnp.einsum(
                    "uljf,pjf->pl",
                    gradient_bfloat_cast,
                    bucket_indicator,
                    preferred_element_type=jnp.float32,
                )
                + jnp.einsum(
                    "uljf,pjf->pl",
                    remainder_portion,
                    bucket_indicator,
                    preferred_element_type=jnp.float32,
                )
            )
        return ((grad_query, grad_keys, grad_values, grad_bias), None)

    result, ignored = lax.scan(single_block_tile, initial, jnp.arange(block_count, dtype=jnp.int32))
    return result


def streamed_shards(
    tokens,
    memory,
    piece_order,
    bucket_table,
    passage_lengths,
    self_gain,
    cross_gain,
    hidden_gain,
    position_bias,
    self_query,
    self_attention_key,
    self_value,
    self_output,
    cross_query,
    cross_key,
    cross_value,
    cross_output,
    hidden_in,
    hidden_out,
    grad_output,
):
    (
        gain_one,
        gain_two,
        gain_three,
        position_bias_lookup,
        query_full,
        key_full,
        value_full,
        output_full,
        cross_query_full,
        cross_key_full,
        cross_value_full,
        cross_output_full,
        inner_full,
        outer_full,
    ) = (
        lax.all_gather(self_gain, "fsdp", axis=0, tiled=True),
        lax.all_gather(cross_gain, "fsdp", axis=0, tiled=True),
        lax.all_gather(hidden_gain, "fsdp", axis=0, tiled=True),
        lax.all_gather(position_bias, "fsdp", axis=0, tiled=True),
        lax.all_gather(self_query, "fsdp", axis=0, tiled=True),
        lax.all_gather(self_attention_key, "fsdp", axis=0, tiled=True),
        lax.all_gather(self_value, "fsdp", axis=0, tiled=True),
        lax.all_gather(self_output, "fsdp", axis=0, tiled=True),
        lax.all_gather(cross_query, "fsdp", axis=0, tiled=True),
        lax.all_gather(cross_key, "fsdp", axis=0, tiled=True),
        lax.all_gather(cross_value, "fsdp", axis=0, tiled=True),
        lax.all_gather(cross_output, "fsdp", axis=0, tiled=True),
        lax.all_gather(hidden_in, "fsdp", axis=0, tiled=True),
        lax.all_gather(hidden_out, "fsdp", axis=0, tiled=True),
    )
    gain_one = gain_one.astype(jnp.float32)
    gain_two = gain_two.astype(jnp.float32)
    gain_three = gain_three.astype(jnp.float32)
    sequence_count = tokens.shape[0]
    local_rows = tokens.shape[1]
    sequence_length = (bucket_table.shape[0] + 1) // 2
    memory_length = PSG * PLEN
    piece_offsets = jnp.arange(PIECE, dtype=jnp.int32)
    local_pieces = lax.dynamic_slice_in_dim(
        piece_order, lax.axis_index("ctx") * (local_rows // PIECE), local_rows // PIECE
    )
    query_position = (local_pieces[:, None] * PIECE + piece_offsets[None, :]).reshape(local_rows)
    key_position = (piece_order[:, None] * PIECE + piece_offsets[None, :]).reshape(sequence_length)
    bucket_numbers = jnp.arange(BUCKETS, dtype=jnp.int32)

    def self_extras(offset):
        key_block_position = lax.dynamic_slice_in_dim(key_position, offset, KBLK)
        relative_bucket_index = jnp.take(
            bucket_table,
            key_block_position[None, :] - query_position[:, None] + sequence_length - 1,
        )
        bucket_indicator = (
            relative_bucket_index[None, :, :] == bucket_numbers[:, None, None]
        ).astype(jnp.bfloat16)
        added_bias = jnp.einsum(
            "lvj,lf->fvj",
            bucket_indicator,
            position_bias_lookup,
            preferred_element_type=jnp.float32,
        )
        visible = key_block_position[None, :] // BLOCK <= query_position[:, None] // BLOCK
        return (added_bias, visible, bucket_indicator)

    slot_numbers = jnp.arange(PLEN, dtype=jnp.int32)
    memory_valid = (passage_lengths[:, :, None] > slot_numbers[None, None, :]).reshape(
        sequence_count, memory_length
    )

    def cross_extras(offset):
        visible = lax.dynamic_slice_in_dim(memory_valid, offset, KBLK, 1)[:, None, None, :]
        return (0.0, visible, None)

    inputs_wide = tokens.astype(jnp.float32)
    normed_one = norm_scale(inputs_wide, gain_one).astype(jnp.bfloat16)
    queries_one = project(normed_one, query_full).astype(jnp.bfloat16)
    keys_local = project(normed_one, key_full).astype(jnp.bfloat16)
    values_local = project(normed_one, value_full).astype(jnp.bfloat16)
    memory_keys = project(memory, cross_key_full).astype(jnp.bfloat16)
    memory_values = project(memory, cross_value_full).astype(jnp.bfloat16)
    keys_all, values_all, memory_keys_all, memory_values_all = (
        lax.all_gather(keys_local, "ctx", axis=1, tiled=True),
        lax.all_gather(values_local, "ctx", axis=1, tiled=True),
        lax.all_gather(memory_keys, "ctx", axis=1, tiled=True),
        lax.all_gather(memory_values, "ctx", axis=1, tiled=True),
    )
    output_one, maximum_one, total_one = attend_forward(
        to_heads(queries_one), to_heads(keys_all), to_heads(values_all), self_extras
    )
    attended_one = from_heads(output_one).astype(jnp.bfloat16)
    hidden_one = inputs_wide + project(attended_one, output_full)
    normed_two = norm_scale(hidden_one, gain_two).astype(jnp.bfloat16)
    queries_two = project(normed_two, cross_query_full).astype(jnp.bfloat16)
    output_two, maximum_two, total_two = attend_forward(
        to_heads(queries_two), to_heads(memory_keys_all), to_heads(memory_values_all), cross_extras
    )
    attended_two = from_heads(output_two).astype(jnp.bfloat16)
    hidden_two = hidden_one + project(attended_two, cross_output_full)
    normed_three = norm_scale(hidden_two, gain_three).astype(jnp.bfloat16)
    before_gate = project(normed_three, inner_full)
    gated_wide, gate_pullback = jax.vjp(smooth_gate, before_gate)
    activated = gated_wide.astype(jnp.bfloat16)
    layer_output = (hidden_two + project(activated, outer_full)).astype(jnp.bfloat16)
    grad_wide = grad_output.astype(jnp.float32)
    grad_outer = weight_grad(activated, grad_output)
    grad_activated = project_back(grad_output, outer_full)
    grad_before = gate_pullback(grad_activated)[0].astype(jnp.bfloat16)
    grad_inner = weight_grad(normed_three, grad_before)
    ignored, norm_pullback = jax.vjp(norm_scale, hidden_two, gain_three)
    grad_hidden_part, grad_gain_three = norm_pullback(project_back(grad_before, inner_full))
    grad_hidden_two = grad_wide + grad_hidden_part
    branch_two = grad_hidden_two.astype(jnp.bfloat16)
    grad_cross_output = weight_grad(attended_two, branch_two)
    grad_attended_two = project_back(branch_two, cross_output_full).astype(jnp.bfloat16)
    keys_back, values_back, memory_keys_back, memory_values_back = (
        keys_all,
        values_all,
        memory_keys_all,
        memory_values_all,
    )
    grad_query_two, grad_memory_keys, grad_memory_values, unused_bias = attend_backward(
        to_heads(queries_two),
        to_heads(memory_keys_back),
        to_heads(memory_values_back),
        cross_extras,
        heads_first(grad_attended_two),
        output_two,
        maximum_two,
        total_two,
    )
    memory_key_sum, memory_value_sum = (
        lax.psum_scatter(
            grad_memory_keys.reshape(sequence_count, memory_length, D),
            "ctx",
            scatter_dimension=1,
            tiled=True,
        ),
        lax.psum_scatter(
            grad_memory_values.reshape(sequence_count, memory_length, D),
            "ctx",
            scatter_dimension=1,
            tiled=True,
        ),
    )
    memory_key_rounded = memory_key_sum.astype(jnp.bfloat16)
    memory_value_rounded = memory_value_sum.astype(jnp.bfloat16)
    query_two_rounded = grad_query_two.reshape(sequence_count, local_rows, D).astype(jnp.bfloat16)
    grad_cross_query = weight_grad(normed_two, query_two_rounded)
    grad_cross_key = weight_grad(memory, memory_key_rounded)
    grad_cross_value = weight_grad(memory, memory_value_rounded)
    grad_memory = (
        project_back(memory_key_rounded, cross_key_full)
        + project_back(memory_value_rounded, cross_value_full)
    ).astype(jnp.bfloat16)
    ignored, norm_pullback = jax.vjp(norm_scale, hidden_one, gain_two)
    grad_hidden_part, grad_gain_two = norm_pullback(
        project_back(query_two_rounded, cross_query_full)
    )
    grad_hidden_one = grad_hidden_two + grad_hidden_part
    branch_one = grad_hidden_one.astype(jnp.bfloat16)
    grad_self_output = weight_grad(attended_one, branch_one)
    grad_attended_one = project_back(branch_one, output_full).astype(jnp.bfloat16)
    grad_query_one, grad_keys_all, grad_values_all, grad_bias = attend_backward(
        to_heads(queries_one),
        to_heads(keys_back),
        to_heads(values_back),
        self_extras,
        heads_first(grad_attended_one),
        output_one,
        maximum_one,
        total_one,
    )
    key_sum, value_sum = (
        lax.psum_scatter(
            grad_keys_all.reshape(sequence_count, sequence_length, D),
            "ctx",
            scatter_dimension=1,
            tiled=True,
        ),
        lax.psum_scatter(
            grad_values_all.reshape(sequence_count, sequence_length, D),
            "ctx",
            scatter_dimension=1,
            tiled=True,
        ),
    )
    query_one_rounded = grad_query_one.reshape(sequence_count, local_rows, D).astype(jnp.bfloat16)
    first_key_bfloat_cast = key_sum.astype(jnp.bfloat16)
    value_one_rounded = value_sum.astype(jnp.bfloat16)
    grad_self_query = weight_grad(normed_one, query_one_rounded)
    grad_self_key = weight_grad(normed_one, first_key_bfloat_cast)
    grad_self_value = weight_grad(normed_one, value_one_rounded)
    grad_normed_one = (
        project_back(query_one_rounded, query_full)
        + project_back(first_key_bfloat_cast, key_full)
        + project_back(value_one_rounded, value_full)
    )
    ignored, norm_pullback = jax.vjp(norm_scale, inputs_wide, gain_one)
    grad_input_part, grad_gain_one = norm_pullback(grad_normed_one)
    grad_tokens = (grad_hidden_one + grad_input_part).astype(jnp.bfloat16)
    (
        shard_gain_one,
        shard_gain_two,
        shard_gain_three,
        shard_bias,
        shard_query,
        shard_key,
        shard_value,
        shard_output,
        shard_cross_query,
        shard_cross_key,
        shard_cross_value,
        shard_cross_output,
        shard_inner,
        shard_outer,
    ) = (
        lax.psum_scatter(
            grad_gain_one.astype(jnp.bfloat16), "fsdp", scatter_dimension=0, tiled=True
        ).astype(jnp.float32),
        lax.psum_scatter(
            grad_gain_two.astype(jnp.bfloat16), "fsdp", scatter_dimension=0, tiled=True
        ).astype(jnp.float32),
        lax.psum_scatter(
            grad_gain_three.astype(jnp.bfloat16), "fsdp", scatter_dimension=0, tiled=True
        ).astype(jnp.float32),
        lax.psum_scatter(
            grad_bias.astype(jnp.bfloat16), "fsdp", scatter_dimension=0, tiled=True
        ).astype(jnp.float32),
        lax.psum_scatter(
            grad_self_query.astype(jnp.bfloat16), "fsdp", scatter_dimension=0, tiled=True
        ).astype(jnp.float32),
        lax.psum_scatter(
            grad_self_key.astype(jnp.bfloat16), "fsdp", scatter_dimension=0, tiled=True
        ).astype(jnp.float32),
        lax.psum_scatter(
            grad_self_value.astype(jnp.bfloat16), "fsdp", scatter_dimension=0, tiled=True
        ).astype(jnp.float32),
        lax.psum_scatter(
            grad_self_output.astype(jnp.bfloat16), "fsdp", scatter_dimension=0, tiled=True
        ).astype(jnp.float32),
        lax.psum_scatter(
            grad_cross_query.astype(jnp.bfloat16), "fsdp", scatter_dimension=0, tiled=True
        ).astype(jnp.float32),
        lax.psum_scatter(
            grad_cross_key.astype(jnp.bfloat16), "fsdp", scatter_dimension=0, tiled=True
        ).astype(jnp.float32),
        lax.psum_scatter(
            grad_cross_value.astype(jnp.bfloat16), "fsdp", scatter_dimension=0, tiled=True
        ).astype(jnp.float32),
        lax.psum_scatter(
            grad_cross_output.astype(jnp.bfloat16), "fsdp", scatter_dimension=0, tiled=True
        ).astype(jnp.float32),
        lax.psum_scatter(
            grad_inner.astype(jnp.bfloat16), "fsdp", scatter_dimension=0, tiled=True
        ).astype(jnp.float32),
        lax.psum_scatter(
            grad_outer.astype(jnp.bfloat16), "fsdp", scatter_dimension=0, tiled=True
        ).astype(jnp.float32),
    )
    (
        total_gain_one,
        total_gain_two,
        total_gain_three,
        total_bias,
        total_query,
        total_key,
        total_value,
        total_output,
        total_cross_query,
        total_cross_key,
        total_cross_value,
        total_cross_output,
        total_inner,
        total_outer,
    ) = lax.psum(
        (
            shard_gain_one,
            shard_gain_two,
            shard_gain_three,
            shard_bias,
            shard_query,
            shard_key,
            shard_value,
            shard_output,
            shard_cross_query,
            shard_cross_key,
            shard_cross_value,
            shard_cross_output,
            shard_inner,
            shard_outer,
        ),
        "ctx",
    )
    return (
        layer_output,
        grad_tokens,
        grad_memory,
        total_gain_one,
        total_gain_two,
        total_gain_three,
        total_bias,
        total_query,
        total_key,
        total_value,
        total_output,
        total_cross_query,
        total_cross_key,
        total_cross_value,
        total_cross_output,
        total_inner,
        total_outer,
    )


MESH = pl.DeviceIdType.MESH
WAYS = 4


class Place:
    def __init__(self, peers):
        self.depth = peers // 2
        c, f = lax.axis_index("ctx"), lax.axis_index("fsdp")
        self.c, self.f = c, f
        self.a, self.b, self.x, self.k = c // 2, c % 2, f // 2, f % 2
        self.core = (c, self.x * 2 + 1 - self.k)
        self.across = (c, (1 - self.x) * 2 + self.k)
        self.beside = (self.a * 2 + 1 - self.b, f)

    def ahead(self, d):
        return lax.rem(self.a + d, self.depth)

    def behind(self, d):
        return lax.rem(self.a + self.depth - d, self.depth)

    def column(self, a):
        return (a * 2 + self.b, self.f)

    def group(self, d):
        return (self.c, lax.rem(self.f + d, WAYS))


def greet(targets):
    barrier = pltpu.get_barrier_semaphore()
    for target in targets:
        pl.semaphore_signal(barrier, inc=1, device_id=target, device_id_type=MESH)
    pl.semaphore_wait(barrier, len(targets))


def remote(src, dst, sems, index, target):
    return pltpu.make_async_remote_copy(
        src_ref=src,
        dst_ref=dst,
        send_sem=sems[0].at[index],
        recv_sem=sems[1].at[index],
        device_id=target,
        device_id_type=MESH,
    )


def sems(count):
    return [pltpu.SemaphoreType.DMA((count,)), pltpu.SemaphoreType.DMA((count,))]


class Wire:
    def __init__(self, peers):
        self.at = Place(peers)
        self.depth = self.at.depth
        self.sent = []

    def go(self, copy):
        copy.start()
        self.sent.append(copy)

    def drain(self):
        for copy in self.sent:
            copy.wait_send()

    def partners(self):
        at = self.at
        return (
            [at.group(d) for d in range(1, WAYS)]
            + [at.beside]
            + [at.column(at.ahead(d)) for d in range(1, self.depth)]
        )

    def near(self, step):
        a, last = self.at.a, self.depth - 1
        low = jnp.where(step - 1 < a, step - 1, step)
        mirrored = jnp.where(step - 1 < last - a, step - 1, step)
        return jnp.where(2 * a < last, low, last - mirrored)

    def slot(self, buf, c):
        if len(buf.shape) == 3:
            return buf.at[c]
        rows = buf.shape[0] // (2 * self.depth)
        return buf.at[pl.ds(pl.multiple_of(c * rows, rows), rows)]

    def spread(self, src, buf, sem):
        at = self.at
        slot = self.slot(buf, at.c)
        self.go(remote(src, slot, sem, at.a, at.beside))
        for step in range(1, self.depth):
            self.go(remote(src, slot, sem, self.depth + at.a, at.column(self.near(step))))

    def relay(self, buf, sem, step):
        a = self.near(step)
        slot = self.slot(buf, a * 2 + self.at.b)
        remote(slot, slot, sem, self.depth + a, self.at.beside).wait_recv()
        self.go(remote(slot, slot, sem, a, self.at.beside))

    def from_beside(self, buf, sem, a):
        slot = self.slot(buf, a * 2 + 1 - self.at.b)
        remote(slot, slot, sem, a, self.at.beside).wait_recv()

    def shard(self, full, f):
        quarter = full.shape[0] // WAYS
        return full.at[pl.ds(pl.multiple_of(f * quarter, quarter), quarter)]

    def weight_start(self, src, full, sem, i):
        at = self.at
        slot = self.shard(full, at.f)
        slot[...] = src[...]
        self.go(remote(src, slot, sem, 3 * i, at.across))
        self.go(remote(src, slot, sem, 3 * i + 1, at.core))

    def weight_relay(self, full, sem, i):
        at = self.at
        slot = self.shard(full, (1 - at.x) * 2 + at.k)
        remote(slot, slot, sem, 3 * i, at.across).wait_recv()
        self.go(remote(slot, slot, sem, 3 * i + 2, at.core))

    def weight_ready(self, full, sem, i):
        at = self.at
        slot = self.shard(full, at.x * 2 + 1 - at.k)
        remote(slot, slot, sem, 3 * i + 1, at.core).wait_recv()
        slot = self.shard(full, (1 - at.x) * 2 + 1 - at.k)
        remote(slot, slot, sem, 3 * i + 2, at.core).wait_recv()


def own_bias(table, lines, own, out):
    full = table.shape[1]
    rows, length = out.shape[1], out.shape[2]

    def head(h, c):
        base = shear(pltpu.roll(jnp.broadcast_to(table[pl.ds(h, 1), :], (8, full)), 1, 1), 1)
        lines[0] = base
        lines[1] = pltpu.roll(base, PIECE, 1)
        for i in range(rows // PIECE):
            window = lines[own[i, 1], :, pl.ds(own[i, 2] * LANES, length + LANES)]
            for g in range(0, PIECE // 8, 2):
                both = [pltpu.roll(window, 8 * k, 1) if k else window for k in (g, g + 1)]
                both = jnp.concatenate(both, 0)[:, LANES:]
                out[h, i * PIECE + 8 * g : i * PIECE + 8 * g + 16, :] = both.astype(BF16)
        return c

    lax.fori_loop(0, HEADS, head, 0)


def diagonal_sums(block):
    rows, length = block.shape
    wide = jnp.concatenate([block, jnp.zeros((rows, LANES), F32)], axis=1)
    total = pltpu.roll(wide[0:8], LANES, 1)
    for g in range(1, rows // 8):
        total += pltpu.roll(wide[8 * g : 8 * g + 8], LANES - 8 * g, 1)
    return jnp.sum(shear(total, -1), axis=0, keepdims=True)


N_FRONT = 7
N_GAINS = 16


def front_kernel(peers, *refs):
    inv, own, tok, pack, buckets, buckets_back = refs[:6]
    shards_in = refs[6 : 6 + N_FRONT]
    (w_self, w_rest, gains, ahead, behind, q_nat, k_nat, v_nat, a1, o1, h1, a2, q2, lse) = refs[6 + N_FRONT : 20 + N_FRONT]
    (tok_all, pack_all, table, lines, q_own, *sem) = refs[20 + N_FRONT :]
    weights = [w_self.at[i] for i in range(3)] + [w_rest.at[i] for i in range(N_FRONT - 3)]
    sem_t, sem_w, sem_p = sem[0:2], sem[2:4], sem[4:6]
    wire = Wire(peers)
    at, depth = wire.at, wire.depth
    rows = tok.shape[0]
    length = peers * rows
    mine, per = rows // PIECE, BLOCK // PIECE
    greet(wire.partners())
    for d in range(1, WAYS):
        wire.go(remote(pack, pack_all.at[at.f], sem_p, d, at.group(d)))
    wire.spread(tok, tok_all, sem_t)
    for i in range(3):
        wire.weight_start(shards_in[i], weights[i], sem_w, i)
    wire.slot(tok_all, at.c)[...] = tok[...]
    pack_all[at.f] = pack[...]
    for d in range(1, WAYS):
        slot = pack_all.at[lax.rem(at.f + WAYS - d, WAYS)]
        remote(slot, slot, sem_p, d, at.group(WAYS - d)).wait_recv()
    everything = pack_all[0].astype(F32) + pack_all[1].astype(F32) + pack_all[2].astype(F32) + pack_all[3].astype(F32)
    gains[...] = everything[0:8, :]
    bias = everything[N_GAINS:, 0:LANES].astype(BF16)
    bucket = lax.broadcasted_iota(jnp.int32, (bias.shape[0], 2 * length), 0)
    for line, out in ((buckets, ahead), (buckets_back, behind)):
        hot = jnp.where(line[...] == bucket, 1.0, 0.0).astype(BF16)
        table[...] = tn(bias, hot)[0:16, :]
        own_bias(table, lines, own, out)
    for step in range(1, depth):
        wire.relay(tok_all, sem_t, step)
    for i in range(3):
        wire.weight_relay(weights[i], sem_w, i)
    for i in range(3, N_FRONT):
        wire.weight_start(shards_in[i], weights[i], sem_w, i)
    first = gains[0:1, :]
    a1[...] = normed(tok[...].astype(F32), first).astype(BF16)
    for i in range(3):
        wire.weight_ready(weights[i], sem_w, i)
    for step in range(depth):
        wire.from_beside(tok_all, sem_t, step)

    def tile(t, c):
        parts = []
        for i in range(per):
            parts.append(tok_all[pl.ds(inv[t * per + i] * PIECE, PIECE), :])
        a = normed(jnp.concatenate(parts, 0).astype(F32), first).astype(BF16)
        dst = pl.ds(pl.multiple_of(t * BLOCK, BLOCK), BLOCK)
        for j, out in enumerate((q_nat, k_nat, v_nat)):
            out[dst, :] = nn(a, weights[j][...]).astype(BF16)
        return c

    lax.fori_loop(0, length // BLOCK, tile, 0)
    for i in range(mine):
        q_own[i * PIECE : (i + 1) * PIECE, :] = q_nat[pl.ds(own[i, 0] * PIECE, PIECE), :]
    wire.weight_relay(weights[3], sem_w, 3)
    lane = lax.broadcasted_iota(jnp.int32, (rows, length), 1)
    limit = jnp.concatenate([jnp.full((PIECE, 1), own[i, 3], jnp.int32) for i in range(mine)], 0)
    visible = lane < limit
    stat_lane = lax.broadcasted_iota(jnp.int32, (rows, LANES), 1)

    def pair(p, stats):
        sl = lanes_of(p)
        q, k, v = q_own[:, sl], k_nat[:, sl], v_nat[:, sl]
        total = jnp.zeros((rows, LANES), F32)
        for half in range(2):
            h = 2 * p + half
            s = jnp.where(visible, nt(q, half_mask(k, half)) + ahead[h].astype(F32), NEGATIVE)
            m = jnp.max(s, axis=1, keepdims=True)
            e = jnp.exp(s - m)
            l = jnp.sum(e, axis=1, keepdims=True)
            total += nn(e.astype(BF16), half_mask(v, half)) / l
            stats = jnp.where(stat_lane == h, m + jnp.log(l), stats)
        o1[:, sl] = total.astype(BF16)
        return stats

    stats = lax.fori_loop(0, PAIRS // 2, pair, jnp.zeros((rows, LANES), F32))
    wire.weight_relay(weights[4], sem_w, 4)
    lse[...] = lax.fori_loop(PAIRS // 2, PAIRS, pair, stats)
    wire.weight_relay(weights[5], sem_w, 5)
    wire.weight_ready(weights[3], sem_w, 3)
    h = tok[...].astype(F32) + nn(o1[...], weights[3][...])
    h1[...] = h
    a = normed(h, gains[1:2, :]).astype(BF16)
    a2[...] = a
    wire.weight_ready(weights[4], sem_w, 4)
    q2[...] = nn(a, weights[4][...]).astype(BF16)
    wire.weight_relay(weights[6], sem_w, 6)
    for i in (5, 6):
        wire.weight_ready(weights[i], sem_w, i)
    wire.drain()


def front(peers, inv, own, tok, pack, buckets, buckets_back, weight_shards):
    rows = tok.shape[0]
    length, depth = peers * rows, peers // 2
    block = lambda dtype: sds((rows, D), dtype)
    return pl.pallas_call(
        functools.partial(front_kernel, peers),
        name="front",
        out_shape=[sds((3, D, D), BF16), sds((N_FRONT - 3, D, D), BF16), sds((8, D), F32)]
        + [sds((HEADS, rows, length), BF16)] * 2
        + [sds((length, D), BF16)] * 3
        + [block(BF16), block(BF16), block(F32), block(BF16), block(BF16), sds((rows, LANES), F32)],
        in_specs=[smem_spec()] * 2 + [full_spec()] * (4 + N_FRONT),
        out_specs=[full_spec()] * 14,
        scratch_shapes=[
            pltpu.VMEM((length, D), BF16),
            pltpu.VMEM((WAYS,) + pack.shape, BF16),
            pltpu.VMEM((16, 2 * length), F32),
            pltpu.VMEM((2, 8, 2 * length), F32),
            pltpu.VMEM((rows, D), BF16),
        ]
        + sems(2 * depth) + sems(3 * N_FRONT) + sems(WAYS),
        compiler_params=pltpu.CompilerParams(collective_id=1, has_side_effects=True, vmem_limit_bytes=VMEM_LIMIT),
    )(inv, own, tok, pack, buckets, buckets_back, *weight_shards)


STAT = 16


def split(x):
    high = x.astype(BF16)
    return high, (x - high.astype(F32)).astype(BF16)


def head_matrix(rows):
    row = lax.broadcasted_iota(jnp.int32, (rows, D), 0)
    lane = lax.broadcasted_iota(jnp.int32, (rows, D), 1)
    return jnp.where(lane // HEAD_DIM == row, 1.0, 0.0).astype(BF16)


def per_head_sums(x, heads):
    high, low = split(x)
    return nt(heads, high) + nt(heads, low)


def blend(parts, stats, heads):
    top = functools.reduce(jnp.maximum, stats)
    shares = [jnp.exp(s - top) for s in stats]
    total = functools.reduce(jnp.add, shares)
    value = 0.0
    for part, share in zip(parts, shares):
        high, low = split(share / total)
        value = value + (tn(high, heads) + tn(low, heads)) * part.astype(F32)
    return value, top + jnp.log(total)


def norm_back_rows(x, gain, dy):
    r = lax.rsqrt(jnp.mean(x * x, axis=-1, keepdims=True) + EPSILON)
    gdy = gain * dy
    dx = r * gdy - x * (r * r * r) * jnp.mean(x * gdy, axis=-1, keepdims=True)
    return dx, jnp.sum(dy * x * r, axis=0, keepdims=True)


def round_trip(wire, gathered, filler, compute, ship, fold):
    at = wire.at
    b = at.b
    first, second, third = [wire.near(step) for step in (1, 2, 3)]

    def relay(step):
        for buf, sem in gathered:
            wire.relay(buf, sem, step)

    def ready(a):
        for buf, sem in gathered:
            wire.from_beside(buf, sem, a)

    filler()
    relay(1)
    ready(at.a)
    compute(at.c, at.a * 2 + 1 - b)
    ship(at.a)
    relay(2)
    relay(3)
    compute(first * 2 + b, second * 2 + b)
    ready(third)
    ready(second)
    compute(third * 2 + 1 - b, second * 2 + 1 - b)
    ship(third)
    ship(second)
    ready(first)
    compute(third * 2 + b, first * 2 + 1 - b)
    ship(first)
    fold(third)
    fold(second)
    fold(first)


def middle_kernel(peers, *refs):
    (q2, h1, o1, lse1, w_rest, gains, mem, mask_row, mask_col, grad, co_shard, in_shard, w_out) = refs[:13]
    (o2_out, branch2_out, dq2_out, dk2_out, dv2_out, branch1_out, dh1_out, do1_out, stat1_out, g_in, g_out, layer_out, gmem_out, small) = refs[13:27]
    (q_all, k2, v2, part, part_lse, from_b, from_b_lse, joined, joined_lse, from_z, from_z_lse,
     w_co, w_in, g_all, a3_all, dact, act, dpre, da3_send, da3_in, out_send, out_in,
     do_all, stat_all, stat_own, dk_acc, dv_acc, dqp, dq_b, dq_j, dq_z, *sem) = refs[27:]
    sem = [sem[2 * i : 2 * i + 2] for i in range(len(sem) // 2)]
    (s_q, s_w, s_in, s_g, s_y, s_yl, s_z, s_zl, s_a3, s_da3, s_out, s_do, s_st, s_dy, s_dz) = sem
    wire = Wire(peers)
    at, depth = wire.at, wire.depth
    rows = q2.shape[0]
    heads = head_matrix(STAT)
    quarter = co_shard.shape[0]
    units = w_out.shape[0]
    block = lambda f: pl.ds(pl.multiple_of(f * rows, rows), rows)
    greet(wire.partners())
    wire.spread(q2, q_all, s_q)
    q_all[at.c] = q2[...]
    wire.weight_start(co_shard, w_co, s_w, 0)
    for d in range(1, WAYS):
        f = lax.rem(at.f + d, WAYS)
        wire.go(remote(grad, g_all.at[block(at.f)], s_g, d, at.group(d)))
        wire.go(remote(in_shard.at[:, pl.ds(pl.multiple_of(f * units, LANES), units)], wire.shard(w_in, at.f), s_in, d, at.group(d)))
    g_all[block(at.f), :] = grad[...]
    wire.shard(w_in, at.f)[...] = in_shard[:, pl.ds(pl.multiple_of(at.f * units, LANES), units)]

    def project_memory():
        k2[...] = nn(mem[...], w_rest[2]).astype(BF16)
        v2[...] = nn(mem[...], w_rest[3]).astype(BF16)

    stat_lane = lax.broadcasted_iota(jnp.int32, (2 * rows, LANES), 1)

    def attend(c1, c2):
        def pair(p, stats):
            sl = lanes_of(p)
            q = jnp.concatenate([q_all[c1, :, sl], q_all[c2, :, sl]], 0)
            k, v = k2[:, sl], v2[:, sl]
            total = jnp.zeros((2 * rows, LANES), F32)
            for half in range(2):
                s = nt(q, half_mask(k, half)) + mask_row[...]
                m = jnp.max(s, axis=1, keepdims=True)
                e = jnp.exp(s - m)
                l = jnp.sum(e, axis=1, keepdims=True)
                total += nn(e.astype(BF16), half_mask(v, half)) / l
                stats = jnp.where(stat_lane == 2 * p + half, m + jnp.log(l), stats)
            part[c1, :, sl] = total[:rows].astype(BF16)
            part[c2, :, sl] = total[rows:].astype(BF16)
            return stats

        stats = lax.fori_loop(0, PAIRS, pair, jnp.zeros((2 * rows, LANES), F32))
        part_lse[c1] = stats[:rows].T[:STAT]
        part_lse[c2] = stats[rows:].T[:STAT]

    def ship_part(a):
        other = a * 2 + 1 - at.b
        wire.go(remote(part.at[other], from_b.at[a], s_y, a, at.beside))
        wire.go(remote(part_lse.at[other], from_b_lse.at[a], s_yl, a, at.beside))

    def blend_column(a):
        remote(from_b.at[a], from_b.at[a], s_y, a, at.beside).wait_recv()
        remote(from_b_lse.at[a], from_b_lse.at[a], s_yl, a, at.beside).wait_recv()
        c = a * 2 + at.b
        return blend([part[c], from_b[a]], [part_lse[c], from_b_lse[a]], heads)

    def fold_part(a):
        value, stat = blend_column(a)
        joined[a] = value.astype(BF16)
        joined_lse[a] = stat
        wire.go(remote(joined.at[a], from_z.at[at.a], s_z, at.a, at.column(a)))
        wire.go(remote(joined_lse.at[a], from_z_lse.at[at.a], s_zl, at.a, at.column(a)))

    round_trip(wire, [(q_all, s_q)], project_memory, attend, ship_part, fold_part)
    wire.weight_relay(w_co, s_w, 0)
    value, stat = blend_column(at.a)
    parts, stats = [value], [stat]
    for step in range(1, depth):
        a = wire.near(step)
        remote(from_z.at[a], from_z.at[a], s_z, a, at.column(a)).wait_recv()
        remote(from_z_lse.at[a], from_z_lse.at[a], s_zl, a, at.column(a)).wait_recv()
        parts.append(from_z[a])
        stats.append(from_z_lse[a])
    out2, lse2 = blend(parts, stats, heads)
    o2 = out2.astype(BF16)
    o2_out[...] = o2
    wire.weight_ready(w_co, s_w, 0)
    h2 = h1[...] + nn(o2, w_co[...])
    a3 = normed(h2, gains[2:3, :]).astype(BF16)
    a3_all[block(at.f), :] = a3
    for d in range(1, WAYS):
        spot = a3_all.at[block(at.f)]
        wire.go(remote(spot, spot, s_a3, d, at.group(d)))

    def arrive(buf, sem, size):
        for d in range(1, WAYS):
            f = lax.rem(at.f + WAYS - d, WAYS)
            spot = buf.at[pl.ds(pl.multiple_of(f * size, size), size)]
            remote(spot, spot, sem, d, at.group(WAYS - d)).wait_recv()

    arrive(g_all, s_g, rows)
    tiles = [slice(2 * rows * t, 2 * rows * (t + 1)) for t in range(WAYS // 2)]
    for rs in tiles:
        dact[rs, :] = nt(g_all[rs, :], w_out[...])
    arrive(w_in, s_in, quarter)
    arrive(a3_all, s_a3, rows)
    for rs in tiles:
        pre = nn(a3_all[rs, :], w_in[...])
        square = pre * pre
        t = jnp.tanh(0.7978845608028654 * (pre + 0.044715 * pre * square))
        act[rs, :] = (0.5 * pre * (1.0 + t)).astype(BF16)
        slope = 0.5 * (1.0 + t) + 0.5 * pre * (1.0 - t * t) * (0.7978845608028654 * (1.0 + 3 * 0.044715 * square))
        d = (dact[rs, :] * slope).astype(BF16)
        dpre[rs, :] = d
        da3_send[rs, :] = nt(d, w_in[...]).astype(BF16)

    def exchange(src, dst, sem):
        for d in range(1, WAYS):
            f = lax.rem(at.f + d, WAYS)
            wire.go(remote(src.at[block(f)], dst.at[block(at.f)], sem, d, at.group(d)))

    def collect(src, dst, sem):
        arrive(dst, sem, rows)
        value = src[block(at.f), :].astype(F32)
        for d in range(1, WAYS):
            value += dst[block(lax.rem(at.f + WAYS - d, WAYS)), :].astype(F32)
        return value

    exchange(da3_send, da3_in, s_da3)
    for rs in tiles:
        out_send[rs, :] = nn(act[rs, :], w_out[...]).astype(BF16)
    exchange(out_send, out_in, s_out)
    da3 = collect(da3_send, da3_in, s_da3)
    dx, dgain = norm_back_rows(h2, gains[2:3, :], da3)
    small[...] = jnp.zeros_like(small)
    small[1:2, :] = dgain
    dh2 = grad[...].astype(F32) + dx
    branch2 = dh2.astype(BF16)
    branch2_out[...] = branch2
    do2 = nt(branch2, w_co[...]).astype(BF16)
    do_all[at.c] = do2
    stat_own[0] = jnp.concatenate([lse2, per_head_sums(do2.astype(F32) * out2, heads)], 0)
    stat_all[at.c] = stat_own[0]
    wire.spread(do_all.at[at.c], do_all, s_do)
    wire.spread(stat_own.at[0], stat_all, s_st)

    def feed_forward_grads():
        layer_out[...] = (h2 + collect(out_send, out_in, s_out)).astype(BF16)
        g_out[...] = tn(act[...], g_all[...]).astype(BF16)
        g_in[...] = tn(a3_all[...], dpre[...]).astype(BF16)
        dk_acc[...] = jnp.zeros_like(dk_acc)
        dv_acc[...] = jnp.zeros_like(dv_acc)

    def attend_back(c1, c2):
        def pair(p, carry):
            sl = lanes_of(p)
            q = jnp.concatenate([q_all[c1, :, sl], q_all[c2, :, sl]], 0)
            do = jnp.concatenate([do_all[c1, :, sl], do_all[c2, :, sl]], 0)
            k, v = k2[:, sl], v2[:, sl]
            dkp, dvp = dk_acc[:, sl], dv_acc[:, sl]
            dq = jnp.zeros((2 * rows, LANES), F32)
            for half in range(2):
                line = lambda i: jnp.concatenate([stat_all[c1, pl.ds(i, 1), :], stat_all[c2, pl.ds(i, 1), :]], 1)
                h = 2 * p + half
                km = half_mask(k, half)
                s = nt(km, q) + mask_col[...]
                e = jnp.exp(s - line(h))
                dvp = dvp + nn(e.astype(BF16), half_mask(do, half))
                ds = (e * (nt(half_mask(v, half), do) - line(STAT + h))).astype(BF16)
                dkp = dkp + nn(ds, half_mask(q, half))
                dq = dq + tn(ds, km)
            dk_acc[:, sl] = dkp
            dv_acc[:, sl] = dvp
            dqp[c1, :, sl] = dq[:rows].astype(BF16)
            dqp[c2, :, sl] = dq[rows:].astype(BF16)
            return carry

        lax.fori_loop(0, PAIRS, pair, 0)

    def ship_dq(a):
        wire.go(remote(dqp.at[a * 2 + 1 - at.b], dq_b.at[a], s_dy, a, at.beside))

    def column_dq(a):
        remote(dq_b.at[a], dq_b.at[a], s_dy, a, at.beside).wait_recv()
        return dqp[a * 2 + at.b].astype(F32) + dq_b[a].astype(F32)

    def fold_dq(a):
        dq_j[a] = column_dq(a).astype(BF16)
        wire.go(remote(dq_j.at[a], dq_z.at[at.a], s_dz, at.a, at.column(a)))

    round_trip(wire, [(do_all, s_do), (stat_all, s_st)], feed_forward_grads, attend_back, ship_dq, fold_dq)
    dk2_out[...] = dk_acc[...].astype(BF16)
    dv2_out[...] = dv_acc[...].astype(BF16)
    value = column_dq(at.a)
    for step in range(1, depth):
        a = wire.near(step)
        remote(dq_z.at[a], dq_z.at[a], s_dz, a, at.column(a)).wait_recv()
        value += dq_z[a].astype(F32)
    dq2 = value.astype(BF16)
    dq2_out[...] = dq2
    dx, dgain = norm_back_rows(h1[...], gains[1:2, :], nt(dq2, w_rest[1]))
    small[0:1, :] = dgain
    dh1 = dh2 + dx
    dh1_out[...] = dh1
    branch1 = dh1.astype(BF16)
    branch1_out[...] = branch1
    do1 = nt(branch1, w_rest[0]).astype(BF16)
    do1_out[...] = do1
    stat_own[1] = jnp.concatenate([lse1[...].T[:STAT], per_head_sums(do1.astype(F32) * o1[...].astype(F32), heads)], 0)
    stat1_out[...] = stat_own[1]
    gmem_out[...] = (nt(dk2_out[...], w_rest[2]) + nt(dv2_out[...], w_rest[3])).astype(BF16)
    wire.drain()


def middle(peers, q2, h1, o1, lse1, w_rest, gains, mem, mask_row, mask_col, grad, co_shard, in_shard, w_out):
    rows, slots = q2.shape[0], mem.shape[0]
    depth = peers // 2
    units = w_out.shape[0]
    row = lambda dtype: sds((rows, D), dtype)
    store = lambda n, dtype=BF16: pltpu.VMEM((n, rows, D), dtype)
    stat = lambda n, k=STAT: pltpu.VMEM((n, k, rows), F32)
    group = lambda width, dtype=BF16: pltpu.VMEM((WAYS * rows, width), dtype)
    return pl.pallas_call(
        functools.partial(middle_kernel, peers),
        name="middle",
        out_shape=[
            row(BF16),
            row(BF16),
            row(BF16),
            sds((slots, D), BF16),
            sds((slots, D), BF16),
            row(BF16),
            row(F32),
            row(BF16),
            sds((2 * STAT, rows), F32),
            sds((D, units), BF16),
            sds((units, D), BF16),
            row(BF16),
            sds((slots, D), BF16),
            sds((8, D), F32),
        ],
        in_specs=[full_spec()] * 13,
        out_specs=[full_spec()] * 14,
        scratch_shapes=[
            store(peers), pltpu.VMEM((slots, D), BF16), pltpu.VMEM((slots, D), BF16),
            store(peers), stat(peers), store(depth), stat(depth), store(depth), stat(depth), store(depth), stat(depth),
            pltpu.VMEM((D, D), BF16), pltpu.VMEM((D, units), BF16),
            group(D), group(D), group(units, F32), group(units), group(units), group(D), group(D), group(D), group(D),
            store(peers), stat(peers, 2 * STAT), stat(2, 2 * STAT),
            pltpu.VMEM((slots, D), F32), pltpu.VMEM((slots, D), F32),
            store(peers), store(depth), store(depth), store(depth),
        ]
        + sems(2 * depth) + sems(3) + sems(WAYS) + sems(WAYS)
        + sems(depth) * 4
        + sems(WAYS) * 3
        + sems(2 * depth) * 2
        + sems(depth) * 2,
        compiler_params=pltpu.CompilerParams(collective_id=2, has_side_effects=True, vmem_limit_bytes=VMEM_LIMIT),
    )(q2, h1, o1, lse1, w_rest, gains, mem, mask_row, mask_col, grad, co_shard, in_shard, w_out)


def tail_kernel(peers, *refs):
    (inv, own, do1, stat1, q_nat, k_nat, v_nat, bias, bias_back, tok, w_self, gains, dh1, bucket_rows,
     a1, o1, branch1, a2, dq2, mem, dk2, dv2, o2, branch2, g_in, g_out, small_mid) = refs[:27]
    out, small_out, grad_tokens = refs[27:30]
    (prod, ra, sb, rb, sc, rc, sd, rd, tiny, tiny_in, do_all, do_nat, stat_all, stat_rows, stat_t, q_own, k_own, v_own,
     dq1, dk1, dv1, diagonals, s_w, *sem) = refs[30:]
    sem = [sem[2 * i : 2 * i + 2] for i in range(len(sem) // 2)]
    s_do, s_st, sem_a, sem_b, sem_c, sem_d, sem_e, sem_f, sem_g, sem_t = sem
    wire = Wire(peers)
    at, depth, go = wire.at, wire.depth, wire.go
    rows, length = do1.shape[0], q_nat.shape[0]
    mine, pieces = rows // PIECE, length // PIECE
    total, quarter, wide = out.shape
    half_width, part = wide // 2, quarter // depth
    pairs = [(o2, branch2), (mem, dk2), (mem, dv2), (a2, dq2), (o1, branch1), (a1, dq1), (a1, dk1), (a1, dv1)]
    n_mats = len(pairs)
    columns = lambda b: pl.ds(pl.multiple_of(b * half_width, LANES), half_width)
    shard_rows = lambda f: pl.ds(pl.multiple_of(f * quarter, quarter), quarter)
    part_rows = lambda a: pl.ds(pl.multiple_of(a * part, part), part)
    own_half, other_half = columns(at.b), columns(1 - at.b)

    def stage_a(i):
        left, right = pairs[i]
        prod[i] = tn(left[...], right[...]).astype(BF16)
        for x in range(2):
            go(remote(prod.at[i, shard_rows(x * 2 + 1 - at.k)], ra.at[i, x], sem_a, 2 * i + x, at.core))

    def stage_b(i):
        for x in range(2):
            remote(ra.at[i, x], ra.at[i, x], sem_a, 2 * i + x, at.core).wait_recv()
        x = 1 - at.x
        sb[i] = (prod[i, shard_rows(x * 2 + at.k), :].astype(F32) + ra[i, x].astype(F32)).astype(BF16)
        go(remote(sb.at[i], rb.at[i], sem_b, i, at.across))

    def source(j):
        if j < n_mats + WAYS:
            return sc.at[j]
        q = j - n_mats - WAYS
        return g_out.at[q * quarter : (q + 1) * quarter]

    def stage_c(j):
        if j < n_mats:
            remote(sb.at[j], rb.at[j], sem_b, j, at.across).wait_recv()
            value = prod[j, shard_rows(at.f), :].astype(F32) + ra[j, at.x].astype(F32) + rb[j].astype(F32)
            sc[j] = value.astype(BF16)
        go(remote(source(j).at[:, other_half], rc.at[j], sem_c, j, at.beside))

    def stage_d(j):
        remote(rc.at[j], rc.at[j], sem_c, j, at.beside).wait_recv()
        value = source(j)[:, own_half].astype(F32) + rc[j].astype(F32)
        sd[j] = value.astype(BF16)
        for d in range(1, depth):
            spot = rd.at[j, part_rows(at.a)]
            go(remote(sd.at[j, part_rows(at.ahead(d))], spot, sem_d, j * depth + d, at.column(at.ahead(d))))

    def stage_e(j):
        value = sd[j, part_rows(at.a), :].astype(F32)
        for d in range(1, depth):
            spot = rd.at[j, part_rows(at.behind(d))]
            remote(spot, spot, sem_d, j * depth + d, at.column(at.behind(d))).wait_recv()
            value += spot[...].astype(F32)
        spot = out.at[j, part_rows(at.a), own_half]
        spot[...] = value.astype(BF16)
        for d in range(1, depth):
            go(remote(spot, spot, sem_e, j * depth + d, at.column(at.ahead(d))))

    def stage_f(j):
        for d in range(1, depth):
            spot = out.at[j, part_rows(at.behind(d)), own_half]
            remote(spot, spot, sem_e, j * depth + d, at.column(at.behind(d))).wait_recv()
        go(remote(out.at[j, :, own_half], out.at[j, :, own_half], sem_f, j, at.beside))

    def stage_g(j):
        spot = out.at[j, :, other_half]
        remote(spot, spot, sem_f, j, at.beside).wait_recv()

    def send_g_in():
        sc[n_mats + at.f] = g_in[shard_rows(at.f), :]
        for d in range(1, WAYS):
            f = lax.rem(at.f + d, WAYS)
            go(remote(g_in.at[shard_rows(f)], sc.at[n_mats + at.f], sem_g, d, at.group(d)))

    def have_g_in():
        for d in range(1, WAYS):
            spot = sc.at[n_mats + lax.rem(at.f + WAYS - d, WAYS)]
            remote(spot, spot, sem_g, d, at.group(WAYS - d)).wait_recv()

    hops = [at.core, at.across, at.beside]

    def small_hop(t):
        if t:
            remote(tiny_in.at[t - 1], tiny_in.at[t - 1], sem_t, t - 1, hops[t - 1]).wait_recv()
            tiny[t] = tiny[t - 1] + tiny_in[t - 1]
        if t < 3:
            go(remote(tiny.at[t], tiny_in.at[t], sem_t, t, hops[t]))
        else:
            for d in range(1, depth):
                go(remote(tiny.at[3], tiny_in.at[2 + d], sem_t, 2 + d, at.column(at.ahead(d))))

    def small_end():
        value = tiny[3]
        for d in range(1, depth):
            remote(tiny_in.at[2 + d], tiny_in.at[2 + d], sem_t, 2 + d, at.column(at.behind(d))).wait_recv()
            value += tiny_in[2 + d]
        small_out[...] = value

    gathered = [(do_all, s_do), (stat_all, s_st)]

    def relay(step):
        for buf, s in gathered:
            wire.relay(buf, s, step)

    def prepare():
        for a in range(depth):
            for buf, s in gathered:
                wire.from_beside(buf, s, a)
        for c in range(peers):
            spread = jnp.concatenate([stat_all[c], jnp.zeros((LANES - 2 * STAT, rows), F32)], 0)
            stat_rows[c * rows : (c + 1) * rows, :] = spread.T
        for i in range(pieces):
            do_nat[i * PIECE : (i + 1) * PIECE, :] = do_all[pl.ds(inv[i] * PIECE, PIECE), :]
        per = LANES // PIECE
        for t in range(length // LANES):
            lines = [stat_rows[pl.ds(inv[t * per + i] * PIECE, PIECE), :] for i in range(per)]
            stat_t[:, t * LANES : (t + 1) * LANES] = jnp.concatenate(lines, 0).T
        for i in range(mine):
            dst = slice(i * PIECE, (i + 1) * PIECE)
            src = pl.ds(own[i, 0] * PIECE, PIECE)
            q_own[dst, :] = q_nat[src, :]
            k_own[dst, :] = k_nat[src, :]
            v_own[dst, :] = v_nat[src, :]

    def own_column(i):
        return jnp.concatenate([jnp.full((PIECE, 1), own[j, i], jnp.int32) for j in range(mine)], 0)

    def attend_back(low, high):
        lane = lax.broadcasted_iota(jnp.int32, (rows, length), 1)
        visible, seen = lane < own_column(3), lane >= own_column(4)
        stat_lane = lax.broadcasted_iota(jnp.int32, (rows, LANES), 1)
        stat_own = jnp.concatenate([stat1[...], jnp.zeros((LANES - 2 * STAT, rows), F32)], 0).T

        def column(h):
            return jnp.sum(jnp.where(stat_lane == h, stat_own, 0.0), axis=1, keepdims=True)

        def pair(p, c):
            sl = lanes_of(p)
            q, k, v, do = q_own[:, sl], k_nat[:, sl], v_nat[:, sl], do1[:, sl]
            kq, vq, qa, da = k_own[:, sl], v_own[:, sl], q_nat[:, sl], do_nat[:, sl]
            dq = dk = dv = jnp.zeros((rows, LANES), F32)
            for half in range(2):
                h = 2 * p + half
                km, vm = half_mask(k, half), half_mask(v, half)
                s = jnp.where(visible, nt(q, km) + bias[h].astype(F32), NEGATIVE)
                e = jnp.exp(s - column(h))
                ds = e * (nt(do, vm) - column(STAT + h))
                dq += nn(ds.astype(BF16), km)
                for i in range(mine):
                    diagonals[i, pl.ds(h, 1), :] = diagonal_sums(ds[i * PIECE : (i + 1) * PIECE, :])
                s = jnp.where(seen, nt(half_mask(kq, half), qa) + bias_back[h].astype(F32), NEGATIVE)
                e = jnp.exp(s - stat_t[pl.ds(h, 1), :])
                dv += nn(e.astype(BF16), half_mask(da, half))
                ds = e * (nt(half_mask(vq, half), da) - stat_t[pl.ds(STAT + h, 1), :])
                dk += nn(ds.astype(BF16), half_mask(qa, half))
            dq1[:, sl] = dq.astype(BF16)
            dk1[:, sl] = dk.astype(BF16)
            dv1[:, sl] = dv.astype(BF16)
            return c

        lax.fori_loop(low, high, pair, 0)

    def finish_tokens():
        weights_here.wait()
        da1 = nt(dq1[...], prod[5]) + nt(dk1[...], prod[6]) + nt(dv1[...], prod[7])
        dx, dgain = norm_back_rows(tok[...].astype(F32), gains[0:1, :], da1)
        grad_tokens[...] = (dh1[...] + dx).astype(BF16)
        sums = jnp.zeros((STAT, BUCKETS), F32)
        number = lax.broadcasted_iota(jnp.int32, (BUCKETS, length + LANES), 0)
        for i in range(mine):
            line = bucket_rows[pl.ds(own[i, 1], 1), pl.ds(own[i, 2] * LANES, length + LANES)]
            hot = jnp.where(line == number, 1.0, 0.0).astype(BF16)
            high, low = split(diagonals[i])
            sums += nt(high, hot) + nt(low, hot)
        tiny[0] = jnp.zeros(tiny.shape[1:], F32)
        tiny[0, 0:1, :] = dgain
        tiny[0, 1:3, :] = small_mid[0:2, :]
        tiny[0, 8 : 8 + STAT, 0:BUCKETS] = sums

    weights_here = pltpu.make_async_copy(w_self, prod.at[5:8], s_w)
    weights_here.start()
    greet(wire.partners())
    wire.spread(do1, do_all, s_do)
    wire.spread(stat1, stat_all, s_st)
    wire.slot(do_all, at.c)[...] = do1[...]
    stat_all[at.c] = stat1[...]
    diagonals[...] = jnp.zeros_like(diagonals)
    order = [12, 13, 14, 15, 0, 1, 2, 3, 4, 8, 9, 10, 11, 5, 6, 7]
    lag = 1.5
    events = []
    for tick, j in enumerate(order):
        if j < n_mats:
            events += [(tick - 2, 1, lambda j=j: stage_a(j)), (tick - 1, 2, lambda j=j: stage_b(j))]
        for k, stage in enumerate((stage_c, stage_d, stage_e, stage_f, stage_g)):
            events.append((tick + k * lag, 3 + k, lambda j=j, stage=stage: stage(j)))
    events += [(2.5, 0, send_g_in), (8.5, 0, have_g_in)]
    events += [(0.5, 0, lambda: relay(1)), (1.5, 0, lambda: relay(2)), (1.6, 0, lambda: relay(3)), (3.5, 0, prepare)]
    events += [(4.5 + i, 0, lambda i=i: attend_back(2 * i, 2 * i + 2)) for i in range(PAIRS // 2)]
    events += [(8.6, 0, finish_tokens)]
    events += [(9.5 + t, 0, lambda t=t: small_hop(t)) for t in range(4)] + [(14.5, 0, small_end)]
    for _, _, event in sorted(events, key=lambda e: (e[0], -e[1])):
        event()
    wire.drain()


def tail(peers, inv, own, do1, stat1, q_nat, k_nat, v_nat, bias, bias_back, tok, w_self, gains, dh1, bucket_rows, *rest):
    rows, length = do1.shape[0], q_nat.shape[0]
    n, depth = 8, peers // 2
    total = n + 2 * WAYS
    quarter, half = D // WAYS, D // 2
    shard = lambda k, width=D: pltpu.VMEM((k, quarter, width), BF16)
    row = lambda: pltpu.VMEM((rows, D), BF16)
    tiny = lambda k: pltpu.VMEM((k, 8 + STAT, D), F32)
    operands = (do1, stat1, q_nat, k_nat, v_nat, bias, bias_back, tok, w_self, gains, dh1, bucket_rows) + rest
    return pl.pallas_call(
        functools.partial(tail_kernel, peers),
        name="tail",
        out_shape=[sds((total, quarter, D), BF16), sds((8 + STAT, D), F32), sds((rows, D), BF16)],
        in_specs=[smem_spec()] * 2
        + [pl.BlockSpec(memory_space=pl.ANY) if x is w_self else full_spec() for x in operands],
        out_specs=[full_spec()] * 3,
        scratch_shapes=[
            pltpu.VMEM((n, D, D), BF16), pltpu.VMEM((n, 2, quarter, D), BF16), shard(n), shard(n),
            shard(n + WAYS), shard(total, half), shard(total, half), shard(total, half),
            tiny(4), tiny(3 + depth),
            pltpu.VMEM((length, D), BF16), pltpu.VMEM((length, D), BF16),
            pltpu.VMEM((peers, 2 * STAT, rows), F32), pltpu.VMEM((length, LANES), F32), pltpu.VMEM((LANES, length), F32),
            row(), row(), row(), row(), row(), row(),
            pltpu.VMEM((rows // PIECE, STAT, length + LANES), F32),
            pltpu.SemaphoreType.DMA,
        ]
        + sems(2 * depth) + sems(2 * depth)
        + sems(2 * n) + sems(n) + sems(total) + sems(total * depth) + sems(total * depth) + sems(total) + sems(WAYS) + sems(3 + depth),
        compiler_params=pltpu.CompilerParams(collective_id=0, has_side_effects=True, vmem_limit_bytes=TAIL_VMEM),
    )(inv, own, *operands)


def shards(
    tokens,
    memory,
    piece_order,
    bucket_table,
    passage_lengths,
    self_gain,
    cross_gain,
    hidden_gain,
    position_bias,
    self_query,
    self_attention_key,
    self_value,
    self_output,
    cross_query,
    cross_key,
    cross_value,
    cross_output,
    hidden_in,
    hidden_out,
    grad_output,
):
    tok, mem, grad = tokens[0], memory[0], grad_output[0]
    rows, slots = tok.shape[0], mem.shape[0]
    length = (bucket_table.shape[0] + 1) // 2
    peers = length // rows
    index = lax.axis_index("ctx")
    own = lax.dynamic_slice_in_dim(piece_order, index * (rows // PIECE), rows // PIECE)
    f = lax.axis_index("fsdp")
    quarter, eighth = self_query.shape[0], position_bias.shape[0]
    slots_all = jnp.arange(piece_order.shape[0], dtype=jnp.int32)
    inv = jnp.sum(jnp.where(piece_order[None, :] == slots_all[:, None], slots_all[None, :], 0), axis=1)
    block_start = own * PIECE // BLOCK * BLOCK
    own_facts = jnp.stack(
        [own, own % 2, (length - (own - own % 2) * PIECE) // LANES - 1, block_start + BLOCK, block_start], axis=1
    )
    pack = jnp.zeros((N_GAINS + BUCKETS, D), BF16)
    pack = lax.dynamic_update_slice(pack, jnp.stack([self_gain, cross_gain, hidden_gain]), (0, f * quarter))
    pack = lax.dynamic_update_slice(pack, position_bias, (N_GAINS + f * eighth, 0))
    buckets = jnp.pad(bucket_table, (0, 1), constant_values=-1)[None]
    buckets_back = jnp.pad(bucket_table[::-1], (0, 1), constant_values=-1)[None]
    bucket_rows = jnp.concatenate([jnp.roll(buckets, 1, 1), jnp.roll(buckets, 1 + PIECE, 1)], 0)
    w_self, w_rest, gains, ahead, behind, q1_nat, k1_nat, v1_nat, a1, o1, h1, a2, q2, lse1 = front(
        peers,
        inv,
        own_facts,
        tok,
        pack,
        buckets,
        buckets_back,
        [self_query, self_attention_key, self_value, self_output, cross_query, cross_key, cross_value],
    )
    taken = jnp.arange(PLEN, dtype=jnp.int32)[None, :] < passage_lengths[0][:, None]
    hidden = jnp.where(lax.dynamic_slice_in_dim(taken.reshape(-1), index * slots, slots), 0.0, NEGATIVE)
    (
        o2,
        branch2,
        dq2,
        dk2,
        dv2,
        branch1,
        dh1,
        do1,
        stat1,
        g_in,
        g_out,
        layer_output,
        grad_memory,
        small_mid,
    ) = middle(
        peers,
        q2,
        h1,
        o1,
        lse1,
        w_rest,
        gains,
        mem,
        hidden[None, :],
        hidden[:, None],
        grad,
        cross_output,
        hidden_in,
        hidden_out,
    )
    total, small, grad_tokens = tail(
        peers,
        inv,
        own_facts,
        do1,
        stat1,
        q1_nat,
        k1_nat,
        v1_nat,
        ahead,
        behind,
        tok,
        w_self,
        gains,
        dh1,
        bucket_rows,
        a1,
        o1,
        branch1,
        a2,
        dq2,
        mem,
        dk2,
        dv2,
        o2,
        branch2,
        g_in,
        g_out,
        small_mid,
    )
    total = total.astype(F32)
    gain = lambda i: lax.dynamic_slice_in_dim(small[i], f * quarter, quarter)
    bias_out = lax.dynamic_slice_in_dim(small[8:, :BUCKETS].T, f * eighth, eighth)[:, :HEADS]
    places = [5, 6, 7, 4, 3, 1, 2, 0]
    count = len(places)
    return (
        layer_output[None],
        grad_tokens[None],
        grad_memory[None],
        gain(0),
        gain(1),
        gain(2),
        bias_out,
        *[total[i] for i in places],
        jnp.concatenate([total[count + i] for i in range(WAYS)], 1),
        total[count + WAYS :].reshape(-1, D),
    )


def pick(*arrays):
    resident = (arrays[3].shape[0] + 1) // 2 <= RESIDENT_ROWS
    return (shards if resident else streamed_shards)(*arrays)


def solution(mesh):
    return jax.shard_map(
        pick,
        mesh=mesh,
        in_specs=(
            P("fsdp", "ctx", None),
            P("fsdp", "ctx", None),
            P(),
            P(),
            P("fsdp", None),
            P("fsdp"),
            P("fsdp"),
            P("fsdp"),
            P("fsdp", None),
            P("fsdp", None),
            P("fsdp", None),
            P("fsdp", None),
            P("fsdp", None),
            P("fsdp", None),
            P("fsdp", None),
            P("fsdp", None),
            P("fsdp", None),
            P("fsdp", None),
            P("fsdp", None),
            P("fsdp", "ctx", None),
        ),
        out_specs=(
            P("fsdp", "ctx", None),
            P("fsdp", "ctx", None),
            P("fsdp", "ctx", None),
            P("fsdp"),
            P("fsdp"),
            P("fsdp"),
            P("fsdp", None),
            P("fsdp", None),
            P("fsdp", None),
            P("fsdp", None),
            P("fsdp", None),
            P("fsdp", None),
            P("fsdp", None),
            P("fsdp", None),
            P("fsdp", None),
            P("fsdp", None),
            P("fsdp", None),
        ),
        check_vma=False,
    )
```

```python
import functools

import jax
import jax.numpy as jnp
from jax import lax
from jax.experimental import pallas as pl
from jax.experimental.pallas import tpu as pltpu
from jax.sharding import PartitionSpec as P

D = 768
HEADS = 12
PAIRS = HEADS // 2
HEAD_DIM = 64
PIECE = 64
BLOCK = 256
PLEN = 256
KBLK = 512
PSG = 20
BUCKETS = 32
RESIDENT_ROWS = 1024
LANES = 128
EPSILON = 1e-06
NEGATIVE = -1e30
F32 = jnp.float32
BF16 = jnp.bfloat16
VMEM_LIMIT = 60 * 2**20
TAIL_VMEM = 63 * 2**20

def nn(a, b):
    return lax.dot_general(a, b, (((1,), (0,)), ((), ())), preferred_element_type=F32)
def nt(a, b):
    return lax.dot_general(a, b, (((1,), (1,)), ((), ())), preferred_element_type=F32)
def tn(a, b):
    return lax.dot_general(a, b, (((0,), (0,)), ((), ())), preferred_element_type=F32)

def normed(x, gain):
    return x * lax.rsqrt(jnp.mean(x * x, axis=-1, keepdims=True) + EPSILON) * gain

def half_mask(x, half):
    lane = lax.broadcasted_iota(jnp.int32, x.shape, 1) // HEAD_DIM
    return jnp.where(lane == half, x, jnp.zeros_like(x))

def lanes_of(pair):
    return pl.ds(pl.multiple_of(pair * LANES, LANES), LANES)

def shear(x, sign):
    row = lax.broadcasted_iota(jnp.int32, x.shape, 0)
    for bit in (1, 2, 4):
        x = jnp.where(row & bit != 0, pltpu.roll(x, (sign * bit) % x.shape[1], 1), x)
    return x

def full_spec():
    return pl.BlockSpec(memory_space=pltpu.VMEM)
def any_spec():
    return pl.BlockSpec(memory_space=pl.ANY)


def smem_spec():
    return pl.BlockSpec(memory_space=pltpu.SMEM)
def sds(shape, dtype):
    return jax.ShapeDtypeStruct(shape, dtype)

def norm_scale(values, gain_vector):
    return (
        values
        * lax.rsqrt(jnp.mean(values * values, axis=-1, keepdims=True) + EPSILON)
        * gain_vector
    )


def smooth_gate(values):
    return jax.nn.gelu(values, approximate=True)


def project(operand, matrix):
    return jnp.dot(operand, matrix, preferred_element_type=jnp.float32)


def project_back(operand, matrix):
    return jnp.einsum("sra,ba->srb", operand, matrix, preferred_element_type=jnp.float32)


def weight_grad(inputs, upstream):
    return jnp.einsum("sra,srb->ab", inputs, upstream, preferred_element_type=jnp.float32)


def to_heads(matrix):
    return matrix.reshape(matrix.shape[0], matrix.shape[1], HEADS, HEAD_DIM)


def heads_first(matrix):
    return jnp.transpose(to_heads(matrix), (0, 2, 1, 3))


def from_heads(tensor):
    return jnp.transpose(tensor, (0, 2, 1, 3)).reshape(
        tensor.shape[0], tensor.shape[2], HEADS * HEAD_DIM
    )


def block_scores(queries, keys_all, values_all, extras, offset):
    key_block = lax.dynamic_slice_in_dim(keys_all, offset, KBLK, 1)
    value_block = lax.dynamic_slice_in_dim(values_all, offset, KBLK, 1)
    added_bias, visible, bucket_indicator = extras(offset)
    scores = (
        jnp.einsum("sqhd,skhd->shqk", queries, key_block, preferred_element_type=jnp.float32)
        + added_bias
    )
    block_maximum = jnp.max(jnp.where(visible, scores, NEGATIVE), axis=-1)
    weights = jnp.exp(jnp.where(visible, scores - block_maximum[..., None], NEGATIVE))
    return (key_block, value_block, bucket_indicator, block_maximum, weights)


def attend_forward(queries, keys_all, values_all, extras):
    block_count = keys_all.shape[1] // KBLK

    def single_block_tile(carried, block_index):
        key_block, value_block, bucket_indicator, block_maximum, weights = block_scores(
            queries, keys_all, values_all, extras, block_index * KBLK
        )
        numerator = jnp.einsum(
            "shqk,skhd->shqd",
            weights.astype(jnp.bfloat16),
            value_block,
            preferred_element_type=jnp.float32,
        )
        return (carried, (block_maximum, jnp.sum(weights, axis=-1), numerator))

    ignored, stacked = lax.scan(
        single_block_tile, jnp.zeros((), jnp.float32), jnp.arange(block_count, dtype=jnp.int32)
    )
    block_maximum, block_sum, numerator = stacked
    row_maximum = jnp.max(block_maximum, axis=0)
    rescale = jnp.exp(block_maximum - row_maximum)
    row_total = jnp.sum(rescale * block_sum, axis=0)
    output = jnp.sum(rescale[..., None] * numerator, axis=0) / row_total[..., None]
    return (output, row_maximum, row_total)


def attend_backward(
    queries, keys_all, values_all, extras, grad_out, output, row_maximum, row_total
):
    block_count = keys_all.shape[1] // KBLK
    grad_wide = grad_out.astype(jnp.float32)
    row_dot = jnp.sum(grad_wide * output, axis=-1)
    scaled = grad_wide / row_total[..., None]
    sum_weight = -row_dot / row_total
    initial = (
        jnp.zeros(queries.shape, jnp.float32),
        jnp.zeros(keys_all.shape, jnp.float32),
        jnp.zeros(values_all.shape, jnp.float32),
        jnp.zeros((BUCKETS, HEADS), jnp.float32),
    )

    def single_block_tile(carried, block_index):
        grad_query, grad_keys, grad_values, grad_bias = carried
        offset = block_index * KBLK
        key_block, value_block, bucket_indicator, block_maximum, weights = block_scores(
            queries, keys_all, values_all, extras, offset
        )
        rescale = jnp.exp(block_maximum - row_maximum)
        grad_numerator = (scaled * rescale[..., None]).astype(jnp.bfloat16)
        grad_weights = (
            jnp.einsum(
                "shqd,skhd->shqk", grad_numerator, value_block, preferred_element_type=jnp.float32
            )
            + (sum_weight * rescale)[..., None]
        )
        grad_scores = weights * grad_weights
        gradient_bfloat_cast = grad_scores.astype(jnp.bfloat16)
        grad_query = grad_query + jnp.einsum(
            "shqk,skhd->sqhd", gradient_bfloat_cast, key_block, preferred_element_type=jnp.float32
        )
        key_part = jnp.einsum(
            "shqk,sqhd->skhd", gradient_bfloat_cast, queries, preferred_element_type=jnp.float32
        )
        value_part = jnp.einsum(
            "shqk,shqd->skhd",
            weights.astype(jnp.bfloat16),
            grad_numerator,
            preferred_element_type=jnp.float32,
        )
        grad_keys = lax.dynamic_update_slice_in_dim(grad_keys, key_part, offset, 1)
        grad_values = lax.dynamic_update_slice_in_dim(grad_values, value_part, offset, 1)
        if bucket_indicator is not None:
            remainder_portion = (grad_scores - gradient_bfloat_cast.astype(jnp.float32)).astype(
                jnp.bfloat16
            )
            grad_bias = (
                grad_bias
                + jnp.einsum(
                    "uljf,pjf->pl",
                    gradient_bfloat_cast,
                    bucket_indicator,
                    preferred_element_type=jnp.float32,
                )
                + jnp.einsum(
                    "uljf,pjf->pl",
                    remainder_portion,
                    bucket_indicator,
                    preferred_element_type=jnp.float32,
                )
            )
        return ((grad_query, grad_keys, grad_values, grad_bias), None)

    result, ignored = lax.scan(single_block_tile, initial, jnp.arange(block_count, dtype=jnp.int32))
    return result


def streamed_shards(
    tokens,
    memory,
    piece_order,
    bucket_table,
    passage_lengths,
    self_gain,
    cross_gain,
    hidden_gain,
    position_bias,
    self_query,
    self_attention_key,
    self_value,
    self_output,
    cross_query,
    cross_key,
    cross_value,
    cross_output,
    hidden_in,
    hidden_out,
    grad_output,
):
    (
        gain_one,
        gain_two,
        gain_three,
        position_bias_lookup,
        query_full,
        key_full,
        value_full,
        output_full,
        cross_query_full,
        cross_key_full,
        cross_value_full,
        cross_output_full,
        inner_full,
        outer_full,
    ) = (
        lax.all_gather(self_gain, "fsdp", axis=0, tiled=True),
        lax.all_gather(cross_gain, "fsdp", axis=0, tiled=True),
        lax.all_gather(hidden_gain, "fsdp", axis=0, tiled=True),
        lax.all_gather(position_bias, "fsdp", axis=0, tiled=True),
        lax.all_gather(self_query, "fsdp", axis=0, tiled=True),
        lax.all_gather(self_attention_key, "fsdp", axis=0, tiled=True),
        lax.all_gather(self_value, "fsdp", axis=0, tiled=True),
        lax.all_gather(self_output, "fsdp", axis=0, tiled=True),
        lax.all_gather(cross_query, "fsdp", axis=0, tiled=True),
        lax.all_gather(cross_key, "fsdp", axis=0, tiled=True),
        lax.all_gather(cross_value, "fsdp", axis=0, tiled=True),
        lax.all_gather(cross_output, "fsdp", axis=0, tiled=True),
        lax.all_gather(hidden_in, "fsdp", axis=0, tiled=True),
        lax.all_gather(hidden_out, "fsdp", axis=0, tiled=True),
    )
    gain_one = gain_one.astype(jnp.float32)
    gain_two = gain_two.astype(jnp.float32)
    gain_three = gain_three.astype(jnp.float32)
    sequence_count = tokens.shape[0]
    local_rows = tokens.shape[1]
    sequence_length = (bucket_table.shape[0] + 1) // 2
    memory_length = PSG * PLEN
    piece_offsets = jnp.arange(PIECE, dtype=jnp.int32)
    local_pieces = lax.dynamic_slice_in_dim(
        piece_order, lax.axis_index("ctx") * (local_rows // PIECE), local_rows // PIECE
    )
    query_position = (local_pieces[:, None] * PIECE + piece_offsets[None, :]).reshape(local_rows)
    key_position = (piece_order[:, None] * PIECE + piece_offsets[None, :]).reshape(sequence_length)
    bucket_numbers = jnp.arange(BUCKETS, dtype=jnp.int32)

    def self_extras(offset):
        key_block_position = lax.dynamic_slice_in_dim(key_position, offset, KBLK)
        relative_bucket_index = jnp.take(
            bucket_table,
            key_block_position[None, :] - query_position[:, None] + sequence_length - 1,
        )
        bucket_indicator = (
            relative_bucket_index[None, :, :] == bucket_numbers[:, None, None]
        ).astype(jnp.bfloat16)
        added_bias = jnp.einsum(
            "lvj,lf->fvj",
            bucket_indicator,
            position_bias_lookup,
            preferred_element_type=jnp.float32,
        )
        visible = key_block_position[None, :] // BLOCK <= query_position[:, None] // BLOCK
        return (added_bias, visible, bucket_indicator)

    slot_numbers = jnp.arange(PLEN, dtype=jnp.int32)
    memory_valid = (passage_lengths[:, :, None] > slot_numbers[None, None, :]).reshape(
        sequence_count, memory_length
    )

    def cross_extras(offset):
        visible = lax.dynamic_slice_in_dim(memory_valid, offset, KBLK, 1)[:, None, None, :]
        return (0.0, visible, None)

    inputs_wide = tokens.astype(jnp.float32)
    normed_one = norm_scale(inputs_wide, gain_one).astype(jnp.bfloat16)
    queries_one = project(normed_one, query_full).astype(jnp.bfloat16)
    keys_local = project(normed_one, key_full).astype(jnp.bfloat16)
    values_local = project(normed_one, value_full).astype(jnp.bfloat16)
    memory_keys = project(memory, cross_key_full).astype(jnp.bfloat16)
    memory_values = project(memory, cross_value_full).astype(jnp.bfloat16)
    keys_all, values_all, memory_keys_all, memory_values_all = (
        lax.all_gather(keys_local, "ctx", axis=1, tiled=True),
        lax.all_gather(values_local, "ctx", axis=1, tiled=True),
        lax.all_gather(memory_keys, "ctx", axis=1, tiled=True),
        lax.all_gather(memory_values, "ctx", axis=1, tiled=True),
    )
    output_one, maximum_one, total_one = attend_forward(
        to_heads(queries_one), to_heads(keys_all), to_heads(values_all), self_extras
    )
    attended_one = from_heads(output_one).astype(jnp.bfloat16)
    hidden_one = inputs_wide + project(attended_one, output_full)
    normed_two = norm_scale(hidden_one, gain_two).astype(jnp.bfloat16)
    queries_two = project(normed_two, cross_query_full).astype(jnp.bfloat16)
    output_two, maximum_two, total_two = attend_forward(
        to_heads(queries_two), to_heads(memory_keys_all), to_heads(memory_values_all), cross_extras
    )
    attended_two = from_heads(output_two).astype(jnp.bfloat16)
    hidden_two = hidden_one + project(attended_two, cross_output_full)
    normed_three = norm_scale(hidden_two, gain_three).astype(jnp.bfloat16)
    before_gate = project(normed_three, inner_full)
    gated_wide, gate_pullback = jax.vjp(smooth_gate, before_gate)
    activated = gated_wide.astype(jnp.bfloat16)
    layer_output = (hidden_two + project(activated, outer_full)).astype(jnp.bfloat16)
    grad_wide = grad_output.astype(jnp.float32)
    grad_outer = weight_grad(activated, grad_output)
    grad_activated = project_back(grad_output, outer_full)
    grad_before = gate_pullback(grad_activated)[0].astype(jnp.bfloat16)
    grad_inner = weight_grad(normed_three, grad_before)
    ignored, norm_pullback = jax.vjp(norm_scale, hidden_two, gain_three)
    grad_hidden_part, grad_gain_three = norm_pullback(project_back(grad_before, inner_full))
    grad_hidden_two = grad_wide + grad_hidden_part
    branch_two = grad_hidden_two.astype(jnp.bfloat16)
    grad_cross_output = weight_grad(attended_two, branch_two)
    grad_attended_two = project_back(branch_two, cross_output_full).astype(jnp.bfloat16)
    keys_back, values_back, memory_keys_back, memory_values_back = (
        keys_all,
        values_all,
        memory_keys_all,
        memory_values_all,
    )
    grad_query_two, grad_memory_keys, grad_memory_values, unused_bias = attend_backward(
        to_heads(queries_two),
        to_heads(memory_keys_back),
        to_heads(memory_values_back),
        cross_extras,
        heads_first(grad_attended_two),
        output_two,
        maximum_two,
        total_two,
    )
    memory_key_sum, memory_value_sum = (
        lax.psum_scatter(
            grad_memory_keys.reshape(sequence_count, memory_length, D),
            "ctx",
            scatter_dimension=1,
            tiled=True,
        ),
        lax.psum_scatter(
            grad_memory_values.reshape(sequence_count, memory_length, D),
            "ctx",
            scatter_dimension=1,
            tiled=True,
        ),
    )
    memory_key_rounded = memory_key_sum.astype(jnp.bfloat16)
    memory_value_rounded = memory_value_sum.astype(jnp.bfloat16)
    query_two_rounded = grad_query_two.reshape(sequence_count, local_rows, D).astype(jnp.bfloat16)
    grad_cross_query = weight_grad(normed_two, query_two_rounded)
    grad_cross_key = weight_grad(memory, memory_key_rounded)
    grad_cross_value = weight_grad(memory, memory_value_rounded)
    grad_memory = (
        project_back(memory_key_rounded, cross_key_full)
        + project_back(memory_value_rounded, cross_value_full)
    ).astype(jnp.bfloat16)
    ignored, norm_pullback = jax.vjp(norm_scale, hidden_one, gain_two)
    grad_hidden_part, grad_gain_two = norm_pullback(
        project_back(query_two_rounded, cross_query_full)
    )
    grad_hidden_one = grad_hidden_two + grad_hidden_part
    branch_one = grad_hidden_one.astype(jnp.bfloat16)
    grad_self_output = weight_grad(attended_one, branch_one)
    grad_attended_one = project_back(branch_one, output_full).astype(jnp.bfloat16)
    grad_query_one, grad_keys_all, grad_values_all, grad_bias = attend_backward(
        to_heads(queries_one),
        to_heads(keys_back),
        to_heads(values_back),
        self_extras,
        heads_first(grad_attended_one),
        output_one,
        maximum_one,
        total_one,
    )
    key_sum, value_sum = (
        lax.psum_scatter(
            grad_keys_all.reshape(sequence_count, sequence_length, D),
            "ctx",
            scatter_dimension=1,
            tiled=True,
        ),
        lax.psum_scatter(
            grad_values_all.reshape(sequence_count, sequence_length, D),
            "ctx",
            scatter_dimension=1,
            tiled=True,
        ),
    )
    query_one_rounded = grad_query_one.reshape(sequence_count, local_rows, D).astype(jnp.bfloat16)
    first_key_bfloat_cast = key_sum.astype(jnp.bfloat16)
    value_one_rounded = value_sum.astype(jnp.bfloat16)
    grad_self_query = weight_grad(normed_one, query_one_rounded)
    grad_self_key = weight_grad(normed_one, first_key_bfloat_cast)
    grad_self_value = weight_grad(normed_one, value_one_rounded)
    grad_normed_one = (
        project_back(query_one_rounded, query_full)
        + project_back(first_key_bfloat_cast, key_full)
        + project_back(value_one_rounded, value_full)
    )
    ignored, norm_pullback = jax.vjp(norm_scale, inputs_wide, gain_one)
    grad_input_part, grad_gain_one = norm_pullback(grad_normed_one)
    grad_tokens = (grad_hidden_one + grad_input_part).astype(jnp.bfloat16)
    (
        shard_gain_one,
        shard_gain_two,
        shard_gain_three,
        shard_bias,
        shard_query,
        shard_key,
        shard_value,
        shard_output,
        shard_cross_query,
        shard_cross_key,
        shard_cross_value,
        shard_cross_output,
        shard_inner,
        shard_outer,
    ) = (
        lax.psum_scatter(
            grad_gain_one.astype(jnp.bfloat16), "fsdp", scatter_dimension=0, tiled=True
        ).astype(jnp.float32),
        lax.psum_scatter(
            grad_gain_two.astype(jnp.bfloat16), "fsdp", scatter_dimension=0, tiled=True
        ).astype(jnp.float32),
        lax.psum_scatter(
            grad_gain_three.astype(jnp.bfloat16), "fsdp", scatter_dimension=0, tiled=True
        ).astype(jnp.float32),
        lax.psum_scatter(
            grad_bias.astype(jnp.bfloat16), "fsdp", scatter_dimension=0, tiled=True
        ).astype(jnp.float32),
        lax.psum_scatter(
            grad_self_query.astype(jnp.bfloat16), "fsdp", scatter_dimension=0, tiled=True
        ).astype(jnp.float32),
        lax.psum_scatter(
            grad_self_key.astype(jnp.bfloat16), "fsdp", scatter_dimension=0, tiled=True
        ).astype(jnp.float32),
        lax.psum_scatter(
            grad_self_value.astype(jnp.bfloat16), "fsdp", scatter_dimension=0, tiled=True
        ).astype(jnp.float32),
        lax.psum_scatter(
            grad_self_output.astype(jnp.bfloat16), "fsdp", scatter_dimension=0, tiled=True
        ).astype(jnp.float32),
        lax.psum_scatter(
            grad_cross_query.astype(jnp.bfloat16), "fsdp", scatter_dimension=0, tiled=True
        ).astype(jnp.float32),
        lax.psum_scatter(
            grad_cross_key.astype(jnp.bfloat16), "fsdp", scatter_dimension=0, tiled=True
        ).astype(jnp.float32),
        lax.psum_scatter(
            grad_cross_value.astype(jnp.bfloat16), "fsdp", scatter_dimension=0, tiled=True
        ).astype(jnp.float32),
        lax.psum_scatter(
            grad_cross_output.astype(jnp.bfloat16), "fsdp", scatter_dimension=0, tiled=True
        ).astype(jnp.float32),
        lax.psum_scatter(
            grad_inner.astype(jnp.bfloat16), "fsdp", scatter_dimension=0, tiled=True
        ).astype(jnp.float32),
        lax.psum_scatter(
            grad_outer.astype(jnp.bfloat16), "fsdp", scatter_dimension=0, tiled=True
        ).astype(jnp.float32),
    )
    (
        total_gain_one,
        total_gain_two,
        total_gain_three,
        total_bias,
        total_query,
        total_key,
        total_value,
        total_output,
        total_cross_query,
        total_cross_key,
        total_cross_value,
        total_cross_output,
        total_inner,
        total_outer,
    ) = lax.psum(
        (
            shard_gain_one,
            shard_gain_two,
            shard_gain_three,
            shard_bias,
            shard_query,
            shard_key,
            shard_value,
            shard_output,
            shard_cross_query,
            shard_cross_key,
            shard_cross_value,
            shard_cross_output,
            shard_inner,
            shard_outer,
        ),
        "ctx",
    )
    return (
        layer_output,
        grad_tokens,
        grad_memory,
        total_gain_one,
        total_gain_two,
        total_gain_three,
        total_bias,
        total_query,
        total_key,
        total_value,
        total_output,
        total_cross_query,
        total_cross_key,
        total_cross_value,
        total_cross_output,
        total_inner,
        total_outer,
    )


MESH = pl.DeviceIdType.MESH
WAYS = 4


class Place:
    def __init__(self, peers):
        self.depth = peers // 2
        c, f = lax.axis_index("ctx"), lax.axis_index("fsdp")
        self.c, self.f = c, f
        self.a, self.b, self.x, self.k = c // 2, c % 2, f // 2, f % 2
        self.core = (c, self.x * 2 + 1 - self.k)
        self.across = (c, (1 - self.x) * 2 + self.k)
        self.beside = (self.a * 2 + 1 - self.b, f)

    def ahead(self, d):
        return lax.rem(self.a + d, self.depth)

    def behind(self, d):
        return lax.rem(self.a + self.depth - d, self.depth)

    def column(self, a):
        return (a * 2 + self.b, self.f)

    def group(self, d):
        return (self.c, lax.rem(self.f + d, WAYS))


def greet(targets):
    barrier = pltpu.get_barrier_semaphore()
    for target in targets:
        pl.semaphore_signal(barrier, inc=1, device_id=target, device_id_type=MESH)
    pl.semaphore_wait(barrier, len(targets))


def remote(src, dst, sems, index, target):
    return pltpu.make_async_remote_copy(
        src_ref=src,
        dst_ref=dst,
        send_sem=sems[0].at[index],
        recv_sem=sems[1].at[index],
        device_id=target,
        device_id_type=MESH,
    )


def apart(src, dst, sems, send_index, recv_index, target):
    return pltpu.make_async_remote_copy(
        src_ref=src,
        dst_ref=dst,
        send_sem=sems[0].at[send_index],
        recv_sem=sems[1].at[recv_index],
        device_id=target,
        device_id_type=MESH,
    )


def line_sems(depth, chunks):
    return sems((2 * depth + 2) * chunks)


def sems(count):
    return [pltpu.SemaphoreType.DMA((count,)), pltpu.SemaphoreType.DMA((count,))]


class Wire:
    def __init__(self, peers):
        self.at = Place(peers)
        self.depth = self.at.depth
        self.sent = []

    def go(self, copy):
        copy.start()
        self.sent.append((None, copy.wait_send))

    def go_if(self, condition, make):
        pl.when(condition)(lambda: make().start())
        self.sent.append((condition, lambda: make().wait_send()))

    def drain(self):
        for condition, wait in self.sent:
            if condition is None:
                wait()
            else:
                pl.when(condition)(wait)

    def partners(self):
        at = self.at
        return (
            [at.group(d) for d in range(1, WAYS)]
            + [at.beside]
            + [at.column(at.ahead(d)) for d in range(1, self.depth)]
        )

    def near(self, step):
        a, last = self.at.a, self.depth - 1
        low = jnp.where(step - 1 < a, step - 1, step)
        mirrored = jnp.where(step - 1 < last - a, step - 1, step)
        return jnp.where(2 * a < last, low, last - mirrored)

    def piece(self, buf, c, chunk, chunks):
        if len(buf.shape) == 3:
            size = buf.shape[1] // chunks
            return buf.at[c, chunk * size : (chunk + 1) * size]
        rows = buf.shape[0] // (2 * self.depth)
        size = rows // chunks
        return buf.at[pl.ds(pl.multiple_of(c * rows + chunk * size, size), size)]

    def slot(self, buf, c):
        return self.piece(buf, c, 0, 1)

    def pass_on(self, src, dst, sem, up, beside, own, chunk, chunks, origin):
        at, a = self.at, self.at.a
        line = origin * chunks + chunk
        side = (self.depth + origin) * chunks + chunk
        for step in (1, -1):
            if own or (step == 1) == up:
                first = (2 * self.depth + (step == 1)) * chunks + chunk if own else line
                self.go_if(
                    a + 1 < self.depth if step == 1 else a > 0,
                    lambda step=step, first=first: apart(src, dst, sem, first, line, at.column(a + step)),
                )
        if beside:
            self.go(apart(src, dst, sem, side, side, at.beside))

    def spread(self, src, buf, sem, chunks):
        at = self.at
        size = src.shape[0] // chunks
        for chunk in range(chunks):
            part = src.at[chunk * size : (chunk + 1) * size]
            self.pass_on(part, self.piece(buf, at.c, chunk, chunks), sem, True, True, True, chunk, chunks, at.a)

    def relay(self, gathered, step):
        at, depth = self.at, self.depth
        for buf, sem, chunks in gathered:
            for chunk in range(chunks):
                for up in (True, False):
                    origin = at.a - step if up else at.a + step
                    inside = origin >= 0 if up else origin < depth
                    onward = at.a + 1 < depth if up else at.a > 0
                    line = origin * chunks + chunk
                    side = (depth + origin) * chunks + chunk
                    spot = lambda: self.piece(buf, origin * 2 + at.b, chunk, chunks)
                    target = at.column(at.a + 1 if up else at.a - 1)

                    def forward(_):
                        return apart(spot(), spot(), sem, line, line, target)

                    def sideways(_):
                        return apart(spot(), spot(), sem, side, side, at.beside)

                    @pl.when(inside)
                    def _():
                        apart(spot(), spot(), sem, line, line, at.beside).wait_recv()
                        sideways(0).start()
                        pl.when(onward)(lambda: forward(0).start())

                    self.sent.append((inside, self.later(buf, sem, side, origin, chunk, chunks, at.beside)))
                    self.sent.append(
                        (jnp.logical_and(inside, onward), self.later(buf, sem, line, origin, chunk, chunks, target))
                    )

    def later(self, buf, sem, index, origin, chunk, chunks, target):
        def wait():
            spot = self.piece(buf, origin * 2 + self.at.b, chunk, chunks)
            apart(spot, spot, sem, index, index, target).wait_send()

        return wait

    def from_beside(self, gathered, a):
        for buf, sem, chunks in gathered:
            for chunk in range(chunks):
                spot = self.piece(buf, a * 2 + 1 - self.at.b, chunk, chunks)
                index = (self.depth + a) * chunks + chunk
                apart(spot, spot, sem, index, index, self.at.beside).wait_recv()

    def shard(self, full, f):
        quarter = full.shape[0] // WAYS
        return full.at[pl.ds(pl.multiple_of(f * quarter, quarter), quarter)]

    def weight_start(self, src, full, sem, i):
        at = self.at
        slot = self.shard(full, at.f)
        slot[...] = src[...]
        self.go(remote(src, slot, sem, 3 * i, at.across))
        self.go(remote(src, slot, sem, 3 * i + 1, at.core))

    def weight_relay(self, full, sem, i):
        at = self.at
        slot = self.shard(full, (1 - at.x) * 2 + at.k)
        remote(slot, slot, sem, 3 * i, at.across).wait_recv()
        self.go(remote(slot, slot, sem, 3 * i + 2, at.core))

    def weight_ready(self, full, sem, i):
        at = self.at
        slot = self.shard(full, at.x * 2 + 1 - at.k)
        remote(slot, slot, sem, 3 * i + 1, at.core).wait_recv()
        slot = self.shard(full, (1 - at.x) * 2 + 1 - at.k)
        remote(slot, slot, sem, 3 * i + 2, at.core).wait_recv()


def two_heads(x):
    return jnp.concatenate([half_mask(x, 0), half_mask(x, 1)], 0)


def ones_beside(x):
    ones = jnp.ones_like(x)
    return jnp.concatenate([two_heads(x), two_heads(ones)], 1)


def softmax_pair(scores, v, stats, p):
    weights, tops = [], []
    for s in scores:
        m = jnp.max(s, axis=1, keepdims=True)
        weights.append(jnp.exp(s - m).astype(BF16))
        tops.append(m)
    both = nn(jnp.concatenate(weights, 1), ones_beside(v))
    sums = both[:, LANES:]
    logs = jnp.log(sums)
    turned = pltpu.roll(logs, HEAD_DIM, 1)
    lane = lax.broadcasted_iota(jnp.int32, logs.shape, 1)
    inside = lane < HEAD_DIM
    stats = jnp.where(lane == 2 * p, tops[0] + jnp.where(inside, logs, turned), stats)
    stats = jnp.where(lane == 2 * p + 1, tops[1] + jnp.where(inside, turned, logs), stats)
    return both[:, :LANES] / sums, stats


def fill_inverse(order, inv):
    count = order.shape[0]
    for p in range(count):
        slot = jnp.int32(0)
        for s in range(count):
            slot = jnp.where(order[s] == p, s, slot)
        inv[p] = slot


def own_facts(order, c, count, length):
    per = (BLOCK // PIECE).bit_length() - 1
    facts = []
    for i in range(count):
        n = order[c * count + i]
        start = lax.shift_right_logical(n, per) * BLOCK
        facts.append((n, n & 1, length // LANES - 1 - lax.shift_right_logical(n, 1), start + BLOCK, start))
    return facts


def own_column(facts, i):
    return jnp.concatenate([jnp.full((PIECE, 1), fact[i], jnp.int32) for fact in facts], 0)


def own_bias(table, lines, own, out):
    full = table.shape[1]
    rows, length = out.shape[1], out.shape[2]

    def head(h, c):
        base = shear(pltpu.roll(jnp.broadcast_to(table[pl.ds(h, 1), :], (8, full)), 1, 1), 1)
        lines[0] = base
        lines[1] = pltpu.roll(base, PIECE, 1)
        for i in range(rows // PIECE):
            window = lines[own[i][1], :, pl.ds(own[i][2] * LANES, length + LANES)]
            for g in range(0, PIECE // 8, 2):
                both = [pltpu.roll(window, 8 * k, 1) if k else window for k in (g, g + 1)]
                both = jnp.concatenate(both, 0)[:, LANES:]
                out[h, i * PIECE + 8 * g : i * PIECE + 8 * g + 16, :] = both.astype(BF16)
        return c

    lax.fori_loop(0, HEADS, head, 0)


def diagonal_sums(block):
    rows, length = block.shape
    wide = jnp.concatenate([block, jnp.zeros((rows, LANES), F32)], axis=1)
    total = pltpu.roll(wide[0:8], LANES, 1)
    for g in range(1, rows // 8):
        total += pltpu.roll(wide[8 * g : 8 * g + 8], LANES - 8 * g, 1)
    return jnp.sum(shear(total, -1), axis=0, keepdims=True)


N_FRONT = 5
CHUNKS = 2
N_GAINS = 16


def front_kernel(peers, *refs):
    order, tok, gain1, gain2, gain3, bias_shard, buckets = refs[:7]
    shards_in = refs[7 : 7 + N_FRONT]
    (w_self_out, w_rest_out, gains, ahead_out, behind_out, q_out, k_out, v_out, a1, o1, h1, a2, q2, lse) = refs[7 + N_FRONT : 21 + N_FRONT]
    (tok_all, pack, pack_all, table, lines, q_own, w_self, w_rest, ahead, behind, q_nat, k_nat, v_nat, s_keep, inv, *sem) = refs[21 + N_FRONT :]
    weights = [w_self.at[i] for i in range(3)] + [w_rest.at[i] for i in range(N_FRONT - 3)]
    sem_t, sem_w, sem_p = sem[0:2], sem[2:4], sem[4:6]
    wire = Wire(peers)
    at, depth = wire.at, wire.depth
    rows = tok.shape[0]
    length = peers * rows
    mine, per = rows // PIECE, BLOCK // PIECE
    kept = []

    def keep(i, src, dst):
        copy = pltpu.make_async_copy(src, dst, s_keep.at[i])
        copy.start()
        kept.append(copy)

    quarter = gain1.shape[1]
    spot = lax.broadcasted_iota(jnp.int32, (quarter, D), 0) + at.f * quarter
    place = jnp.where(lax.broadcasted_iota(jnp.int32, (quarter, D), 1) == spot, 1.0, 0.0).astype(BF16)
    pack[...] = jnp.zeros_like(pack)
    for i, gain in enumerate((gain1, gain2, gain3)):
        pack[i : i + 1, :] = nn(gain[...], place)
    eighth, heads = bias_shard.shape
    spot = lax.broadcasted_iota(jnp.int32, (BUCKETS, eighth), 1) + at.f * eighth
    place = jnp.where(lax.broadcasted_iota(jnp.int32, (BUCKETS, eighth), 0) == spot, 1.0, 0.0).astype(BF16)
    pack[N_GAINS:, 0:heads] = nn(place, bias_shard[...])
    greet(wire.partners())
    for d in range(1, WAYS):
        wire.go(remote(pack, pack_all.at[at.f], sem_p, d, at.group(d)))
    wire.spread(tok, tok_all, sem_t, CHUNKS)
    for i in range(3):
        wire.weight_start(shards_in[i], weights[i], sem_w, i)
    wire.slot(tok_all, at.c)[...] = tok[...]
    pack_all[at.f] = pack[...]
    for d in range(1, WAYS):
        slot = pack_all.at[lax.rem(at.f + WAYS - d, WAYS)]
        remote(slot, slot, sem_p, d, at.group(WAYS - d)).wait_recv()
    everything = pack_all[0] + pack_all[1] + pack_all[2] + pack_all[3]
    fill_inverse(order, inv)
    own = own_facts(order, at.c, mine, length)
    gains[...] = everything[0:8, :]
    bias = everything[N_GAINS:, 0:LANES].astype(BF16)
    bucket = lax.broadcasted_iota(jnp.int32, (bias.shape[0], 2 * length), 0)
    hot = jnp.where(buckets[...] == bucket, 1.0, 0.0).astype(BF16)
    table[0] = tn(bias, hot)[0:16, :]
    shifted = pltpu.roll(table[0], 1, 1).astype(BF16)
    row = lax.broadcasted_iota(jnp.int32, (LANES, LANES), 0)
    mirror = jnp.where(row + lax.broadcasted_iota(jnp.int32, (LANES, LANES), 1) == LANES - 1, 1.0, 0.0).astype(BF16)
    tiles = 2 * length // LANES
    for t in range(tiles):
        u = tiles - 1 - t
        table[1, :, t * LANES : (t + 1) * LANES] = nn(shifted[:, u * LANES : (u + 1) * LANES], mirror)

    gathered = [(tok_all, sem_t, CHUNKS)]
    for step in range(1, depth):
        wire.relay(gathered, step)
    own_bias(table.at[0], lines, own, ahead)
    keep(3, ahead, ahead_out)
    for i in range(3):
        wire.weight_relay(weights[i], sem_w, i)
    for i in range(3, N_FRONT):
        wire.weight_start(shards_in[i], weights[i], sem_w, i)
    first = gains[0:1, :]
    a1[...] = normed(tok[...].astype(F32), first).astype(BF16)
    for i in range(3):
        wire.weight_ready(weights[i], sem_w, i)
    keep(0, w_self, w_self_out)
    for a in range(depth):
        wire.from_beside(gathered, a)

    def tile(t, c):
        parts = []
        for i in range(per):
            parts.append(tok_all[pl.ds(inv[t * per + i] * PIECE, PIECE), :])
        a = normed(jnp.concatenate(parts, 0).astype(F32), first).astype(BF16)
        dst = pl.ds(pl.multiple_of(t * BLOCK, BLOCK), BLOCK)
        for j, out in enumerate((q_nat, k_nat, v_nat)):
            out[dst, :] = nn(a, weights[j][...]).astype(BF16)
        return c

    lax.fori_loop(0, length // BLOCK, tile, 0)
    for i in range(mine):
        q_own[i * PIECE : (i + 1) * PIECE, :] = q_nat[pl.ds(own[i][0] * PIECE, PIECE), :]
    for i, (src, dst) in enumerate(((q_nat, q_out), (k_nat, k_out), (v_nat, v_out))):
        keep(5 + i, src, dst)
    wire.weight_relay(weights[3], sem_w, 3)
    lane = lax.broadcasted_iota(jnp.int32, (rows, length), 1)
    visible = lane < own_column(own, 3)

    def pair(p, stats):
        sl = lanes_of(p)
        s = nt(q_own[:, sl], two_heads(k_nat[:, sl]))
        scores = []
        for half in range(2):
            biased = s[:, half * length : (half + 1) * length] + ahead[2 * p + half].astype(F32)
            scores.append(jnp.where(visible, biased, NEGATIVE))
        value, stats = softmax_pair(scores, v_nat[:, sl], stats, p)
        o1[:, sl] = value.astype(BF16)
        return stats

    stats = lax.fori_loop(0, PAIRS // 2, pair, jnp.zeros((rows, LANES), F32), unroll=True)
    wire.weight_relay(weights[4], sem_w, 4)
    lse[...] = lax.fori_loop(PAIRS // 2, PAIRS, pair, stats, unroll=True)
    wire.weight_ready(weights[3], sem_w, 3)
    h = tok[...].astype(F32) + nn(o1[...], weights[3][...])
    h1[...] = h
    a = normed(h, gains[1:2, :]).astype(BF16)
    a2[...] = a
    wire.weight_ready(weights[4], sem_w, 4)
    q2[...] = nn(a, weights[4][...]).astype(BF16)
    keep(1, w_rest, w_rest_out)
    own_bias(table.at[1], lines, own, behind)
    keep(4, behind, behind_out)
    for copy in kept:
        copy.wait()
    wire.drain()


def front(peers, order, tok, gain_shards, bias_shard, buckets, weight_shards):
    rows = tok.shape[0]
    length, depth = peers * rows, peers // 2
    block = lambda dtype: sds((rows, D), dtype)
    return pl.pallas_call(
        functools.partial(front_kernel, peers),
        name="front",
        out_shape=[sds((3, D, D), BF16), sds((N_FRONT - 3, D, D), BF16), sds((8, D), F32)]
        + [sds((HEADS, rows, length), BF16)] * 2
        + [sds((length, D), BF16)] * 3
        + [block(BF16), block(BF16), block(F32), block(BF16), block(BF16), sds((rows, LANES), F32)],
        in_specs=[smem_spec()] + [full_spec()] * (6 + N_FRONT),
        out_specs=[any_spec() if i in (0, 1, 3, 4, 5, 6, 7) else full_spec() for i in range(14)],
        scratch_shapes=[
            pltpu.VMEM((length, D), BF16),
            pltpu.VMEM((N_GAINS + BUCKETS, D), F32),
            pltpu.VMEM((WAYS, N_GAINS + BUCKETS, D), F32),
            pltpu.VMEM((2, 16, 2 * length), F32),
            pltpu.VMEM((2, 8, 2 * length), F32),
            pltpu.VMEM((rows, D), BF16),
            pltpu.VMEM((3, D, D), BF16),
            pltpu.VMEM((N_FRONT - 3, D, D), BF16),
        ]
        + [pltpu.VMEM((HEADS, rows, length), BF16)] * 2
        + [pltpu.VMEM((length, D), BF16)] * 3
        + [pltpu.SemaphoreType.DMA((8,)), pltpu.SMEM(order.shape, jnp.int32)]
        + line_sems(depth, CHUNKS) + sems(3 * N_FRONT) + sems(WAYS),
        compiler_params=pltpu.CompilerParams(collective_id=1, has_side_effects=True, vmem_limit_bytes=VMEM_LIMIT),
    )(order, tok, *gain_shards, bias_shard, buckets, *weight_shards)


STAT = 16


def split(x):
    high = x.astype(BF16)
    return high, (x - high.astype(F32)).astype(BF16)


def head_matrix(rows):
    row = lax.broadcasted_iota(jnp.int32, (rows, D), 0)
    lane = lax.broadcasted_iota(jnp.int32, (rows, D), 1)
    return jnp.where(lane // HEAD_DIM == row, 1.0, 0.0).astype(BF16)


def per_head_sums(x, heads):
    high, low = split(x)
    return nt(heads, high) + nt(heads, low)


def blend(parts, stats, heads):
    top = functools.reduce(jnp.maximum, stats)
    shares = [jnp.exp(s - top) for s in stats]
    total = functools.reduce(jnp.add, shares)
    value = 0.0
    for part, share in zip(parts, shares):
        high, low = split(share / total)
        value = value + (tn(high, heads) + tn(low, heads)) * part.astype(F32)
    return value, top + jnp.log(total)


def norm_back_rows(x, gain, dy):
    r = lax.rsqrt(jnp.mean(x * x, axis=-1, keepdims=True) + EPSILON)
    gdy = gain * dy
    dx = r * gdy - x * (r * r * r) * jnp.mean(x * gdy, axis=-1, keepdims=True)
    return dx, jnp.sum(dy * x * r, axis=0, keepdims=True)


def round_trip(wire, gathered, fillers, compute, ship, fold):
    at = wire.at
    b = at.b
    first, second, third = [wire.near(step) for step in (1, 2, 3)]
    for step in range(1, wire.depth):
        fillers[step - 1]()
        wire.relay(gathered, step)
    for filler in fillers[wire.depth - 1 :]:
        filler()
    wire.from_beside(gathered, at.a)
    compute(at.c, at.a * 2 + 1 - b)
    ship(at.a)
    wire.from_beside(gathered, third)
    compute(third * 2 + 1 - b, third * 2 + b)
    ship(third)
    wire.from_beside(gathered, second)
    compute(second * 2 + 1 - b, second * 2 + b)
    ship(second)
    fold(third)
    wire.from_beside(gathered, first)
    compute(first * 2 + 1 - b, first * 2 + b)
    ship(first)
    fold(second)
    fold(first)


def middle_kernel(peers, *refs):
    (lengths, q2, h1, o1, lse1, w_rest, gains, mem, grad, ck_shard, cv_shard, co_shard, in_shard, w_out) = refs[:14]
    (o2_out, branch2_out, dq2_out, dk2_out, dv2_out, branch1_out, dh1_out, do1_out, stat1_out, g_in, g_out, layer_out, gmem_out, small) = refs[14:28]
    (q_all, k2, v2, part, part_lse, from_b, from_b_lse, joined, joined_lse, from_z, from_z_lse,
     w_ck, w_cv, w_co, w_in, g_all, a3_all, dact, act, dpre, da3_send, da3_in, out_send, out_in,
     do_all, stat_all, stat_own, dk_acc, dv_acc, dqp, dq_b, dq_j, dq_z, mask, *sem) = refs[28:]
    sem = [sem[2 * i : 2 * i + 2] for i in range(len(sem) // 2)]
    (s_q, s_w, s_in, s_g, s_y, s_yl, s_z, s_zl, s_a3, s_da3, s_out, s_do, s_st, s_dy, s_dz) = sem
    wire = Wire(peers)
    at, depth = wire.at, wire.depth
    rows = q2.shape[0]
    heads = head_matrix(STAT)
    quarter = co_shard.shape[0]
    units = w_out.shape[0]
    block = lambda f: pl.ds(pl.multiple_of(f * rows, rows), rows)
    greet(wire.partners())
    wire.spread(q2, q_all, s_q, CHUNKS)
    wire.weight_start(ck_shard, w_ck, s_w, 1)
    wire.weight_start(cv_shard, w_cv, s_w, 2)
    q_all[at.c] = q2[...]
    g_all[block(at.f), :] = grad[...]
    wire.shard(w_in, at.f)[...] = in_shard[:, pl.ds(pl.multiple_of(at.f * units, LANES), units)]

    slots, passages = mem.shape[0], lengths.shape[1]
    log = PLEN.bit_length() - 1

    def hidden(shape, axis):
        slot = lax.broadcasted_iota(jnp.int32, shape, axis) + at.c * slots
        first = at.c * slots // PLEN
        taken = jnp.zeros(shape, jnp.int32)
        for i in range(slots // PLEN + 2):
            size = lengths[0, jnp.minimum(first + i, passages - 1)]
            taken = jnp.where(lax.shift_right_logical(slot, log) == first + i, size, taken)
        return jnp.where((slot & (PLEN - 1)) < taken, 0.0, NEGATIVE)

    def fill_mask():
        mask[...] = hidden(mask.shape, 0)

    def next_weights():
        wire.weight_relay(w_ck, s_w, 1)
        wire.weight_start(co_shard, w_co, s_w, 0)

    def project_memory():
        wire.weight_relay(w_cv, s_w, 2)
        feed_forward_operands()
        wire.weight_ready(w_ck, s_w, 1)
        k2[...] = nn(mem[...], w_ck[...]).astype(BF16)
        wire.weight_ready(w_cv, s_w, 2)
        v2[...] = nn(mem[...], w_cv[...]).astype(BF16)

    def feed_forward_operands():
        for d in range(1, WAYS):
            f = lax.rem(at.f + d, WAYS)
            part = in_shard.at[:, pl.ds(pl.multiple_of(f * units, LANES), units)]
            wire.go(remote(grad, g_all.at[block(at.f)], s_g, d, at.group(d)))
            wire.go(remote(part, wire.shard(w_in, at.f), s_in, d, at.group(d)))

    mask_row = hidden((1, slots), 1)

    def attend(c1, c2):
        def pair(p, stats):
            sl = lanes_of(p)
            q = jnp.concatenate([q_all[c1, :, sl], q_all[c2, :, sl]], 0)
            s = nt(q, two_heads(k2[:, sl]))
            value, stats = softmax_pair([s[:, :slots] + mask_row, s[:, slots:] + mask_row], v2[:, sl], stats, p)
            part[c1, :, sl] = value[:rows].astype(BF16)
            part[c2, :, sl] = value[rows:].astype(BF16)
            return stats

        stats = lax.fori_loop(0, PAIRS, pair, jnp.zeros((2 * rows, LANES), F32), unroll=True)
        part_lse[c1] = stats[:rows].T[:STAT]
        part_lse[c2] = stats[rows:].T[:STAT]

    def ship_part(a):
        other = a * 2 + 1 - at.b
        wire.go(remote(part.at[other], from_b.at[a], s_y, a, at.beside))
        wire.go(remote(part_lse.at[other], from_b_lse.at[a], s_yl, a, at.beside))

    def blend_column(a):
        remote(from_b.at[a], from_b.at[a], s_y, a, at.beside).wait_recv()
        remote(from_b_lse.at[a], from_b_lse.at[a], s_yl, a, at.beside).wait_recv()
        c = a * 2 + at.b
        return blend([part[c], from_b[a]], [part_lse[c], from_b_lse[a]], heads)

    def fold_part(a):
        value, stat = blend_column(a)
        joined[a] = value.astype(BF16)
        joined_lse[a] = stat
        wire.go(remote(joined.at[a], from_z.at[at.a], s_z, at.a, at.column(a)))
        wire.go(remote(joined_lse.at[a], from_z_lse.at[at.a], s_zl, at.a, at.column(a)))

    round_trip(wire, [(q_all, s_q, CHUNKS)], [fill_mask, lambda: None, next_weights, project_memory], attend, ship_part, fold_part)
    wire.weight_relay(w_co, s_w, 0)
    value, stat = blend_column(at.a)
    parts, stats = [value], [stat]
    for step in range(1, depth):
        a = wire.near(step)
        remote(from_z.at[a], from_z.at[a], s_z, a, at.column(a)).wait_recv()
        remote(from_z_lse.at[a], from_z_lse.at[a], s_zl, a, at.column(a)).wait_recv()
        parts.append(from_z[a])
        stats.append(from_z_lse[a])
    out2, lse2 = blend(parts, stats, heads)
    o2 = out2.astype(BF16)
    o2_out[...] = o2
    wire.weight_ready(w_co, s_w, 0)
    h2 = h1[...] + nn(o2, w_co[...])
    a3 = normed(h2, gains[2:3, :]).astype(BF16)
    a3_all[block(at.f), :] = a3
    for d in range(1, WAYS):
        spot = a3_all.at[block(at.f)]
        wire.go(remote(spot, spot, s_a3, d, at.group(d)))

    def arrive(buf, sem, size):
        for d in range(1, WAYS):
            f = lax.rem(at.f + WAYS - d, WAYS)
            spot = buf.at[pl.ds(pl.multiple_of(f * size, size), size)]
            remote(spot, spot, sem, d, at.group(WAYS - d)).wait_recv()

    arrive(g_all, s_g, rows)
    tiles = [slice(2 * rows * t, 2 * rows * (t + 1)) for t in range(WAYS // 2)]
    for rs in tiles:
        dact[rs, :] = nt(g_all[rs, :], w_out[...])
    arrive(w_in, s_in, quarter)
    arrive(a3_all, s_a3, rows)
    for rs in tiles:
        pre = nn(a3_all[rs, :], w_in[...])
        square = pre * pre
        t = jnp.tanh(0.7978845608028654 * (pre + 0.044715 * pre * square))
        act[rs, :] = (0.5 * pre * (1.0 + t)).astype(BF16)
        slope = 0.5 * (1.0 + t) + 0.5 * pre * (1.0 - t * t) * (0.7978845608028654 * (1.0 + 3 * 0.044715 * square))
        d = (dact[rs, :] * slope).astype(BF16)
        dpre[rs, :] = d
        da3_send[rs, :] = nt(d, w_in[...]).astype(BF16)

    def exchange(src, dst, sem):
        for d in range(1, WAYS):
            f = lax.rem(at.f + d, WAYS)
            wire.go(remote(src.at[block(f)], dst.at[block(at.f)], sem, d, at.group(d)))

    def collect(src, dst, sem):
        arrive(dst, sem, rows)
        value = src[block(at.f), :].astype(F32)
        for d in range(1, WAYS):
            value += dst[block(lax.rem(at.f + WAYS - d, WAYS)), :].astype(F32)
        return value

    exchange(da3_send, da3_in, s_da3)
    for rs in tiles:
        out_send[rs, :] = nn(act[rs, :], w_out[...]).astype(BF16)
    exchange(out_send, out_in, s_out)
    da3 = collect(da3_send, da3_in, s_da3)
    dx, dgain = norm_back_rows(h2, gains[2:3, :], da3)
    small[...] = jnp.zeros_like(small)
    small[1:2, :] = dgain
    dh2 = grad[...].astype(F32) + dx
    branch2 = dh2.astype(BF16)
    branch2_out[...] = branch2
    do2 = nt(branch2, w_co[...]).astype(BF16)
    do_all[at.c] = do2
    stat_own[0] = jnp.concatenate([lse2, per_head_sums(do2.astype(F32) * out2, heads)], 0)
    stat_all[at.c] = stat_own[0]
    wire.spread(do_all.at[at.c], do_all, s_do, CHUNKS)
    wire.spread(stat_own.at[0], stat_all, s_st, 1)

    def finish_output():
        layer_out[...] = (h2 + collect(out_send, out_in, s_out)).astype(BF16)
        dk_acc[...] = jnp.zeros_like(dk_acc)
        dv_acc[...] = jnp.zeros_like(dv_acc)

    def out_grads():
        g_out[...] = tn(act[...], g_all[...]).astype(BF16)

    def in_grads():
        g_in[...] = tn(a3_all[...], dpre[...]).astype(BF16)

    def attend_back(c1, c2):
        def pair(p, carry):
            sl = lanes_of(p)
            q = jnp.concatenate([q_all[c1, :, sl], q_all[c2, :, sl]], 0)
            do = jnp.concatenate([do_all[c1, :, sl], do_all[c2, :, sl]], 0)
            kk = two_heads(k2[:, sl])
            s = nt(kk, q)
            d = nt(two_heads(v2[:, sl]), do)
            line = lambda i: jnp.concatenate([stat_all[c1, pl.ds(i, 1), :], stat_all[c2, pl.ds(i, 1), :]], 1)
            weights, slopes = [], []
            for half in range(2):
                h, hs = 2 * p + half, slice(half * slots, (half + 1) * slots)
                e = jnp.exp(s[hs] + mask[...] - line(h))
                weights.append(e.astype(BF16))
                slopes.append((e * (d[hs] - line(STAT + h))).astype(BF16))
            dv_acc[:, sl] += nn(jnp.concatenate(weights, 1), two_heads(do))
            dk_acc[:, sl] += nn(jnp.concatenate(slopes, 1), two_heads(q))
            dq = tn(kk, jnp.concatenate(slopes, 0)).T
            dqp[c1, :, sl] = dq[:rows].astype(BF16)
            dqp[c2, :, sl] = dq[rows:].astype(BF16)
            return carry

        lax.fori_loop(0, PAIRS, pair, 0, unroll=True)

    def ship_dq(a):
        wire.go(remote(dqp.at[a * 2 + 1 - at.b], dq_b.at[a], s_dy, a, at.beside))

    def column_dq(a):
        remote(dq_b.at[a], dq_b.at[a], s_dy, a, at.beside).wait_recv()
        return dqp[a * 2 + at.b].astype(F32) + dq_b[a].astype(F32)

    def fold_dq(a):
        dq_j[a] = column_dq(a).astype(BF16)
        wire.go(remote(dq_j.at[a], dq_z.at[at.a], s_dz, at.a, at.column(a)))

    round_trip(wire, [(do_all, s_do, CHUNKS), (stat_all, s_st, 1)], [finish_output, out_grads, in_grads], attend_back, ship_dq, fold_dq)
    dk2_out[...] = dk_acc[...].astype(BF16)
    dv2_out[...] = dv_acc[...].astype(BF16)
    value = column_dq(at.a)
    for step in range(1, depth):
        a = wire.near(step)
        remote(dq_z.at[a], dq_z.at[a], s_dz, a, at.column(a)).wait_recv()
        value += dq_z[a].astype(F32)
    dq2 = value.astype(BF16)
    dq2_out[...] = dq2
    dx, dgain = norm_back_rows(h1[...], gains[1:2, :], nt(dq2, w_rest[1]))
    small[0:1, :] = dgain
    dh1 = dh2 + dx
    dh1_out[...] = dh1
    branch1 = dh1.astype(BF16)
    branch1_out[...] = branch1
    do1 = nt(branch1, w_rest[0]).astype(BF16)
    do1_out[...] = do1
    stat_own[1] = jnp.concatenate([lse1[...].T[:STAT], per_head_sums(do1.astype(F32) * o1[...].astype(F32), heads)], 0)
    stat1_out[...] = stat_own[1]
    gmem_out[...] = (nt(dk2_out[...], w_ck[...]) + nt(dv2_out[...], w_cv[...])).astype(BF16)
    wire.drain()


def middle(peers, lengths, q2, h1, o1, lse1, w_rest, gains, mem, grad, ck_shard, cv_shard, co_shard, in_shard, w_out):
    rows, slots = q2.shape[0], mem.shape[0]
    depth = peers // 2
    units = w_out.shape[0]
    row = lambda dtype: sds((rows, D), dtype)
    store = lambda n, dtype=BF16: pltpu.VMEM((n, rows, D), dtype)
    stat = lambda n, k=STAT: pltpu.VMEM((n, k, rows), F32)
    group = lambda width, dtype=BF16: pltpu.VMEM((WAYS * rows, width), dtype)
    return pl.pallas_call(
        functools.partial(middle_kernel, peers),
        name="middle",
        out_shape=[
            row(BF16),
            row(BF16),
            row(BF16),
            sds((slots, D), BF16),
            sds((slots, D), BF16),
            row(BF16),
            row(F32),
            row(BF16),
            sds((2 * STAT, rows), F32),
            sds((D, units), BF16),
            sds((units, D), BF16),
            row(BF16),
            sds((slots, D), BF16),
            sds((8, D), F32),
        ],
        in_specs=[smem_spec()] + [full_spec()] * 13,
        out_specs=[full_spec()] * 14,
        scratch_shapes=[
            store(peers), pltpu.VMEM((slots, D), BF16), pltpu.VMEM((slots, D), BF16),
            store(peers), stat(peers), store(depth), stat(depth), store(depth), stat(depth), store(depth), stat(depth),
            pltpu.VMEM((D, D), BF16), pltpu.VMEM((D, D), BF16), pltpu.VMEM((D, D), BF16), pltpu.VMEM((D, units), BF16),
            group(D), group(D), group(units, F32), group(units), group(units), group(D), group(D), group(D), group(D),
            store(peers), stat(peers, 2 * STAT), stat(2, 2 * STAT),
            pltpu.VMEM((slots, D), F32), pltpu.VMEM((slots, D), F32),
            store(peers), store(depth), store(depth), store(depth),
            pltpu.VMEM((slots, 2 * rows), F32),
        ]
        + line_sems(depth, CHUNKS) + sems(9) + sems(WAYS) + sems(WAYS)
        + sems(depth) * 4
        + sems(WAYS) * 3
        + line_sems(depth, CHUNKS) + line_sems(depth, 1)
        + sems(depth) * 2,
        compiler_params=pltpu.CompilerParams(collective_id=2, has_side_effects=True, vmem_limit_bytes=VMEM_LIMIT),
    )(lengths, q2, h1, o1, lse1, w_rest, gains, mem, grad, ck_shard, cv_shard, co_shard, in_shard, w_out)


def tail_kernel(peers, *refs):
    (order, do1, stat1, q_far, k_far, v_far, bias_far, bias_back_far, tok, w_self, gains, dh1, buckets,
     a1, o1, branch1, a2, dq2, mem, dk2, dv2, o2, branch2, g_in, g_out, small_mid) = refs[:26]
    out, small_out, grad_tokens = refs[26:29]
    (prod, ra, sb, rb, sc, rc, sd, rd, tiny, tiny_in, do_all, do_nat, stat_all, stat_rows, stat_t, q_own, k_own, v_own,
     dq1, dk1, dv1, diagonals, q_nat, k_nat, v_nat, bias, bias_back, bucket_rows, inv, s_w, s_far, *sem) = refs[29:]
    sem = [sem[2 * i : 2 * i + 2] for i in range(len(sem) // 2)]
    s_do, s_st, sem_a, sem_b, sem_c, sem_d, sem_e, sem_f, sem_g, sem_t = sem
    wire = Wire(peers)
    at, depth, go = wire.at, wire.depth, wire.go
    rows, length = do1.shape[0], q_far.shape[0]
    mine, pieces = rows // PIECE, length // PIECE
    total, quarter, wide = out.shape
    half_width, part = wide // 2, quarter // depth
    pairs = [(o2, branch2), (mem, dk2), (mem, dv2), (a2, dq2), (o1, branch1), (a1, dq1), (a1, dk1), (a1, dv1)]
    n_mats = len(pairs)
    columns = lambda b: pl.ds(pl.multiple_of(b * half_width, LANES), half_width)
    shard_rows = lambda f: pl.ds(pl.multiple_of(f * quarter, quarter), quarter)
    part_rows = lambda a: pl.ds(pl.multiple_of(a * part, part), part)
    own_half, other_half = columns(at.b), columns(1 - at.b)

    def stage_a(i):
        left, right = pairs[i]
        prod[i] = tn(left[...], right[...]).astype(BF16)
        for x in range(2):
            go(remote(prod.at[i, shard_rows(x * 2 + 1 - at.k)], ra.at[i, x], sem_a, 2 * i + x, at.core))

    def stage_b(i):
        for x in range(2):
            remote(ra.at[i, x], ra.at[i, x], sem_a, 2 * i + x, at.core).wait_recv()
        x = 1 - at.x
        sb[i] = (prod[i, shard_rows(x * 2 + at.k), :].astype(F32) + ra[i, x].astype(F32)).astype(BF16)
        go(remote(sb.at[i], rb.at[i], sem_b, i, at.across))

    def source(j):
        if j < n_mats + WAYS:
            return sc.at[j]
        q = j - n_mats - WAYS
        return g_out.at[q * quarter : (q + 1) * quarter]

    def stage_c(j):
        if j < n_mats:
            remote(sb.at[j], rb.at[j], sem_b, j, at.across).wait_recv()
            value = prod[j, shard_rows(at.f), :].astype(F32) + ra[j, at.x].astype(F32) + rb[j].astype(F32)
            sc[j] = value.astype(BF16)
        go(remote(source(j).at[:, other_half], rc.at[j], sem_c, j, at.beside))

    def stage_d(j):
        remote(rc.at[j], rc.at[j], sem_c, j, at.beside).wait_recv()
        value = source(j)[:, own_half].astype(F32) + rc[j].astype(F32)
        sd[j] = value.astype(BF16)
        for d in range(1, depth):
            spot = rd.at[j, part_rows(at.a)]
            go(remote(sd.at[j, part_rows(at.ahead(d))], spot, sem_d, j * depth + d, at.column(at.ahead(d))))

    def stage_e(j):
        value = sd[j, part_rows(at.a), :].astype(F32)
        for d in range(1, depth):
            spot = rd.at[j, part_rows(at.behind(d))]
            remote(spot, spot, sem_d, j * depth + d, at.column(at.behind(d))).wait_recv()
            value += spot[...].astype(F32)
        spot = out.at[j, part_rows(at.a), own_half]
        spot[...] = value.astype(BF16)
        for d in range(1, depth):
            go(remote(spot, spot, sem_e, j * depth + d, at.column(at.ahead(d))))

    def stage_f(j):
        for d in range(1, depth):
            spot = out.at[j, part_rows(at.behind(d)), own_half]
            remote(spot, spot, sem_e, j * depth + d, at.column(at.behind(d))).wait_recv()
        go(remote(out.at[j, :, own_half], out.at[j, :, own_half], sem_f, j, at.beside))

    def stage_g(j):
        spot = out.at[j, :, other_half]
        remote(spot, spot, sem_f, j, at.beside).wait_recv()

    def send_g_in():
        sc[n_mats + at.f] = g_in[shard_rows(at.f), :]
        for d in range(1, WAYS):
            f = lax.rem(at.f + d, WAYS)
            go(remote(g_in.at[shard_rows(f)], sc.at[n_mats + at.f], sem_g, d, at.group(d)))

    def have_g_in():
        for d in range(1, WAYS):
            spot = sc.at[n_mats + lax.rem(at.f + WAYS - d, WAYS)]
            remote(spot, spot, sem_g, d, at.group(WAYS - d)).wait_recv()

    hops = [at.core, at.across, at.beside]

    def small_hop(t):
        if t:
            remote(tiny_in.at[t - 1], tiny_in.at[t - 1], sem_t, t - 1, hops[t - 1]).wait_recv()
            tiny[t] = tiny[t - 1] + tiny_in[t - 1]
        if t < 3:
            go(remote(tiny.at[t], tiny_in.at[t], sem_t, t, hops[t]))
        else:
            for d in range(1, depth):
                go(remote(tiny.at[3], tiny_in.at[2 + d], sem_t, 2 + d, at.column(at.ahead(d))))

    def small_end():
        value = tiny[3]
        for d in range(1, depth):
            remote(tiny_in.at[2 + d], tiny_in.at[2 + d], sem_t, 2 + d, at.column(at.behind(d))).wait_recv()
            value += tiny_in[2 + d]
        small_out[...] = value

    gathered = [(do_all, s_do, CHUNKS), (stat_all, s_st, 1)]

    def relay(step):
        wire.relay(gathered, step)

    def prepare():
        for copy in coming:
            copy.wait()
        for a in range(depth):
            wire.from_beside(gathered, a)
        for c in range(peers):
            spread = jnp.concatenate([stat_all[c], jnp.zeros((LANES - 2 * STAT, rows), F32)], 0)
            stat_rows[c * rows : (c + 1) * rows, :] = spread.T
        for i in range(pieces):
            do_nat[i * PIECE : (i + 1) * PIECE, :] = do_all[pl.ds(inv[i] * PIECE, PIECE), :]
        per = LANES // PIECE
        for t in range(length // LANES):
            lines = [stat_rows[pl.ds(inv[t * per + i] * PIECE, PIECE), :] for i in range(per)]
            stat_t[:, t * LANES : (t + 1) * LANES] = jnp.concatenate(lines, 0).T
        for i in range(mine):
            dst = slice(i * PIECE, (i + 1) * PIECE)
            src = pl.ds(own[i][0] * PIECE, PIECE)
            q_own[dst, :] = q_nat[src, :]
            k_own[dst, :] = k_nat[src, :]
            v_own[dst, :] = v_nat[src, :]

    def attend_back(low, high):
        lane = lax.broadcasted_iota(jnp.int32, (rows, length), 1)
        visible, seen = lane < own_column(own, 3), lane >= own_column(own, 4)
        stat_lane = lax.broadcasted_iota(jnp.int32, (rows, LANES), 1)
        stat_own = jnp.concatenate([stat1[...], jnp.zeros((LANES - 2 * STAT, rows), F32)], 0).T

        def column(h):
            return jnp.sum(jnp.where(stat_lane == h, stat_own, 0.0), axis=1, keepdims=True)

        def pair(p, c):
            sl = lanes_of(p)
            q, k, v, do = q_own[:, sl], k_nat[:, sl], v_nat[:, sl], do1[:, sl]
            kq, vq, qa, da = k_own[:, sl], v_own[:, sl], q_nat[:, sl], do_nat[:, sl]
            dq = dk = dv = jnp.zeros((rows, LANES), F32)
            for half in range(2):
                h = 2 * p + half
                km, vm = half_mask(k, half), half_mask(v, half)
                s = jnp.where(visible, nt(q, km) + bias[h].astype(F32), NEGATIVE)
                e = jnp.exp(s - column(h))
                ds = e * (nt(do, vm) - column(STAT + h))
                dq += nn(ds.astype(BF16), km)
                for i in range(mine):
                    diagonals[i, pl.ds(h, 1), :] = diagonal_sums(ds[i * PIECE : (i + 1) * PIECE, :])
                s = jnp.where(seen, nt(half_mask(kq, half), qa) + bias_back[h].astype(F32), NEGATIVE)
                e = jnp.exp(s - stat_t[pl.ds(h, 1), :])
                dv += nn(e.astype(BF16), half_mask(da, half))
                ds = e * (nt(half_mask(vq, half), da) - stat_t[pl.ds(STAT + h, 1), :])
                dk += nn(ds.astype(BF16), half_mask(qa, half))
            dq1[:, sl] = dq.astype(BF16)
            dk1[:, sl] = dk.astype(BF16)
            dv1[:, sl] = dv.astype(BF16)
            return c

        lax.fori_loop(low, high, pair, 0)

    def finish_tokens():
        weights_here.wait()
        da1 = nt(dq1[...], prod[5]) + nt(dk1[...], prod[6]) + nt(dv1[...], prod[7])
        dx, dgain = norm_back_rows(tok[...].astype(F32), gains[0:1, :], da1)
        grad_tokens[...] = (dh1[...] + dx).astype(BF16)
        sums = jnp.zeros((STAT, BUCKETS), F32)
        number = lax.broadcasted_iota(jnp.int32, (BUCKETS, length + LANES), 0)
        for i in range(mine):
            line = bucket_rows[pl.ds(own[i][1], 1), pl.ds(own[i][2] * LANES, length + LANES)]
            hot = jnp.where(line == number, 1.0, 0.0).astype(BF16)
            high, low = split(diagonals[i])
            sums += nt(high, hot) + nt(low, hot)
        tiny[0] = jnp.zeros(tiny.shape[1:], F32)
        tiny[0, 0:1, :] = dgain
        tiny[0, 1:3, :] = small_mid[0:2, :]
        tiny[0, 8 : 8 + STAT, 0:BUCKETS] = sums

    weights_here = pltpu.make_async_copy(w_self, prod.at[5:8], s_w)
    weights_here.start()
    coming = []
    for i, (src, dst) in enumerate(
        ((q_far, q_nat), (k_far, k_nat), (v_far, v_nat), (bias_far, bias), (bias_back_far, bias_back))
    ):
        coming.append(pltpu.make_async_copy(src, dst, s_far.at[i]))
        coming[-1].start()
    own = own_facts(order, at.c, mine, length)
    greet(wire.partners())
    wire.spread(do1, do_all, s_do, CHUNKS)
    wire.spread(stat1, stat_all, s_st, 1)
    wire.slot(do_all, at.c)[...] = do1[...]
    stat_all[at.c] = stat1[...]
    fill_inverse(order, inv)
    diagonals[...] = jnp.zeros_like(diagonals)
    bucket_rows[0:1, :] = pltpu.roll(buckets[...], 1, 1)
    bucket_rows[1:2, :] = pltpu.roll(buckets[...], 1 + PIECE, 1)
    turns = [12, 13, 14, 15, 0, 1, 2, 3, 4, 8, 9, 10, 11, 5, 6, 7]
    lag = 1.5
    events = []
    for tick, j in enumerate(turns):
        if j < n_mats:
            events += [(tick - 2, 1, lambda j=j: stage_a(j)), (tick - 1, 2, lambda j=j: stage_b(j))]
        for k, stage in enumerate((stage_c, stage_d, stage_e, stage_f, stage_g)):
            events.append((tick + k * lag, 3 + k, lambda j=j, stage=stage: stage(j)))
    events += [(2.5, 0, send_g_in), (8.5, 0, have_g_in)]
    events += [(0.5, 0, lambda: relay(1)), (1.5, 0, lambda: relay(2)), (1.6, 0, lambda: relay(3)), (3.5, 0, prepare)]
    events += [(4.5 + i, 0, lambda i=i: attend_back(2 * i, 2 * i + 2)) for i in range(PAIRS // 2)]
    events += [(8.6, 0, finish_tokens)]
    events += [(9.5 + t, 0, lambda t=t: small_hop(t)) for t in range(4)] + [(14.5, 0, small_end)]
    for _, _, event in sorted(events, key=lambda e: (e[0], -e[1])):
        event()
    wire.drain()


def tail(peers, order, do1, stat1, q_nat, k_nat, v_nat, bias, bias_back, tok, w_self, gains, dh1, buckets, *rest):
    rows, length = do1.shape[0], q_nat.shape[0]
    n, depth = 8, peers // 2
    total = n + 2 * WAYS
    quarter, half = D // WAYS, D // 2
    shard = lambda k, width=D: pltpu.VMEM((k, quarter, width), BF16)
    row = lambda: pltpu.VMEM((rows, D), BF16)
    tiny = lambda k: pltpu.VMEM((k, 8 + STAT, D), F32)
    operands = (do1, stat1, q_nat, k_nat, v_nat, bias, bias_back, tok, w_self, gains, dh1, buckets) + rest
    return pl.pallas_call(
        functools.partial(tail_kernel, peers),
        name="tail",
        out_shape=[sds((total, quarter, D), BF16), sds((8 + STAT, D), F32), sds((rows, D), BF16)],
        in_specs=[smem_spec()]
        + [any_spec() if i in (2, 3, 4, 5, 6, 8) else full_spec() for i in range(len(operands))],
        out_specs=[full_spec()] * 3,
        scratch_shapes=[
            pltpu.VMEM((n, D, D), BF16), pltpu.VMEM((n, 2, quarter, D), BF16), shard(n), shard(n),
            shard(n + WAYS), shard(total, half), shard(total, half), shard(total, half),
            tiny(4), tiny(3 + depth),
            pltpu.VMEM((length, D), BF16), pltpu.VMEM((length, D), BF16),
            pltpu.VMEM((peers, 2 * STAT, rows), F32), pltpu.VMEM((length, LANES), F32), pltpu.VMEM((LANES, length), F32),
            row(), row(), row(), row(), row(), row(),
            pltpu.VMEM((rows // PIECE, STAT, length + LANES), F32),
        ]
        + [pltpu.VMEM((length, D), BF16)] * 3
        + [pltpu.VMEM((HEADS, rows, length), BF16)] * 2
        + [pltpu.VMEM((2, 2 * length), jnp.int32), pltpu.SMEM(order.shape, jnp.int32)]
        + [pltpu.SemaphoreType.DMA, pltpu.SemaphoreType.DMA((5,))]
        + line_sems(depth, CHUNKS) + line_sems(depth, 1)
        + sems(2 * n) + sems(n) + sems(total) + sems(total * depth) + sems(total * depth) + sems(total) + sems(WAYS) + sems(3 + depth),
        compiler_params=pltpu.CompilerParams(collective_id=0, has_side_effects=True, vmem_limit_bytes=TAIL_VMEM),
    )(order, *operands)


def widen_kernel(src, *refs):
    outs, sem = refs[:-2], refs[-1]
    wide = refs[-2]
    copies = []
    count = src.shape[0]
    quarter, width = src.shape[1], src.shape[2]
    for j in range(count):
        wide[j] = src[j].astype(F32)
        if j < count - 2 * WAYS:
            dst = outs[j]
        elif j < count - WAYS:
            i = j - (count - 2 * WAYS)
            dst = outs[-2].at[:, i * width : (i + 1) * width]
        else:
            i = j - (count - WAYS)
            dst = outs[-1].at[i * quarter : (i + 1) * quarter]
        copies.append(pltpu.make_async_copy(wide.at[j], dst, sem.at[j]))
        copies[-1].start()
    for copy in copies:
        copy.wait()


def widen(total):
    count, quarter, width = total.shape
    each = [sds((quarter, width), F32)] * (count - 2 * WAYS)
    return pl.pallas_call(
        widen_kernel,
        name="widen",
        out_shape=each + [sds((quarter, WAYS * width), F32), sds((WAYS * quarter, width), F32)],
        in_specs=[full_spec()],
        out_specs=[any_spec()] * (len(each) + 2),
        scratch_shapes=[pltpu.VMEM(total.shape, F32), pltpu.SemaphoreType.DMA((count,))],
        compiler_params=pltpu.CompilerParams(vmem_limit_bytes=VMEM_LIMIT),
    )(total)


def shards(
    tokens,
    memory,
    piece_order,
    bucket_table,
    passage_lengths,
    self_gain,
    cross_gain,
    hidden_gain,
    position_bias,
    self_query,
    self_attention_key,
    self_value,
    self_output,
    cross_query,
    cross_key,
    cross_value,
    cross_output,
    hidden_in,
    hidden_out,
    grad_output,
):
    tok, mem, grad = tokens[0], memory[0], grad_output[0]
    rows, slots = tok.shape[0], mem.shape[0]
    length = (bucket_table.shape[0] + 1) // 2
    peers = length // rows
    f = lax.axis_index("fsdp")
    quarter, eighth = self_query.shape[0], position_bias.shape[0]
    buckets = jnp.pad(bucket_table, (0, 1), constant_values=-1)[None]
    w_self, w_rest, gains, ahead, behind, q1_nat, k1_nat, v1_nat, a1, o1, h1, a2, q2, lse1 = front(
        peers,
        piece_order,
        tok,
        [self_gain[None], cross_gain[None], hidden_gain[None]],
        position_bias,
        buckets,
        [self_query, self_attention_key, self_value, self_output, cross_query],
    )
    (
        o2,
        branch2,
        dq2,
        dk2,
        dv2,
        branch1,
        dh1,
        do1,
        stat1,
        g_in,
        g_out,
        layer_output,
        grad_memory,
        small_mid,
    ) = middle(
        peers,
        passage_lengths,
        q2,
        h1,
        o1,
        lse1,
        w_rest,
        gains,
        mem,
        grad,
        cross_key,
        cross_value,
        cross_output,
        hidden_in,
        hidden_out,
    )
    total, small, grad_tokens = tail(
        peers,
        piece_order,
        do1,
        stat1,
        q1_nat,
        k1_nat,
        v1_nat,
        ahead,
        behind,
        tok,
        w_self,
        gains,
        dh1,
        buckets,
        a1,
        o1,
        branch1,
        a2,
        dq2,
        mem,
        dk2,
        dv2,
        o2,
        branch2,
        g_in,
        g_out,
        small_mid,
    )
    *each, sum_in, sum_out = widen(total)
    gain = lambda i: lax.dynamic_slice_in_dim(small[i], f * quarter, quarter)
    bias_out = lax.dynamic_slice_in_dim(small[8:, :BUCKETS].T, f * eighth, eighth)[:, :HEADS]
    return (
        layer_output[None],
        grad_tokens[None],
        grad_memory[None],
        gain(0),
        gain(1),
        gain(2),
        bias_out,
        *[each[i] for i in (5, 6, 7, 4, 3, 1, 2, 0)],
        sum_in,
        sum_out,
    )


def pick(*arrays):
    resident = (arrays[3].shape[0] + 1) // 2 <= RESIDENT_ROWS
    return (shards if resident else streamed_shards)(*arrays)


def solution(mesh):
    return jax.shard_map(
        pick,
        mesh=mesh,
        in_specs=(
            P("fsdp", "ctx", None),
            P("fsdp", "ctx", None),
            P(),
            P(),
            P("fsdp", None),
            P("fsdp"),
            P("fsdp"),
            P("fsdp"),
            P("fsdp", None),
            P("fsdp", None),
            P("fsdp", None),
            P("fsdp", None),
            P("fsdp", None),
            P("fsdp", None),
            P("fsdp", None),
            P("fsdp", None),
            P("fsdp", None),
            P("fsdp", None),
            P("fsdp", None),
            P("fsdp", "ctx", None),
        ),
        out_specs=(
            P("fsdp", "ctx", None),
            P("fsdp", "ctx", None),
            P("fsdp", "ctx", None),
            P("fsdp"),
            P("fsdp"),
            P("fsdp"),
            P("fsdp", None),
            P("fsdp", None),
            P("fsdp", None),
            P("fsdp", None),
            P("fsdp", None),
            P("fsdp", None),
            P("fsdp", None),
            P("fsdp", None),
            P("fsdp", None),
            P("fsdp", None),
            P("fsdp", None),
        ),
        check_vma=False,
    )
```

```python
import functools

import jax
import jax.numpy as jnp
from jax import lax
from jax.experimental import pallas as pl
from jax.experimental.pallas import tpu as pltpu
from jax.sharding import PartitionSpec as P

D = 768
HEADS = 12
PAIRS = HEADS // 2
HEAD_DIM = 64
PIECE = 64
BLOCK = 256
PLEN = 256
KBLK = 512
PSG = 20
BUCKETS = 32
RESIDENT_ROWS = 1024
LANES = 128
EPSILON = 1e-06
NEGATIVE = -1e30
F32 = jnp.float32
BF16 = jnp.bfloat16
VMEM_LIMIT = 60 * 2**20
TAIL_VMEM = 63 * 2**20

def nn(a, b):
    return lax.dot_general(a, b, (((1,), (0,)), ((), ())), preferred_element_type=F32)
def nt(a, b):
    return lax.dot_general(a, b, (((1,), (1,)), ((), ())), preferred_element_type=F32)
def tn(a, b):
    return lax.dot_general(a, b, (((0,), (0,)), ((), ())), preferred_element_type=F32)

def normed(x, gain):
    return x * lax.rsqrt(jnp.mean(x * x, axis=-1, keepdims=True) + EPSILON) * gain

def half_mask(x, half):
    lane = lax.broadcasted_iota(jnp.int32, x.shape, 1) // HEAD_DIM
    return jnp.where(lane == half, x, jnp.zeros_like(x))

def lanes_of(pair):
    return pl.ds(pl.multiple_of(pair * LANES, LANES), LANES)

def shear(x, sign):
    row = lax.broadcasted_iota(jnp.int32, x.shape, 0)
    for bit in (1, 2, 4):
        x = jnp.where(row & bit != 0, pltpu.roll(x, (sign * bit) % x.shape[1], 1), x)
    return x

def full_spec():
    return pl.BlockSpec(memory_space=pltpu.VMEM)
def any_spec():
    return pl.BlockSpec(memory_space=pl.ANY)


def smem_spec():
    return pl.BlockSpec(memory_space=pltpu.SMEM)
def sds(shape, dtype):
    return jax.ShapeDtypeStruct(shape, dtype)

def norm_scale(values, gain_vector):
    return (
        values
        * lax.rsqrt(jnp.mean(values * values, axis=-1, keepdims=True) + EPSILON)
        * gain_vector
    )


def smooth_gate(values):
    return jax.nn.gelu(values, approximate=True)


def project(operand, matrix):
    return jnp.dot(operand, matrix, preferred_element_type=jnp.float32)


def project_back(operand, matrix):
    return jnp.einsum("sra,ba->srb", operand, matrix, preferred_element_type=jnp.float32)


def weight_grad(inputs, upstream):
    return jnp.einsum("sra,srb->ab", inputs, upstream, preferred_element_type=jnp.float32)


def to_heads(matrix):
    return matrix.reshape(matrix.shape[0], matrix.shape[1], HEADS, HEAD_DIM)


def heads_first(matrix):
    return jnp.transpose(to_heads(matrix), (0, 2, 1, 3))


def from_heads(tensor):
    return jnp.transpose(tensor, (0, 2, 1, 3)).reshape(
        tensor.shape[0], tensor.shape[2], HEADS * HEAD_DIM
    )


def block_scores(queries, keys_all, values_all, extras, offset):
    key_block = lax.dynamic_slice_in_dim(keys_all, offset, KBLK, 1)
    value_block = lax.dynamic_slice_in_dim(values_all, offset, KBLK, 1)
    added_bias, visible, bucket_indicator = extras(offset)
    scores = (
        jnp.einsum("sqhd,skhd->shqk", queries, key_block, preferred_element_type=jnp.float32)
        + added_bias
    )
    block_maximum = jnp.max(jnp.where(visible, scores, NEGATIVE), axis=-1)
    weights = jnp.exp(jnp.where(visible, scores - block_maximum[..., None], NEGATIVE))
    return (key_block, value_block, bucket_indicator, block_maximum, weights)


def attend_forward(queries, keys_all, values_all, extras):
    block_count = keys_all.shape[1] // KBLK

    def single_block_tile(carried, block_index):
        key_block, value_block, bucket_indicator, block_maximum, weights = block_scores(
            queries, keys_all, values_all, extras, block_index * KBLK
        )
        numerator = jnp.einsum(
            "shqk,skhd->shqd",
            weights.astype(jnp.bfloat16),
            value_block,
            preferred_element_type=jnp.float32,
        )
        return (carried, (block_maximum, jnp.sum(weights, axis=-1), numerator))

    ignored, stacked = lax.scan(
        single_block_tile, jnp.zeros((), jnp.float32), jnp.arange(block_count, dtype=jnp.int32)
    )
    block_maximum, block_sum, numerator = stacked
    row_maximum = jnp.max(block_maximum, axis=0)
    rescale = jnp.exp(block_maximum - row_maximum)
    row_total = jnp.sum(rescale * block_sum, axis=0)
    output = jnp.sum(rescale[..., None] * numerator, axis=0) / row_total[..., None]
    return (output, row_maximum, row_total)


def attend_backward(
    queries, keys_all, values_all, extras, grad_out, output, row_maximum, row_total
):
    block_count = keys_all.shape[1] // KBLK
    grad_wide = grad_out.astype(jnp.float32)
    row_dot = jnp.sum(grad_wide * output, axis=-1)
    scaled = grad_wide / row_total[..., None]
    sum_weight = -row_dot / row_total
    initial = (
        jnp.zeros(queries.shape, jnp.float32),
        jnp.zeros(keys_all.shape, jnp.float32),
        jnp.zeros(values_all.shape, jnp.float32),
        jnp.zeros((BUCKETS, HEADS), jnp.float32),
    )

    def single_block_tile(carried, block_index):
        grad_query, grad_keys, grad_values, grad_bias = carried
        offset = block_index * KBLK
        key_block, value_block, bucket_indicator, block_maximum, weights = block_scores(
            queries, keys_all, values_all, extras, offset
        )
        rescale = jnp.exp(block_maximum - row_maximum)
        grad_numerator = (scaled * rescale[..., None]).astype(jnp.bfloat16)
        grad_weights = (
            jnp.einsum(
                "shqd,skhd->shqk", grad_numerator, value_block, preferred_element_type=jnp.float32
            )
            + (sum_weight * rescale)[..., None]
        )
        grad_scores = weights * grad_weights
        gradient_bfloat_cast = grad_scores.astype(jnp.bfloat16)
        grad_query = grad_query + jnp.einsum(
            "shqk,skhd->sqhd", gradient_bfloat_cast, key_block, preferred_element_type=jnp.float32
        )
        key_part = jnp.einsum(
            "shqk,sqhd->skhd", gradient_bfloat_cast, queries, preferred_element_type=jnp.float32
        )
        value_part = jnp.einsum(
            "shqk,shqd->skhd",
            weights.astype(jnp.bfloat16),
            grad_numerator,
            preferred_element_type=jnp.float32,
        )
        grad_keys = lax.dynamic_update_slice_in_dim(grad_keys, key_part, offset, 1)
        grad_values = lax.dynamic_update_slice_in_dim(grad_values, value_part, offset, 1)
        if bucket_indicator is not None:
            remainder_portion = (grad_scores - gradient_bfloat_cast.astype(jnp.float32)).astype(
                jnp.bfloat16
            )
            grad_bias = (
                grad_bias
                + jnp.einsum(
                    "uljf,pjf->pl",
                    gradient_bfloat_cast,
                    bucket_indicator,
                    preferred_element_type=jnp.float32,
                )
                + jnp.einsum(
                    "uljf,pjf->pl",
                    remainder_portion,
                    bucket_indicator,
                    preferred_element_type=jnp.float32,
                )
            )
        return ((grad_query, grad_keys, grad_values, grad_bias), None)

    result, ignored = lax.scan(single_block_tile, initial, jnp.arange(block_count, dtype=jnp.int32))
    return result


def streamed_shards(
    tokens,
    memory,
    piece_order,
    bucket_table,
    passage_lengths,
    self_gain,
    cross_gain,
    hidden_gain,
    position_bias,
    self_query,
    self_attention_key,
    self_value,
    self_output,
    cross_query,
    cross_key,
    cross_value,
    cross_output,
    hidden_in,
    hidden_out,
    grad_output,
):
    (
        gain_one,
        gain_two,
        gain_three,
        position_bias_lookup,
        query_full,
        key_full,
        value_full,
        output_full,
        cross_query_full,
        cross_key_full,
        cross_value_full,
        cross_output_full,
        inner_full,
        outer_full,
    ) = (
        lax.all_gather(self_gain, "fsdp", axis=0, tiled=True),
        lax.all_gather(cross_gain, "fsdp", axis=0, tiled=True),
        lax.all_gather(hidden_gain, "fsdp", axis=0, tiled=True),
        lax.all_gather(position_bias, "fsdp", axis=0, tiled=True),
        lax.all_gather(self_query, "fsdp", axis=0, tiled=True),
        lax.all_gather(self_attention_key, "fsdp", axis=0, tiled=True),
        lax.all_gather(self_value, "fsdp", axis=0, tiled=True),
        lax.all_gather(self_output, "fsdp", axis=0, tiled=True),
        lax.all_gather(cross_query, "fsdp", axis=0, tiled=True),
        lax.all_gather(cross_key, "fsdp", axis=0, tiled=True),
        lax.all_gather(cross_value, "fsdp", axis=0, tiled=True),
        lax.all_gather(cross_output, "fsdp", axis=0, tiled=True),
        lax.all_gather(hidden_in, "fsdp", axis=0, tiled=True),
        lax.all_gather(hidden_out, "fsdp", axis=0, tiled=True),
    )
    gain_one = gain_one.astype(jnp.float32)
    gain_two = gain_two.astype(jnp.float32)
    gain_three = gain_three.astype(jnp.float32)
    sequence_count = tokens.shape[0]
    local_rows = tokens.shape[1]
    sequence_length = (bucket_table.shape[0] + 1) // 2
    memory_length = PSG * PLEN
    piece_offsets = jnp.arange(PIECE, dtype=jnp.int32)
    local_pieces = lax.dynamic_slice_in_dim(
        piece_order, lax.axis_index("ctx") * (local_rows // PIECE), local_rows // PIECE
    )
    query_position = (local_pieces[:, None] * PIECE + piece_offsets[None, :]).reshape(local_rows)
    key_position = (piece_order[:, None] * PIECE + piece_offsets[None, :]).reshape(sequence_length)
    bucket_numbers = jnp.arange(BUCKETS, dtype=jnp.int32)

    def self_extras(offset):
        key_block_position = lax.dynamic_slice_in_dim(key_position, offset, KBLK)
        relative_bucket_index = jnp.take(
            bucket_table,
            key_block_position[None, :] - query_position[:, None] + sequence_length - 1,
        )
        bucket_indicator = (
            relative_bucket_index[None, :, :] == bucket_numbers[:, None, None]
        ).astype(jnp.bfloat16)
        added_bias = jnp.einsum(
            "lvj,lf->fvj",
            bucket_indicator,
            position_bias_lookup,
            preferred_element_type=jnp.float32,
        )
        visible = key_block_position[None, :] // BLOCK <= query_position[:, None] // BLOCK
        return (added_bias, visible, bucket_indicator)

    slot_numbers = jnp.arange(PLEN, dtype=jnp.int32)
    memory_valid = (passage_lengths[:, :, None] > slot_numbers[None, None, :]).reshape(
        sequence_count, memory_length
    )

    def cross_extras(offset):
        visible = lax.dynamic_slice_in_dim(memory_valid, offset, KBLK, 1)[:, None, None, :]
        return (0.0, visible, None)

    inputs_wide = tokens.astype(jnp.float32)
    normed_one = norm_scale(inputs_wide, gain_one).astype(jnp.bfloat16)
    queries_one = project(normed_one, query_full).astype(jnp.bfloat16)
    keys_local = project(normed_one, key_full).astype(jnp.bfloat16)
    values_local = project(normed_one, value_full).astype(jnp.bfloat16)
    memory_keys = project(memory, cross_key_full).astype(jnp.bfloat16)
    memory_values = project(memory, cross_value_full).astype(jnp.bfloat16)
    keys_all, values_all, memory_keys_all, memory_values_all = (
        lax.all_gather(keys_local, "ctx", axis=1, tiled=True),
        lax.all_gather(values_local, "ctx", axis=1, tiled=True),
        lax.all_gather(memory_keys, "ctx", axis=1, tiled=True),
        lax.all_gather(memory_values, "ctx", axis=1, tiled=True),
    )
    output_one, maximum_one, total_one = attend_forward(
        to_heads(queries_one), to_heads(keys_all), to_heads(values_all), self_extras
    )
    attended_one = from_heads(output_one).astype(jnp.bfloat16)
    hidden_one = inputs_wide + project(attended_one, output_full)
    normed_two = norm_scale(hidden_one, gain_two).astype(jnp.bfloat16)
    queries_two = project(normed_two, cross_query_full).astype(jnp.bfloat16)
    output_two, maximum_two, total_two = attend_forward(
        to_heads(queries_two), to_heads(memory_keys_all), to_heads(memory_values_all), cross_extras
    )
    attended_two = from_heads(output_two).astype(jnp.bfloat16)
    hidden_two = hidden_one + project(attended_two, cross_output_full)
    normed_three = norm_scale(hidden_two, gain_three).astype(jnp.bfloat16)
    before_gate = project(normed_three, inner_full)
    gated_wide, gate_pullback = jax.vjp(smooth_gate, before_gate)
    activated = gated_wide.astype(jnp.bfloat16)
    layer_output = (hidden_two + project(activated, outer_full)).astype(jnp.bfloat16)
    grad_wide = grad_output.astype(jnp.float32)
    grad_outer = weight_grad(activated, grad_output)
    grad_activated = project_back(grad_output, outer_full)
    grad_before = gate_pullback(grad_activated)[0].astype(jnp.bfloat16)
    grad_inner = weight_grad(normed_three, grad_before)
    ignored, norm_pullback = jax.vjp(norm_scale, hidden_two, gain_three)
    grad_hidden_part, grad_gain_three = norm_pullback(project_back(grad_before, inner_full))
    grad_hidden_two = grad_wide + grad_hidden_part
    branch_two = grad_hidden_two.astype(jnp.bfloat16)
    grad_cross_output = weight_grad(attended_two, branch_two)
    grad_attended_two = project_back(branch_two, cross_output_full).astype(jnp.bfloat16)
    keys_back, values_back, memory_keys_back, memory_values_back = (
        keys_all,
        values_all,
        memory_keys_all,
        memory_values_all,
    )
    grad_query_two, grad_memory_keys, grad_memory_values, unused_bias = attend_backward(
        to_heads(queries_two),
        to_heads(memory_keys_back),
        to_heads(memory_values_back),
        cross_extras,
        heads_first(grad_attended_two),
        output_two,
        maximum_two,
        total_two,
    )
    memory_key_sum, memory_value_sum = (
        lax.psum_scatter(
            grad_memory_keys.reshape(sequence_count, memory_length, D),
            "ctx",
            scatter_dimension=1,
            tiled=True,
        ),
        lax.psum_scatter(
            grad_memory_values.reshape(sequence_count, memory_length, D),
            "ctx",
            scatter_dimension=1,
            tiled=True,
        ),
    )
    memory_key_rounded = memory_key_sum.astype(jnp.bfloat16)
    memory_value_rounded = memory_value_sum.astype(jnp.bfloat16)
    query_two_rounded = grad_query_two.reshape(sequence_count, local_rows, D).astype(jnp.bfloat16)
    grad_cross_query = weight_grad(normed_two, query_two_rounded)
    grad_cross_key = weight_grad(memory, memory_key_rounded)
    grad_cross_value = weight_grad(memory, memory_value_rounded)
    grad_memory = (
        project_back(memory_key_rounded, cross_key_full)
        + project_back(memory_value_rounded, cross_value_full)
    ).astype(jnp.bfloat16)
    ignored, norm_pullback = jax.vjp(norm_scale, hidden_one, gain_two)
    grad_hidden_part, grad_gain_two = norm_pullback(
        project_back(query_two_rounded, cross_query_full)
    )
    grad_hidden_one = grad_hidden_two + grad_hidden_part
    branch_one = grad_hidden_one.astype(jnp.bfloat16)
    grad_self_output = weight_grad(attended_one, branch_one)
    grad_attended_one = project_back(branch_one, output_full).astype(jnp.bfloat16)
    grad_query_one, grad_keys_all, grad_values_all, grad_bias = attend_backward(
        to_heads(queries_one),
        to_heads(keys_back),
        to_heads(values_back),
        self_extras,
        heads_first(grad_attended_one),
        output_one,
        maximum_one,
        total_one,
    )
    key_sum, value_sum = (
        lax.psum_scatter(
            grad_keys_all.reshape(sequence_count, sequence_length, D),
            "ctx",
            scatter_dimension=1,
            tiled=True,
        ),
        lax.psum_scatter(
            grad_values_all.reshape(sequence_count, sequence_length, D),
            "ctx",
            scatter_dimension=1,
            tiled=True,
        ),
    )
    query_one_rounded = grad_query_one.reshape(sequence_count, local_rows, D).astype(jnp.bfloat16)
    first_key_bfloat_cast = key_sum.astype(jnp.bfloat16)
    value_one_rounded = value_sum.astype(jnp.bfloat16)
    grad_self_query = weight_grad(normed_one, query_one_rounded)
    grad_self_key = weight_grad(normed_one, first_key_bfloat_cast)
    grad_self_value = weight_grad(normed_one, value_one_rounded)
    grad_normed_one = (
        project_back(query_one_rounded, query_full)
        + project_back(first_key_bfloat_cast, key_full)
        + project_back(value_one_rounded, value_full)
    )
    ignored, norm_pullback = jax.vjp(norm_scale, inputs_wide, gain_one)
    grad_input_part, grad_gain_one = norm_pullback(grad_normed_one)
    grad_tokens = (grad_hidden_one + grad_input_part).astype(jnp.bfloat16)
    (
        shard_gain_one,
        shard_gain_two,
        shard_gain_three,
        shard_bias,
        shard_query,
        shard_key,
        shard_value,
        shard_output,
        shard_cross_query,
        shard_cross_key,
        shard_cross_value,
        shard_cross_output,
        shard_inner,
        shard_outer,
    ) = (
        lax.psum_scatter(
            grad_gain_one.astype(jnp.bfloat16), "fsdp", scatter_dimension=0, tiled=True
        ).astype(jnp.float32),
        lax.psum_scatter(
            grad_gain_two.astype(jnp.bfloat16), "fsdp", scatter_dimension=0, tiled=True
        ).astype(jnp.float32),
        lax.psum_scatter(
            grad_gain_three.astype(jnp.bfloat16), "fsdp", scatter_dimension=0, tiled=True
        ).astype(jnp.float32),
        lax.psum_scatter(
            grad_bias.astype(jnp.bfloat16), "fsdp", scatter_dimension=0, tiled=True
        ).astype(jnp.float32),
        lax.psum_scatter(
            grad_self_query.astype(jnp.bfloat16), "fsdp", scatter_dimension=0, tiled=True
        ).astype(jnp.float32),
        lax.psum_scatter(
            grad_self_key.astype(jnp.bfloat16), "fsdp", scatter_dimension=0, tiled=True
        ).astype(jnp.float32),
        lax.psum_scatter(
            grad_self_value.astype(jnp.bfloat16), "fsdp", scatter_dimension=0, tiled=True
        ).astype(jnp.float32),
        lax.psum_scatter(
            grad_self_output.astype(jnp.bfloat16), "fsdp", scatter_dimension=0, tiled=True
        ).astype(jnp.float32),
        lax.psum_scatter(
            grad_cross_query.astype(jnp.bfloat16), "fsdp", scatter_dimension=0, tiled=True
        ).astype(jnp.float32),
        lax.psum_scatter(
            grad_cross_key.astype(jnp.bfloat16), "fsdp", scatter_dimension=0, tiled=True
        ).astype(jnp.float32),
        lax.psum_scatter(
            grad_cross_value.astype(jnp.bfloat16), "fsdp", scatter_dimension=0, tiled=True
        ).astype(jnp.float32),
        lax.psum_scatter(
            grad_cross_output.astype(jnp.bfloat16), "fsdp", scatter_dimension=0, tiled=True
        ).astype(jnp.float32),
        lax.psum_scatter(
            grad_inner.astype(jnp.bfloat16), "fsdp", scatter_dimension=0, tiled=True
        ).astype(jnp.float32),
        lax.psum_scatter(
            grad_outer.astype(jnp.bfloat16), "fsdp", scatter_dimension=0, tiled=True
        ).astype(jnp.float32),
    )
    (
        total_gain_one,
        total_gain_two,
        total_gain_three,
        total_bias,
        total_query,
        total_key,
        total_value,
        total_output,
        total_cross_query,
        total_cross_key,
        total_cross_value,
        total_cross_output,
        total_inner,
        total_outer,
    ) = lax.psum(
        (
            shard_gain_one,
            shard_gain_two,
            shard_gain_three,
            shard_bias,
            shard_query,
            shard_key,
            shard_value,
            shard_output,
            shard_cross_query,
            shard_cross_key,
            shard_cross_value,
            shard_cross_output,
            shard_inner,
            shard_outer,
        ),
        "ctx",
    )
    return (
        layer_output,
        grad_tokens,
        grad_memory,
        total_gain_one,
        total_gain_two,
        total_gain_three,
        total_bias,
        total_query,
        total_key,
        total_value,
        total_output,
        total_cross_query,
        total_cross_key,
        total_cross_value,
        total_cross_output,
        total_inner,
        total_outer,
    )


MESH = pl.DeviceIdType.MESH
WAYS = 4


class Place:
    def __init__(self, peers):
        self.depth = peers // 2
        c, f = lax.axis_index("ctx"), lax.axis_index("fsdp")
        self.c, self.f = c, f
        self.a, self.b, self.x, self.k = c // 2, c % 2, f // 2, f % 2
        self.core = (c, self.x * 2 + 1 - self.k)
        self.across = (c, (1 - self.x) * 2 + self.k)
        self.beside = (self.a * 2 + 1 - self.b, f)

    def ahead(self, d):
        return lax.rem(self.a + d, self.depth)

    def behind(self, d):
        return lax.rem(self.a + self.depth - d, self.depth)

    def column(self, a):
        return (a * 2 + self.b, self.f)

    def group(self, d):
        return (self.c, lax.rem(self.f + d, WAYS))


def greet(targets):
    barrier = pltpu.get_barrier_semaphore()
    for target in targets:
        pl.semaphore_signal(barrier, inc=1, device_id=target, device_id_type=MESH)
    pl.semaphore_wait(barrier, len(targets))


def remote(src, dst, sems, index, target):
    return pltpu.make_async_remote_copy(
        src_ref=src,
        dst_ref=dst,
        send_sem=sems[0].at[index],
        recv_sem=sems[1].at[index],
        device_id=target,
        device_id_type=MESH,
    )


def apart(src, dst, sems, send_index, recv_index, target):
    return pltpu.make_async_remote_copy(
        src_ref=src,
        dst_ref=dst,
        send_sem=sems[0].at[send_index],
        recv_sem=sems[1].at[recv_index],
        device_id=target,
        device_id_type=MESH,
    )


def line_sems(depth, chunks):
    return sems((2 * depth + 2) * chunks)


def sems(count):
    return [pltpu.SemaphoreType.DMA((count,)), pltpu.SemaphoreType.DMA((count,))]


class Wire:
    def __init__(self, peers):
        self.at = Place(peers)
        self.depth = self.at.depth
        self.sent = []

    def go(self, copy):
        copy.start()
        self.sent.append((None, copy.wait_send))

    def go_if(self, condition, make):
        pl.when(condition)(lambda: make().start())
        self.sent.append((condition, lambda: make().wait_send()))

    def drain(self):
        for condition, wait in self.sent:
            if condition is None:
                wait()
            else:
                pl.when(condition)(wait)

    def partners(self):
        at = self.at
        return (
            [at.group(d) for d in range(1, WAYS)]
            + [at.beside]
            + [at.column(at.ahead(d)) for d in range(1, self.depth)]
        )

    def near(self, step):
        a, last = self.at.a, self.depth - 1
        low = jnp.where(step - 1 < a, step - 1, step)
        mirrored = jnp.where(step - 1 < last - a, step - 1, step)
        return jnp.where(2 * a < last, low, last - mirrored)

    def piece(self, buf, c, chunk, chunks):
        if len(buf.shape) == 3:
            size = buf.shape[1] // chunks
            return buf.at[c, chunk * size : (chunk + 1) * size]
        rows = buf.shape[0] // (2 * self.depth)
        size = rows // chunks
        return buf.at[pl.ds(pl.multiple_of(c * rows + chunk * size, size), size)]

    def slot(self, buf, c):
        return self.piece(buf, c, 0, 1)

    def pass_on(self, src, dst, sem, up, beside, own, chunk, chunks, origin):
        at, a = self.at, self.at.a
        line = origin * chunks + chunk
        side = (self.depth + origin) * chunks + chunk
        for step in (1, -1):
            if own or (step == 1) == up:
                first = (2 * self.depth + (step == 1)) * chunks + chunk if own else line
                self.go_if(
                    a + 1 < self.depth if step == 1 else a > 0,
                    lambda step=step, first=first: apart(src, dst, sem, first, line, at.column(a + step)),
                )
        if beside:
            self.go(apart(src, dst, sem, side, side, at.beside))

    def spread(self, src, buf, sem, chunks):
        at = self.at
        size = src.shape[0] // chunks
        for chunk in range(chunks):
            part = src.at[chunk * size : (chunk + 1) * size]
            self.pass_on(part, self.piece(buf, at.c, chunk, chunks), sem, True, True, True, chunk, chunks, at.a)

    def relay(self, gathered, step):
        at, depth = self.at, self.depth
        for buf, sem, chunks in gathered:
            for chunk in range(chunks):
                for up in (True, False):
                    origin = at.a - step if up else at.a + step
                    inside = origin >= 0 if up else origin < depth
                    onward = at.a + 1 < depth if up else at.a > 0
                    line = origin * chunks + chunk
                    side = (depth + origin) * chunks + chunk
                    spot = lambda: self.piece(buf, origin * 2 + at.b, chunk, chunks)
                    target = at.column(at.a + 1 if up else at.a - 1)

                    def forward(_):
                        return apart(spot(), spot(), sem, line, line, target)

                    def sideways(_):
                        return apart(spot(), spot(), sem, side, side, at.beside)

                    @pl.when(inside)
                    def _():
                        apart(spot(), spot(), sem, line, line, at.beside).wait_recv()
                        sideways(0).start()
                        pl.when(onward)(lambda: forward(0).start())

                    self.sent.append((inside, self.later(buf, sem, side, origin, chunk, chunks, at.beside)))
                    self.sent.append(
                        (jnp.logical_and(inside, onward), self.later(buf, sem, line, origin, chunk, chunks, target))
                    )

    def later(self, buf, sem, index, origin, chunk, chunks, target):
        def wait():
            spot = self.piece(buf, origin * 2 + self.at.b, chunk, chunks)
            apart(spot, spot, sem, index, index, target).wait_send()

        return wait

    def from_beside(self, gathered, a):
        for buf, sem, chunks in gathered:
            for chunk in range(chunks):
                spot = self.piece(buf, a * 2 + 1 - self.at.b, chunk, chunks)
                index = (self.depth + a) * chunks + chunk
                apart(spot, spot, sem, index, index, self.at.beside).wait_recv()

    def shard(self, full, f):
        quarter = full.shape[0] // WAYS
        return full.at[pl.ds(pl.multiple_of(f * quarter, quarter), quarter)]

    def weight_start(self, src, full, sem, i):
        at = self.at
        slot = self.shard(full, at.f)
        slot[...] = src[...]
        self.go(remote(src, slot, sem, 3 * i, at.across))
        self.go(remote(src, slot, sem, 3 * i + 1, at.core))

    def weight_relay(self, full, sem, i):
        at = self.at
        slot = self.shard(full, (1 - at.x) * 2 + at.k)
        remote(slot, slot, sem, 3 * i, at.across).wait_recv()
        self.go(remote(slot, slot, sem, 3 * i + 2, at.core))

    def weight_ready(self, full, sem, i):
        at = self.at
        slot = self.shard(full, at.x * 2 + 1 - at.k)
        remote(slot, slot, sem, 3 * i + 1, at.core).wait_recv()
        slot = self.shard(full, (1 - at.x) * 2 + 1 - at.k)
        remote(slot, slot, sem, 3 * i + 2, at.core).wait_recv()


class Summed:
    def __init__(self, wire, source, out, rc, sd, rd, sem_c, sem_d, sem_e, sem_f):
        self.wire, self.source, self.out, self.rc, self.sd, self.rd = wire, source, out, rc, sd, rd
        self.sem_c, self.sem_d, self.sem_e, self.sem_f = sem_c, sem_d, sem_e, sem_f
        at = wire.at
        half, part = out.shape[2] // 2, out.shape[1] // wire.depth
        columns = lambda b: pl.ds(pl.multiple_of(b * half, LANES), half)
        self.mine, self.theirs = columns(at.b), columns(1 - at.b)
        self.rows = lambda a: pl.ds(pl.multiple_of(a * part, part), part)

    def stage_c(self, j):
        at = self.wire.at
        self.wire.go(remote(self.source(j).at[:, self.theirs], self.rc.at[j], self.sem_c, j, at.beside))

    def stage_d(self, j):
        at, depth = self.wire.at, self.wire.depth
        remote(self.rc.at[j], self.rc.at[j], self.sem_c, j, at.beside).wait_recv()
        value = self.source(j)[:, self.mine].astype(F32) + self.rc[j].astype(F32)
        self.sd[j] = value.astype(BF16)
        for d in range(1, depth):
            spot = self.rd.at[j, self.rows(at.a)]
            target = at.ahead(d)
            self.wire.go(remote(self.sd.at[j, self.rows(target)], spot, self.sem_d, j * depth + d, at.column(target)))

    def stage_e(self, j):
        at, depth = self.wire.at, self.wire.depth
        value = self.sd[j, self.rows(at.a), :].astype(F32)
        for d in range(1, depth):
            spot = self.rd.at[j, self.rows(at.behind(d))]
            remote(spot, spot, self.sem_d, j * depth + d, at.column(at.behind(d))).wait_recv()
            value += spot[...].astype(F32)
        spot = self.out.at[j, self.rows(at.a), self.mine]
        spot[...] = value.astype(BF16)
        for d in range(1, depth):
            self.wire.go(remote(spot, spot, self.sem_e, j * depth + d, at.column(at.ahead(d))))

    def stage_f(self, j):
        at, depth = self.wire.at, self.wire.depth
        for d in range(1, depth):
            spot = self.out.at[j, self.rows(at.behind(d)), self.mine]
            remote(spot, spot, self.sem_e, j * depth + d, at.column(at.behind(d))).wait_recv()
        spot = self.out.at[j, :, self.mine]
        self.wire.go(remote(spot, spot, self.sem_f, j, at.beside))

    def stage_g(self, j):
        spot = self.out.at[j, :, self.theirs]
        remote(spot, spot, self.sem_f, j, self.wire.at.beside).wait_recv()


def two_heads(x):
    return jnp.concatenate([half_mask(x, 0), half_mask(x, 1)], 0)


def ones_beside(x):
    ones = jnp.ones_like(x)
    return jnp.concatenate([two_heads(x), two_heads(ones)], 1)


def softmax_pair(scores, v, stats, p):
    weights, tops = [], []
    for s in scores:
        m = jnp.max(s, axis=1, keepdims=True)
        weights.append(jnp.exp(s - m).astype(BF16))
        tops.append(m)
    both = nn(jnp.concatenate(weights, 1), ones_beside(v))
    sums = both[:, LANES:]
    logs = jnp.log(sums)
    turned = pltpu.roll(logs, HEAD_DIM, 1)
    lane = lax.broadcasted_iota(jnp.int32, logs.shape, 1)
    inside = lane < HEAD_DIM
    stats = jnp.where(lane == 2 * p, tops[0] + jnp.where(inside, logs, turned), stats)
    stats = jnp.where(lane == 2 * p + 1, tops[1] + jnp.where(inside, turned, logs), stats)
    return both[:, :LANES] / sums, stats


def fill_inverse(order, inv):
    count = order.shape[0]
    for p in range(count):
        slot = jnp.int32(0)
        for s in range(count):
            slot = jnp.where(order[s] == p, s, slot)
        inv[p] = slot


def own_facts(order, c, count, length):
    per = (BLOCK // PIECE).bit_length() - 1
    facts = []
    for i in range(count):
        n = order[c * count + i]
        start = lax.shift_right_logical(n, per) * BLOCK
        facts.append((n, n & 1, length // LANES - 1 - lax.shift_right_logical(n, 1), start + BLOCK, start))
    return facts


def own_column(facts, i):
    return jnp.concatenate([jnp.full((PIECE, 1), fact[i], jnp.int32) for fact in facts], 0)


def own_bias(table, lines, own, out, low, high):
    full = table.shape[1]
    rows, length = out.shape[1], out.shape[2]

    def head(h, c):
        base = shear(pltpu.roll(jnp.broadcast_to(table[pl.ds(h, 1), :], (8, full)), 1, 1), 1)
        lines[0] = base
        lines[1] = pltpu.roll(base, PIECE, 1)
        for i in range(rows // PIECE):
            window = lines[own[i][1], :, pl.ds(own[i][2] * LANES, length + LANES)]
            for g in range(0, PIECE // 8, 2):
                both = [pltpu.roll(window, 8 * k, 1) if k else window for k in (g, g + 1)]
                both = jnp.concatenate(both, 0)[:, LANES:]
                out[h, i * PIECE + 8 * g : i * PIECE + 8 * g + 16, :] = both.astype(BF16)
        return c

    lax.fori_loop(low, high, head, 0)


def diagonal_sums(block):
    rows, length = block.shape
    wide = jnp.concatenate([block, jnp.zeros((rows, LANES), F32)], axis=1)
    total = pltpu.roll(wide[0:8], LANES, 1)
    for g in range(1, rows // 8):
        total += pltpu.roll(wide[8 * g : 8 * g + 8], LANES - 8 * g, 1)
    return jnp.sum(shear(total, -1), axis=0, keepdims=True)


N_FRONT = 5
CHUNKS = 2
N_GAINS = 16


def front_kernel(peers, *refs):
    order, tok, gain1, gain2, gain3, bias_shard, buckets = refs[:7]
    shards_in = refs[7 : 7 + N_FRONT]
    (w_self_out, w_rest_out, gains, ahead_out, table_out, q_out, k_out, v_out, a1, o1, h1, a2, q2, lse) = refs[7 + N_FRONT : 21 + N_FRONT]
    (tok_all, pack, pack_all, marks, marks_all, table, lines, q_own, w_self, w_rest, ahead, q_nat, k_nat, v_nat, s_keep, inv, *sem) = refs[21 + N_FRONT :]
    weights = [w_self.at[i] for i in range(3)] + [w_rest.at[i] for i in range(N_FRONT - 3)]
    sem_t, sem_w, sem_p, sem_m = sem[0:2], sem[2:4], sem[4:6], sem[6:8]
    wire = Wire(peers)
    at, depth = wire.at, wire.depth
    rows = tok.shape[0]
    length = peers * rows
    mine, per = rows // PIECE, BLOCK // PIECE
    kept = []

    def keep(i, src, dst):
        copy = pltpu.make_async_copy(src, dst, s_keep.at[i])
        copy.start()
        kept.append(copy)

    quarter = gain1.shape[1]
    spot = lax.broadcasted_iota(jnp.int32, (quarter, D), 0) + at.f * quarter
    place = jnp.where(lax.broadcasted_iota(jnp.int32, (quarter, D), 1) == spot, 1.0, 0.0).astype(BF16)
    pack[...] = jnp.zeros_like(pack)
    for i, gain in enumerate((gain1, gain2, gain3)):
        pack[i : i + 1, :] = nn(gain[...], place).astype(BF16)
    eighth, heads = bias_shard.shape
    spot = lax.broadcasted_iota(jnp.int32, (BUCKETS, eighth), 1) + at.f * eighth
    place = jnp.where(lax.broadcasted_iota(jnp.int32, (BUCKETS, eighth), 0) == spot, 1.0, 0.0).astype(BF16)
    marks[...] = jnp.zeros_like(marks)
    marks[:, 0:heads] = nn(place, bias_shard[...]).astype(BF16)
    greet(wire.partners())
    for d in range(1, WAYS):
        wire.go(remote(pack, pack_all.at[at.f], sem_p, d, at.group(d)))
        wire.go(remote(marks, marks_all.at[at.f], sem_m, d, at.group(d)))
    wire.spread(tok, tok_all, sem_t, CHUNKS)
    for i in range(3):
        wire.weight_start(shards_in[i], weights[i], sem_w, i)
    wire.slot(tok_all, at.c)[...] = tok[...]
    pack_all[at.f] = pack[...]
    marks_all[at.f] = marks[...]
    for d in range(1, WAYS):
        slot = pack_all.at[lax.rem(at.f + WAYS - d, WAYS)]
        remote(slot, slot, sem_p, d, at.group(WAYS - d)).wait_recv()
        slot = marks_all.at[lax.rem(at.f + WAYS - d, WAYS)]
        remote(slot, slot, sem_m, d, at.group(WAYS - d)).wait_recv()
    whole = lambda x: x[0].astype(F32) + x[1].astype(F32) + x[2].astype(F32) + x[3].astype(F32)
    fill_inverse(order, inv)
    own = own_facts(order, at.c, mine, length)
    gains[...] = whole(pack_all)[0:8, :]
    bias = whole(marks_all).astype(BF16)
    bucket = lax.broadcasted_iota(jnp.int32, (bias.shape[0], 2 * length), 0)
    hot = jnp.where(buckets[...] == bucket, 1.0, 0.0).astype(BF16)
    table[0] = tn(bias, hot)[0:16, :]
    shifted = pltpu.roll(table[0], 1, 1).astype(BF16)
    row = lax.broadcasted_iota(jnp.int32, (LANES, LANES), 0)
    mirror = jnp.where(row + lax.broadcasted_iota(jnp.int32, (LANES, LANES), 1) == LANES - 1, 1.0, 0.0).astype(BF16)
    tiles = 2 * length // LANES
    for t in range(tiles):
        u = tiles - 1 - t
        table_out[:, t * LANES : (t + 1) * LANES] = nn(shifted[:, u * LANES : (u + 1) * LANES], mirror)

    gathered = [(tok_all, sem_t, CHUNKS)]
    share = HEADS // (depth - 1)
    for step in range(1, depth):
        wire.relay(gathered, step)
        own_bias(table.at[0], lines, own, ahead, (step - 1) * share, step * share)
    keep(3, ahead, ahead_out)
    for i in range(3):
        wire.weight_relay(weights[i], sem_w, i)
    for i in range(3, N_FRONT):
        wire.weight_start(shards_in[i], weights[i], sem_w, i)
    first = gains[0:1, :]
    a1[...] = normed(tok[...].astype(F32), first).astype(BF16)
    for i in range(3):
        wire.weight_ready(weights[i], sem_w, i)
    keep(0, w_self, w_self_out)
    for a in range(depth):
        wire.from_beside(gathered, a)

    def tile(t, c):
        parts = []
        for i in range(per):
            parts.append(tok_all[pl.ds(inv[t * per + i] * PIECE, PIECE), :])
        a = normed(jnp.concatenate(parts, 0).astype(F32), first).astype(BF16)
        dst = pl.ds(pl.multiple_of(t * BLOCK, BLOCK), BLOCK)
        for j, out in enumerate((q_nat, k_nat, v_nat)):
            out[dst, :] = nn(a, weights[j][...]).astype(BF16)
        return c

    lax.fori_loop(0, length // BLOCK, tile, 0)
    for i in range(mine):
        q_own[i * PIECE : (i + 1) * PIECE, :] = q_nat[pl.ds(own[i][0] * PIECE, PIECE), :]
    for i, (src, dst) in enumerate(((q_nat, q_out), (k_nat, k_out), (v_nat, v_out))):
        keep(5 + i, src, dst)
    wire.weight_relay(weights[3], sem_w, 3)
    lane = lax.broadcasted_iota(jnp.int32, (rows, length), 1)
    visible = lane < own_column(own, 3)

    def pair(p, stats):
        sl = lanes_of(p)
        s = nt(q_own[:, sl], two_heads(k_nat[:, sl]))
        scores = []
        for half in range(2):
            biased = s[:, half * length : (half + 1) * length] + ahead[2 * p + half].astype(F32)
            scores.append(jnp.where(visible, biased, NEGATIVE))
        value, stats = softmax_pair(scores, v_nat[:, sl], stats, p)
        o1[:, sl] = value.astype(BF16)
        return stats

    stats = lax.fori_loop(0, PAIRS // 2, pair, jnp.zeros((rows, LANES), F32), unroll=True)
    wire.weight_relay(weights[4], sem_w, 4)
    lse[...] = lax.fori_loop(PAIRS // 2, PAIRS, pair, stats, unroll=True)
    wire.weight_ready(weights[3], sem_w, 3)
    h = tok[...].astype(F32) + nn(o1[...], weights[3][...])
    h1[...] = h
    a = normed(h, gains[1:2, :]).astype(BF16)
    a2[...] = a
    wire.weight_ready(weights[4], sem_w, 4)
    q2[...] = nn(a, weights[4][...]).astype(BF16)
    keep(1, w_rest, w_rest_out)
    for copy in kept:
        copy.wait()
    wire.drain()


def front(peers, order, tok, gain_shards, bias_shard, buckets, weight_shards):
    rows = tok.shape[0]
    length, depth = peers * rows, peers // 2
    block = lambda dtype: sds((rows, D), dtype)
    return pl.pallas_call(
        functools.partial(front_kernel, peers),
        name="front",
        out_shape=[sds((3, D, D), BF16), sds((N_FRONT - 3, D, D), BF16), sds((8, D), F32)]
        + [sds((HEADS, rows, length), BF16), sds((16, 2 * length), F32)]
        + [sds((length, D), BF16)] * 3
        + [block(BF16), block(BF16), block(F32), block(BF16), block(BF16), sds((rows, LANES), F32)],
        in_specs=[smem_spec()] + [full_spec()] * (6 + N_FRONT),
        out_specs=[any_spec() if i in (0, 1, 3, 5, 6, 7) else full_spec() for i in range(14)],
        scratch_shapes=[
            pltpu.VMEM((length, D), BF16),
            pltpu.VMEM((N_GAINS, D), BF16),
            pltpu.VMEM((WAYS, N_GAINS, D), BF16),
            pltpu.VMEM((BUCKETS, LANES), BF16),
            pltpu.VMEM((WAYS, BUCKETS, LANES), BF16),
            pltpu.VMEM((1, 16, 2 * length), F32),
            pltpu.VMEM((2, 8, 2 * length), F32),
            pltpu.VMEM((rows, D), BF16),
            pltpu.VMEM((3, D, D), BF16),
            pltpu.VMEM((N_FRONT - 3, D, D), BF16),
        ]
        + [pltpu.VMEM((HEADS, rows, length), BF16)]
        + [pltpu.VMEM((length, D), BF16)] * 3
        + [pltpu.SemaphoreType.DMA((8,)), pltpu.SMEM(order.shape, jnp.int32)]
        + line_sems(depth, CHUNKS) + sems(3 * N_FRONT) + sems(WAYS) + sems(WAYS),
        compiler_params=pltpu.CompilerParams(collective_id=1, has_side_effects=True, vmem_limit_bytes=VMEM_LIMIT),
    )(order, tok, *gain_shards, bias_shard, buckets, *weight_shards)


STAT = 16


def split(x):
    high = x.astype(BF16)
    return high, (x - high.astype(F32)).astype(BF16)


def head_matrix(rows):
    row = lax.broadcasted_iota(jnp.int32, (rows, D), 0)
    lane = lax.broadcasted_iota(jnp.int32, (rows, D), 1)
    return jnp.where(lane // HEAD_DIM == row, 1.0, 0.0).astype(BF16)


def per_head_sums(x, heads):
    high, low = split(x)
    return nt(heads, high) + nt(heads, low)


def blend(parts, stats, heads):
    top = functools.reduce(jnp.maximum, stats)
    shares = [jnp.exp(s - top) for s in stats]
    total = functools.reduce(jnp.add, shares)
    value = 0.0
    for part, share in zip(parts, shares):
        high, low = split(share / total)
        value = value + (tn(high, heads) + tn(low, heads)) * part.astype(F32)
    return value, top + jnp.log(total)


def norm_back_rows(x, gain, dy):
    r = lax.rsqrt(jnp.mean(x * x, axis=-1, keepdims=True) + EPSILON)
    gdy = gain * dy
    dx = r * gdy - x * (r * r * r) * jnp.mean(x * gdy, axis=-1, keepdims=True)
    return dx, jnp.sum(dy * x * r, axis=0, keepdims=True)


def round_trip(wire, gathered, fillers, compute, ship, fold, after):
    at = wire.at
    b = at.b
    first, second, third = [wire.near(step) for step in (1, 2, 3)]
    for step in range(1, wire.depth):
        fillers[step - 1]()
        wire.relay(gathered, step)
    for filler in fillers[wire.depth - 1 :]:
        filler()
    wire.from_beside(gathered, at.a)
    compute(at.c, at.a * 2 + 1 - b)
    ship(at.a)
    after[0]()
    wire.from_beside(gathered, third)
    compute(third * 2 + 1 - b, third * 2 + b)
    ship(third)
    after[1]()
    wire.from_beside(gathered, second)
    compute(second * 2 + 1 - b, second * 2 + b)
    ship(second)
    after[2]()
    fold(third)
    wire.from_beside(gathered, first)
    compute(first * 2 + 1 - b, first * 2 + b)
    ship(first)
    after[3]()
    fold(second)
    fold(first)


def middle_kernel(peers, *refs):
    (lengths, q2, h1, o1, lse1, w_rest, gains, mem, grad, ck_shard, cv_shard, co_shard, in_shard, w_out) = refs[:14]
    (o2_out, branch2_out, dq2_out, dk2_out, dv2_out, branch1_out, dh1_out, do1_out, stat1_out, in_all, out_sum, layer_out, gmem_out, small) = refs[14:28]
    (q_all, k2, v2, part, part_lse, from_b, from_b_lse, joined, joined_lse, from_z, from_z_lse,
     w_ck, w_cv, w_co, w_in, g_all, a3_all, dact, act, dpre, da3_send, da3_in, out_send, out_in,
     do_all, stat_all, stat_own, dk_acc, dv_acc, dqp, dq_b, dq_j, dq_z, mask, g_in, g_out, rc, sd, rd, *sem) = refs[28:]
    sem = [sem[2 * i : 2 * i + 2] for i in range(len(sem) // 2)]
    (s_q, s_w, s_in, s_g, s_y, s_yl, s_z, s_zl, s_a3, s_da3, s_out, s_do, s_st, s_dy, s_dz, s_gi, *s_sum) = sem
    wire = Wire(peers)
    at, depth = wire.at, wire.depth
    rows = q2.shape[0]
    heads = head_matrix(STAT)
    quarter = co_shard.shape[0]
    units = w_out.shape[0]
    block = lambda f: pl.ds(pl.multiple_of(f * rows, rows), rows)
    greet(wire.partners())
    wire.spread(q2, q_all, s_q, CHUNKS)
    wire.weight_start(ck_shard, w_ck, s_w, 1)
    wire.weight_start(cv_shard, w_cv, s_w, 2)
    q_all[at.c] = q2[...]
    g_all[block(at.f), :] = grad[...]
    wire.shard(w_in, at.f)[...] = in_shard[:, pl.ds(pl.multiple_of(at.f * units, LANES), units)]

    slots, passages = mem.shape[0], lengths.shape[1]
    log = PLEN.bit_length() - 1

    def hidden(shape, axis):
        slot = lax.broadcasted_iota(jnp.int32, shape, axis) + at.c * slots
        first = at.c * slots // PLEN
        taken = jnp.zeros(shape, jnp.int32)
        for i in range(slots // PLEN + 2):
            size = lengths[0, jnp.minimum(first + i, passages - 1)]
            taken = jnp.where(lax.shift_right_logical(slot, log) == first + i, size, taken)
        return jnp.where((slot & (PLEN - 1)) < taken, 0.0, NEGATIVE)

    def fill_mask():
        mask[...] = hidden(mask.shape, 0)

    def next_weights():
        wire.weight_relay(w_ck, s_w, 1)
        wire.weight_start(co_shard, w_co, s_w, 0)

    def project_memory():
        wire.weight_relay(w_cv, s_w, 2)
        feed_forward_operands()
        wire.weight_ready(w_ck, s_w, 1)
        k2[...] = nn(mem[...], w_ck[...]).astype(BF16)
        wire.weight_ready(w_cv, s_w, 2)
        v2[...] = nn(mem[...], w_cv[...]).astype(BF16)

    def feed_forward_operands():
        for d in range(1, WAYS):
            f = lax.rem(at.f + d, WAYS)
            part = in_shard.at[:, pl.ds(pl.multiple_of(f * units, LANES), units)]
            wire.go(remote(grad, g_all.at[block(at.f)], s_g, d, at.group(d)))
            wire.go(remote(part, wire.shard(w_in, at.f), s_in, d, at.group(d)))

    mask_row = hidden((1, slots), 1)

    def attend(c1, c2):
        def pair(p, stats):
            sl = lanes_of(p)
            q = jnp.concatenate([q_all[c1, :, sl], q_all[c2, :, sl]], 0)
            s = nt(q, two_heads(k2[:, sl]))
            value, stats = softmax_pair([s[:, :slots] + mask_row, s[:, slots:] + mask_row], v2[:, sl], stats, p)
            part[c1, :, sl] = value[:rows].astype(BF16)
            part[c2, :, sl] = value[rows:].astype(BF16)
            return stats

        stats = lax.fori_loop(0, PAIRS, pair, jnp.zeros((2 * rows, LANES), F32), unroll=True)
        part_lse[c1] = stats[:rows].T[:STAT]
        part_lse[c2] = stats[rows:].T[:STAT]

    def ship_part(a):
        other = a * 2 + 1 - at.b
        wire.go(remote(part.at[other], from_b.at[a], s_y, a, at.beside))
        wire.go(remote(part_lse.at[other], from_b_lse.at[a], s_yl, a, at.beside))

    def blend_column(a):
        remote(from_b.at[a], from_b.at[a], s_y, a, at.beside).wait_recv()
        remote(from_b_lse.at[a], from_b_lse.at[a], s_yl, a, at.beside).wait_recv()
        c = a * 2 + at.b
        return blend([part[c], from_b[a]], [part_lse[c], from_b_lse[a]], heads)

    def fold_part(a):
        value, stat = blend_column(a)
        joined[a] = value.astype(BF16)
        joined_lse[a] = stat
        wire.go(remote(joined.at[a], from_z.at[at.a], s_z, at.a, at.column(a)))
        wire.go(remote(joined_lse.at[a], from_z_lse.at[at.a], s_zl, at.a, at.column(a)))

    round_trip(wire, [(q_all, s_q, CHUNKS)], [fill_mask, lambda: None, next_weights, project_memory], attend, ship_part, fold_part, [lambda: None] * 4)
    wire.weight_relay(w_co, s_w, 0)
    value, stat = blend_column(at.a)
    parts, stats = [value], [stat]
    for step in range(1, depth):
        a = wire.near(step)
        remote(from_z.at[a], from_z.at[a], s_z, a, at.column(a)).wait_recv()
        remote(from_z_lse.at[a], from_z_lse.at[a], s_zl, a, at.column(a)).wait_recv()
        parts.append(from_z[a])
        stats.append(from_z_lse[a])
    out2, lse2 = blend(parts, stats, heads)
    o2 = out2.astype(BF16)
    o2_out[...] = o2
    wire.weight_ready(w_co, s_w, 0)
    h2 = h1[...] + nn(o2, w_co[...])
    a3 = normed(h2, gains[2:3, :]).astype(BF16)
    a3_all[block(at.f), :] = a3
    for d in range(1, WAYS):
        spot = a3_all.at[block(at.f)]
        wire.go(remote(spot, spot, s_a3, d, at.group(d)))

    def arrive(buf, sem, size):
        for d in range(1, WAYS):
            f = lax.rem(at.f + WAYS - d, WAYS)
            spot = buf.at[pl.ds(pl.multiple_of(f * size, size), size)]
            remote(spot, spot, sem, d, at.group(WAYS - d)).wait_recv()

    arrive(g_all, s_g, rows)
    tiles = [slice(2 * rows * t, 2 * rows * (t + 1)) for t in range(WAYS // 2)]
    for rs in tiles:
        dact[rs, :] = nt(g_all[rs, :], w_out[...])
    arrive(w_in, s_in, quarter)
    arrive(a3_all, s_a3, rows)
    for rs in tiles:
        pre = nn(a3_all[rs, :], w_in[...])
        square = pre * pre
        t = jnp.tanh(0.7978845608028654 * (pre + 0.044715 * pre * square))
        act[rs, :] = (0.5 * pre * (1.0 + t)).astype(BF16)
        slope = 0.5 * (1.0 + t) + 0.5 * pre * (1.0 - t * t) * (0.7978845608028654 * (1.0 + 3 * 0.044715 * square))
        d = (dact[rs, :] * slope).astype(BF16)
        dpre[rs, :] = d
        da3_send[rs, :] = nt(d, w_in[...]).astype(BF16)

    def exchange(src, dst, sem):
        for d in range(1, WAYS):
            f = lax.rem(at.f + d, WAYS)
            wire.go(remote(src.at[block(f)], dst.at[block(at.f)], sem, d, at.group(d)))

    def collect(src, dst, sem):
        arrive(dst, sem, rows)
        value = src[block(at.f), :].astype(F32)
        for d in range(1, WAYS):
            value += dst[block(lax.rem(at.f + WAYS - d, WAYS)), :].astype(F32)
        return value

    exchange(da3_send, da3_in, s_da3)
    sums = Summed(wire, lambda j: g_out.at[j * quarter : (j + 1) * quarter], out_sum, rc, sd, rd, *s_sum)
    g_out[...] = tn(act[...], g_all[...]).astype(BF16)
    for j in range(WAYS):
        sums.stage_c(j)
    for rs in tiles:
        out_send[rs, :] = nn(act[rs, :], w_out[...]).astype(BF16)
    sums.stage_d(0)
    sums.stage_d(1)
    da3 = collect(da3_send, da3_in, s_da3)
    dx, dgain = norm_back_rows(h2, gains[2:3, :], da3)
    small[...] = jnp.zeros_like(small)
    small[1:2, :] = dgain
    dh2 = grad[...].astype(F32) + dx
    branch2 = dh2.astype(BF16)
    branch2_out[...] = branch2
    do2 = nt(branch2, w_co[...]).astype(BF16)
    do_all[at.c] = do2
    stat_own[0] = jnp.concatenate([lse2, per_head_sums(do2.astype(F32) * out2, heads)], 0)
    stat_all[at.c] = stat_own[0]
    wire.spread(do_all.at[at.c], do_all, s_do, CHUNKS)
    wire.spread(stat_own.at[0], stat_all, s_st, 1)
    exchange(out_send, out_in, s_out)

    def clear():
        dk_acc[...] = jnp.zeros_like(dk_acc)
        dv_acc[...] = jnp.zeros_like(dv_acc)

    def finish_output():
        layer_out[...] = (h2 + collect(out_send, out_in, s_out)).astype(BF16)

    def stages(stage, *js):
        return lambda: [stage(j) for j in js]

    def in_grads():
        g_in[...] = tn(a3_all[...], dpre[...]).astype(BF16)
        rows_of = lambda f: pl.ds(pl.multiple_of(f * quarter, quarter), quarter)
        in_all[at.f] = g_in[rows_of(at.f), :]
        for d in range(1, WAYS):
            f = lax.rem(at.f + d, WAYS)
            wire.go(remote(g_in.at[rows_of(f)], in_all.at[at.f], s_gi, d, at.group(d)))

    def attend_back(c1, c2):
        def pair(p, carry):
            sl = lanes_of(p)
            q = jnp.concatenate([q_all[c1, :, sl], q_all[c2, :, sl]], 0)
            do = jnp.concatenate([do_all[c1, :, sl], do_all[c2, :, sl]], 0)
            kk = two_heads(k2[:, sl])
            s = nt(kk, q)
            d = nt(two_heads(v2[:, sl]), do)
            line = lambda i: jnp.concatenate([stat_all[c1, pl.ds(i, 1), :], stat_all[c2, pl.ds(i, 1), :]], 1)
            weights, slopes = [], []
            for half in range(2):
                h, hs = 2 * p + half, slice(half * slots, (half + 1) * slots)
                e = jnp.exp(s[hs] + mask[...] - line(h))
                weights.append(e.astype(BF16))
                slopes.append((e * (d[hs] - line(STAT + h))).astype(BF16))
            dv_acc[:, sl] += nn(jnp.concatenate(weights, 1), two_heads(do))
            dk_acc[:, sl] += nn(jnp.concatenate(slopes, 1), two_heads(q))
            dq = tn(kk, jnp.concatenate(slopes, 0)).T
            dqp[c1, :, sl] = dq[:rows].astype(BF16)
            dqp[c2, :, sl] = dq[rows:].astype(BF16)
            return carry

        lax.fori_loop(0, PAIRS, pair, 0, unroll=True)

    def ship_dq(a):
        wire.go(remote(dqp.at[a * 2 + 1 - at.b], dq_b.at[a], s_dy, a, at.beside))

    def column_dq(a):
        remote(dq_b.at[a], dq_b.at[a], s_dy, a, at.beside).wait_recv()
        return dqp[a * 2 + at.b].astype(F32) + dq_b[a].astype(F32)

    def fold_dq(a):
        dq_j[a] = column_dq(a).astype(BF16)
        wire.go(remote(dq_j.at[a], dq_z.at[at.a], s_dz, at.a, at.column(a)))

    round_trip(
        wire, [(do_all, s_do, CHUNKS), (stat_all, s_st, 1)], [clear, in_grads, lambda: None, stages(sums.stage_d, 2, 3)], attend_back, ship_dq, fold_dq,
        [stages(sums.stage_e, 0, 1), stages(sums.stage_e, 2, 3), stages(sums.stage_f, 0, 1), stages(sums.stage_f, 2, 3)],
    )
    dk2_out[...] = dk_acc[...].astype(BF16)
    dv2_out[...] = dv_acc[...].astype(BF16)
    value = column_dq(at.a)
    for step in range(1, depth):
        a = wire.near(step)
        remote(dq_z.at[a], dq_z.at[a], s_dz, a, at.column(a)).wait_recv()
        value += dq_z[a].astype(F32)
    dq2 = value.astype(BF16)
    dq2_out[...] = dq2
    dx, dgain = norm_back_rows(h1[...], gains[1:2, :], nt(dq2, w_rest[1]))
    small[0:1, :] = dgain
    dh1 = dh2 + dx
    dh1_out[...] = dh1
    branch1 = dh1.astype(BF16)
    branch1_out[...] = branch1
    do1 = nt(branch1, w_rest[0]).astype(BF16)
    do1_out[...] = do1
    stat_own[1] = jnp.concatenate([lse1[...].T[:STAT], per_head_sums(do1.astype(F32) * o1[...].astype(F32), heads)], 0)
    stat1_out[...] = stat_own[1]
    gmem_out[...] = (nt(dk2_out[...], w_ck[...]) + nt(dv2_out[...], w_cv[...])).astype(BF16)
    finish_output()
    for d in range(1, WAYS):
        spot = in_all.at[lax.rem(at.f + WAYS - d, WAYS)]
        remote(spot, spot, s_gi, d, at.group(WAYS - d)).wait_recv()
    for j in range(WAYS):
        sums.stage_g(j)
    wire.drain()


def middle(peers, lengths, q2, h1, o1, lse1, w_rest, gains, mem, grad, ck_shard, cv_shard, co_shard, in_shard, w_out):
    rows, slots = q2.shape[0], mem.shape[0]
    depth = peers // 2
    units = w_out.shape[0]
    row = lambda dtype: sds((rows, D), dtype)
    store = lambda n, dtype=BF16: pltpu.VMEM((n, rows, D), dtype)
    stat = lambda n, k=STAT: pltpu.VMEM((n, k, rows), F32)
    group = lambda width, dtype=BF16: pltpu.VMEM((WAYS * rows, width), dtype)
    return pl.pallas_call(
        functools.partial(middle_kernel, peers),
        name="middle",
        out_shape=[
            row(BF16),
            row(BF16),
            row(BF16),
            sds((slots, D), BF16),
            sds((slots, D), BF16),
            row(BF16),
            row(F32),
            row(BF16),
            sds((2 * STAT, rows), F32),
            sds((WAYS, D // WAYS, units), BF16),
            sds((WAYS, units // WAYS, D), BF16),
            row(BF16),
            sds((slots, D), BF16),
            sds((8, D), F32),
        ],
        in_specs=[smem_spec()] + [full_spec()] * 13,
        out_specs=[full_spec()] * 14,
        scratch_shapes=[
            store(peers), pltpu.VMEM((slots, D), BF16), pltpu.VMEM((slots, D), BF16),
            store(peers), stat(peers), store(depth), stat(depth), store(depth), stat(depth), store(depth), stat(depth),
            pltpu.VMEM((D, D), BF16), pltpu.VMEM((D, D), BF16), pltpu.VMEM((D, D), BF16), pltpu.VMEM((D, units), BF16),
            group(D), group(D), group(units, F32), group(units), group(units), group(D), group(D), group(D), group(D),
            store(peers), stat(peers, 2 * STAT), stat(2, 2 * STAT),
            pltpu.VMEM((slots, D), F32), pltpu.VMEM((slots, D), F32),
            store(peers), store(depth), store(depth), store(depth),
            pltpu.VMEM((slots, 2 * rows), F32),
            pltpu.VMEM((D, units), BF16),
            pltpu.VMEM((units, D), BF16),
        ]
        + [pltpu.VMEM((WAYS, units // WAYS, D // 2), BF16)] * 3
        + line_sems(depth, CHUNKS) + sems(9) + sems(WAYS) + sems(WAYS)
        + sems(depth) * 4
        + sems(WAYS) * 3
        + line_sems(depth, CHUNKS) + line_sems(depth, 1)
        + sems(depth) * 2
        + sems(WAYS) + sems(WAYS) + sems(WAYS * depth) + sems(WAYS * depth) + sems(WAYS),
        compiler_params=pltpu.CompilerParams(collective_id=2, has_side_effects=True, vmem_limit_bytes=VMEM_LIMIT),
    )(lengths, q2, h1, o1, lse1, w_rest, gains, mem, grad, ck_shard, cv_shard, co_shard, in_shard, w_out)


def tail_kernel(peers, *refs):
    (order, do1, stat1, q_far, k_far, v_far, bias_far, table_back, tok, w_self, gains, dh1, buckets,
     a1, o1, branch1, a2, dq2, mem, dk2, dv2, o2, branch2, in_all, small_mid) = refs[:25]
    out, small_out, grad_tokens = refs[25:28]
    (prod, ra, sb, rb, sc, rc, sd, rd, tiny, tiny_in, do_all, do_nat, stat_all, stat_rows, stat_t, q_own, k_own, v_own,
     dq1, dk1, dv1, diagonals, q_nat, k_nat, v_nat, bias, bias_back, lines, bucket_rows, inv, s_w, s_far, *sem) = refs[28:]
    sem = [sem[2 * i : 2 * i + 2] for i in range(len(sem) // 2)]
    s_do, s_st, sem_a, sem_b, sem_c, sem_d, sem_e, sem_f, sem_t = sem
    wire = Wire(peers)
    at, depth, go = wire.at, wire.depth, wire.go
    rows, length = do1.shape[0], q_far.shape[0]
    mine, pieces = rows // PIECE, length // PIECE
    total, quarter, wide = out.shape
    pairs = [(o2, branch2), (mem, dk2), (mem, dv2), (a2, dq2), (o1, branch1), (a1, dq1), (a1, dk1), (a1, dv1)]
    n_mats = len(pairs)
    shard_rows = lambda f: pl.ds(pl.multiple_of(f * quarter, quarter), quarter)

    def stage_a(i):
        left, right = pairs[i]
        prod[i] = tn(left[...], right[...]).astype(BF16)
        for x in range(2):
            go(remote(prod.at[i, shard_rows(x * 2 + 1 - at.k)], ra.at[i, x], sem_a, 2 * i + x, at.core))

    def stage_b(i):
        for x in range(2):
            remote(ra.at[i, x], ra.at[i, x], sem_a, 2 * i + x, at.core).wait_recv()
        x = 1 - at.x
        sb[i] = (prod[i, shard_rows(x * 2 + at.k), :].astype(F32) + ra[i, x].astype(F32)).astype(BF16)
        go(remote(sb.at[i], rb.at[i], sem_b, i, at.across))

    sums = Summed(wire, lambda j: sc.at[j] if j < n_mats else in_all.at[j - n_mats], out, rc, sd, rd, sem_c, sem_d, sem_e, sem_f)

    def stage_c(j):
        if j < n_mats:
            remote(sb.at[j], rb.at[j], sem_b, j, at.across).wait_recv()
            value = prod[j, shard_rows(at.f), :].astype(F32) + ra[j, at.x].astype(F32) + rb[j].astype(F32)
            sc[j] = value.astype(BF16)
        sums.stage_c(j)

    hops = [at.core, at.across, at.beside]

    def small_hop(t):
        if t:
            remote(tiny_in.at[t - 1], tiny_in.at[t - 1], sem_t, t - 1, hops[t - 1]).wait_recv()
            tiny[t] = tiny[t - 1] + tiny_in[t - 1]
        if t < 3:
            go(remote(tiny.at[t], tiny_in.at[t], sem_t, t, hops[t]))
        else:
            for d in range(1, depth):
                go(remote(tiny.at[3], tiny_in.at[2 + d], sem_t, 2 + d, at.column(at.ahead(d))))

    def small_end():
        value = tiny[3]
        for d in range(1, depth):
            remote(tiny_in.at[2 + d], tiny_in.at[2 + d], sem_t, 2 + d, at.column(at.behind(d))).wait_recv()
            value += tiny_in[2 + d]
        small_out[...] = value

    gathered = [(do_all, s_do, CHUNKS), (stat_all, s_st, 1)]

    def relay(step):
        wire.relay(gathered, step)

    def prepare():
        for copy in coming:
            copy.wait()
        for a in range(depth):
            wire.from_beside(gathered, a)
        for c in range(peers):
            spread = jnp.concatenate([stat_all[c], jnp.zeros((LANES - 2 * STAT, rows), F32)], 0)
            stat_rows[c * rows : (c + 1) * rows, :] = spread.T
        for i in range(pieces):
            do_nat[i * PIECE : (i + 1) * PIECE, :] = do_all[pl.ds(inv[i] * PIECE, PIECE), :]
        per = LANES // PIECE
        for t in range(length // LANES):
            lines = [stat_rows[pl.ds(inv[t * per + i] * PIECE, PIECE), :] for i in range(per)]
            stat_t[:, t * LANES : (t + 1) * LANES] = jnp.concatenate(lines, 0).T
        for i in range(mine):
            dst = slice(i * PIECE, (i + 1) * PIECE)
            src = pl.ds(own[i][0] * PIECE, PIECE)
            q_own[dst, :] = q_nat[src, :]
            k_own[dst, :] = k_nat[src, :]
            v_own[dst, :] = v_nat[src, :]

    def attend_back(low, high):
        lane = lax.broadcasted_iota(jnp.int32, (rows, length), 1)
        visible, seen = lane < own_column(own, 3), lane >= own_column(own, 4)
        stat_lane = lax.broadcasted_iota(jnp.int32, (rows, LANES), 1)
        stat_own = jnp.concatenate([stat1[...], jnp.zeros((LANES - 2 * STAT, rows), F32)], 0).T

        def column(h):
            return jnp.sum(jnp.where(stat_lane == h, stat_own, 0.0), axis=1, keepdims=True)

        def pair(p, c):
            sl = lanes_of(p)
            q, k, v, do = q_own[:, sl], k_nat[:, sl], v_nat[:, sl], do1[:, sl]
            kq, vq, qa, da = k_own[:, sl], v_own[:, sl], q_nat[:, sl], do_nat[:, sl]
            dq = dk = dv = jnp.zeros((rows, LANES), F32)
            for half in range(2):
                h = 2 * p + half
                km, vm = half_mask(k, half), half_mask(v, half)
                s = jnp.where(visible, nt(q, km) + bias[h].astype(F32), NEGATIVE)
                e = jnp.exp(s - column(h))
                ds = e * (nt(do, vm) - column(STAT + h))
                dq += nn(ds.astype(BF16), km)
                for i in range(mine):
                    diagonals[i, pl.ds(h, 1), :] = diagonal_sums(ds[i * PIECE : (i + 1) * PIECE, :])
                s = jnp.where(seen, nt(half_mask(kq, half), qa) + bias_back[h].astype(F32), NEGATIVE)
                e = jnp.exp(s - stat_t[pl.ds(h, 1), :])
                dv += nn(e.astype(BF16), half_mask(da, half))
                ds = e * (nt(half_mask(vq, half), da) - stat_t[pl.ds(STAT + h, 1), :])
                dk += nn(ds.astype(BF16), half_mask(qa, half))
            dq1[:, sl] = dq.astype(BF16)
            dk1[:, sl] = dk.astype(BF16)
            dv1[:, sl] = dv.astype(BF16)
            return c

        lax.fori_loop(low, high, pair, 0)

    def finish_tokens():
        weights_here.wait()
        da1 = nt(dq1[...], prod[5]) + nt(dk1[...], prod[6]) + nt(dv1[...], prod[7])
        dx, dgain = norm_back_rows(tok[...].astype(F32), gains[0:1, :], da1)
        grad_tokens[...] = (dh1[...] + dx).astype(BF16)
        sums = jnp.zeros((STAT, BUCKETS), F32)
        number = lax.broadcasted_iota(jnp.int32, (BUCKETS, length + LANES), 0)
        for i in range(mine):
            line = bucket_rows[pl.ds(own[i][1], 1), pl.ds(own[i][2] * LANES, length + LANES)]
            hot = jnp.where(line == number, 1.0, 0.0).astype(BF16)
            high, low = split(diagonals[i])
            sums += nt(high, hot) + nt(low, hot)
        tiny[0] = jnp.zeros(tiny.shape[1:], F32)
        tiny[0, 0:1, :] = dgain
        tiny[0, 1:3, :] = small_mid[0:2, :]
        tiny[0, 8 : 8 + STAT, 0:BUCKETS] = sums

    weights_here = pltpu.make_async_copy(w_self, prod.at[5:8], s_w)
    weights_here.start()
    coming = []
    for i, (src, dst) in enumerate(
        ((q_far, q_nat), (k_far, k_nat), (v_far, v_nat), (bias_far, bias))
    ):
        coming.append(pltpu.make_async_copy(src, dst, s_far.at[i]))
        coming[-1].start()
    own = own_facts(order, at.c, mine, length)
    greet(wire.partners())
    wire.spread(do1, do_all, s_do, CHUNKS)
    wire.spread(stat1, stat_all, s_st, 1)
    wire.slot(do_all, at.c)[...] = do1[...]
    stat_all[at.c] = stat1[...]
    fill_inverse(order, inv)
    diagonals[...] = jnp.zeros_like(diagonals)
    bucket_rows[0:1, :] = pltpu.roll(buckets[...], 1, 1)
    bucket_rows[1:2, :] = pltpu.roll(buckets[...], 1 + PIECE, 1)
    turns = [8, 9, 10, 11, 0, 1, 2, 3, 4, 5, 6, 7]
    lag = 1.5
    events = []
    for tick, j in enumerate(turns):
        if j < n_mats:
            events += [(tick - 2, 1, lambda j=j: stage_a(j)), (tick - 1, 2, lambda j=j: stage_b(j))]
        for k, stage in enumerate((stage_c, sums.stage_d, sums.stage_e, sums.stage_f, sums.stage_g)):
            events.append((tick + k * lag, 3 + k, lambda j=j, stage=stage: stage(j)))
    share = HEADS // 3
    for i in range(3):
        events.append((i + 0.3, 0, lambda i=i: own_bias(table_back, lines, own, bias_back, i * share, (i + 1) * share)))
        events.append((0.5 * i + 0.2, 0, lambda i=i: relay(i + 1)))
    events.append((2.4, 0, prepare))
    events += [(2.6 + 0.5 * i, 0, lambda i=i: attend_back(i, i + 1)) for i in range(PAIRS)]
    events.append((5.7, 0, finish_tokens))
    events += [(6.6 + t, 0, lambda t=t: small_hop(t)) for t in range(4)] + [(11.5, 0, small_end)]
    for _, _, event in sorted(events, key=lambda e: (e[0], -e[1])):
        event()
    wire.drain()


def tail(peers, order, do1, stat1, q_nat, k_nat, v_nat, bias, table_back, tok, w_self, gains, dh1, buckets, *rest):
    rows, length = do1.shape[0], q_nat.shape[0]
    n, depth = 8, peers // 2
    total = n + WAYS
    quarter, half = D // WAYS, D // 2
    shard = lambda k, width=D: pltpu.VMEM((k, quarter, width), BF16)
    row = lambda: pltpu.VMEM((rows, D), BF16)
    tiny = lambda k: pltpu.VMEM((k, 8 + STAT, D), F32)
    operands = (do1, stat1, q_nat, k_nat, v_nat, bias, table_back, tok, w_self, gains, dh1, buckets) + rest
    return pl.pallas_call(
        functools.partial(tail_kernel, peers),
        name="tail",
        out_shape=[sds((total, quarter, D), BF16), sds((8 + STAT, D), F32), sds((rows, D), BF16)],
        in_specs=[smem_spec()]
        + [any_spec() if i in (2, 3, 4, 5, 8) else full_spec() for i in range(len(operands))],
        out_specs=[full_spec()] * 3,
        scratch_shapes=[
            pltpu.VMEM((n, D, D), BF16), pltpu.VMEM((n, 2, quarter, D), BF16), shard(n), shard(n),
            shard(n), shard(total, half), shard(total, half), shard(total, half),
            tiny(4), tiny(3 + depth),
            pltpu.VMEM((length, D), BF16), pltpu.VMEM((length, D), BF16),
            pltpu.VMEM((peers, 2 * STAT, rows), F32), pltpu.VMEM((length, LANES), F32), pltpu.VMEM((LANES, length), F32),
            row(), row(), row(), row(), row(), row(),
            pltpu.VMEM((rows // PIECE, STAT, length + LANES), F32),
        ]
        + [pltpu.VMEM((length, D), BF16)] * 3
        + [pltpu.VMEM((HEADS, rows, length), BF16)] * 2
        + [pltpu.VMEM((2, 8, 2 * length), F32), pltpu.VMEM((2, 2 * length), jnp.int32), pltpu.SMEM(order.shape, jnp.int32)]
        + [pltpu.SemaphoreType.DMA, pltpu.SemaphoreType.DMA((4,))]
        + line_sems(depth, CHUNKS) + line_sems(depth, 1)
        + sems(2 * n) + sems(n) + sems(total) + sems(total * depth) + sems(total * depth) + sems(total) + sems(3 + depth),
        compiler_params=pltpu.CompilerParams(collective_id=0, has_side_effects=True, vmem_limit_bytes=TAIL_VMEM),
    )(order, *operands)


def widen_kernel(first, last, *refs):
    outs, sem = refs[:-2], refs[-1]
    wide = refs[-2]
    copies = []
    count = first.shape[0] + last.shape[0]
    quarter, width = first.shape[1], first.shape[2]
    for j in range(count):
        wide[j] = (first[j] if j < count - WAYS else last[j - (count - WAYS)]).astype(F32)
        if j < count - 2 * WAYS:
            dst = outs[j]
        elif j < count - WAYS:
            i = j - (count - 2 * WAYS)
            dst = outs[-2].at[:, i * width : (i + 1) * width]
        else:
            i = j - (count - WAYS)
            dst = outs[-1].at[i * quarter : (i + 1) * quarter]
        copies.append(pltpu.make_async_copy(wide.at[j], dst, sem.at[j]))
        copies[-1].start()
    for copy in copies:
        copy.wait()


def widen(first, last):
    quarter, width = first.shape[1:]
    count = first.shape[0] + last.shape[0]
    each = [sds((quarter, width), F32)] * (count - 2 * WAYS)
    return pl.pallas_call(
        widen_kernel,
        name="widen",
        out_shape=each + [sds((quarter, WAYS * width), F32), sds((WAYS * quarter, width), F32)],
        in_specs=[full_spec()] * 2,
        out_specs=[any_spec()] * (len(each) + 2),
        scratch_shapes=[pltpu.VMEM((count, quarter, width), F32), pltpu.SemaphoreType.DMA((count,))],
        compiler_params=pltpu.CompilerParams(vmem_limit_bytes=VMEM_LIMIT),
    )(first, last)


def shards(
    tokens,
    memory,
    piece_order,
    bucket_table,
    passage_lengths,
    self_gain,
    cross_gain,
    hidden_gain,
    position_bias,
    self_query,
    self_attention_key,
    self_value,
    self_output,
    cross_query,
    cross_key,
    cross_value,
    cross_output,
    hidden_in,
    hidden_out,
    grad_output,
):
    tok, mem, grad = tokens[0], memory[0], grad_output[0]
    rows, slots = tok.shape[0], mem.shape[0]
    length = (bucket_table.shape[0] + 1) // 2
    peers = length // rows
    f = lax.axis_index("fsdp")
    quarter, eighth = self_query.shape[0], position_bias.shape[0]
    buckets = jnp.pad(bucket_table, (0, 1), constant_values=-1)[None]
    w_self, w_rest, gains, ahead, table_back, q1_nat, k1_nat, v1_nat, a1, o1, h1, a2, q2, lse1 = front(
        peers,
        piece_order,
        tok,
        [self_gain[None], cross_gain[None], hidden_gain[None]],
        position_bias,
        buckets,
        [self_query, self_attention_key, self_value, self_output, cross_query],
    )
    (
        o2,
        branch2,
        dq2,
        dk2,
        dv2,
        branch1,
        dh1,
        do1,
        stat1,
        in_all,
        out_sum,
        layer_output,
        grad_memory,
        small_mid,
    ) = middle(
        peers,
        passage_lengths,
        q2,
        h1,
        o1,
        lse1,
        w_rest,
        gains,
        mem,
        grad,
        cross_key,
        cross_value,
        cross_output,
        hidden_in,
        hidden_out,
    )
    total, small, grad_tokens = tail(
        peers,
        piece_order,
        do1,
        stat1,
        q1_nat,
        k1_nat,
        v1_nat,
        ahead,
        table_back,
        tok,
        w_self,
        gains,
        dh1,
        buckets,
        a1,
        o1,
        branch1,
        a2,
        dq2,
        mem,
        dk2,
        dv2,
        o2,
        branch2,
        in_all,
        small_mid,
    )
    *each, sum_in, sum_out = widen(total, out_sum)
    gain = lambda i: lax.dynamic_slice_in_dim(small[i], f * quarter, quarter)
    bias_out = lax.dynamic_slice_in_dim(small[8:, :BUCKETS].T, f * eighth, eighth)[:, :HEADS]
    return (
        layer_output[None],
        grad_tokens[None],
        grad_memory[None],
        gain(0),
        gain(1),
        gain(2),
        bias_out,
        *[each[i] for i in (5, 6, 7, 4, 3, 1, 2, 0)],
        sum_in,
        sum_out,
    )


def pick(*arrays):
    resident = (arrays[3].shape[0] + 1) // 2 <= RESIDENT_ROWS
    return (shards if resident else streamed_shards)(*arrays)


def solution(mesh):
    return jax.shard_map(
        pick,
        mesh=mesh,
        in_specs=(
            P("fsdp", "ctx", None),
            P("fsdp", "ctx", None),
            P(),
            P(),
            P("fsdp", None),
            P("fsdp"),
            P("fsdp"),
            P("fsdp"),
            P("fsdp", None),
            P("fsdp", None),
            P("fsdp", None),
            P("fsdp", None),
            P("fsdp", None),
            P("fsdp", None),
            P("fsdp", None),
            P("fsdp", None),
            P("fsdp", None),
            P("fsdp", None),
            P("fsdp", None),
            P("fsdp", "ctx", None),
        ),
        out_specs=(
            P("fsdp", "ctx", None),
            P("fsdp", "ctx", None),
            P("fsdp", "ctx", None),
            P("fsdp"),
            P("fsdp"),
            P("fsdp"),
            P("fsdp", None),
            P("fsdp", None),
            P("fsdp", None),
            P("fsdp", None),
            P("fsdp", None),
            P("fsdp", None),
            P("fsdp", None),
            P("fsdp", None),
            P("fsdp", None),
            P("fsdp", None),
            P("fsdp", None),
        ),
        check_vma=False,
    )
```

```python
import functools

import jax
import jax.numpy as jnp
from jax import lax
from jax.experimental import pallas as pl
from jax.experimental.pallas import tpu as pltpu
from jax.sharding import PartitionSpec as P

D = 768
HEADS = 12
PAIRS = HEADS // 2
HEAD_DIM = 64
PIECE = 64
BLOCK = 256
PLEN = 256
KBLK = 512
PSG = 20
BUCKETS = 32
RESIDENT_ROWS = 1024
LANES = 128
EPSILON = 1e-06
NEGATIVE = -1e30
F32 = jnp.float32
BF16 = jnp.bfloat16
VMEM_LIMIT = 60 * 2**20
TAIL_VMEM = 63 * 2**20

def nn(a, b):
    return lax.dot_general(a, b, (((1,), (0,)), ((), ())), preferred_element_type=F32)
def nt(a, b):
    return lax.dot_general(a, b, (((1,), (1,)), ((), ())), preferred_element_type=F32)
def tn(a, b):
    return lax.dot_general(a, b, (((0,), (0,)), ((), ())), preferred_element_type=F32)

def normed(x, gain):
    return x * lax.rsqrt(jnp.mean(x * x, axis=-1, keepdims=True) + EPSILON) * gain

def half_mask(x, half):
    lane = lax.broadcasted_iota(jnp.int32, x.shape, 1) // HEAD_DIM
    return jnp.where(lane == half, x, jnp.zeros_like(x))

def lanes_of(pair):
    return pl.ds(pl.multiple_of(pair * LANES, LANES), LANES)

def shear(x, sign):
    row = lax.broadcasted_iota(jnp.int32, x.shape, 0)
    for bit in (1, 2, 4):
        x = jnp.where(row & bit != 0, pltpu.roll(x, (sign * bit) % x.shape[1], 1), x)
    return x

def full_spec():
    return pl.BlockSpec(memory_space=pltpu.VMEM)
def any_spec():
    return pl.BlockSpec(memory_space=pl.ANY)


def smem_spec():
    return pl.BlockSpec(memory_space=pltpu.SMEM)
def sds(shape, dtype):
    return jax.ShapeDtypeStruct(shape, dtype)

def norm_scale(values, gain_vector):
    return (
        values
        * lax.rsqrt(jnp.mean(values * values, axis=-1, keepdims=True) + EPSILON)
        * gain_vector
    )


def smooth_gate(values):
    return jax.nn.gelu(values, approximate=True)


def project(operand, matrix):
    return jnp.dot(operand, matrix, preferred_element_type=jnp.float32)


def project_back(operand, matrix):
    return jnp.einsum("sra,ba->srb", operand, matrix, preferred_element_type=jnp.float32)


def weight_grad(inputs, upstream):
    return jnp.einsum("sra,srb->ab", inputs, upstream, preferred_element_type=jnp.float32)


def to_heads(matrix):
    return matrix.reshape(matrix.shape[0], matrix.shape[1], HEADS, HEAD_DIM)


def heads_first(matrix):
    return jnp.transpose(to_heads(matrix), (0, 2, 1, 3))


def from_heads(tensor):
    return jnp.transpose(tensor, (0, 2, 1, 3)).reshape(
        tensor.shape[0], tensor.shape[2], HEADS * HEAD_DIM
    )


def block_scores(queries, keys_all, values_all, extras, offset):
    key_block = lax.dynamic_slice_in_dim(keys_all, offset, KBLK, 1)
    value_block = lax.dynamic_slice_in_dim(values_all, offset, KBLK, 1)
    added_bias, visible, bucket_indicator = extras(offset)
    scores = (
        jnp.einsum("sqhd,skhd->shqk", queries, key_block, preferred_element_type=jnp.float32)
        + added_bias
    )
    block_maximum = jnp.max(jnp.where(visible, scores, NEGATIVE), axis=-1)
    weights = jnp.exp(jnp.where(visible, scores - block_maximum[..., None], NEGATIVE))
    return (key_block, value_block, bucket_indicator, block_maximum, weights)


def attend_forward(queries, keys_all, values_all, extras):
    block_count = keys_all.shape[1] // KBLK

    def single_block_tile(carried, block_index):
        key_block, value_block, bucket_indicator, block_maximum, weights = block_scores(
            queries, keys_all, values_all, extras, block_index * KBLK
        )
        numerator = jnp.einsum(
            "shqk,skhd->shqd",
            weights.astype(jnp.bfloat16),
            value_block,
            preferred_element_type=jnp.float32,
        )
        return (carried, (block_maximum, jnp.sum(weights, axis=-1), numerator))

    ignored, stacked = lax.scan(
        single_block_tile, jnp.zeros((), jnp.float32), jnp.arange(block_count, dtype=jnp.int32)
    )
    block_maximum, block_sum, numerator = stacked
    row_maximum = jnp.max(block_maximum, axis=0)
    rescale = jnp.exp(block_maximum - row_maximum)
    row_total = jnp.sum(rescale * block_sum, axis=0)
    output = jnp.sum(rescale[..., None] * numerator, axis=0) / row_total[..., None]
    return (output, row_maximum, row_total)


def attend_backward(
    queries, keys_all, values_all, extras, grad_out, output, row_maximum, row_total
):
    block_count = keys_all.shape[1] // KBLK
    grad_wide = grad_out.astype(jnp.float32)
    row_dot = jnp.sum(grad_wide * output, axis=-1)
    scaled = grad_wide / row_total[..., None]
    sum_weight = -row_dot / row_total
    initial = (
        jnp.zeros(queries.shape, jnp.float32),
        jnp.zeros(keys_all.shape, jnp.float32),
        jnp.zeros(values_all.shape, jnp.float32),
        jnp.zeros((BUCKETS, HEADS), jnp.float32),
    )

    def single_block_tile(carried, block_index):
        grad_query, grad_keys, grad_values, grad_bias = carried
        offset = block_index * KBLK
        key_block, value_block, bucket_indicator, block_maximum, weights = block_scores(
            queries, keys_all, values_all, extras, offset
        )
        rescale = jnp.exp(block_maximum - row_maximum)
        grad_numerator = (scaled * rescale[..., None]).astype(jnp.bfloat16)
        grad_weights = (
            jnp.einsum(
                "shqd,skhd->shqk", grad_numerator, value_block, preferred_element_type=jnp.float32
            )
            + (sum_weight * rescale)[..., None]
        )
        grad_scores = weights * grad_weights
        gradient_bfloat_cast = grad_scores.astype(jnp.bfloat16)
        grad_query = grad_query + jnp.einsum(
            "shqk,skhd->sqhd", gradient_bfloat_cast, key_block, preferred_element_type=jnp.float32
        )
        key_part = jnp.einsum(
            "shqk,sqhd->skhd", gradient_bfloat_cast, queries, preferred_element_type=jnp.float32
        )
        value_part = jnp.einsum(
            "shqk,shqd->skhd",
            weights.astype(jnp.bfloat16),
            grad_numerator,
            preferred_element_type=jnp.float32,
        )
        grad_keys = lax.dynamic_update_slice_in_dim(grad_keys, key_part, offset, 1)
        grad_values = lax.dynamic_update_slice_in_dim(grad_values, value_part, offset, 1)
        if bucket_indicator is not None:
            remainder_portion = (grad_scores - gradient_bfloat_cast.astype(jnp.float32)).astype(
                jnp.bfloat16
            )
            grad_bias = (
                grad_bias
                + jnp.einsum(
                    "uljf,pjf->pl",
                    gradient_bfloat_cast,
                    bucket_indicator,
                    preferred_element_type=jnp.float32,
                )
                + jnp.einsum(
                    "uljf,pjf->pl",
                    remainder_portion,
                    bucket_indicator,
                    preferred_element_type=jnp.float32,
                )
            )
        return ((grad_query, grad_keys, grad_values, grad_bias), None)

    result, ignored = lax.scan(single_block_tile, initial, jnp.arange(block_count, dtype=jnp.int32))
    return result


def streamed_shards(
    tokens,
    memory,
    piece_order,
    bucket_table,
    passage_lengths,
    self_gain,
    cross_gain,
    hidden_gain,
    position_bias,
    self_query,
    self_attention_key,
    self_value,
    self_output,
    cross_query,
    cross_key,
    cross_value,
    cross_output,
    hidden_in,
    hidden_out,
    grad_output,
):
    (
        gain_one,
        gain_two,
        gain_three,
        position_bias_lookup,
        query_full,
        key_full,
        value_full,
        output_full,
        cross_query_full,
        cross_key_full,
        cross_value_full,
        cross_output_full,
        inner_full,
        outer_full,
    ) = (
        lax.all_gather(self_gain, "fsdp", axis=0, tiled=True),
        lax.all_gather(cross_gain, "fsdp", axis=0, tiled=True),
        lax.all_gather(hidden_gain, "fsdp", axis=0, tiled=True),
        lax.all_gather(position_bias, "fsdp", axis=0, tiled=True),
        lax.all_gather(self_query, "fsdp", axis=0, tiled=True),
        lax.all_gather(self_attention_key, "fsdp", axis=0, tiled=True),
        lax.all_gather(self_value, "fsdp", axis=0, tiled=True),
        lax.all_gather(self_output, "fsdp", axis=0, tiled=True),
        lax.all_gather(cross_query, "fsdp", axis=0, tiled=True),
        lax.all_gather(cross_key, "fsdp", axis=0, tiled=True),
        lax.all_gather(cross_value, "fsdp", axis=0, tiled=True),
        lax.all_gather(cross_output, "fsdp", axis=0, tiled=True),
        lax.all_gather(hidden_in, "fsdp", axis=0, tiled=True),
        lax.all_gather(hidden_out, "fsdp", axis=0, tiled=True),
    )
    gain_one = gain_one.astype(jnp.float32)
    gain_two = gain_two.astype(jnp.float32)
    gain_three = gain_three.astype(jnp.float32)
    sequence_count = tokens.shape[0]
    local_rows = tokens.shape[1]
    sequence_length = (bucket_table.shape[0] + 1) // 2
    memory_length = PSG * PLEN
    piece_offsets = jnp.arange(PIECE, dtype=jnp.int32)
    local_pieces = lax.dynamic_slice_in_dim(
        piece_order, lax.axis_index("ctx") * (local_rows // PIECE), local_rows // PIECE
    )
    query_position = (local_pieces[:, None] * PIECE + piece_offsets[None, :]).reshape(local_rows)
    key_position = (piece_order[:, None] * PIECE + piece_offsets[None, :]).reshape(sequence_length)
    bucket_numbers = jnp.arange(BUCKETS, dtype=jnp.int32)

    def self_extras(offset):
        key_block_position = lax.dynamic_slice_in_dim(key_position, offset, KBLK)
        relative_bucket_index = jnp.take(
            bucket_table,
            key_block_position[None, :] - query_position[:, None] + sequence_length - 1,
        )
        bucket_indicator = (
            relative_bucket_index[None, :, :] == bucket_numbers[:, None, None]
        ).astype(jnp.bfloat16)
        added_bias = jnp.einsum(
            "lvj,lf->fvj",
            bucket_indicator,
            position_bias_lookup,
            preferred_element_type=jnp.float32,
        )
        visible = key_block_position[None, :] // BLOCK <= query_position[:, None] // BLOCK
        return (added_bias, visible, bucket_indicator)

    slot_numbers = jnp.arange(PLEN, dtype=jnp.int32)
    memory_valid = (passage_lengths[:, :, None] > slot_numbers[None, None, :]).reshape(
        sequence_count, memory_length
    )

    def cross_extras(offset):
        visible = lax.dynamic_slice_in_dim(memory_valid, offset, KBLK, 1)[:, None, None, :]
        return (0.0, visible, None)

    inputs_wide = tokens.astype(jnp.float32)
    normed_one = norm_scale(inputs_wide, gain_one).astype(jnp.bfloat16)
    queries_one = project(normed_one, query_full).astype(jnp.bfloat16)
    keys_local = project(normed_one, key_full).astype(jnp.bfloat16)
    values_local = project(normed_one, value_full).astype(jnp.bfloat16)
    memory_keys = project(memory, cross_key_full).astype(jnp.bfloat16)
    memory_values = project(memory, cross_value_full).astype(jnp.bfloat16)
    keys_all, values_all, memory_keys_all, memory_values_all = (
        lax.all_gather(keys_local, "ctx", axis=1, tiled=True),
        lax.all_gather(values_local, "ctx", axis=1, tiled=True),
        lax.all_gather(memory_keys, "ctx", axis=1, tiled=True),
        lax.all_gather(memory_values, "ctx", axis=1, tiled=True),
    )
    output_one, maximum_one, total_one = attend_forward(
        to_heads(queries_one), to_heads(keys_all), to_heads(values_all), self_extras
    )
    attended_one = from_heads(output_one).astype(jnp.bfloat16)
    hidden_one = inputs_wide + project(attended_one, output_full)
    normed_two = norm_scale(hidden_one, gain_two).astype(jnp.bfloat16)
    queries_two = project(normed_two, cross_query_full).astype(jnp.bfloat16)
    output_two, maximum_two, total_two = attend_forward(
        to_heads(queries_two), to_heads(memory_keys_all), to_heads(memory_values_all), cross_extras
    )
    attended_two = from_heads(output_two).astype(jnp.bfloat16)
    hidden_two = hidden_one + project(attended_two, cross_output_full)
    normed_three = norm_scale(hidden_two, gain_three).astype(jnp.bfloat16)
    before_gate = project(normed_three, inner_full)
    gated_wide, gate_pullback = jax.vjp(smooth_gate, before_gate)
    activated = gated_wide.astype(jnp.bfloat16)
    layer_output = (hidden_two + project(activated, outer_full)).astype(jnp.bfloat16)
    grad_wide = grad_output.astype(jnp.float32)
    grad_outer = weight_grad(activated, grad_output)
    grad_activated = project_back(grad_output, outer_full)
    grad_before = gate_pullback(grad_activated)[0].astype(jnp.bfloat16)
    grad_inner = weight_grad(normed_three, grad_before)
    ignored, norm_pullback = jax.vjp(norm_scale, hidden_two, gain_three)
    grad_hidden_part, grad_gain_three = norm_pullback(project_back(grad_before, inner_full))
    grad_hidden_two = grad_wide + grad_hidden_part
    branch_two = grad_hidden_two.astype(jnp.bfloat16)
    grad_cross_output = weight_grad(attended_two, branch_two)
    grad_attended_two = project_back(branch_two, cross_output_full).astype(jnp.bfloat16)
    keys_back, values_back, memory_keys_back, memory_values_back = (
        keys_all,
        values_all,
        memory_keys_all,
        memory_values_all,
    )
    grad_query_two, grad_memory_keys, grad_memory_values, unused_bias = attend_backward(
        to_heads(queries_two),
        to_heads(memory_keys_back),
        to_heads(memory_values_back),
        cross_extras,
        heads_first(grad_attended_two),
        output_two,
        maximum_two,
        total_two,
    )
    memory_key_sum, memory_value_sum = (
        lax.psum_scatter(
            grad_memory_keys.reshape(sequence_count, memory_length, D),
            "ctx",
            scatter_dimension=1,
            tiled=True,
        ),
        lax.psum_scatter(
            grad_memory_values.reshape(sequence_count, memory_length, D),
            "ctx",
            scatter_dimension=1,
            tiled=True,
        ),
    )
    memory_key_rounded = memory_key_sum.astype(jnp.bfloat16)
    memory_value_rounded = memory_value_sum.astype(jnp.bfloat16)
    query_two_rounded = grad_query_two.reshape(sequence_count, local_rows, D).astype(jnp.bfloat16)
    grad_cross_query = weight_grad(normed_two, query_two_rounded)
    grad_cross_key = weight_grad(memory, memory_key_rounded)
    grad_cross_value = weight_grad(memory, memory_value_rounded)
    grad_memory = (
        project_back(memory_key_rounded, cross_key_full)
        + project_back(memory_value_rounded, cross_value_full)
    ).astype(jnp.bfloat16)
    ignored, norm_pullback = jax.vjp(norm_scale, hidden_one, gain_two)
    grad_hidden_part, grad_gain_two = norm_pullback(
        project_back(query_two_rounded, cross_query_full)
    )
    grad_hidden_one = grad_hidden_two + grad_hidden_part
    branch_one = grad_hidden_one.astype(jnp.bfloat16)
    grad_self_output = weight_grad(attended_one, branch_one)
    grad_attended_one = project_back(branch_one, output_full).astype(jnp.bfloat16)
    grad_query_one, grad_keys_all, grad_values_all, grad_bias = attend_backward(
        to_heads(queries_one),
        to_heads(keys_back),
        to_heads(values_back),
        self_extras,
        heads_first(grad_attended_one),
        output_one,
        maximum_one,
        total_one,
    )
    key_sum, value_sum = (
        lax.psum_scatter(
            grad_keys_all.reshape(sequence_count, sequence_length, D),
            "ctx",
            scatter_dimension=1,
            tiled=True,
        ),
        lax.psum_scatter(
            grad_values_all.reshape(sequence_count, sequence_length, D),
            "ctx",
            scatter_dimension=1,
            tiled=True,
        ),
    )
    query_one_rounded = grad_query_one.reshape(sequence_count, local_rows, D).astype(jnp.bfloat16)
    first_key_bfloat_cast = key_sum.astype(jnp.bfloat16)
    value_one_rounded = value_sum.astype(jnp.bfloat16)
    grad_self_query = weight_grad(normed_one, query_one_rounded)
    grad_self_key = weight_grad(normed_one, first_key_bfloat_cast)
    grad_self_value = weight_grad(normed_one, value_one_rounded)
    grad_normed_one = (
        project_back(query_one_rounded, query_full)
        + project_back(first_key_bfloat_cast, key_full)
        + project_back(value_one_rounded, value_full)
    )
    ignored, norm_pullback = jax.vjp(norm_scale, inputs_wide, gain_one)
    grad_input_part, grad_gain_one = norm_pullback(grad_normed_one)
    grad_tokens = (grad_hidden_one + grad_input_part).astype(jnp.bfloat16)
    (
        shard_gain_one,
        shard_gain_two,
        shard_gain_three,
        shard_bias,
        shard_query,
        shard_key,
        shard_value,
        shard_output,
        shard_cross_query,
        shard_cross_key,
        shard_cross_value,
        shard_cross_output,
        shard_inner,
        shard_outer,
    ) = (
        lax.psum_scatter(
            grad_gain_one.astype(jnp.bfloat16), "fsdp", scatter_dimension=0, tiled=True
        ).astype(jnp.float32),
        lax.psum_scatter(
            grad_gain_two.astype(jnp.bfloat16), "fsdp", scatter_dimension=0, tiled=True
        ).astype(jnp.float32),
        lax.psum_scatter(
            grad_gain_three.astype(jnp.bfloat16), "fsdp", scatter_dimension=0, tiled=True
        ).astype(jnp.float32),
        lax.psum_scatter(
            grad_bias.astype(jnp.bfloat16), "fsdp", scatter_dimension=0, tiled=True
        ).astype(jnp.float32),
        lax.psum_scatter(
            grad_self_query.astype(jnp.bfloat16), "fsdp", scatter_dimension=0, tiled=True
        ).astype(jnp.float32),
        lax.psum_scatter(
            grad_self_key.astype(jnp.bfloat16), "fsdp", scatter_dimension=0, tiled=True
        ).astype(jnp.float32),
        lax.psum_scatter(
            grad_self_value.astype(jnp.bfloat16), "fsdp", scatter_dimension=0, tiled=True
        ).astype(jnp.float32),
        lax.psum_scatter(
            grad_self_output.astype(jnp.bfloat16), "fsdp", scatter_dimension=0, tiled=True
        ).astype(jnp.float32),
        lax.psum_scatter(
            grad_cross_query.astype(jnp.bfloat16), "fsdp", scatter_dimension=0, tiled=True
        ).astype(jnp.float32),
        lax.psum_scatter(
            grad_cross_key.astype(jnp.bfloat16), "fsdp", scatter_dimension=0, tiled=True
        ).astype(jnp.float32),
        lax.psum_scatter(
            grad_cross_value.astype(jnp.bfloat16), "fsdp", scatter_dimension=0, tiled=True
        ).astype(jnp.float32),
        lax.psum_scatter(
            grad_cross_output.astype(jnp.bfloat16), "fsdp", scatter_dimension=0, tiled=True
        ).astype(jnp.float32),
        lax.psum_scatter(
            grad_inner.astype(jnp.bfloat16), "fsdp", scatter_dimension=0, tiled=True
        ).astype(jnp.float32),
        lax.psum_scatter(
            grad_outer.astype(jnp.bfloat16), "fsdp", scatter_dimension=0, tiled=True
        ).astype(jnp.float32),
    )
    (
        total_gain_one,
        total_gain_two,
        total_gain_three,
        total_bias,
        total_query,
        total_key,
        total_value,
        total_output,
        total_cross_query,
        total_cross_key,
        total_cross_value,
        total_cross_output,
        total_inner,
        total_outer,
    ) = lax.psum(
        (
            shard_gain_one,
            shard_gain_two,
            shard_gain_three,
            shard_bias,
            shard_query,
            shard_key,
            shard_value,
            shard_output,
            shard_cross_query,
            shard_cross_key,
            shard_cross_value,
            shard_cross_output,
            shard_inner,
            shard_outer,
        ),
        "ctx",
    )
    return (
        layer_output,
        grad_tokens,
        grad_memory,
        total_gain_one,
        total_gain_two,
        total_gain_three,
        total_bias,
        total_query,
        total_key,
        total_value,
        total_output,
        total_cross_query,
        total_cross_key,
        total_cross_value,
        total_cross_output,
        total_inner,
        total_outer,
    )


MESH = pl.DeviceIdType.MESH
WAYS = 4


class Place:
    def __init__(self, peers):
        self.depth = peers // 2
        c, f = lax.axis_index("ctx"), lax.axis_index("fsdp")
        self.c, self.f = c, f
        self.a, self.b, self.x, self.k = c // 2, c % 2, f // 2, f % 2
        self.core = (c, self.x * 2 + 1 - self.k)
        self.across = (c, (1 - self.x) * 2 + self.k)
        self.beside = (self.a * 2 + 1 - self.b, f)

    def ahead(self, d):
        return lax.rem(self.a + d, self.depth)

    def behind(self, d):
        return lax.rem(self.a + self.depth - d, self.depth)

    def column(self, a):
        return (a * 2 + self.b, self.f)

    def group(self, d):
        return (self.c, lax.rem(self.f + d, WAYS))


def greet(targets):
    barrier = pltpu.get_barrier_semaphore()
    for target in targets:
        pl.semaphore_signal(barrier, inc=1, device_id=target, device_id_type=MESH)
    pl.semaphore_wait(barrier, len(targets))


def remote(src, dst, sems, index, target):
    return pltpu.make_async_remote_copy(
        src_ref=src,
        dst_ref=dst,
        send_sem=sems[0].at[index],
        recv_sem=sems[1].at[index],
        device_id=target,
        device_id_type=MESH,
    )


def apart(src, dst, sems, send_index, recv_index, target):
    return pltpu.make_async_remote_copy(
        src_ref=src,
        dst_ref=dst,
        send_sem=sems[0].at[send_index],
        recv_sem=sems[1].at[recv_index],
        device_id=target,
        device_id_type=MESH,
    )


def line_sems(depth, chunks):
    return sems((2 * depth + 2) * chunks)


def sems(count):
    return [pltpu.SemaphoreType.DMA((count,)), pltpu.SemaphoreType.DMA((count,))]


class Wire:
    def __init__(self, peers):
        self.at = Place(peers)
        self.depth = self.at.depth
        self.sent = []

    def go(self, copy):
        copy.start()
        self.sent.append((None, copy.wait_send))

    def go_if(self, condition, make):
        pl.when(condition)(lambda: make().start())
        self.sent.append((condition, lambda: make().wait_send()))

    def drain(self):
        for condition, wait in self.sent:
            if condition is None:
                wait()
            else:
                pl.when(condition)(wait)

    def partners(self):
        at = self.at
        return (
            [at.group(d) for d in range(1, WAYS)]
            + [at.beside]
            + [at.column(at.ahead(d)) for d in range(1, self.depth)]
        )

    def near(self, step):
        a, last = self.at.a, self.depth - 1
        low = jnp.where(step - 1 < a, step - 1, step)
        mirrored = jnp.where(step - 1 < last - a, step - 1, step)
        return jnp.where(2 * a < last, low, last - mirrored)

    def piece(self, buf, c, chunk, chunks):
        if len(buf.shape) == 3:
            size = buf.shape[1] // chunks
            return buf.at[c, chunk * size : (chunk + 1) * size]
        rows = buf.shape[0] // (2 * self.depth)
        size = rows // chunks
        return buf.at[pl.ds(pl.multiple_of(c * rows + chunk * size, size), size)]

    def slot(self, buf, c):
        return self.piece(buf, c, 0, 1)

    def pass_on(self, src, dst, sem, up, beside, own, chunk, chunks, origin):
        at, a = self.at, self.at.a
        line = origin * chunks + chunk
        side = (self.depth + origin) * chunks + chunk
        for step in (1, -1):
            if own or (step == 1) == up:
                first = (2 * self.depth + (step == 1)) * chunks + chunk if own else line
                self.go_if(
                    a + 1 < self.depth if step == 1 else a > 0,
                    lambda step=step, first=first: apart(src, dst, sem, first, line, at.column(a + step)),
                )
        if beside:
            self.go(apart(src, dst, sem, side, side, at.beside))

    def spread(self, src, buf, sem, chunks):
        at = self.at
        size = src.shape[0] // chunks
        for chunk in range(chunks):
            part = src.at[chunk * size : (chunk + 1) * size]
            self.pass_on(part, self.piece(buf, at.c, chunk, chunks), sem, True, True, True, chunk, chunks, at.a)

    def relay(self, gathered, step):
        at, depth = self.at, self.depth
        for buf, sem, chunks in gathered:
            for chunk in range(chunks):
                for up in (True, False):
                    origin = at.a - step if up else at.a + step
                    inside = origin >= 0 if up else origin < depth
                    onward = at.a + 1 < depth if up else at.a > 0
                    line = origin * chunks + chunk
                    side = (depth + origin) * chunks + chunk
                    spot = lambda: self.piece(buf, origin * 2 + at.b, chunk, chunks)
                    target = at.column(at.a + 1 if up else at.a - 1)

                    def forward(_):
                        return apart(spot(), spot(), sem, line, line, target)

                    def sideways(_):
                        return apart(spot(), spot(), sem, side, side, at.beside)

                    @pl.when(inside)
                    def _():
                        apart(spot(), spot(), sem, line, line, at.beside).wait_recv()
                        sideways(0).start()
                        pl.when(onward)(lambda: forward(0).start())

                    self.sent.append((inside, self.later(buf, sem, side, origin, chunk, chunks, at.beside)))
                    self.sent.append(
                        (jnp.logical_and(inside, onward), self.later(buf, sem, line, origin, chunk, chunks, target))
                    )

    def later(self, buf, sem, index, origin, chunk, chunks, target):
        def wait():
            spot = self.piece(buf, origin * 2 + self.at.b, chunk, chunks)
            apart(spot, spot, sem, index, index, target).wait_send()

        return wait

    def from_beside(self, gathered, a):
        for buf, sem, chunks in gathered:
            for chunk in range(chunks):
                spot = self.piece(buf, a * 2 + 1 - self.at.b, chunk, chunks)
                index = (self.depth + a) * chunks + chunk
                apart(spot, spot, sem, index, index, self.at.beside).wait_recv()

    def shard(self, full, f):
        quarter = full.shape[0] // WAYS
        return full.at[pl.ds(pl.multiple_of(f * quarter, quarter), quarter)]

    def weight_start(self, src, full, sem, i):
        at = self.at
        slot = self.shard(full, at.f)
        slot[...] = src[...]
        self.go(remote(src, slot, sem, 3 * i, at.across))
        self.go(remote(src, slot, sem, 3 * i + 1, at.core))

    def weight_relay(self, full, sem, i):
        at = self.at
        slot = self.shard(full, (1 - at.x) * 2 + at.k)
        remote(slot, slot, sem, 3 * i, at.across).wait_recv()
        self.go(remote(slot, slot, sem, 3 * i + 2, at.core))

    def weight_ready(self, full, sem, i):
        at = self.at
        slot = self.shard(full, at.x * 2 + 1 - at.k)
        remote(slot, slot, sem, 3 * i + 1, at.core).wait_recv()
        slot = self.shard(full, (1 - at.x) * 2 + 1 - at.k)
        remote(slot, slot, sem, 3 * i + 2, at.core).wait_recv()


class Summed:
    def __init__(self, wire, source, out, rc, sd, rd, sem_c, sem_d, sem_e, sem_f):
        self.wire, self.source, self.out, self.rc, self.sd, self.rd = wire, source, out, rc, sd, rd
        self.sem_c, self.sem_d, self.sem_e, self.sem_f = sem_c, sem_d, sem_e, sem_f
        at = wire.at
        half, part = out.shape[2] // 2, out.shape[1] // wire.depth
        columns = lambda b: pl.ds(pl.multiple_of(b * half, LANES), half)
        self.mine, self.theirs = columns(at.b), columns(1 - at.b)
        self.rows = lambda a: pl.ds(pl.multiple_of(a * part, part), part)

    def stage_c(self, j):
        at = self.wire.at
        self.wire.go(remote(self.source(j).at[:, self.theirs], self.rc.at[j], self.sem_c, j, at.beside))

    def stage_d(self, j):
        at, depth = self.wire.at, self.wire.depth
        remote(self.rc.at[j], self.rc.at[j], self.sem_c, j, at.beside).wait_recv()
        value = self.source(j)[:, self.mine].astype(F32) + self.rc[j].astype(F32)
        self.sd[j] = value.astype(BF16)
        for d in range(1, depth):
            spot = self.rd.at[j, self.rows(at.a)]
            target = at.ahead(d)
            self.wire.go(remote(self.sd.at[j, self.rows(target)], spot, self.sem_d, j * depth + d, at.column(target)))

    def stage_e(self, j):
        at, depth = self.wire.at, self.wire.depth
        value = self.sd[j, self.rows(at.a), :].astype(F32)
        for d in range(1, depth):
            spot = self.rd.at[j, self.rows(at.behind(d))]
            remote(spot, spot, self.sem_d, j * depth + d, at.column(at.behind(d))).wait_recv()
            value += spot[...].astype(F32)
        spot = self.out.at[j, self.rows(at.a), self.mine]
        spot[...] = value.astype(BF16)
        for d in range(1, depth):
            self.wire.go(remote(spot, spot, self.sem_e, j * depth + d, at.column(at.ahead(d))))

    def stage_f(self, j):
        at, depth = self.wire.at, self.wire.depth
        for d in range(1, depth):
            spot = self.out.at[j, self.rows(at.behind(d)), self.mine]
            remote(spot, spot, self.sem_e, j * depth + d, at.column(at.behind(d))).wait_recv()
        spot = self.out.at[j, :, self.mine]
        self.wire.go(remote(spot, spot, self.sem_f, j, at.beside))

    def stage_g(self, j):
        spot = self.out.at[j, :, self.theirs]
        remote(spot, spot, self.sem_f, j, self.wire.at.beside).wait_recv()


def two_heads(x):
    return jnp.concatenate([half_mask(x, 0), half_mask(x, 1)], 0)


def ones_beside(x):
    ones = jnp.ones_like(x)
    return jnp.concatenate([two_heads(x), two_heads(ones)], 1)


def softmax_pair(scores, v, stats, p):
    weights, tops = [], []
    for s in scores:
        m = jnp.max(s, axis=1, keepdims=True)
        weights.append(jnp.exp(s - m).astype(BF16))
        tops.append(m)
    both = nn(jnp.concatenate(weights, 1), ones_beside(v))
    sums = both[:, LANES:]
    logs = jnp.log(sums)
    turned = pltpu.roll(logs, HEAD_DIM, 1)
    lane = lax.broadcasted_iota(jnp.int32, logs.shape, 1)
    inside = lane < HEAD_DIM
    stats = jnp.where(lane == 2 * p, tops[0] + jnp.where(inside, logs, turned), stats)
    stats = jnp.where(lane == 2 * p + 1, tops[1] + jnp.where(inside, turned, logs), stats)
    return both[:, :LANES] / sums, stats


def fill_inverse(order, inv):
    count = order.shape[0]
    for p in range(count):
        slot = jnp.int32(0)
        for s in range(count):
            slot = jnp.where(order[s] == p, s, slot)
        inv[p] = slot


def own_facts(order, c, count, length):
    per = (BLOCK // PIECE).bit_length() - 1
    facts = []
    for i in range(count):
        n = order[c * count + i]
        start = lax.shift_right_logical(n, per) * BLOCK
        facts.append((n, n & 1, length // LANES - 1 - lax.shift_right_logical(n, 1), start + BLOCK, start))
    return facts


def own_column(facts, i):
    return jnp.concatenate([jnp.full((PIECE, 1), fact[i], jnp.int32) for fact in facts], 0)


def own_bias(table, lines, own, out, low, high):
    full = table.shape[1]
    rows, length = out.shape[1], out.shape[2]

    def head(h, c):
        base = shear(pltpu.roll(jnp.broadcast_to(table[pl.ds(h, 1), :], (8, full)), 1, 1), 1)
        lines[0] = base
        lines[1] = pltpu.roll(base, PIECE, 1)
        for i in range(rows // PIECE):
            window = lines[own[i][1], :, pl.ds(own[i][2] * LANES, length + LANES)]
            for g in range(0, PIECE // 8, 2):
                both = [pltpu.roll(window, 8 * k, 1) if k else window for k in (g, g + 1)]
                both = jnp.concatenate(both, 0)[:, LANES:]
                out[h, i * PIECE + 8 * g : i * PIECE + 8 * g + 16, :] = both.astype(BF16)
        return c

    lax.fori_loop(low, high, head, 0)


def diagonal_sums(block):
    rows, length = block.shape
    wide = jnp.concatenate([block, jnp.zeros((rows, LANES), F32)], axis=1)
    total = pltpu.roll(wide[0:8], LANES, 1)
    for g in range(1, rows // 8):
        total += pltpu.roll(wide[8 * g : 8 * g + 8], LANES - 8 * g, 1)
    return jnp.sum(shear(total, -1), axis=0, keepdims=True)


N_FRONT = 5
CHUNKS = 2
N_GAINS = 16


def front_kernel(peers, *refs):
    order, tok, gain_row, bias_shard, buckets = refs[:5]
    shards_in = refs[5 : 5 + N_FRONT]
    (w_self_out, w_rest_out, gains, ahead_out, table_out, q_out, k_out, v_out, a1, o1, h1, a2, q2, lse) = refs[5 + N_FRONT : 19 + N_FRONT]
    (tok_all, pack, pack_all, marks, marks_all, table, lines, q_own, w_self, w_rest, ahead, q_nat, k_nat, v_nat, s_keep, inv, *sem) = refs[19 + N_FRONT :]
    weights = [w_self.at[i] for i in range(3)] + [w_rest.at[i] for i in range(N_FRONT - 3)]
    sem_t, sem_w, sem_p, sem_m = sem[0:2], sem[2:4], sem[4:6], sem[6:8]
    wire = Wire(peers)
    at, depth = wire.at, wire.depth
    rows = tok.shape[0]
    length = peers * rows
    mine, per = rows // PIECE, BLOCK // PIECE
    kept = []

    def keep(i, src, dst):
        copy = pltpu.make_async_copy(src, dst, s_keep.at[i])
        copy.start()
        kept.append(copy)

    quarter = gain_row.shape[1] // 3
    spot = lax.broadcasted_iota(jnp.int32, (quarter, D), 0) + at.f * quarter
    place = jnp.where(lax.broadcasted_iota(jnp.int32, (quarter, D), 1) == spot, 1.0, 0.0).astype(BF16)
    pack[...] = jnp.zeros_like(pack)
    for i in range(3):
        pack[i : i + 1, :] = nn(gain_row[:, i * quarter : (i + 1) * quarter], place).astype(BF16)
    eighth, heads = bias_shard.shape
    spot = lax.broadcasted_iota(jnp.int32, (BUCKETS, eighth), 1) + at.f * eighth
    place = jnp.where(lax.broadcasted_iota(jnp.int32, (BUCKETS, eighth), 0) == spot, 1.0, 0.0).astype(BF16)
    marks[...] = jnp.zeros_like(marks)
    marks[:, 0:heads] = nn(place, bias_shard[...]).astype(BF16)
    greet(wire.partners())
    for d in range(1, WAYS):
        wire.go(remote(pack, pack_all.at[at.f], sem_p, d, at.group(d)))
        wire.go(remote(marks, marks_all.at[at.f], sem_m, d, at.group(d)))
    wire.spread(tok, tok_all, sem_t, CHUNKS)
    for i in range(3):
        wire.weight_start(shards_in[i], weights[i], sem_w, i)
    wire.slot(tok_all, at.c)[...] = tok[...]
    pack_all[at.f] = pack[...]
    marks_all[at.f] = marks[...]
    for d in range(1, WAYS):
        slot = pack_all.at[lax.rem(at.f + WAYS - d, WAYS)]
        remote(slot, slot, sem_p, d, at.group(WAYS - d)).wait_recv()
        slot = marks_all.at[lax.rem(at.f + WAYS - d, WAYS)]
        remote(slot, slot, sem_m, d, at.group(WAYS - d)).wait_recv()
    whole = lambda x: x[0].astype(F32) + x[1].astype(F32) + x[2].astype(F32) + x[3].astype(F32)
    fill_inverse(order, inv)
    own = own_facts(order, at.c, mine, length)
    gains[...] = whole(pack_all)[0:8, :]
    bias = whole(marks_all).astype(BF16)
    bucket = lax.broadcasted_iota(jnp.int32, (bias.shape[0], 2 * length), 0)
    hot = jnp.where(buckets[...] == bucket, 1.0, 0.0).astype(BF16)
    table[0] = tn(bias, hot)[0:16, :]
    shifted = pltpu.roll(table[0], 1, 1).astype(BF16)
    row = lax.broadcasted_iota(jnp.int32, (LANES, LANES), 0)
    mirror = jnp.where(row + lax.broadcasted_iota(jnp.int32, (LANES, LANES), 1) == LANES - 1, 1.0, 0.0).astype(BF16)
    tiles = 2 * length // LANES
    for t in range(tiles):
        u = tiles - 1 - t
        table_out[:, t * LANES : (t + 1) * LANES] = nn(shifted[:, u * LANES : (u + 1) * LANES], mirror)

    gathered = [(tok_all, sem_t, CHUNKS)]
    share = HEADS // (depth - 1)
    for step in range(1, depth):
        wire.relay(gathered, step)
        own_bias(table.at[0], lines, own, ahead, (step - 1) * share, step * share)
    keep(3, ahead, ahead_out)
    for i in range(3):
        wire.weight_relay(weights[i], sem_w, i)
    for i in range(3, N_FRONT):
        wire.weight_start(shards_in[i], weights[i], sem_w, i)
    first = gains[0:1, :]
    a1[...] = normed(tok[...].astype(F32), first).astype(BF16)
    for i in range(3):
        wire.weight_ready(weights[i], sem_w, i)
    keep(0, w_self, w_self_out)
    for a in range(depth):
        wire.from_beside(gathered, a)

    def tile(t, c):
        parts = []
        for i in range(per):
            parts.append(tok_all[pl.ds(inv[t * per + i] * PIECE, PIECE), :])
        a = normed(jnp.concatenate(parts, 0).astype(F32), first).astype(BF16)
        dst = pl.ds(pl.multiple_of(t * BLOCK, BLOCK), BLOCK)
        for j, out in enumerate((q_nat, k_nat, v_nat)):
            out[dst, :] = nn(a, weights[j][...]).astype(BF16)
        return c

    lax.fori_loop(0, length // BLOCK, tile, 0)
    for i in range(mine):
        q_own[i * PIECE : (i + 1) * PIECE, :] = q_nat[pl.ds(own[i][0] * PIECE, PIECE), :]
    for i, (src, dst) in enumerate(((q_nat, q_out), (k_nat, k_out), (v_nat, v_out))):
        keep(5 + i, src, dst)
    wire.weight_relay(weights[3], sem_w, 3)
    lane = lax.broadcasted_iota(jnp.int32, (rows, length), 1)
    visible = lane < own_column(own, 3)

    def pair(p, stats):
        sl = lanes_of(p)
        s = nt(q_own[:, sl], two_heads(k_nat[:, sl]))
        scores = []
        for half in range(2):
            biased = s[:, half * length : (half + 1) * length] + ahead[2 * p + half].astype(F32)
            scores.append(jnp.where(visible, biased, NEGATIVE))
        value, stats = softmax_pair(scores, v_nat[:, sl], stats, p)
        o1[:, sl] = value.astype(BF16)
        return stats

    stats = lax.fori_loop(0, PAIRS // 2, pair, jnp.zeros((rows, LANES), F32), unroll=True)
    wire.weight_relay(weights[4], sem_w, 4)
    lse[...] = lax.fori_loop(PAIRS // 2, PAIRS, pair, stats, unroll=True)
    wire.weight_ready(weights[3], sem_w, 3)
    h = tok[...].astype(F32) + nn(o1[...], weights[3][...])
    h1[...] = h
    a = normed(h, gains[1:2, :]).astype(BF16)
    a2[...] = a
    wire.weight_ready(weights[4], sem_w, 4)
    q2[...] = nn(a, weights[4][...]).astype(BF16)
    keep(1, w_rest, w_rest_out)
    for copy in kept:
        copy.wait()
    wire.drain()


def front(peers, order, tok, gain_row, bias_shard, buckets, weight_shards):
    rows = tok.shape[0]
    length, depth = peers * rows, peers // 2
    block = lambda dtype: sds((rows, D), dtype)
    return pl.pallas_call(
        functools.partial(front_kernel, peers),
        name="front",
        out_shape=[sds((3, D, D), BF16), sds((N_FRONT - 3, D, D), BF16), sds((8, D), F32)]
        + [sds((HEADS, rows, length), BF16), sds((16, 2 * length), F32)]
        + [sds((length, D), BF16)] * 3
        + [block(BF16), block(BF16), block(F32), block(BF16), block(BF16), sds((rows, LANES), F32)],
        in_specs=[smem_spec()] + [full_spec()] * (4 + N_FRONT),
        out_specs=[any_spec() if i in (0, 1, 3, 5, 6, 7) else full_spec() for i in range(14)],
        scratch_shapes=[
            pltpu.VMEM((length, D), BF16),
            pltpu.VMEM((N_GAINS, D), BF16),
            pltpu.VMEM((WAYS, N_GAINS, D), BF16),
            pltpu.VMEM((BUCKETS, LANES), BF16),
            pltpu.VMEM((WAYS, BUCKETS, LANES), BF16),
            pltpu.VMEM((1, 16, 2 * length), F32),
            pltpu.VMEM((2, 8, 2 * length), F32),
            pltpu.VMEM((rows, D), BF16),
            pltpu.VMEM((3, D, D), BF16),
            pltpu.VMEM((N_FRONT - 3, D, D), BF16),
        ]
        + [pltpu.VMEM((HEADS, rows, length), BF16)]
        + [pltpu.VMEM((length, D), BF16)] * 3
        + [pltpu.SemaphoreType.DMA((8,)), pltpu.SMEM(order.shape, jnp.int32)]
        + line_sems(depth, CHUNKS) + sems(3 * N_FRONT) + sems(WAYS) + sems(WAYS),
        compiler_params=pltpu.CompilerParams(collective_id=1, has_side_effects=True, vmem_limit_bytes=VMEM_LIMIT),
    )(order, tok, gain_row, bias_shard, buckets, *weight_shards)


STAT = 16


def split(x):
    high = x.astype(BF16)
    return high, (x - high.astype(F32)).astype(BF16)


def head_matrix(rows):
    row = lax.broadcasted_iota(jnp.int32, (rows, D), 0)
    lane = lax.broadcasted_iota(jnp.int32, (rows, D), 1)
    return jnp.where(lane // HEAD_DIM == row, 1.0, 0.0).astype(BF16)


def per_head_sums(x, heads):
    high, low = split(x)
    return nt(heads, high) + nt(heads, low)


def blend(parts, stats, heads):
    top = functools.reduce(jnp.maximum, stats)
    shares = [jnp.exp(s - top) for s in stats]
    total = functools.reduce(jnp.add, shares)
    value = 0.0
    for part, share in zip(parts, shares):
        high, low = split(share / total)
        value = value + (tn(high, heads) + tn(low, heads)) * part.astype(F32)
    return value, top + jnp.log(total)


def norm_back_rows(x, gain, dy):
    r = lax.rsqrt(jnp.mean(x * x, axis=-1, keepdims=True) + EPSILON)
    gdy = gain * dy
    dx = r * gdy - x * (r * r * r) * jnp.mean(x * gdy, axis=-1, keepdims=True)
    return dx, jnp.sum(dy * x * r, axis=0, keepdims=True)


def round_trip(wire, gathered, fillers, compute, ship, fold, after):
    at = wire.at
    b = at.b
    first, second, third = [wire.near(step) for step in (1, 2, 3)]
    for step in range(1, wire.depth):
        fillers[step - 1]()
        wire.relay(gathered, step)
    for filler in fillers[wire.depth - 1 :]:
        filler()
    wire.from_beside(gathered, at.a)
    compute(at.c, at.a * 2 + 1 - b)
    ship(at.a)
    after[0]()
    wire.from_beside(gathered, third)
    compute(third * 2 + 1 - b, third * 2 + b)
    ship(third)
    after[1]()
    wire.from_beside(gathered, second)
    compute(second * 2 + 1 - b, second * 2 + b)
    ship(second)
    after[2]()
    fold(third)
    wire.from_beside(gathered, first)
    compute(first * 2 + 1 - b, first * 2 + b)
    ship(first)
    after[3]()
    fold(second)
    fold(first)


def middle_kernel(peers, *refs):
    (lengths, q2, h1, o1, lse1, w_rest, gains, mem, grad, ck_shard, cv_shard, co_shard, in_shard, w_out) = refs[:14]
    (o2_out, branch2_out, dq2_out, dk2_out, dv2_out, branch1_out, dh1_out, do1_out, stat1_out, in_all, out_sum, layer_out, gmem_out, small) = refs[14:28]
    (q_all, k2, v2, part, part_lse, from_b, from_b_lse, joined, joined_lse, from_z, from_z_lse,
     w_ck, w_cv, w_co, w_in, g_all, a3_all, dact, act, dpre, da3_send, da3_in, out_send, out_in,
     do_all, stat_all, stat_own, dk_acc, dv_acc, dqp, dq_b, dq_j, dq_z, mask, g_in, g_out, rc, sd, rd, *sem) = refs[28:]
    sem = [sem[2 * i : 2 * i + 2] for i in range(len(sem) // 2)]
    (s_q, s_w, s_in, s_g, s_y, s_yl, s_z, s_zl, s_a3, s_da3, s_out, s_do, s_st, s_dy, s_dz, s_gi, *s_sum) = sem
    wire = Wire(peers)
    at, depth = wire.at, wire.depth
    rows = q2.shape[0]
    heads = head_matrix(STAT)
    quarter = co_shard.shape[0]
    units = w_out.shape[0]
    block = lambda f: pl.ds(pl.multiple_of(f * rows, rows), rows)
    greet(wire.partners())
    wire.spread(q2, q_all, s_q, CHUNKS)
    wire.weight_start(ck_shard, w_ck, s_w, 1)
    wire.weight_start(cv_shard, w_cv, s_w, 2)
    q_all[at.c] = q2[...]
    g_all[block(at.f), :] = grad[...]
    wire.shard(w_in, at.f)[...] = in_shard[:, pl.ds(pl.multiple_of(at.f * units, LANES), units)]

    slots, passages = mem.shape[0], lengths.shape[1]
    log = PLEN.bit_length() - 1

    def hidden(shape, axis):
        slot = lax.broadcasted_iota(jnp.int32, shape, axis) + at.c * slots
        first = at.c * slots // PLEN
        taken = jnp.zeros(shape, jnp.int32)
        for i in range(slots // PLEN + 2):
            size = lengths[0, jnp.minimum(first + i, passages - 1)]
            taken = jnp.where(lax.shift_right_logical(slot, log) == first + i, size, taken)
        return jnp.where((slot & (PLEN - 1)) < taken, 0.0, NEGATIVE)

    def fill_mask():
        mask[...] = hidden(mask.shape, 0)

    def next_weights():
        wire.weight_relay(w_ck, s_w, 1)
        wire.weight_start(co_shard, w_co, s_w, 0)

    def project_memory():
        wire.weight_relay(w_cv, s_w, 2)
        feed_forward_operands()
        wire.weight_ready(w_ck, s_w, 1)
        k2[...] = nn(mem[...], w_ck[...]).astype(BF16)
        wire.weight_ready(w_cv, s_w, 2)
        v2[...] = nn(mem[...], w_cv[...]).astype(BF16)

    def feed_forward_operands():
        for d in range(1, WAYS):
            f = lax.rem(at.f + d, WAYS)
            part = in_shard.at[:, pl.ds(pl.multiple_of(f * units, LANES), units)]
            wire.go(remote(grad, g_all.at[block(at.f)], s_g, d, at.group(d)))
            wire.go(remote(part, wire.shard(w_in, at.f), s_in, d, at.group(d)))

    mask_row = hidden((1, slots), 1)

    def attend(c1, c2):
        def pair(p, stats):
            sl = lanes_of(p)
            q = jnp.concatenate([q_all[c1, :, sl], q_all[c2, :, sl]], 0)
            s = nt(q, two_heads(k2[:, sl]))
            value, stats = softmax_pair([s[:, :slots] + mask_row, s[:, slots:] + mask_row], v2[:, sl], stats, p)
            part[c1, :, sl] = value[:rows].astype(BF16)
            part[c2, :, sl] = value[rows:].astype(BF16)
            return stats

        stats = lax.fori_loop(0, PAIRS, pair, jnp.zeros((2 * rows, LANES), F32), unroll=True)
        part_lse[c1] = stats[:rows].T[:STAT]
        part_lse[c2] = stats[rows:].T[:STAT]

    def ship_part(a):
        other = a * 2 + 1 - at.b
        wire.go(remote(part.at[other], from_b.at[a], s_y, a, at.beside))
        wire.go(remote(part_lse.at[other], from_b_lse.at[a], s_yl, a, at.beside))

    def blend_column(a):
        remote(from_b.at[a], from_b.at[a], s_y, a, at.beside).wait_recv()
        remote(from_b_lse.at[a], from_b_lse.at[a], s_yl, a, at.beside).wait_recv()
        c = a * 2 + at.b
        return blend([part[c], from_b[a]], [part_lse[c], from_b_lse[a]], heads)

    def fold_part(a):
        value, stat = blend_column(a)
        joined[a] = value.astype(BF16)
        joined_lse[a] = stat
        wire.go(remote(joined.at[a], from_z.at[at.a], s_z, at.a, at.column(a)))
        wire.go(remote(joined_lse.at[a], from_z_lse.at[at.a], s_zl, at.a, at.column(a)))

    round_trip(wire, [(q_all, s_q, CHUNKS)], [fill_mask, lambda: None, next_weights, project_memory], attend, ship_part, fold_part, [lambda: None] * 4)
    wire.weight_relay(w_co, s_w, 0)
    value, stat = blend_column(at.a)
    parts, stats = [value], [stat]
    for step in range(1, depth):
        a = wire.near(step)
        remote(from_z.at[a], from_z.at[a], s_z, a, at.column(a)).wait_recv()
        remote(from_z_lse.at[a], from_z_lse.at[a], s_zl, a, at.column(a)).wait_recv()
        parts.append(from_z[a])
        stats.append(from_z_lse[a])
    out2, lse2 = blend(parts, stats, heads)
    o2 = out2.astype(BF16)
    o2_out[...] = o2
    wire.weight_ready(w_co, s_w, 0)
    h2 = h1[...] + nn(o2, w_co[...])
    a3 = normed(h2, gains[2:3, :]).astype(BF16)
    a3_all[block(at.f), :] = a3
    spot = a3_all.at[block(at.f)]
    wire.go(remote(spot, spot, s_a3, 0, at.across))
    wire.go(remote(spot, spot, s_a3, 1, at.core))

    def arrive(buf, sem, size):
        for d in range(1, WAYS):
            f = lax.rem(at.f + WAYS - d, WAYS)
            spot = buf.at[pl.ds(pl.multiple_of(f * size, size), size)]
            remote(spot, spot, sem, d, at.group(WAYS - d)).wait_recv()

    arrive(g_all, s_g, rows)
    tiles = [slice(2 * rows * t, 2 * rows * (t + 1)) for t in range(WAYS // 2)]
    for rs in tiles:
        dact[rs, :] = nt(g_all[rs, :], w_out[...])
    arrive(w_in, s_in, quarter)
    wire.weight_relay(a3_all, s_a3, 0)
    wire.weight_ready(a3_all, s_a3, 0)
    for rs in tiles:
        pre = nn(a3_all[rs, :], w_in[...])
        square = pre * pre
        t = jnp.tanh(0.7978845608028654 * (pre + 0.044715 * pre * square))
        act[rs, :] = (0.5 * pre * (1.0 + t)).astype(BF16)
        slope = 0.5 * (1.0 + t) + 0.5 * pre * (1.0 - t * t) * (0.7978845608028654 * (1.0 + 3 * 0.044715 * square))
        d = (dact[rs, :] * slope).astype(BF16)
        dpre[rs, :] = d
        da3_send[rs, :] = nt(d, w_in[...]).astype(BF16)

    def exchange(src, dst, sem):
        for d in range(1, WAYS):
            f = lax.rem(at.f + d, WAYS)
            wire.go(remote(src.at[block(f)], dst.at[block(at.f)], sem, d, at.group(d)))

    def collect(src, dst, sem):
        arrive(dst, sem, rows)
        value = src[block(at.f), :].astype(F32)
        for d in range(1, WAYS):
            value += dst[block(lax.rem(at.f + WAYS - d, WAYS)), :].astype(F32)
        return value

    from_core, to_pass, from_across, passed = [slice(rows * i, rows * (i + 1)) for i in range(WAYS)]
    beyond = (1 - at.x) * 2
    wire.go(remote(da3_send.at[block(beyond + 1 - at.k)], da3_in.at[to_pass], s_da3, 1, at.core))
    wire.go(remote(da3_send.at[block(at.x * 2 + 1 - at.k)], da3_in.at[from_core], s_da3, 0, at.core))
    remote(da3_in.at[to_pass], da3_in.at[to_pass], s_da3, 1, at.core).wait_recv()
    pair_sum = da3_send[block(beyond + at.k), :].astype(F32) + da3_in[to_pass, :].astype(F32)
    da3_in[passed, :] = pair_sum.astype(BF16)
    wire.go(remote(da3_in.at[passed], da3_in.at[from_across], s_da3, 2, at.across))
    sums = Summed(wire, lambda j: g_out.at[j * quarter : (j + 1) * quarter], out_sum, rc, sd, rd, *s_sum)
    g_out[...] = tn(act[...], g_all[...]).astype(BF16)
    for j in range(WAYS):
        sums.stage_c(j)
    for rs in tiles:
        out_send[rs, :] = nn(act[rs, :], w_out[...]).astype(BF16)
    sums.stage_d(0)
    sums.stage_d(1)
    remote(da3_in.at[from_core], da3_in.at[from_core], s_da3, 0, at.core).wait_recv()
    remote(da3_in.at[from_across], da3_in.at[from_across], s_da3, 2, at.across).wait_recv()
    da3 = da3_send[block(at.f), :].astype(F32) + da3_in[from_core, :].astype(F32) + da3_in[from_across, :].astype(F32)
    dx, dgain = norm_back_rows(h2, gains[2:3, :], da3)
    small[...] = jnp.zeros_like(small)
    small[1:2, :] = dgain
    dh2 = grad[...].astype(F32) + dx
    branch2 = dh2.astype(BF16)
    branch2_out[...] = branch2
    do2 = nt(branch2, w_co[...]).astype(BF16)
    do_all[at.c] = do2
    stat_own[0] = jnp.concatenate([lse2, per_head_sums(do2.astype(F32) * out2, heads)], 0)
    stat_all[at.c] = stat_own[0]
    wire.spread(do_all.at[at.c], do_all, s_do, CHUNKS)
    wire.spread(stat_own.at[0], stat_all, s_st, 1)
    exchange(out_send, out_in, s_out)

    def clear():
        dk_acc[...] = jnp.zeros_like(dk_acc)
        dv_acc[...] = jnp.zeros_like(dv_acc)

    def finish_output():
        layer_out[...] = (h2 + collect(out_send, out_in, s_out)).astype(BF16)

    def stages(stage, *js):
        return lambda: [stage(j) for j in js]

    def in_grads():
        g_in[...] = tn(a3_all[...], dpre[...]).astype(BF16)
        rows_of = lambda f: pl.ds(pl.multiple_of(f * quarter, quarter), quarter)
        in_all[at.f] = g_in[rows_of(at.f), :]
        for d in range(1, WAYS):
            f = lax.rem(at.f + d, WAYS)
            wire.go(remote(g_in.at[rows_of(f)], in_all.at[at.f], s_gi, d, at.group(d)))

    def attend_back(c1, c2):
        def pair(p, carry):
            sl = lanes_of(p)
            q = jnp.concatenate([q_all[c1, :, sl], q_all[c2, :, sl]], 0)
            do = jnp.concatenate([do_all[c1, :, sl], do_all[c2, :, sl]], 0)
            kk = two_heads(k2[:, sl])
            s = nt(kk, q)
            d = nt(two_heads(v2[:, sl]), do)
            line = lambda i: jnp.concatenate([stat_all[c1, pl.ds(i, 1), :], stat_all[c2, pl.ds(i, 1), :]], 1)
            weights, slopes = [], []
            for half in range(2):
                h, hs = 2 * p + half, slice(half * slots, (half + 1) * slots)
                e = jnp.exp(s[hs] + mask[...] - line(h))
                weights.append(e.astype(BF16))
                slopes.append((e * (d[hs] - line(STAT + h))).astype(BF16))
            dv_acc[:, sl] += nn(jnp.concatenate(weights, 1), two_heads(do))
            dk_acc[:, sl] += nn(jnp.concatenate(slopes, 1), two_heads(q))
            dq = tn(kk, jnp.concatenate(slopes, 0)).T
            dqp[c1, :, sl] = dq[:rows].astype(BF16)
            dqp[c2, :, sl] = dq[rows:].astype(BF16)
            return carry

        lax.fori_loop(0, PAIRS, pair, 0, unroll=True)

    def ship_dq(a):
        wire.go(remote(dqp.at[a * 2 + 1 - at.b], dq_b.at[a], s_dy, a, at.beside))

    def column_dq(a):
        remote(dq_b.at[a], dq_b.at[a], s_dy, a, at.beside).wait_recv()
        return dqp[a * 2 + at.b].astype(F32) + dq_b[a].astype(F32)

    def fold_dq(a):
        dq_j[a] = column_dq(a).astype(BF16)
        wire.go(remote(dq_j.at[a], dq_z.at[at.a], s_dz, at.a, at.column(a)))

    round_trip(
        wire, [(do_all, s_do, CHUNKS), (stat_all, s_st, 1)], [clear, in_grads, lambda: None, stages(sums.stage_d, 2, 3)], attend_back, ship_dq, fold_dq,
        [stages(sums.stage_e, 0, 1), stages(sums.stage_e, 2, 3), stages(sums.stage_f, 0, 1), stages(sums.stage_f, 2, 3)],
    )
    dk2_out[...] = dk_acc[...].astype(BF16)
    dv2_out[...] = dv_acc[...].astype(BF16)
    value = column_dq(at.a)
    for step in range(1, depth):
        a = wire.near(step)
        remote(dq_z.at[a], dq_z.at[a], s_dz, a, at.column(a)).wait_recv()
        value += dq_z[a].astype(F32)
    dq2 = value.astype(BF16)
    dq2_out[...] = dq2
    dx, dgain = norm_back_rows(h1[...], gains[1:2, :], nt(dq2, w_rest[1]))
    small[0:1, :] = dgain
    dh1 = dh2 + dx
    dh1_out[...] = dh1
    branch1 = dh1.astype(BF16)
    branch1_out[...] = branch1
    do1 = nt(branch1, w_rest[0]).astype(BF16)
    do1_out[...] = do1
    stat_own[1] = jnp.concatenate([lse1[...].T[:STAT], per_head_sums(do1.astype(F32) * o1[...].astype(F32), heads)], 0)
    stat1_out[...] = stat_own[1]
    gmem_out[...] = (nt(dk2_out[...], w_ck[...]) + nt(dv2_out[...], w_cv[...])).astype(BF16)
    finish_output()
    for d in range(1, WAYS):
        spot = in_all.at[lax.rem(at.f + WAYS - d, WAYS)]
        remote(spot, spot, s_gi, d, at.group(WAYS - d)).wait_recv()
    for j in range(WAYS):
        sums.stage_g(j)
    wire.drain()


def middle(peers, lengths, q2, h1, o1, lse1, w_rest, gains, mem, grad, ck_shard, cv_shard, co_shard, in_shard, w_out):
    rows, slots = q2.shape[0], mem.shape[0]
    depth = peers // 2
    units = w_out.shape[0]
    row = lambda dtype: sds((rows, D), dtype)
    store = lambda n, dtype=BF16: pltpu.VMEM((n, rows, D), dtype)
    stat = lambda n, k=STAT: pltpu.VMEM((n, k, rows), F32)
    group = lambda width, dtype=BF16: pltpu.VMEM((WAYS * rows, width), dtype)
    return pl.pallas_call(
        functools.partial(middle_kernel, peers),
        name="middle",
        out_shape=[
            row(BF16),
            row(BF16),
            row(BF16),
            sds((slots, D), BF16),
            sds((slots, D), BF16),
            row(BF16),
            row(F32),
            row(BF16),
            sds((2 * STAT, rows), F32),
            sds((WAYS, D // WAYS, units), BF16),
            sds((WAYS, units // WAYS, D), BF16),
            row(BF16),
            sds((slots, D), BF16),
            sds((8, D), F32),
        ],
        in_specs=[smem_spec()] + [full_spec()] * 13,
        out_specs=[full_spec()] * 14,
        scratch_shapes=[
            store(peers), pltpu.VMEM((slots, D), BF16), pltpu.VMEM((slots, D), BF16),
            store(peers), stat(peers), store(depth), stat(depth), store(depth), stat(depth), store(depth), stat(depth),
            pltpu.VMEM((D, D), BF16), pltpu.VMEM((D, D), BF16), pltpu.VMEM((D, D), BF16), pltpu.VMEM((D, units), BF16),
            group(D), group(D), group(units, F32), group(units), group(units), group(D), group(D), group(D), group(D),
            store(peers), stat(peers, 2 * STAT), stat(2, 2 * STAT),
            pltpu.VMEM((slots, D), F32), pltpu.VMEM((slots, D), F32),
            store(peers), store(depth), store(depth), store(depth),
            pltpu.VMEM((slots, 2 * rows), F32),
            pltpu.VMEM((D, units), BF16),
            pltpu.VMEM((units, D), BF16),
        ]
        + [pltpu.VMEM((WAYS, units // WAYS, D // 2), BF16)] * 3
        + line_sems(depth, CHUNKS) + sems(9) + sems(WAYS) + sems(WAYS)
        + sems(depth) * 4
        + sems(WAYS) * 3
        + line_sems(depth, CHUNKS) + line_sems(depth, 1)
        + sems(depth) * 2
        + sems(WAYS) + sems(WAYS) + sems(WAYS * depth) + sems(WAYS * depth) + sems(WAYS),
        compiler_params=pltpu.CompilerParams(collective_id=2, has_side_effects=True, vmem_limit_bytes=VMEM_LIMIT),
    )(lengths, q2, h1, o1, lse1, w_rest, gains, mem, grad, ck_shard, cv_shard, co_shard, in_shard, w_out)


def tail_kernel(peers, *refs):
    (order, do1, stat1, q_far, k_far, v_far, bias_far, table_back, tok, w_self, gains, dh1, buckets,
     a1, o1, branch1, a2, dq2, mem, dk2, dv2, o2, branch2, in_all, small_mid) = refs[:25]
    out, small_out, grad_tokens = refs[25:28]
    (prod, ra, sb, rb, sc, rc, sd, rd, tiny, tiny_in, do_all, do_nat, stat_all, stat_rows, stat_t, q_own, k_own, v_own,
     dq1, dk1, dv1, diagonals, q_nat, k_nat, v_nat, bias, bias_back, lines, bucket_rows, inv, s_w, s_far, *sem) = refs[28:]
    sem = [sem[2 * i : 2 * i + 2] for i in range(len(sem) // 2)]
    s_do, s_st, sem_a, sem_b, sem_c, sem_d, sem_e, sem_f, sem_t = sem
    wire = Wire(peers)
    at, depth, go = wire.at, wire.depth, wire.go
    rows, length = do1.shape[0], q_far.shape[0]
    mine, pieces = rows // PIECE, length // PIECE
    total, quarter, wide = out.shape
    pairs = [(o2, branch2), (mem, dk2), (mem, dv2), (a2, dq2), (o1, branch1), (a1, dq1), (a1, dk1), (a1, dv1)]
    n_mats = len(pairs)
    shard_rows = lambda f: pl.ds(pl.multiple_of(f * quarter, quarter), quarter)

    def stage_a(i):
        left, right = pairs[i]
        prod[i] = tn(left[...], right[...]).astype(BF16)
        for x in range(2):
            go(remote(prod.at[i, shard_rows(x * 2 + 1 - at.k)], ra.at[i, x], sem_a, 2 * i + x, at.core))

    def stage_b(i):
        for x in range(2):
            remote(ra.at[i, x], ra.at[i, x], sem_a, 2 * i + x, at.core).wait_recv()
        x = 1 - at.x
        sb[i] = (prod[i, shard_rows(x * 2 + at.k), :].astype(F32) + ra[i, x].astype(F32)).astype(BF16)
        go(remote(sb.at[i], rb.at[i], sem_b, i, at.across))

    sums = Summed(wire, lambda j: sc.at[j] if j < n_mats else in_all.at[j - n_mats], out, rc, sd, rd, sem_c, sem_d, sem_e, sem_f)

    def stage_c(j):
        if j < n_mats:
            remote(sb.at[j], rb.at[j], sem_b, j, at.across).wait_recv()
            value = prod[j, shard_rows(at.f), :].astype(F32) + ra[j, at.x].astype(F32) + rb[j].astype(F32)
            sc[j] = value.astype(BF16)
        sums.stage_c(j)

    hops = [at.core, at.across, at.beside]

    def small_hop(t):
        if t:
            remote(tiny_in.at[t - 1], tiny_in.at[t - 1], sem_t, t - 1, hops[t - 1]).wait_recv()
            tiny[t] = tiny[t - 1] + tiny_in[t - 1]
        if t < 3:
            go(remote(tiny.at[t], tiny_in.at[t], sem_t, t, hops[t]))
        else:
            for d in range(1, depth):
                go(remote(tiny.at[3], tiny_in.at[2 + d], sem_t, 2 + d, at.column(at.ahead(d))))

    def small_end():
        value = tiny[3]
        for d in range(1, depth):
            remote(tiny_in.at[2 + d], tiny_in.at[2 + d], sem_t, 2 + d, at.column(at.behind(d))).wait_recv()
            value += tiny_in[2 + d]
        small_out[...] = value

    gathered = [(do_all, s_do, CHUNKS), (stat_all, s_st, 1)]

    def relay(step):
        wire.relay(gathered, step)

    def prepare():
        for copy in coming:
            copy.wait()
        for a in range(depth):
            wire.from_beside(gathered, a)
        for c in range(peers):
            spread = jnp.concatenate([stat_all[c], jnp.zeros((LANES - 2 * STAT, rows), F32)], 0)
            stat_rows[c * rows : (c + 1) * rows, :] = spread.T
        for i in range(pieces):
            do_nat[i * PIECE : (i + 1) * PIECE, :] = do_all[pl.ds(inv[i] * PIECE, PIECE), :]
        per = LANES // PIECE
        for t in range(length // LANES):
            lines = [stat_rows[pl.ds(inv[t * per + i] * PIECE, PIECE), :] for i in range(per)]
            stat_t[:, t * LANES : (t + 1) * LANES] = jnp.concatenate(lines, 0).T
        for i in range(mine):
            dst = slice(i * PIECE, (i + 1) * PIECE)
            src = pl.ds(own[i][0] * PIECE, PIECE)
            q_own[dst, :] = q_nat[src, :]
            k_own[dst, :] = k_nat[src, :]
            v_own[dst, :] = v_nat[src, :]

    def attend_back(low, high):
        lane = lax.broadcasted_iota(jnp.int32, (rows, length), 1)
        visible, seen = lane < own_column(own, 3), lane >= own_column(own, 4)
        stat_lane = lax.broadcasted_iota(jnp.int32, (rows, LANES), 1)
        stat_own = jnp.concatenate([stat1[...], jnp.zeros((LANES - 2 * STAT, rows), F32)], 0).T

        def column(h):
            return jnp.sum(jnp.where(stat_lane == h, stat_own, 0.0), axis=1, keepdims=True)

        def pair(p, c):
            sl = lanes_of(p)
            q, k, v, do = q_own[:, sl], k_nat[:, sl], v_nat[:, sl], do1[:, sl]
            kq, vq, qa, da = k_own[:, sl], v_own[:, sl], q_nat[:, sl], do_nat[:, sl]
            dq = dk = dv = jnp.zeros((rows, LANES), F32)
            for half in range(2):
                h = 2 * p + half
                km, vm = half_mask(k, half), half_mask(v, half)
                s = jnp.where(visible, nt(q, km) + bias[h].astype(F32), NEGATIVE)
                e = jnp.exp(s - column(h))
                ds = e * (nt(do, vm) - column(STAT + h))
                dq += nn(ds.astype(BF16), km)
                for i in range(mine):
                    diagonals[i, pl.ds(h, 1), :] = diagonal_sums(ds[i * PIECE : (i + 1) * PIECE, :])
                s = jnp.where(seen, nt(half_mask(kq, half), qa) + bias_back[h].astype(F32), NEGATIVE)
                e = jnp.exp(s - stat_t[pl.ds(h, 1), :])
                dv += nn(e.astype(BF16), half_mask(da, half))
                ds = e * (nt(half_mask(vq, half), da) - stat_t[pl.ds(STAT + h, 1), :])
                dk += nn(ds.astype(BF16), half_mask(qa, half))
            dq1[:, sl] = dq.astype(BF16)
            dk1[:, sl] = dk.astype(BF16)
            dv1[:, sl] = dv.astype(BF16)
            return c

        lax.fori_loop(low, high, pair, 0)

    def finish_tokens():
        weights_here.wait()
        da1 = nt(dq1[...], prod[5]) + nt(dk1[...], prod[6]) + nt(dv1[...], prod[7])
        dx, dgain = norm_back_rows(tok[...].astype(F32), gains[0:1, :], da1)
        grad_tokens[...] = (dh1[...] + dx).astype(BF16)
        sums = jnp.zeros((STAT, BUCKETS), F32)
        number = lax.broadcasted_iota(jnp.int32, (BUCKETS, length + LANES), 0)
        for i in range(mine):
            line = bucket_rows[pl.ds(own[i][1], 1), pl.ds(own[i][2] * LANES, length + LANES)]
            hot = jnp.where(line == number, 1.0, 0.0).astype(BF16)
            high, low = split(diagonals[i])
            sums += nt(high, hot) + nt(low, hot)
        tiny[0] = jnp.zeros(tiny.shape[1:], F32)
        tiny[0, 0:1, :] = dgain
        tiny[0, 1:3, :] = small_mid[0:2, :]
        tiny[0, 8 : 8 + STAT, 0:BUCKETS] = sums

    weights_here = pltpu.make_async_copy(w_self, prod.at[5:8], s_w)
    weights_here.start()
    coming = []
    for i, (src, dst) in enumerate(
        ((q_far, q_nat), (k_far, k_nat), (v_far, v_nat), (bias_far, bias))
    ):
        coming.append(pltpu.make_async_copy(src, dst, s_far.at[i]))
        coming[-1].start()
    own = own_facts(order, at.c, mine, length)
    greet(wire.partners())
    wire.spread(do1, do_all, s_do, CHUNKS)
    wire.spread(stat1, stat_all, s_st, 1)
    wire.slot(do_all, at.c)[...] = do1[...]
    stat_all[at.c] = stat1[...]
    fill_inverse(order, inv)
    diagonals[...] = jnp.zeros_like(diagonals)
    bucket_rows[0:1, :] = pltpu.roll(buckets[...], 1, 1)
    bucket_rows[1:2, :] = pltpu.roll(buckets[...], 1 + PIECE, 1)
    turns = [8, 9, 10, 11, 0, 1, 2, 3, 4, 5, 6, 7]
    lag = 1.5
    events = []
    for tick, j in enumerate(turns):
        if j < n_mats:
            events += [(tick - 2, 1, lambda j=j: stage_a(j)), (tick - 1, 2, lambda j=j: stage_b(j))]
        for k, stage in enumerate((stage_c, sums.stage_d, sums.stage_e, sums.stage_f, sums.stage_g)):
            events.append((tick + k * lag, 3 + k, lambda j=j, stage=stage: stage(j)))
    share = HEADS // 3
    for i in range(3):
        events.append((i + 0.3, 0, lambda i=i: own_bias(table_back, lines, own, bias_back, i * share, (i + 1) * share)))
        events.append((0.5 * i + 0.2, 0, lambda i=i: relay(i + 1)))
    events.append((2.4, 0, prepare))
    events += [(2.6 + 0.5 * i, 0, lambda i=i: attend_back(i, i + 1)) for i in range(PAIRS)]
    events.append((5.7, 0, finish_tokens))
    events += [(6.6 + t, 0, lambda t=t: small_hop(t)) for t in range(4)] + [(11.5, 0, small_end)]
    for _, _, event in sorted(events, key=lambda e: (e[0], -e[1])):
        event()
    wire.drain()


def tail(peers, order, do1, stat1, q_nat, k_nat, v_nat, bias, table_back, tok, w_self, gains, dh1, buckets, *rest):
    rows, length = do1.shape[0], q_nat.shape[0]
    n, depth = 8, peers // 2
    total = n + WAYS
    quarter, half = D // WAYS, D // 2
    shard = lambda k, width=D: pltpu.VMEM((k, quarter, width), BF16)
    row = lambda: pltpu.VMEM((rows, D), BF16)
    tiny = lambda k: pltpu.VMEM((k, 8 + STAT, D), F32)
    operands = (do1, stat1, q_nat, k_nat, v_nat, bias, table_back, tok, w_self, gains, dh1, buckets) + rest
    return pl.pallas_call(
        functools.partial(tail_kernel, peers),
        name="tail",
        out_shape=[sds((total, quarter, D), BF16), sds((8 + STAT, D), F32), sds((rows, D), BF16)],
        in_specs=[smem_spec()]
        + [any_spec() if i in (2, 3, 4, 5, 8) else full_spec() for i in range(len(operands))],
        out_specs=[full_spec()] * 3,
        scratch_shapes=[
            pltpu.VMEM((n, D, D), BF16), pltpu.VMEM((n, 2, quarter, D), BF16), shard(n), shard(n),
            shard(n), shard(total, half), shard(total, half), shard(total, half),
            tiny(4), tiny(3 + depth),
            pltpu.VMEM((length, D), BF16), pltpu.VMEM((length, D), BF16),
            pltpu.VMEM((peers, 2 * STAT, rows), F32), pltpu.VMEM((length, LANES), F32), pltpu.VMEM((LANES, length), F32),
            row(), row(), row(), row(), row(), row(),
            pltpu.VMEM((rows // PIECE, STAT, length + LANES), F32),
        ]
        + [pltpu.VMEM((length, D), BF16)] * 3
        + [pltpu.VMEM((HEADS, rows, length), BF16)] * 2
        + [pltpu.VMEM((2, 8, 2 * length), F32), pltpu.VMEM((2, 2 * length), jnp.int32), pltpu.SMEM(order.shape, jnp.int32)]
        + [pltpu.SemaphoreType.DMA, pltpu.SemaphoreType.DMA((4,))]
        + line_sems(depth, CHUNKS) + line_sems(depth, 1)
        + sems(2 * n) + sems(n) + sems(total) + sems(total * depth) + sems(total * depth) + sems(total) + sems(3 + depth),
        compiler_params=pltpu.CompilerParams(collective_id=0, has_side_effects=True, vmem_limit_bytes=TAIL_VMEM),
    )(order, *operands)


def widen_kernel(first, last, small, *refs):
    ready, outs, gains_out, bias_out = refs[:3], refs[3:16], refs[16], refs[17]
    wide, sem, sem_ready = refs[18:]
    copies = [pltpu.make_async_copy(ready[i], outs[i], sem_ready.at[i]) for i in range(3)]
    for copy in copies:
        copy.start()
    outs = outs[3:]
    count = first.shape[0] + last.shape[0]
    quarter, width = first.shape[1], first.shape[2]
    for j in range(count):
        wide[j] = (first[j] if j < count - WAYS else last[j - (count - WAYS)]).astype(F32)
        if j < count - 2 * WAYS:
            dst = outs[j]
        elif j < count - WAYS:
            i = j - (count - 2 * WAYS)
            dst = outs[-2].at[:, i * width : (i + 1) * width]
        else:
            i = j - (count - WAYS)
            dst = outs[-1].at[i * quarter : (i + 1) * quarter]
        copies.append(pltpu.make_async_copy(wide.at[j], dst, sem.at[j]))
        copies[-1].start()
    f = lax.axis_index("fsdp")
    turned = pltpu.roll(small[0:8, :], lax.rem(WAYS - f, WAYS) * quarter, 1)
    gains_out[...] = turned[:, :quarter]
    eighth = bias_out.shape[0]
    sums = jnp.concatenate([small[8:, 0:LANES], jnp.zeros((LANES - STAT, LANES), F32)], 0)
    flipped = sums.T
    part = flipped[0:eighth, :]
    for i in range(1, WAYS):
        part = jnp.where(f == i, flipped[i * eighth : (i + 1) * eighth, :], part)
    bias_out[...] = part[:, :HEADS]
    for copy in copies:
        copy.wait()


def widen(first, last, small, ready):
    quarter, width = first.shape[1:]
    count = first.shape[0] + last.shape[0]
    each = [sds((quarter, width), F32)] * (count - 2 * WAYS)
    big = [sds(x.shape, x.dtype) for x in ready] + each
    big += [sds((quarter, WAYS * width), F32), sds((WAYS * quarter, width), F32)]
    return pl.pallas_call(
        widen_kernel,
        name="widen",
        out_shape=big + [sds((8, quarter), F32), sds((BUCKETS // WAYS, HEADS), F32)],
        in_specs=[full_spec()] * 6,
        out_specs=[any_spec()] * len(big) + [full_spec()] * 2,
        scratch_shapes=[
            pltpu.VMEM((count, quarter, width), F32),
            pltpu.SemaphoreType.DMA((count,)),
            pltpu.SemaphoreType.DMA((3,)),
        ],
        compiler_params=pltpu.CompilerParams(vmem_limit_bytes=VMEM_LIMIT),
    )(first, last, small, *ready)


def shards(
    tokens,
    memory,
    piece_order,
    bucket_table,
    passage_lengths,
    self_gain,
    cross_gain,
    hidden_gain,
    position_bias,
    self_query,
    self_attention_key,
    self_value,
    self_output,
    cross_query,
    cross_key,
    cross_value,
    cross_output,
    hidden_in,
    hidden_out,
    grad_output,
):
    tok, mem, grad = tokens[0], memory[0], grad_output[0]
    rows, slots = tok.shape[0], mem.shape[0]
    length = (bucket_table.shape[0] + 1) // 2
    peers = length // rows
    f = lax.axis_index("fsdp")
    quarter, eighth = self_query.shape[0], position_bias.shape[0]
    buckets = jnp.pad(bucket_table, (0, 1), constant_values=-1)[None]
    w_self, w_rest, gains, ahead, table_back, q1_nat, k1_nat, v1_nat, a1, o1, h1, a2, q2, lse1 = front(
        peers,
        piece_order,
        tok,
        jnp.concatenate([self_gain, cross_gain, hidden_gain])[None],
        position_bias,
        buckets,
        [self_query, self_attention_key, self_value, self_output, cross_query],
    )
    (
        o2,
        branch2,
        dq2,
        dk2,
        dv2,
        branch1,
        dh1,
        do1,
        stat1,
        in_all,
        out_sum,
        layer_output,
        grad_memory,
        small_mid,
    ) = middle(
        peers,
        passage_lengths,
        q2,
        h1,
        o1,
        lse1,
        w_rest,
        gains,
        mem,
        grad,
        cross_key,
        cross_value,
        cross_output,
        hidden_in,
        hidden_out,
    )
    total, small, grad_tokens = tail(
        peers,
        piece_order,
        do1,
        stat1,
        q1_nat,
        k1_nat,
        v1_nat,
        ahead,
        table_back,
        tok,
        w_self,
        gains,
        dh1,
        buckets,
        a1,
        o1,
        branch1,
        a2,
        dq2,
        mem,
        dk2,
        dv2,
        o2,
        branch2,
        in_all,
        small_mid,
    )
    ready = [layer_output, grad_tokens, grad_memory]
    *ready, e0, e1, e2, e3, e4, e5, e6, e7, sum_in, sum_out, gains_out, bias_out = widen(total, out_sum, small, ready)
    return (
        ready[0][None],
        ready[1][None],
        ready[2][None],
        gains_out[0],
        gains_out[1],
        gains_out[2],
        bias_out,
        e5,
        e6,
        e7,
        e4,
        e3,
        e1,
        e2,
        e0,
        sum_in,
        sum_out,
    )


def pick(*arrays):
    resident = (arrays[3].shape[0] + 1) // 2 <= RESIDENT_ROWS
    return (shards if resident else streamed_shards)(*arrays)


def solution(mesh):
    return jax.shard_map(
        pick,
        mesh=mesh,
        in_specs=(
            P("fsdp", "ctx", None),
            P("fsdp", "ctx", None),
            P(),
            P(),
            P("fsdp", None),
            P("fsdp"),
            P("fsdp"),
            P("fsdp"),
            P("fsdp", None),
            P("fsdp", None),
            P("fsdp", None),
            P("fsdp", None),
            P("fsdp", None),
            P("fsdp", None),
            P("fsdp", None),
            P("fsdp", None),
            P("fsdp", None),
            P("fsdp", None),
            P("fsdp", None),
            P("fsdp", "ctx", None),
        ),
        out_specs=(
            P("fsdp", "ctx", None),
            P("fsdp", "ctx", None),
            P("fsdp", "ctx", None),
            P("fsdp"),
            P("fsdp"),
            P("fsdp"),
            P("fsdp", None),
            P("fsdp", None),
            P("fsdp", None),
            P("fsdp", None),
            P("fsdp", None),
            P("fsdp", None),
            P("fsdp", None),
            P("fsdp", None),
            P("fsdp", None),
            P("fsdp", None),
            P("fsdp", None),
        ),
        check_vma=False,
    )
```

```python
import functools

import jax
import jax.numpy as jnp
from jax import lax
from jax.experimental import pallas as pl
from jax.experimental.pallas import tpu as pltpu
from jax.sharding import PartitionSpec as P

D = 768
HEADS = 12
PAIRS = HEADS // 2
HEAD_DIM = 64
PIECE = 64
BLOCK = 256
PLEN = 256
KBLK = 512
PSG = 20
BUCKETS = 32
RESIDENT_ROWS = 1024
LANES = 128
EPSILON = 1e-06
NEGATIVE = -1e30
F32 = jnp.float32
BF16 = jnp.bfloat16
VMEM_LIMIT = 60 * 2**20
TAIL_VMEM = 63 * 2**20

def nn(a, b):
    return lax.dot_general(a, b, (((1,), (0,)), ((), ())), preferred_element_type=F32)
def nt(a, b):
    return lax.dot_general(a, b, (((1,), (1,)), ((), ())), preferred_element_type=F32)
def tn(a, b):
    return lax.dot_general(a, b, (((0,), (0,)), ((), ())), preferred_element_type=F32)

def normed(x, gain):
    return x * lax.rsqrt(jnp.mean(x * x, axis=-1, keepdims=True) + EPSILON) * gain

def half_mask(x, half):
    lane = lax.broadcasted_iota(jnp.int32, x.shape, 1) // HEAD_DIM
    return jnp.where(lane == half, x, jnp.zeros_like(x))

def lanes_of(pair):
    return pl.ds(pl.multiple_of(pair * LANES, LANES), LANES)

def shear(x, sign):
    row = lax.broadcasted_iota(jnp.int32, x.shape, 0)
    for bit in (1, 2, 4):
        x = jnp.where(row & bit != 0, pltpu.roll(x, (sign * bit) % x.shape[1], 1), x)
    return x

def full_spec():
    return pl.BlockSpec(memory_space=pltpu.VMEM)
def any_spec():
    return pl.BlockSpec(memory_space=pl.ANY)


def smem_spec():
    return pl.BlockSpec(memory_space=pltpu.SMEM)
def sds(shape, dtype):
    return jax.ShapeDtypeStruct(shape, dtype)

def norm_scale(values, gain_vector):
    return (
        values
        * lax.rsqrt(jnp.mean(values * values, axis=-1, keepdims=True) + EPSILON)
        * gain_vector
    )


def smooth_gate(values):
    return jax.nn.gelu(values, approximate=True)


def project(operand, matrix):
    return jnp.dot(operand, matrix, preferred_element_type=jnp.float32)


def project_back(operand, matrix):
    return jnp.einsum("sra,ba->srb", operand, matrix, preferred_element_type=jnp.float32)


def weight_grad(inputs, upstream):
    return jnp.einsum("sra,srb->ab", inputs, upstream, preferred_element_type=jnp.float32)


def to_heads(matrix):
    return matrix.reshape(matrix.shape[0], matrix.shape[1], HEADS, HEAD_DIM)


def heads_first(matrix):
    return jnp.transpose(to_heads(matrix), (0, 2, 1, 3))


def from_heads(tensor):
    return jnp.transpose(tensor, (0, 2, 1, 3)).reshape(
        tensor.shape[0], tensor.shape[2], HEADS * HEAD_DIM
    )


def block_scores(queries, keys_all, values_all, extras, offset):
    key_block = lax.dynamic_slice_in_dim(keys_all, offset, KBLK, 1)
    value_block = lax.dynamic_slice_in_dim(values_all, offset, KBLK, 1)
    added_bias, visible, bucket_indicator = extras(offset)
    scores = (
        jnp.einsum("sqhd,skhd->shqk", queries, key_block, preferred_element_type=jnp.float32)
        + added_bias
    )
    block_maximum = jnp.max(jnp.where(visible, scores, NEGATIVE), axis=-1)
    weights = jnp.exp(jnp.where(visible, scores - block_maximum[..., None], NEGATIVE))
    return (key_block, value_block, bucket_indicator, block_maximum, weights)


def attend_forward(queries, keys_all, values_all, extras):
    block_count = keys_all.shape[1] // KBLK

    def single_block_tile(carried, block_index):
        key_block, value_block, bucket_indicator, block_maximum, weights = block_scores(
            queries, keys_all, values_all, extras, block_index * KBLK
        )
        numerator = jnp.einsum(
            "shqk,skhd->shqd",
            weights.astype(jnp.bfloat16),
            value_block,
            preferred_element_type=jnp.float32,
        )
        return (carried, (block_maximum, jnp.sum(weights, axis=-1), numerator))

    ignored, stacked = lax.scan(
        single_block_tile, jnp.zeros((), jnp.float32), jnp.arange(block_count, dtype=jnp.int32)
    )
    block_maximum, block_sum, numerator = stacked
    row_maximum = jnp.max(block_maximum, axis=0)
    rescale = jnp.exp(block_maximum - row_maximum)
    row_total = jnp.sum(rescale * block_sum, axis=0)
    output = jnp.sum(rescale[..., None] * numerator, axis=0) / row_total[..., None]
    return (output, row_maximum, row_total)


def attend_backward(
    queries, keys_all, values_all, extras, grad_out, output, row_maximum, row_total
):
    block_count = keys_all.shape[1] // KBLK
    grad_wide = grad_out.astype(jnp.float32)
    row_dot = jnp.sum(grad_wide * output, axis=-1)
    scaled = grad_wide / row_total[..., None]
    sum_weight = -row_dot / row_total
    initial = (
        jnp.zeros(queries.shape, jnp.float32),
        jnp.zeros(keys_all.shape, jnp.float32),
        jnp.zeros(values_all.shape, jnp.float32),
        jnp.zeros((BUCKETS, HEADS), jnp.float32),
    )

    def single_block_tile(carried, block_index):
        grad_query, grad_keys, grad_values, grad_bias = carried
        offset = block_index * KBLK
        key_block, value_block, bucket_indicator, block_maximum, weights = block_scores(
            queries, keys_all, values_all, extras, offset
        )
        rescale = jnp.exp(block_maximum - row_maximum)
        grad_numerator = (scaled * rescale[..., None]).astype(jnp.bfloat16)
        grad_weights = (
            jnp.einsum(
                "shqd,skhd->shqk", grad_numerator, value_block, preferred_element_type=jnp.float32
            )
            + (sum_weight * rescale)[..., None]
        )
        grad_scores = weights * grad_weights
        gradient_bfloat_cast = grad_scores.astype(jnp.bfloat16)
        grad_query = grad_query + jnp.einsum(
            "shqk,skhd->sqhd", gradient_bfloat_cast, key_block, preferred_element_type=jnp.float32
        )
        key_part = jnp.einsum(
            "shqk,sqhd->skhd", gradient_bfloat_cast, queries, preferred_element_type=jnp.float32
        )
        value_part = jnp.einsum(
            "shqk,shqd->skhd",
            weights.astype(jnp.bfloat16),
            grad_numerator,
            preferred_element_type=jnp.float32,
        )
        grad_keys = lax.dynamic_update_slice_in_dim(grad_keys, key_part, offset, 1)
        grad_values = lax.dynamic_update_slice_in_dim(grad_values, value_part, offset, 1)
        if bucket_indicator is not None:
            remainder_portion = (grad_scores - gradient_bfloat_cast.astype(jnp.float32)).astype(
                jnp.bfloat16
            )
            grad_bias = (
                grad_bias
                + jnp.einsum(
                    "uljf,pjf->pl",
                    gradient_bfloat_cast,
                    bucket_indicator,
                    preferred_element_type=jnp.float32,
                )
                + jnp.einsum(
                    "uljf,pjf->pl",
                    remainder_portion,
                    bucket_indicator,
                    preferred_element_type=jnp.float32,
                )
            )
        return ((grad_query, grad_keys, grad_values, grad_bias), None)

    result, ignored = lax.scan(single_block_tile, initial, jnp.arange(block_count, dtype=jnp.int32))
    return result


def streamed_shards(
    tokens,
    memory,
    piece_order,
    bucket_table,
    passage_lengths,
    self_gain,
    cross_gain,
    hidden_gain,
    position_bias,
    self_query,
    self_attention_key,
    self_value,
    self_output,
    cross_query,
    cross_key,
    cross_value,
    cross_output,
    hidden_in,
    hidden_out,
    grad_output,
):
    (
        gain_one,
        gain_two,
        gain_three,
        position_bias_lookup,
        query_full,
        key_full,
        value_full,
        output_full,
        cross_query_full,
        cross_key_full,
        cross_value_full,
        cross_output_full,
        inner_full,
        outer_full,
    ) = (
        lax.all_gather(self_gain, "fsdp", axis=0, tiled=True),
        lax.all_gather(cross_gain, "fsdp", axis=0, tiled=True),
        lax.all_gather(hidden_gain, "fsdp", axis=0, tiled=True),
        lax.all_gather(position_bias, "fsdp", axis=0, tiled=True),
        lax.all_gather(self_query, "fsdp", axis=0, tiled=True),
        lax.all_gather(self_attention_key, "fsdp", axis=0, tiled=True),
        lax.all_gather(self_value, "fsdp", axis=0, tiled=True),
        lax.all_gather(self_output, "fsdp", axis=0, tiled=True),
        lax.all_gather(cross_query, "fsdp", axis=0, tiled=True),
        lax.all_gather(cross_key, "fsdp", axis=0, tiled=True),
        lax.all_gather(cross_value, "fsdp", axis=0, tiled=True),
        lax.all_gather(cross_output, "fsdp", axis=0, tiled=True),
        lax.all_gather(hidden_in, "fsdp", axis=0, tiled=True),
        lax.all_gather(hidden_out, "fsdp", axis=0, tiled=True),
    )
    gain_one = gain_one.astype(jnp.float32)
    gain_two = gain_two.astype(jnp.float32)
    gain_three = gain_three.astype(jnp.float32)
    sequence_count = tokens.shape[0]
    local_rows = tokens.shape[1]
    sequence_length = (bucket_table.shape[0] + 1) // 2
    memory_length = PSG * PLEN
    piece_offsets = jnp.arange(PIECE, dtype=jnp.int32)
    local_pieces = lax.dynamic_slice_in_dim(
        piece_order, lax.axis_index("ctx") * (local_rows // PIECE), local_rows // PIECE
    )
    query_position = (local_pieces[:, None] * PIECE + piece_offsets[None, :]).reshape(local_rows)
    key_position = (piece_order[:, None] * PIECE + piece_offsets[None, :]).reshape(sequence_length)
    bucket_numbers = jnp.arange(BUCKETS, dtype=jnp.int32)

    def self_extras(offset):
        key_block_position = lax.dynamic_slice_in_dim(key_position, offset, KBLK)
        relative_bucket_index = jnp.take(
            bucket_table,
            key_block_position[None, :] - query_position[:, None] + sequence_length - 1,
        )
        bucket_indicator = (
            relative_bucket_index[None, :, :] == bucket_numbers[:, None, None]
        ).astype(jnp.bfloat16)
        added_bias = jnp.einsum(
            "lvj,lf->fvj",
            bucket_indicator,
            position_bias_lookup,
            preferred_element_type=jnp.float32,
        )
        visible = key_block_position[None, :] // BLOCK <= query_position[:, None] // BLOCK
        return (added_bias, visible, bucket_indicator)

    slot_numbers = jnp.arange(PLEN, dtype=jnp.int32)
    memory_valid = (passage_lengths[:, :, None] > slot_numbers[None, None, :]).reshape(
        sequence_count, memory_length
    )

    def cross_extras(offset):
        visible = lax.dynamic_slice_in_dim(memory_valid, offset, KBLK, 1)[:, None, None, :]
        return (0.0, visible, None)

    inputs_wide = tokens.astype(jnp.float32)
    normed_one = norm_scale(inputs_wide, gain_one).astype(jnp.bfloat16)
    queries_one = project(normed_one, query_full).astype(jnp.bfloat16)
    keys_local = project(normed_one, key_full).astype(jnp.bfloat16)
    values_local = project(normed_one, value_full).astype(jnp.bfloat16)
    memory_keys = project(memory, cross_key_full).astype(jnp.bfloat16)
    memory_values = project(memory, cross_value_full).astype(jnp.bfloat16)
    keys_all, values_all, memory_keys_all, memory_values_all = (
        lax.all_gather(keys_local, "ctx", axis=1, tiled=True),
        lax.all_gather(values_local, "ctx", axis=1, tiled=True),
        lax.all_gather(memory_keys, "ctx", axis=1, tiled=True),
        lax.all_gather(memory_values, "ctx", axis=1, tiled=True),
    )
    output_one, maximum_one, total_one = attend_forward(
        to_heads(queries_one), to_heads(keys_all), to_heads(values_all), self_extras
    )
    attended_one = from_heads(output_one).astype(jnp.bfloat16)
    hidden_one = inputs_wide + project(attended_one, output_full)
    normed_two = norm_scale(hidden_one, gain_two).astype(jnp.bfloat16)
    queries_two = project(normed_two, cross_query_full).astype(jnp.bfloat16)
    output_two, maximum_two, total_two = attend_forward(
        to_heads(queries_two), to_heads(memory_keys_all), to_heads(memory_values_all), cross_extras
    )
    attended_two = from_heads(output_two).astype(jnp.bfloat16)
    hidden_two = hidden_one + project(attended_two, cross_output_full)
    normed_three = norm_scale(hidden_two, gain_three).astype(jnp.bfloat16)
    before_gate = project(normed_three, inner_full)
    gated_wide, gate_pullback = jax.vjp(smooth_gate, before_gate)
    activated = gated_wide.astype(jnp.bfloat16)
    layer_output = (hidden_two + project(activated, outer_full)).astype(jnp.bfloat16)
    grad_wide = grad_output.astype(jnp.float32)
    grad_outer = weight_grad(activated, grad_output)
    grad_activated = project_back(grad_output, outer_full)
    grad_before = gate_pullback(grad_activated)[0].astype(jnp.bfloat16)
    grad_inner = weight_grad(normed_three, grad_before)
    ignored, norm_pullback = jax.vjp(norm_scale, hidden_two, gain_three)
    grad_hidden_part, grad_gain_three = norm_pullback(project_back(grad_before, inner_full))
    grad_hidden_two = grad_wide + grad_hidden_part
    branch_two = grad_hidden_two.astype(jnp.bfloat16)
    grad_cross_output = weight_grad(attended_two, branch_two)
    grad_attended_two = project_back(branch_two, cross_output_full).astype(jnp.bfloat16)
    keys_back, values_back, memory_keys_back, memory_values_back = (
        keys_all,
        values_all,
        memory_keys_all,
        memory_values_all,
    )
    grad_query_two, grad_memory_keys, grad_memory_values, unused_bias = attend_backward(
        to_heads(queries_two),
        to_heads(memory_keys_back),
        to_heads(memory_values_back),
        cross_extras,
        heads_first(grad_attended_two),
        output_two,
        maximum_two,
        total_two,
    )
    memory_key_sum, memory_value_sum = (
        lax.psum_scatter(
            grad_memory_keys.reshape(sequence_count, memory_length, D),
            "ctx",
            scatter_dimension=1,
            tiled=True,
        ),
        lax.psum_scatter(
            grad_memory_values.reshape(sequence_count, memory_length, D),
            "ctx",
            scatter_dimension=1,
            tiled=True,
        ),
    )
    memory_key_rounded = memory_key_sum.astype(jnp.bfloat16)
    memory_value_rounded = memory_value_sum.astype(jnp.bfloat16)
    query_two_rounded = grad_query_two.reshape(sequence_count, local_rows, D).astype(jnp.bfloat16)
    grad_cross_query = weight_grad(normed_two, query_two_rounded)
    grad_cross_key = weight_grad(memory, memory_key_rounded)
    grad_cross_value = weight_grad(memory, memory_value_rounded)
    grad_memory = (
        project_back(memory_key_rounded, cross_key_full)
        + project_back(memory_value_rounded, cross_value_full)
    ).astype(jnp.bfloat16)
    ignored, norm_pullback = jax.vjp(norm_scale, hidden_one, gain_two)
    grad_hidden_part, grad_gain_two = norm_pullback(
        project_back(query_two_rounded, cross_query_full)
    )
    grad_hidden_one = grad_hidden_two + grad_hidden_part
    branch_one = grad_hidden_one.astype(jnp.bfloat16)
    grad_self_output = weight_grad(attended_one, branch_one)
    grad_attended_one = project_back(branch_one, output_full).astype(jnp.bfloat16)
    grad_query_one, grad_keys_all, grad_values_all, grad_bias = attend_backward(
        to_heads(queries_one),
        to_heads(keys_back),
        to_heads(values_back),
        self_extras,
        heads_first(grad_attended_one),
        output_one,
        maximum_one,
        total_one,
    )
    key_sum, value_sum = (
        lax.psum_scatter(
            grad_keys_all.reshape(sequence_count, sequence_length, D),
            "ctx",
            scatter_dimension=1,
            tiled=True,
        ),
        lax.psum_scatter(
            grad_values_all.reshape(sequence_count, sequence_length, D),
            "ctx",
            scatter_dimension=1,
            tiled=True,
        ),
    )
    query_one_rounded = grad_query_one.reshape(sequence_count, local_rows, D).astype(jnp.bfloat16)
    first_key_bfloat_cast = key_sum.astype(jnp.bfloat16)
    value_one_rounded = value_sum.astype(jnp.bfloat16)
    grad_self_query = weight_grad(normed_one, query_one_rounded)
    grad_self_key = weight_grad(normed_one, first_key_bfloat_cast)
    grad_self_value = weight_grad(normed_one, value_one_rounded)
    grad_normed_one = (
        project_back(query_one_rounded, query_full)
        + project_back(first_key_bfloat_cast, key_full)
        + project_back(value_one_rounded, value_full)
    )
    ignored, norm_pullback = jax.vjp(norm_scale, inputs_wide, gain_one)
    grad_input_part, grad_gain_one = norm_pullback(grad_normed_one)
    grad_tokens = (grad_hidden_one + grad_input_part).astype(jnp.bfloat16)
    (
        shard_gain_one,
        shard_gain_two,
        shard_gain_three,
        shard_bias,
        shard_query,
        shard_key,
        shard_value,
        shard_output,
        shard_cross_query,
        shard_cross_key,
        shard_cross_value,
        shard_cross_output,
        shard_inner,
        shard_outer,
    ) = (
        lax.psum_scatter(
            grad_gain_one.astype(jnp.bfloat16), "fsdp", scatter_dimension=0, tiled=True
        ).astype(jnp.float32),
        lax.psum_scatter(
            grad_gain_two.astype(jnp.bfloat16), "fsdp", scatter_dimension=0, tiled=True
        ).astype(jnp.float32),
        lax.psum_scatter(
            grad_gain_three.astype(jnp.bfloat16), "fsdp", scatter_dimension=0, tiled=True
        ).astype(jnp.float32),
        lax.psum_scatter(
            grad_bias.astype(jnp.bfloat16), "fsdp", scatter_dimension=0, tiled=True
        ).astype(jnp.float32),
        lax.psum_scatter(
            grad_self_query.astype(jnp.bfloat16), "fsdp", scatter_dimension=0, tiled=True
        ).astype(jnp.float32),
        lax.psum_scatter(
            grad_self_key.astype(jnp.bfloat16), "fsdp", scatter_dimension=0, tiled=True
        ).astype(jnp.float32),
        lax.psum_scatter(
            grad_self_value.astype(jnp.bfloat16), "fsdp", scatter_dimension=0, tiled=True
        ).astype(jnp.float32),
        lax.psum_scatter(
            grad_self_output.astype(jnp.bfloat16), "fsdp", scatter_dimension=0, tiled=True
        ).astype(jnp.float32),
        lax.psum_scatter(
            grad_cross_query.astype(jnp.bfloat16), "fsdp", scatter_dimension=0, tiled=True
        ).astype(jnp.float32),
        lax.psum_scatter(
            grad_cross_key.astype(jnp.bfloat16), "fsdp", scatter_dimension=0, tiled=True
        ).astype(jnp.float32),
        lax.psum_scatter(
            grad_cross_value.astype(jnp.bfloat16), "fsdp", scatter_dimension=0, tiled=True
        ).astype(jnp.float32),
        lax.psum_scatter(
            grad_cross_output.astype(jnp.bfloat16), "fsdp", scatter_dimension=0, tiled=True
        ).astype(jnp.float32),
        lax.psum_scatter(
            grad_inner.astype(jnp.bfloat16), "fsdp", scatter_dimension=0, tiled=True
        ).astype(jnp.float32),
        lax.psum_scatter(
            grad_outer.astype(jnp.bfloat16), "fsdp", scatter_dimension=0, tiled=True
        ).astype(jnp.float32),
    )
    (
        total_gain_one,
        total_gain_two,
        total_gain_three,
        total_bias,
        total_query,
        total_key,
        total_value,
        total_output,
        total_cross_query,
        total_cross_key,
        total_cross_value,
        total_cross_output,
        total_inner,
        total_outer,
    ) = lax.psum(
        (
            shard_gain_one,
            shard_gain_two,
            shard_gain_three,
            shard_bias,
            shard_query,
            shard_key,
            shard_value,
            shard_output,
            shard_cross_query,
            shard_cross_key,
            shard_cross_value,
            shard_cross_output,
            shard_inner,
            shard_outer,
        ),
        "ctx",
    )
    return (
        layer_output,
        grad_tokens,
        grad_memory,
        total_gain_one,
        total_gain_two,
        total_gain_three,
        total_bias,
        total_query,
        total_key,
        total_value,
        total_output,
        total_cross_query,
        total_cross_key,
        total_cross_value,
        total_cross_output,
        total_inner,
        total_outer,
    )


MESH = pl.DeviceIdType.MESH
WAYS = 4


class Place:
    def __init__(self, peers):
        self.depth = peers // 2
        c, f = lax.axis_index("ctx"), lax.axis_index("fsdp")
        self.c, self.f = c, f
        self.a, self.b, self.x, self.k = c // 2, c % 2, f // 2, f % 2
        self.core = (c, self.x * 2 + 1 - self.k)
        self.across = (c, (1 - self.x) * 2 + self.k)
        self.beside = (self.a * 2 + 1 - self.b, f)

    def ahead(self, d):
        return lax.rem(self.a + d, self.depth)

    def behind(self, d):
        return lax.rem(self.a + self.depth - d, self.depth)

    def column(self, a):
        return (a * 2 + self.b, self.f)

    def group(self, d):
        return (self.c, lax.rem(self.f + d, WAYS))


def greet(targets):
    barrier = pltpu.get_barrier_semaphore()
    for target in targets:
        pl.semaphore_signal(barrier, inc=1, device_id=target, device_id_type=MESH)
    pl.semaphore_wait(barrier, len(targets))


def remote(src, dst, sems, index, target):
    return pltpu.make_async_remote_copy(
        src_ref=src,
        dst_ref=dst,
        send_sem=sems[0].at[index],
        recv_sem=sems[1].at[index],
        device_id=target,
        device_id_type=MESH,
    )


def apart(src, dst, sems, send_index, recv_index, target):
    return pltpu.make_async_remote_copy(
        src_ref=src,
        dst_ref=dst,
        send_sem=sems[0].at[send_index],
        recv_sem=sems[1].at[recv_index],
        device_id=target,
        device_id_type=MESH,
    )


def line_sems(depth, chunks):
    return sems((2 * depth + 2) * chunks)


def sems(count):
    return [pltpu.SemaphoreType.DMA((count,)), pltpu.SemaphoreType.DMA((count,))]


class Wire:
    def __init__(self, peers):
        self.at = Place(peers)
        self.depth = self.at.depth
        self.sent = []

    def go(self, copy):
        copy.start()
        self.sent.append((None, copy.wait_send))

    def go_if(self, condition, make):
        pl.when(condition)(lambda: make().start())
        self.sent.append((condition, lambda: make().wait_send()))

    def drain(self):
        for condition, wait in self.sent:
            if condition is None:
                wait()
            else:
                pl.when(condition)(wait)

    def partners(self):
        at = self.at
        return (
            [at.group(d) for d in range(1, WAYS)]
            + [at.beside]
            + [at.column(at.ahead(d)) for d in range(1, self.depth)]
        )

    def near(self, step):
        a, last = self.at.a, self.depth - 1
        low = jnp.where(step - 1 < a, step - 1, step)
        mirrored = jnp.where(step - 1 < last - a, step - 1, step)
        return jnp.where(2 * a < last, low, last - mirrored)

    def piece(self, buf, c, chunk, chunks):
        if len(buf.shape) == 3:
            size = buf.shape[1] // chunks
            return buf.at[c, chunk * size : (chunk + 1) * size]
        rows = buf.shape[0] // (2 * self.depth)
        size = rows // chunks
        return buf.at[pl.ds(pl.multiple_of(c * rows + chunk * size, size), size)]

    def slot(self, buf, c):
        return self.piece(buf, c, 0, 1)

    def pass_on(self, src, dst, sem, up, beside, own, chunk, chunks, origin):
        at, a = self.at, self.at.a
        line = origin * chunks + chunk
        side = (self.depth + origin) * chunks + chunk
        for step in (1, -1):
            if own or (step == 1) == up:
                first = (2 * self.depth + (step == 1)) * chunks + chunk if own else line
                self.go_if(
                    a + 1 < self.depth if step == 1 else a > 0,
                    lambda step=step, first=first: apart(src, dst, sem, first, line, at.column(a + step)),
                )
        if beside:
            self.go(apart(src, dst, sem, side, side, at.beside))

    def spread(self, src, buf, sem, chunks):
        at = self.at
        size = src.shape[0] // chunks
        for chunk in range(chunks):
            part = src.at[chunk * size : (chunk + 1) * size]
            self.pass_on(part, self.piece(buf, at.c, chunk, chunks), sem, True, True, True, chunk, chunks, at.a)

    def relay(self, gathered, step):
        at, depth = self.at, self.depth
        for buf, sem, chunks in gathered:
            for chunk in range(chunks):
                for up in (True, False):
                    origin = at.a - step if up else at.a + step
                    inside = origin >= 0 if up else origin < depth
                    onward = at.a + 1 < depth if up else at.a > 0
                    line = origin * chunks + chunk
                    side = (depth + origin) * chunks + chunk
                    spot = lambda: self.piece(buf, origin * 2 + at.b, chunk, chunks)
                    target = at.column(at.a + 1 if up else at.a - 1)

                    def forward(_):
                        return apart(spot(), spot(), sem, line, line, target)

                    def sideways(_):
                        return apart(spot(), spot(), sem, side, side, at.beside)

                    @pl.when(inside)
                    def _():
                        apart(spot(), spot(), sem, line, line, at.beside).wait_recv()
                        sideways(0).start()
                        pl.when(onward)(lambda: forward(0).start())

                    self.sent.append((inside, self.later(buf, sem, side, origin, chunk, chunks, at.beside)))
                    self.sent.append(
                        (jnp.logical_and(inside, onward), self.later(buf, sem, line, origin, chunk, chunks, target))
                    )

    def later(self, buf, sem, index, origin, chunk, chunks, target):
        def wait():
            spot = self.piece(buf, origin * 2 + self.at.b, chunk, chunks)
            apart(spot, spot, sem, index, index, target).wait_send()

        return wait

    def from_beside(self, gathered, a):
        for buf, sem, chunks in gathered:
            for chunk in range(chunks):
                spot = self.piece(buf, a * 2 + 1 - self.at.b, chunk, chunks)
                index = (self.depth + a) * chunks + chunk
                apart(spot, spot, sem, index, index, self.at.beside).wait_recv()

    def shard(self, full, f):
        quarter = full.shape[0] // WAYS
        return full.at[pl.ds(pl.multiple_of(f * quarter, quarter), quarter)]

    def weight_start(self, src, full, sem, i):
        at = self.at
        slot = self.shard(full, at.f)
        slot[...] = src[...]
        self.go(remote(src, slot, sem, 3 * i, at.across))
        self.go(remote(src, slot, sem, 3 * i + 1, at.core))

    def weight_relay(self, full, sem, i):
        at = self.at
        slot = self.shard(full, (1 - at.x) * 2 + at.k)
        remote(slot, slot, sem, 3 * i, at.across).wait_recv()
        self.go(remote(slot, slot, sem, 3 * i + 2, at.core))

    def weight_ready(self, full, sem, i):
        at = self.at
        slot = self.shard(full, at.x * 2 + 1 - at.k)
        remote(slot, slot, sem, 3 * i + 1, at.core).wait_recv()
        slot = self.shard(full, (1 - at.x) * 2 + 1 - at.k)
        remote(slot, slot, sem, 3 * i + 2, at.core).wait_recv()


class Summed:
    def __init__(self, wire, source, out, rc, sd, rd, sem_c, sem_d, sem_e, sem_f):
        self.wire, self.source, self.out, self.rc, self.sd, self.rd = wire, source, out, rc, sd, rd
        self.sem_c, self.sem_d, self.sem_e, self.sem_f = sem_c, sem_d, sem_e, sem_f
        at = wire.at
        half, part = out.shape[2] // 2, out.shape[1] // wire.depth
        columns = lambda b: pl.ds(pl.multiple_of(b * half, LANES), half)
        self.mine, self.theirs = columns(at.b), columns(1 - at.b)
        self.rows = lambda a: pl.ds(pl.multiple_of(a * part, part), part)

    def stage_c(self, j):
        at = self.wire.at
        self.wire.go(remote(self.source(j).at[:, self.theirs], self.rc.at[j], self.sem_c, j, at.beside))

    def stage_d(self, j):
        at, depth = self.wire.at, self.wire.depth
        remote(self.rc.at[j], self.rc.at[j], self.sem_c, j, at.beside).wait_recv()
        value = self.source(j)[:, self.mine].astype(F32) + self.rc[j].astype(F32)
        self.sd[j] = value.astype(BF16)
        for d in range(1, depth):
            spot = self.rd.at[j, self.rows(at.a)]
            target = at.ahead(d)
            self.wire.go(remote(self.sd.at[j, self.rows(target)], spot, self.sem_d, j * depth + d, at.column(target)))

    def stage_e(self, j):
        at, depth = self.wire.at, self.wire.depth
        value = self.sd[j, self.rows(at.a), :].astype(F32)
        for d in range(1, depth):
            spot = self.rd.at[j, self.rows(at.behind(d))]
            remote(spot, spot, self.sem_d, j * depth + d, at.column(at.behind(d))).wait_recv()
            value += spot[...].astype(F32)
        spot = self.out.at[j, self.rows(at.a), self.mine]
        spot[...] = value.astype(BF16)
        for d in range(1, depth):
            self.wire.go(remote(spot, spot, self.sem_e, j * depth + d, at.column(at.ahead(d))))

    def stage_f(self, j):
        at, depth = self.wire.at, self.wire.depth
        for d in range(1, depth):
            spot = self.out.at[j, self.rows(at.behind(d)), self.mine]
            remote(spot, spot, self.sem_e, j * depth + d, at.column(at.behind(d))).wait_recv()
        spot = self.out.at[j, :, self.mine]
        self.wire.go(remote(spot, spot, self.sem_f, j, at.beside))

    def stage_g(self, j):
        spot = self.out.at[j, :, self.theirs]
        remote(spot, spot, self.sem_f, j, self.wire.at.beside).wait_recv()


def two_heads(x):
    return jnp.concatenate([half_mask(x, 0), half_mask(x, 1)], 0)


def ones_beside(x):
    ones = jnp.ones_like(x)
    return jnp.concatenate([two_heads(x), two_heads(ones)], 1)


def softmax_pair(scores, v, stats, p):
    weights, tops = [], []
    for s in scores:
        m = jnp.max(s, axis=1, keepdims=True)
        weights.append(jnp.exp(s - m).astype(BF16))
        tops.append(m)
    both = nn(jnp.concatenate(weights, 1), ones_beside(v))
    sums = both[:, LANES:]
    logs = jnp.log(sums)
    turned = pltpu.roll(logs, HEAD_DIM, 1)
    lane = lax.broadcasted_iota(jnp.int32, logs.shape, 1)
    inside = lane < HEAD_DIM
    stats = jnp.where(lane == 2 * p, tops[0] + jnp.where(inside, logs, turned), stats)
    stats = jnp.where(lane == 2 * p + 1, tops[1] + jnp.where(inside, turned, logs), stats)
    return both[:, :LANES] / sums, stats


def fill_inverse(order, inv):
    count = order.shape[0]
    for p in range(count):
        slot = jnp.int32(0)
        for s in range(count):
            slot = jnp.where(order[s] == p, s, slot)
        inv[p] = slot


def own_facts(order, c, count, length):
    per = (BLOCK // PIECE).bit_length() - 1
    facts = []
    for i in range(count):
        n = order[c * count + i]
        start = lax.shift_right_logical(n, per) * BLOCK
        facts.append((n, n & 1, length // LANES - 1 - lax.shift_right_logical(n, 1), start + BLOCK, start))
    return facts


def own_column(facts, i):
    return jnp.concatenate([jnp.full((PIECE, 1), fact[i], jnp.int32) for fact in facts], 0)


def own_bias(table, lines, own, out, low, high):
    full = table.shape[1]
    rows, length = out.shape[1], out.shape[2]

    def head(h, c):
        base = shear(pltpu.roll(jnp.broadcast_to(table[pl.ds(h, 1), :], (8, full)), 1, 1), 1)
        lines[0] = base
        lines[1] = pltpu.roll(base, PIECE, 1)
        for i in range(rows // PIECE):
            window = lines[own[i][1], :, pl.ds(own[i][2] * LANES, length + LANES)]
            for g in range(0, PIECE // 8, 2):
                both = [pltpu.roll(window, 8 * k, 1) if k else window for k in (g, g + 1)]
                both = jnp.concatenate(both, 0)[:, LANES:]
                out[h, i * PIECE + 8 * g : i * PIECE + 8 * g + 16, :] = both.astype(BF16)
        return c

    lax.fori_loop(low, high, head, 0)


def diagonal_sums(block):
    rows, length = block.shape
    wide = jnp.concatenate([block, jnp.zeros((rows, LANES), F32)], axis=1)
    total = pltpu.roll(wide[0:8], LANES, 1)
    for g in range(1, rows // 8):
        total += pltpu.roll(wide[8 * g : 8 * g + 8], LANES - 8 * g, 1)
    return jnp.sum(shear(total, -1), axis=0, keepdims=True)


N_FRONT = 5
CHUNKS = 2
N_GAINS = 16


def front_kernel(peers, *refs):
    order, tok, gain_row, bias_shard, buckets = refs[:5]
    shards_in = refs[5 : 5 + N_FRONT]
    (w_self_out, w_rest_out, gains, ahead_out, table_out, q_out, k_out, v_out, a1, o1, h1, a2, q2, lse) = refs[5 + N_FRONT : 19 + N_FRONT]
    (tok_all, pack, pack_all, marks, marks_all, table, lines, q_own, w_self, w_rest, ahead, q_nat, k_nat, v_nat, s_keep, inv, *sem) = refs[19 + N_FRONT :]
    weights = [w_self.at[i] for i in range(3)] + [w_rest.at[i] for i in range(N_FRONT - 3)]
    sem_t, sem_w, sem_p, sem_m = sem[0:2], sem[2:4], sem[4:6], sem[6:8]
    wire = Wire(peers)
    at, depth = wire.at, wire.depth
    rows = tok.shape[0]
    length = peers * rows
    mine, per = rows // PIECE, BLOCK // PIECE
    kept = []

    def keep(i, src, dst):
        copy = pltpu.make_async_copy(src, dst, s_keep.at[i])
        copy.start()
        kept.append(copy)

    quarter = gain_row.shape[1] // 3
    spot = lax.broadcasted_iota(jnp.int32, (quarter, D), 0) + at.f * quarter
    place = jnp.where(lax.broadcasted_iota(jnp.int32, (quarter, D), 1) == spot, 1.0, 0.0).astype(BF16)
    pack[...] = jnp.zeros_like(pack)
    for i in range(3):
        pack[i : i + 1, :] = nn(gain_row[:, i * quarter : (i + 1) * quarter], place).astype(BF16)
    eighth, heads = bias_shard.shape
    spot = lax.broadcasted_iota(jnp.int32, (BUCKETS, eighth), 1) + at.f * eighth
    place = jnp.where(lax.broadcasted_iota(jnp.int32, (BUCKETS, eighth), 0) == spot, 1.0, 0.0).astype(BF16)
    marks[...] = jnp.zeros_like(marks)
    marks[:, 0:heads] = nn(place, bias_shard[...]).astype(BF16)
    greet(wire.partners())
    for d in range(1, WAYS):
        wire.go(remote(pack, pack_all.at[at.f], sem_p, d, at.group(d)))
        wire.go(remote(marks, marks_all.at[at.f], sem_m, d, at.group(d)))
    wire.spread(tok, tok_all, sem_t, CHUNKS)
    for i in range(3):
        wire.weight_start(shards_in[i], weights[i], sem_w, i)
    wire.slot(tok_all, at.c)[...] = tok[...]
    pack_all[at.f] = pack[...]
    marks_all[at.f] = marks[...]
    for d in range(1, WAYS):
        slot = pack_all.at[lax.rem(at.f + WAYS - d, WAYS)]
        remote(slot, slot, sem_p, d, at.group(WAYS - d)).wait_recv()
        slot = marks_all.at[lax.rem(at.f + WAYS - d, WAYS)]
        remote(slot, slot, sem_m, d, at.group(WAYS - d)).wait_recv()
    whole = lambda x: x[0].astype(F32) + x[1].astype(F32) + x[2].astype(F32) + x[3].astype(F32)
    fill_inverse(order, inv)
    own = own_facts(order, at.c, mine, length)
    gains[...] = whole(pack_all)[0:8, :]
    bias = whole(marks_all).astype(BF16)
    bucket = lax.broadcasted_iota(jnp.int32, (bias.shape[0], 2 * length), 0)
    hot = jnp.where(buckets[...] == bucket, 1.0, 0.0).astype(BF16)
    table[0] = tn(bias, hot)[0:16, :]
    shifted = pltpu.roll(table[0], 1, 1).astype(BF16)
    row = lax.broadcasted_iota(jnp.int32, (LANES, LANES), 0)
    mirror = jnp.where(row + lax.broadcasted_iota(jnp.int32, (LANES, LANES), 1) == LANES - 1, 1.0, 0.0).astype(BF16)
    tiles = 2 * length // LANES
    for t in range(tiles):
        u = tiles - 1 - t
        table_out[:, t * LANES : (t + 1) * LANES] = nn(shifted[:, u * LANES : (u + 1) * LANES], mirror)

    gathered = [(tok_all, sem_t, CHUNKS)]
    share = HEADS // (depth - 1)
    for step in range(1, depth):
        wire.relay(gathered, step)
        own_bias(table.at[0], lines, own, ahead, (step - 1) * share, step * share)
    keep(3, ahead, ahead_out)
    for i in range(3):
        wire.weight_relay(weights[i], sem_w, i)
    for i in range(3, N_FRONT):
        wire.weight_start(shards_in[i], weights[i], sem_w, i)
    first = gains[0:1, :]
    a1[...] = normed(tok[...].astype(F32), first).astype(BF16)
    for i in range(3):
        wire.weight_ready(weights[i], sem_w, i)
    keep(0, w_self, w_self_out)
    for a in range(depth):
        wire.from_beside(gathered, a)

    def tile(t, c):
        parts = []
        for i in range(per):
            parts.append(tok_all[pl.ds(inv[t * per + i] * PIECE, PIECE), :])
        a = normed(jnp.concatenate(parts, 0).astype(F32), first).astype(BF16)
        dst = pl.ds(pl.multiple_of(t * BLOCK, BLOCK), BLOCK)
        for j, out in enumerate((q_nat, k_nat, v_nat)):
            out[dst, :] = nn(a, weights[j][...]).astype(BF16)
        return c

    lax.fori_loop(0, length // BLOCK, tile, 0)
    for i in range(mine):
        q_own[i * PIECE : (i + 1) * PIECE, :] = q_nat[pl.ds(own[i][0] * PIECE, PIECE), :]
    for i, (src, dst) in enumerate(((q_nat, q_out), (k_nat, k_out), (v_nat, v_out))):
        keep(5 + i, src, dst)
    wire.weight_relay(weights[3], sem_w, 3)
    lane = lax.broadcasted_iota(jnp.int32, (rows, length), 1)
    visible = lane < own_column(own, 3)

    def pair(p, stats):
        sl = lanes_of(p)
        s = nt(q_own[:, sl], two_heads(k_nat[:, sl]))
        scores = []
        for half in range(2):
            biased = s[:, half * length : (half + 1) * length] + ahead[2 * p + half].astype(F32)
            scores.append(jnp.where(visible, biased, NEGATIVE))
        value, stats = softmax_pair(scores, v_nat[:, sl], stats, p)
        o1[:, sl] = value.astype(BF16)
        return stats

    stats = lax.fori_loop(0, PAIRS // 2, pair, jnp.zeros((rows, LANES), F32), unroll=True)
    wire.weight_relay(weights[4], sem_w, 4)
    lse[...] = lax.fori_loop(PAIRS // 2, PAIRS, pair, stats, unroll=True)
    wire.weight_ready(weights[3], sem_w, 3)
    h = tok[...].astype(F32) + nn(o1[...], weights[3][...])
    h1[...] = h
    a = normed(h, gains[1:2, :]).astype(BF16)
    a2[...] = a
    wire.weight_ready(weights[4], sem_w, 4)
    q2[...] = nn(a, weights[4][...]).astype(BF16)
    keep(1, w_rest, w_rest_out)
    for copy in kept:
        copy.wait()
    wire.drain()


def front(peers, order, tok, gain_row, bias_shard, buckets, weight_shards):
    rows = tok.shape[0]
    length, depth = peers * rows, peers // 2
    block = lambda dtype: sds((rows, D), dtype)
    return pl.pallas_call(
        functools.partial(front_kernel, peers),
        name="front",
        out_shape=[sds((3, D, D), BF16), sds((N_FRONT - 3, D, D), BF16), sds((8, D), F32)]
        + [sds((HEADS, rows, length), BF16), sds((16, 2 * length), F32)]
        + [sds((length, D), BF16)] * 3
        + [block(BF16), block(BF16), block(F32), block(BF16), block(BF16), sds((rows, LANES), F32)],
        in_specs=[smem_spec()] + [full_spec()] * (4 + N_FRONT),
        out_specs=[any_spec() if i in (0, 1, 3, 5, 6, 7) else full_spec() for i in range(14)],
        scratch_shapes=[
            pltpu.VMEM((length, D), BF16),
            pltpu.VMEM((N_GAINS, D), BF16),
            pltpu.VMEM((WAYS, N_GAINS, D), BF16),
            pltpu.VMEM((BUCKETS, LANES), BF16),
            pltpu.VMEM((WAYS, BUCKETS, LANES), BF16),
            pltpu.VMEM((1, 16, 2 * length), F32),
            pltpu.VMEM((2, 8, 2 * length), F32),
            pltpu.VMEM((rows, D), BF16),
            pltpu.VMEM((3, D, D), BF16),
            pltpu.VMEM((N_FRONT - 3, D, D), BF16),
        ]
        + [pltpu.VMEM((HEADS, rows, length), BF16)]
        + [pltpu.VMEM((length, D), BF16)] * 3
        + [pltpu.SemaphoreType.DMA((8,)), pltpu.SMEM(order.shape, jnp.int32)]
        + line_sems(depth, CHUNKS) + sems(3 * N_FRONT) + sems(WAYS) + sems(WAYS),
        compiler_params=pltpu.CompilerParams(collective_id=1, has_side_effects=True, vmem_limit_bytes=VMEM_LIMIT),
    )(order, tok, gain_row, bias_shard, buckets, *weight_shards)


STAT = 16


def split(x):
    high = x.astype(BF16)
    return high, (x - high.astype(F32)).astype(BF16)


def head_matrix(rows):
    row = lax.broadcasted_iota(jnp.int32, (rows, D), 0)
    lane = lax.broadcasted_iota(jnp.int32, (rows, D), 1)
    return jnp.where(lane // HEAD_DIM == row, 1.0, 0.0).astype(BF16)


def per_head_sums(x, heads):
    high, low = split(x)
    return nt(heads, high) + nt(heads, low)


def blend(parts, stats, heads):
    top = functools.reduce(jnp.maximum, stats)
    shares = [jnp.exp(s - top) for s in stats]
    total = functools.reduce(jnp.add, shares)
    value = 0.0
    for part, share in zip(parts, shares):
        high, low = split(share / total)
        value = value + (tn(high, heads) + tn(low, heads)) * part.astype(F32)
    return value, top + jnp.log(total)


def norm_back_rows(x, gain, dy):
    r = lax.rsqrt(jnp.mean(x * x, axis=-1, keepdims=True) + EPSILON)
    gdy = gain * dy
    dx = r * gdy - x * (r * r * r) * jnp.mean(x * gdy, axis=-1, keepdims=True)
    return dx, jnp.sum(dy * x * r, axis=0, keepdims=True)


def round_trip(wire, gathered, fillers, compute, ship, fold, after):
    at = wire.at
    b = at.b
    first, second, third = [wire.near(step) for step in (1, 2, 3)]
    for step in range(1, wire.depth):
        fillers[step - 1]()
        wire.relay(gathered, step)
    for filler in fillers[wire.depth - 1 :]:
        filler()
    wire.from_beside(gathered, at.a)
    compute(at.c, at.a * 2 + 1 - b)
    ship(at.a)
    after[0]()
    wire.from_beside(gathered, third)
    compute(third * 2 + 1 - b, third * 2 + b)
    ship(third)
    after[1]()
    wire.from_beside(gathered, second)
    compute(second * 2 + 1 - b, second * 2 + b)
    ship(second)
    after[2]()
    fold(third)
    wire.from_beside(gathered, first)
    compute(first * 2 + 1 - b, first * 2 + b)
    ship(first)
    after[3]()
    fold(second)
    fold(first)


def middle_kernel(peers, *refs):
    (lengths, q2, h1, o1, lse1, w_rest, gains, mem, grad, ck_shard, cv_shard, co_shard, in_shard, w_out) = refs[:14]
    (o2_out, branch2_out, dq2_out, dk2_out, dv2_out, branch1_out, dh1_out, do1_out, stat1_out, in_all, out_sum, layer_out, gmem_out, small) = refs[14:28]
    (q_all, k2, v2, part, part_lse, from_b, from_b_lse, joined, joined_lse, from_z, from_z_lse,
     w_ck, w_cv, w_co, w_in, g_all, a3_all, dact, act, dpre, da3_send, da3_in, out_send, out_in,
     do_all, stat_all, stat_own, dk_acc, dv_acc, dqp, dq_b, dq_j, dq_z, mask, g_in, g_out, rc, sd, rd, *sem) = refs[28:]
    sem = [sem[2 * i : 2 * i + 2] for i in range(len(sem) // 2)]
    (s_q, s_w, s_in, s_g, s_y, s_yl, s_z, s_zl, s_a3, s_da3, s_out, s_do, s_st, s_dy, s_dz, s_gi, *s_sum) = sem
    wire = Wire(peers)
    at, depth = wire.at, wire.depth
    rows = q2.shape[0]
    heads = head_matrix(STAT)
    quarter = co_shard.shape[0]
    units = w_out.shape[0]
    block = lambda f: pl.ds(pl.multiple_of(f * rows, rows), rows)
    greet(wire.partners())
    wire.spread(q2, q_all, s_q, CHUNKS)
    wire.weight_start(ck_shard, w_ck, s_w, 1)
    wire.weight_start(cv_shard, w_cv, s_w, 2)
    q_all[at.c] = q2[...]
    g_all[block(at.f), :] = grad[...]
    wire.shard(w_in, at.f)[...] = in_shard[:, pl.ds(pl.multiple_of(at.f * units, LANES), units)]

    slots, passages = mem.shape[0], lengths.shape[1]
    log = PLEN.bit_length() - 1

    def hidden(shape, axis):
        slot = lax.broadcasted_iota(jnp.int32, shape, axis) + at.c * slots
        first = at.c * slots // PLEN
        taken = jnp.zeros(shape, jnp.int32)
        for i in range(slots // PLEN + 2):
            size = lengths[0, jnp.minimum(first + i, passages - 1)]
            taken = jnp.where(lax.shift_right_logical(slot, log) == first + i, size, taken)
        return jnp.where((slot & (PLEN - 1)) < taken, 0.0, NEGATIVE)

    def fill_mask():
        mask[...] = hidden(mask.shape, 0)

    def next_weights():
        wire.weight_relay(w_ck, s_w, 1)
        wire.weight_start(co_shard, w_co, s_w, 0)

    def project_memory():
        wire.weight_relay(w_cv, s_w, 2)
        feed_forward_operands()
        wire.weight_ready(w_ck, s_w, 1)
        k2[...] = nn(mem[...], w_ck[...]).astype(BF16)
        wire.weight_ready(w_cv, s_w, 2)
        v2[...] = nn(mem[...], w_cv[...]).astype(BF16)

    def feed_forward_operands():
        for d in range(1, WAYS):
            f = lax.rem(at.f + d, WAYS)
            part = in_shard.at[:, pl.ds(pl.multiple_of(f * units, LANES), units)]
            wire.go(remote(grad, g_all.at[block(at.f)], s_g, d, at.group(d)))
            wire.go(remote(part, wire.shard(w_in, at.f), s_in, d, at.group(d)))

    mask_row = hidden((1, slots), 1)

    def attend(c1, c2):
        def pair(p, stats):
            sl = lanes_of(p)
            q = jnp.concatenate([q_all[c1, :, sl], q_all[c2, :, sl]], 0)
            s = nt(q, two_heads(k2[:, sl]))
            value, stats = softmax_pair([s[:, :slots] + mask_row, s[:, slots:] + mask_row], v2[:, sl], stats, p)
            part[c1, :, sl] = value[:rows].astype(BF16)
            part[c2, :, sl] = value[rows:].astype(BF16)
            return stats

        stats = lax.fori_loop(0, PAIRS, pair, jnp.zeros((2 * rows, LANES), F32), unroll=True)
        part_lse[c1] = stats[:rows].T[:STAT]
        part_lse[c2] = stats[rows:].T[:STAT]

    def ship_part(a):
        other = a * 2 + 1 - at.b
        wire.go(remote(part.at[other], from_b.at[a], s_y, a, at.beside))
        wire.go(remote(part_lse.at[other], from_b_lse.at[a], s_yl, a, at.beside))

    def blend_column(a):
        remote(from_b.at[a], from_b.at[a], s_y, a, at.beside).wait_recv()
        remote(from_b_lse.at[a], from_b_lse.at[a], s_yl, a, at.beside).wait_recv()
        c = a * 2 + at.b
        return blend([part[c], from_b[a]], [part_lse[c], from_b_lse[a]], heads)

    def fold_part(a):
        value, stat = blend_column(a)
        joined[a] = value.astype(BF16)
        joined_lse[a] = stat
        wire.go(remote(joined.at[a], from_z.at[at.a], s_z, at.a, at.column(a)))
        wire.go(remote(joined_lse.at[a], from_z_lse.at[at.a], s_zl, at.a, at.column(a)))

    round_trip(wire, [(q_all, s_q, CHUNKS)], [fill_mask, lambda: None, next_weights, project_memory], attend, ship_part, fold_part, [lambda: None] * 4)
    wire.weight_relay(w_co, s_w, 0)
    value, stat = blend_column(at.a)
    parts, stats = [value], [stat]
    for step in range(1, depth):
        a = wire.near(step)
        remote(from_z.at[a], from_z.at[a], s_z, a, at.column(a)).wait_recv()
        remote(from_z_lse.at[a], from_z_lse.at[a], s_zl, a, at.column(a)).wait_recv()
        parts.append(from_z[a])
        stats.append(from_z_lse[a])
    out2, lse2 = blend(parts, stats, heads)
    o2 = out2.astype(BF16)
    o2_out[...] = o2
    wire.weight_ready(w_co, s_w, 0)
    h2 = h1[...] + nn(o2, w_co[...])
    a3 = normed(h2, gains[2:3, :]).astype(BF16)
    a3_all[block(at.f), :] = a3
    spot = a3_all.at[block(at.f)]
    wire.go(remote(spot, spot, s_a3, 0, at.across))
    wire.go(remote(spot, spot, s_a3, 1, at.core))

    def arrive(buf, sem, size):
        for d in range(1, WAYS):
            f = lax.rem(at.f + WAYS - d, WAYS)
            spot = buf.at[pl.ds(pl.multiple_of(f * size, size), size)]
            remote(spot, spot, sem, d, at.group(WAYS - d)).wait_recv()

    arrive(g_all, s_g, rows)
    tiles = [slice(2 * rows * t, 2 * rows * (t + 1)) for t in range(WAYS // 2)]
    for rs in tiles:
        dact[rs, :] = nt(g_all[rs, :], w_out[...])
    arrive(w_in, s_in, quarter)
    wire.weight_relay(a3_all, s_a3, 0)
    wire.weight_ready(a3_all, s_a3, 0)
    for rs in tiles:
        pre = nn(a3_all[rs, :], w_in[...])
        square = pre * pre
        t = jnp.tanh(0.7978845608028654 * (pre + 0.044715 * pre * square))
        act[rs, :] = (0.5 * pre * (1.0 + t)).astype(BF16)
        slope = 0.5 * (1.0 + t) + 0.5 * pre * (1.0 - t * t) * (0.7978845608028654 * (1.0 + 3 * 0.044715 * square))
        d = (dact[rs, :] * slope).astype(BF16)
        dpre[rs, :] = d
        da3_send[rs, :] = nt(d, w_in[...]).astype(BF16)

    def exchange(src, dst, sem):
        for d in range(1, WAYS):
            f = lax.rem(at.f + d, WAYS)
            wire.go(remote(src.at[block(f)], dst.at[block(at.f)], sem, d, at.group(d)))

    def collect(src, dst, sem):
        arrive(dst, sem, rows)
        value = src[block(at.f), :].astype(F32)
        for d in range(1, WAYS):
            value += dst[block(lax.rem(at.f + WAYS - d, WAYS)), :].astype(F32)
        return value

    from_core, to_pass, from_across, passed = [slice(rows * i, rows * (i + 1)) for i in range(WAYS)]
    beyond = (1 - at.x) * 2
    wire.go(remote(da3_send.at[block(beyond + 1 - at.k)], da3_in.at[to_pass], s_da3, 1, at.core))
    wire.go(remote(da3_send.at[block(at.x * 2 + 1 - at.k)], da3_in.at[from_core], s_da3, 0, at.core))
    remote(da3_in.at[to_pass], da3_in.at[to_pass], s_da3, 1, at.core).wait_recv()
    pair_sum = da3_send[block(beyond + at.k), :].astype(F32) + da3_in[to_pass, :].astype(F32)
    da3_in[passed, :] = pair_sum.astype(BF16)
    wire.go(remote(da3_in.at[passed], da3_in.at[from_across], s_da3, 2, at.across))
    sums = Summed(wire, lambda j: g_out.at[j * quarter : (j + 1) * quarter], out_sum, rc, sd, rd, *s_sum)
    g_out[...] = tn(act[...], g_all[...]).astype(BF16)
    for j in range(WAYS):
        sums.stage_c(j)
    for rs in tiles:
        out_send[rs, :] = nn(act[rs, :], w_out[...]).astype(BF16)
    sums.stage_d(0)
    sums.stage_d(1)
    remote(da3_in.at[from_core], da3_in.at[from_core], s_da3, 0, at.core).wait_recv()
    remote(da3_in.at[from_across], da3_in.at[from_across], s_da3, 2, at.across).wait_recv()
    da3 = da3_send[block(at.f), :].astype(F32) + da3_in[from_core, :].astype(F32) + da3_in[from_across, :].astype(F32)
    dx, dgain = norm_back_rows(h2, gains[2:3, :], da3)
    small[...] = jnp.zeros_like(small)
    small[1:2, :] = dgain
    dh2 = grad[...].astype(F32) + dx
    branch2 = dh2.astype(BF16)
    branch2_out[...] = branch2
    do2 = nt(branch2, w_co[...]).astype(BF16)
    do_all[at.c] = do2
    stat_own[0] = jnp.concatenate([lse2, per_head_sums(do2.astype(F32) * out2, heads)], 0)
    stat_all[at.c] = stat_own[0]
    wire.spread(do_all.at[at.c], do_all, s_do, CHUNKS)
    wire.spread(stat_own.at[0], stat_all, s_st, 1)
    exchange(out_send, out_in, s_out)

    def clear():
        dk_acc[...] = jnp.zeros_like(dk_acc)
        dv_acc[...] = jnp.zeros_like(dv_acc)

    def finish_output():
        layer_out[...] = (h2 + collect(out_send, out_in, s_out)).astype(BF16)

    def stages(stage, *js):
        return lambda: [stage(j) for j in js]

    def in_grads():
        g_in[...] = tn(a3_all[...], dpre[...]).astype(BF16)
        rows_of = lambda f: pl.ds(pl.multiple_of(f * quarter, quarter), quarter)
        in_all[at.f] = g_in[rows_of(at.f), :]
        for d in range(1, WAYS):
            f = lax.rem(at.f + d, WAYS)
            wire.go(remote(g_in.at[rows_of(f)], in_all.at[at.f], s_gi, d, at.group(d)))

    def attend_back(c1, c2):
        def pair(p, carry):
            sl = lanes_of(p)
            q = jnp.concatenate([q_all[c1, :, sl], q_all[c2, :, sl]], 0)
            do = jnp.concatenate([do_all[c1, :, sl], do_all[c2, :, sl]], 0)
            kk = two_heads(k2[:, sl])
            s = nt(kk, q)
            d = nt(two_heads(v2[:, sl]), do)
            line = lambda i: jnp.concatenate([stat_all[c1, pl.ds(i, 1), :], stat_all[c2, pl.ds(i, 1), :]], 1)
            weights, slopes = [], []
            for half in range(2):
                h, hs = 2 * p + half, slice(half * slots, (half + 1) * slots)
                e = jnp.exp(s[hs] + mask[...] - line(h))
                weights.append(e.astype(BF16))
                slopes.append((e * (d[hs] - line(STAT + h))).astype(BF16))
            dv_acc[:, sl] += nn(jnp.concatenate(weights, 1), two_heads(do))
            dk_acc[:, sl] += nn(jnp.concatenate(slopes, 1), two_heads(q))
            dq = tn(kk, jnp.concatenate(slopes, 0)).T
            dqp[c1, :, sl] = dq[:rows].astype(BF16)
            dqp[c2, :, sl] = dq[rows:].astype(BF16)
            return carry

        lax.fori_loop(0, PAIRS, pair, 0, unroll=True)

    def ship_dq(a):
        wire.go(remote(dqp.at[a * 2 + 1 - at.b], dq_b.at[a], s_dy, a, at.beside))

    def column_dq(a):
        remote(dq_b.at[a], dq_b.at[a], s_dy, a, at.beside).wait_recv()
        return dqp[a * 2 + at.b].astype(F32) + dq_b[a].astype(F32)

    def fold_dq(a):
        dq_j[a] = column_dq(a).astype(BF16)
        wire.go(remote(dq_j.at[a], dq_z.at[at.a], s_dz, at.a, at.column(a)))

    round_trip(
        wire, [(do_all, s_do, CHUNKS), (stat_all, s_st, 1)], [clear, in_grads, lambda: None, stages(sums.stage_d, 2, 3)], attend_back, ship_dq, fold_dq,
        [stages(sums.stage_e, 0, 1), stages(sums.stage_e, 2, 3), stages(sums.stage_f, 0, 1), stages(sums.stage_f, 2, 3)],
    )
    dk2_out[...] = dk_acc[...].astype(BF16)
    dv2_out[...] = dv_acc[...].astype(BF16)
    gmem_out[...] = (nt(dk2_out[...], w_ck[...]) + nt(dv2_out[...], w_cv[...])).astype(BF16)
    finish_output()
    value = column_dq(at.a)
    for step in range(1, depth):
        a = wire.near(step)
        remote(dq_z.at[a], dq_z.at[a], s_dz, a, at.column(a)).wait_recv()
        value += dq_z[a].astype(F32)
    dq2 = value.astype(BF16)
    dq2_out[...] = dq2
    dx, dgain = norm_back_rows(h1[...], gains[1:2, :], nt(dq2, w_rest[1]))
    small[0:1, :] = dgain
    dh1 = dh2 + dx
    dh1_out[...] = dh1
    branch1 = dh1.astype(BF16)
    branch1_out[...] = branch1
    do1 = nt(branch1, w_rest[0]).astype(BF16)
    do1_out[...] = do1
    stat_own[1] = jnp.concatenate([lse1[...].T[:STAT], per_head_sums(do1.astype(F32) * o1[...].astype(F32), heads)], 0)
    stat1_out[...] = stat_own[1]
    for d in range(1, WAYS):
        spot = in_all.at[lax.rem(at.f + WAYS - d, WAYS)]
        remote(spot, spot, s_gi, d, at.group(WAYS - d)).wait_recv()
    for j in range(WAYS):
        sums.stage_g(j)
    wire.drain()


def middle(peers, lengths, q2, h1, o1, lse1, w_rest, gains, mem, grad, ck_shard, cv_shard, co_shard, in_shard, w_out):
    rows, slots = q2.shape[0], mem.shape[0]
    depth = peers // 2
    units = w_out.shape[0]
    row = lambda dtype: sds((rows, D), dtype)
    store = lambda n, dtype=BF16: pltpu.VMEM((n, rows, D), dtype)
    stat = lambda n, k=STAT: pltpu.VMEM((n, k, rows), F32)
    group = lambda width, dtype=BF16: pltpu.VMEM((WAYS * rows, width), dtype)
    return pl.pallas_call(
        functools.partial(middle_kernel, peers),
        name="middle",
        out_shape=[
            row(BF16),
            row(BF16),
            row(BF16),
            sds((slots, D), BF16),
            sds((slots, D), BF16),
            row(BF16),
            row(F32),
            row(BF16),
            sds((2 * STAT, rows), F32),
            sds((WAYS, D // WAYS, units), BF16),
            sds((WAYS, units // WAYS, D), BF16),
            row(BF16),
            sds((slots, D), BF16),
            sds((8, D), F32),
        ],
        in_specs=[smem_spec()] + [full_spec()] * 13,
        out_specs=[full_spec()] * 14,
        scratch_shapes=[
            store(peers), pltpu.VMEM((slots, D), BF16), pltpu.VMEM((slots, D), BF16),
            store(peers), stat(peers), store(depth), stat(depth), store(depth), stat(depth), store(depth), stat(depth),
            pltpu.VMEM((D, D), BF16), pltpu.VMEM((D, D), BF16), pltpu.VMEM((D, D), BF16), pltpu.VMEM((D, units), BF16),
            group(D), group(D), group(units, F32), group(units), group(units), group(D), group(D), group(D), group(D),
            store(peers), stat(peers, 2 * STAT), stat(2, 2 * STAT),
            pltpu.VMEM((slots, D), F32), pltpu.VMEM((slots, D), F32),
            store(peers), store(depth), store(depth), store(depth),
            pltpu.VMEM((slots, 2 * rows), F32),
            pltpu.VMEM((D, units), BF16),
            pltpu.VMEM((units, D), BF16),
        ]
        + [pltpu.VMEM((WAYS, units // WAYS, D // 2), BF16)] * 3
        + line_sems(depth, CHUNKS) + sems(9) + sems(WAYS) + sems(WAYS)
        + sems(depth) * 4
        + sems(WAYS) * 3
        + line_sems(depth, CHUNKS) + line_sems(depth, 1)
        + sems(depth) * 2
        + sems(WAYS) + sems(WAYS) + sems(WAYS * depth) + sems(WAYS * depth) + sems(WAYS),
        compiler_params=pltpu.CompilerParams(collective_id=2, has_side_effects=True, vmem_limit_bytes=VMEM_LIMIT),
    )(lengths, q2, h1, o1, lse1, w_rest, gains, mem, grad, ck_shard, cv_shard, co_shard, in_shard, w_out)


def tail_kernel(peers, *refs):
    (order, do1, stat1, q_far, k_far, v_far, bias_far, table_back, tok, w_self, gains, dh1, buckets,
     a1, o1, branch1, a2, dq2, mem, dk2, dv2, o2, branch2, in_all, small_mid) = refs[:25]
    out, small_out, grad_tokens = refs[25:28]
    (prod, ra, sb, rb, sc, rc, sd, rd, tiny, tiny_in, do_all, do_nat, stat_all, stat_rows, stat_t, q_own, k_own, v_own,
     dq1, dk1, dv1, diagonals, q_nat, k_nat, v_nat, bias, bias_back, lines, bucket_rows, inv, s_w, s_far, *sem) = refs[28:]
    sem = [sem[2 * i : 2 * i + 2] for i in range(len(sem) // 2)]
    s_do, s_st, sem_a, sem_b, sem_c, sem_d, sem_e, sem_f, sem_t = sem
    wire = Wire(peers)
    at, depth, go = wire.at, wire.depth, wire.go
    rows, length = do1.shape[0], q_far.shape[0]
    mine, pieces = rows // PIECE, length // PIECE
    total, quarter, wide = out.shape
    pairs = [(o2, branch2), (mem, dk2), (mem, dv2), (a2, dq2), (o1, branch1), (a1, dq1), (a1, dk1), (a1, dv1)]
    n_mats = len(pairs)
    shard_rows = lambda f: pl.ds(pl.multiple_of(f * quarter, quarter), quarter)

    def stage_a(i):
        left, right = pairs[i]
        prod[i] = tn(left[...], right[...]).astype(BF16)
        for x in range(2):
            go(remote(prod.at[i, shard_rows(x * 2 + 1 - at.k)], ra.at[i, x], sem_a, 2 * i + x, at.core))

    def stage_b(i):
        for x in range(2):
            remote(ra.at[i, x], ra.at[i, x], sem_a, 2 * i + x, at.core).wait_recv()
        x = 1 - at.x
        sb[i] = (prod[i, shard_rows(x * 2 + at.k), :].astype(F32) + ra[i, x].astype(F32)).astype(BF16)
        go(remote(sb.at[i], rb.at[i], sem_b, i, at.across))

    sums = Summed(wire, lambda j: sc.at[j] if j < n_mats else in_all.at[j - n_mats], out, rc, sd, rd, sem_c, sem_d, sem_e, sem_f)

    def stage_c(j):
        if j < n_mats:
            remote(sb.at[j], rb.at[j], sem_b, j, at.across).wait_recv()
            value = prod[j, shard_rows(at.f), :].astype(F32) + ra[j, at.x].astype(F32) + rb[j].astype(F32)
            sc[j] = value.astype(BF16)
        sums.stage_c(j)

    hops = [at.core, at.across, at.beside]

    def small_hop(t):
        if t:
            remote(tiny_in.at[t - 1], tiny_in.at[t - 1], sem_t, t - 1, hops[t - 1]).wait_recv()
            tiny[t] = tiny[t - 1] + tiny_in[t - 1]
        if t < 3:
            go(remote(tiny.at[t], tiny_in.at[t], sem_t, t, hops[t]))
        else:
            for d in range(1, depth):
                go(remote(tiny.at[3], tiny_in.at[2 + d], sem_t, 2 + d, at.column(at.ahead(d))))

    def small_end():
        value = tiny[3]
        for d in range(1, depth):
            remote(tiny_in.at[2 + d], tiny_in.at[2 + d], sem_t, 2 + d, at.column(at.behind(d))).wait_recv()
            value += tiny_in[2 + d]
        small_out[...] = value

    gathered = [(do_all, s_do, CHUNKS), (stat_all, s_st, 1)]

    def relay(step):
        wire.relay(gathered, step)

    def prepare():
        for copy in coming:
            copy.wait()
        for a in range(depth):
            wire.from_beside(gathered, a)
        for c in range(peers):
            spread = jnp.concatenate([stat_all[c], jnp.zeros((LANES - 2 * STAT, rows), F32)], 0)
            stat_rows[c * rows : (c + 1) * rows, :] = spread.T
        for i in range(pieces):
            do_nat[i * PIECE : (i + 1) * PIECE, :] = do_all[pl.ds(inv[i] * PIECE, PIECE), :]
        per = LANES // PIECE
        for t in range(length // LANES):
            lines = [stat_rows[pl.ds(inv[t * per + i] * PIECE, PIECE), :] for i in range(per)]
            stat_t[:, t * LANES : (t + 1) * LANES] = jnp.concatenate(lines, 0).T
        for i in range(mine):
            dst = slice(i * PIECE, (i + 1) * PIECE)
            src = pl.ds(own[i][0] * PIECE, PIECE)
            q_own[dst, :] = q_nat[src, :]
            k_own[dst, :] = k_nat[src, :]
            v_own[dst, :] = v_nat[src, :]

    def attend_back(low, high):
        lane = lax.broadcasted_iota(jnp.int32, (rows, length), 1)
        visible, seen = lane < own_column(own, 3), lane >= own_column(own, 4)
        stat_lane = lax.broadcasted_iota(jnp.int32, (rows, LANES), 1)
        stat_own = jnp.concatenate([stat1[...], jnp.zeros((LANES - 2 * STAT, rows), F32)], 0).T

        def column(h):
            return jnp.sum(jnp.where(stat_lane == h, stat_own, 0.0), axis=1, keepdims=True)

        def pair(p, c):
            sl = lanes_of(p)
            q, k, v, do = q_own[:, sl], k_nat[:, sl], v_nat[:, sl], do1[:, sl]
            kq, vq, qa, da = k_own[:, sl], v_own[:, sl], q_nat[:, sl], do_nat[:, sl]
            dq = dk = dv = jnp.zeros((rows, LANES), F32)
            for half in range(2):
                h = 2 * p + half
                km, vm = half_mask(k, half), half_mask(v, half)
                s = jnp.where(visible, nt(q, km) + bias[h].astype(F32), NEGATIVE)
                e = jnp.exp(s - column(h))
                ds = e * (nt(do, vm) - column(STAT + h))
                dq += nn(ds.astype(BF16), km)
                for i in range(mine):
                    diagonals[i, pl.ds(h, 1), :] = diagonal_sums(ds[i * PIECE : (i + 1) * PIECE, :])
                s = jnp.where(seen, nt(half_mask(kq, half), qa) + bias_back[h].astype(F32), NEGATIVE)
                e = jnp.exp(s - stat_t[pl.ds(h, 1), :])
                dv += nn(e.astype(BF16), half_mask(da, half))
                ds = e * (nt(half_mask(vq, half), da) - stat_t[pl.ds(STAT + h, 1), :])
                dk += nn(ds.astype(BF16), half_mask(qa, half))
            dq1[:, sl] = dq.astype(BF16)
            dk1[:, sl] = dk.astype(BF16)
            dv1[:, sl] = dv.astype(BF16)
            return c

        lax.fori_loop(low, high, pair, 0)

    def finish_tokens():
        weights_here.wait()
        da1 = nt(dq1[...], prod[5]) + nt(dk1[...], prod[6]) + nt(dv1[...], prod[7])
        dx, dgain = norm_back_rows(tok[...].astype(F32), gains[0:1, :], da1)
        grad_tokens[...] = (dh1[...] + dx).astype(BF16)
        sums = jnp.zeros((STAT, BUCKETS), F32)
        number = lax.broadcasted_iota(jnp.int32, (BUCKETS, length + LANES), 0)
        for i in range(mine):
            line = bucket_rows[pl.ds(own[i][1], 1), pl.ds(own[i][2] * LANES, length + LANES)]
            hot = jnp.where(line == number, 1.0, 0.0).astype(BF16)
            high, low = split(diagonals[i])
            sums += nt(high, hot) + nt(low, hot)
        tiny[0] = jnp.zeros(tiny.shape[1:], F32)
        tiny[0, 0:1, :] = dgain
        tiny[0, 1:3, :] = small_mid[0:2, :]
        tiny[0, 8 : 8 + STAT, 0:BUCKETS] = sums

    weights_here = pltpu.make_async_copy(w_self, prod.at[5:8], s_w)
    weights_here.start()
    coming = []
    for i, (src, dst) in enumerate(
        ((q_far, q_nat), (k_far, k_nat), (v_far, v_nat), (bias_far, bias))
    ):
        coming.append(pltpu.make_async_copy(src, dst, s_far.at[i]))
        coming[-1].start()
    own = own_facts(order, at.c, mine, length)
    greet(wire.partners())
    wire.spread(do1, do_all, s_do, CHUNKS)
    wire.spread(stat1, stat_all, s_st, 1)
    wire.slot(do_all, at.c)[...] = do1[...]
    stat_all[at.c] = stat1[...]
    fill_inverse(order, inv)
    diagonals[...] = jnp.zeros_like(diagonals)
    bucket_rows[0:1, :] = pltpu.roll(buckets[...], 1, 1)
    bucket_rows[1:2, :] = pltpu.roll(buckets[...], 1 + PIECE, 1)
    turns = [8, 9, 10, 11, 0, 1, 2, 3, 4, 5, 6, 7]
    lag = 1.5
    events = []
    for tick, j in enumerate(turns):
        if j < n_mats:
            events += [(tick - 2, 1, lambda j=j: stage_a(j)), (tick - 1, 2, lambda j=j: stage_b(j))]
        for k, stage in enumerate((stage_c, sums.stage_d, sums.stage_e, sums.stage_f, sums.stage_g)):
            events.append((tick + k * lag, 3 + k, lambda j=j, stage=stage: stage(j)))
    share = HEADS // 3
    for i in range(3):
        events.append((i + 0.3, 0, lambda i=i: own_bias(table_back, lines, own, bias_back, i * share, (i + 1) * share)))
        events.append((0.5 * i + 0.2, 0, lambda i=i: relay(i + 1)))
    events.append((2.4, 0, prepare))
    events += [(2.6 + 0.5 * i, 0, lambda i=i: attend_back(i, i + 1)) for i in range(PAIRS)]
    events.append((5.7, 0, finish_tokens))
    events += [(6.6 + t, 0, lambda t=t: small_hop(t)) for t in range(4)] + [(11.5, 0, small_end)]
    for _, _, event in sorted(events, key=lambda e: (e[0], -e[1])):
        event()
    wire.drain()


def tail(peers, order, do1, stat1, q_nat, k_nat, v_nat, bias, table_back, tok, w_self, gains, dh1, buckets, *rest):
    rows, length = do1.shape[0], q_nat.shape[0]
    n, depth = 8, peers // 2
    total = n + WAYS
    quarter, half = D // WAYS, D // 2
    shard = lambda k, width=D: pltpu.VMEM((k, quarter, width), BF16)
    row = lambda: pltpu.VMEM((rows, D), BF16)
    tiny = lambda k: pltpu.VMEM((k, 8 + STAT, D), F32)
    operands = (do1, stat1, q_nat, k_nat, v_nat, bias, table_back, tok, w_self, gains, dh1, buckets) + rest
    return pl.pallas_call(
        functools.partial(tail_kernel, peers),
        name="tail",
        out_shape=[sds((total, quarter, D), BF16), sds((8 + STAT, D), F32), sds((rows, D), BF16)],
        in_specs=[smem_spec()]
        + [any_spec() if i in (2, 3, 4, 5, 8) else full_spec() for i in range(len(operands))],
        out_specs=[full_spec()] * 3,
        scratch_shapes=[
            pltpu.VMEM((n, D, D), BF16), pltpu.VMEM((n, 2, quarter, D), BF16), shard(n), shard(n),
            shard(n), shard(total, half), shard(total, half), shard(total, half),
            tiny(4), tiny(3 + depth),
            pltpu.VMEM((length, D), BF16), pltpu.VMEM((length, D), BF16),
            pltpu.VMEM((peers, 2 * STAT, rows), F32), pltpu.VMEM((length, LANES), F32), pltpu.VMEM((LANES, length), F32),
            row(), row(), row(), row(), row(), row(),
            pltpu.VMEM((rows // PIECE, STAT, length + LANES), F32),
        ]
        + [pltpu.VMEM((length, D), BF16)] * 3
        + [pltpu.VMEM((HEADS, rows, length), BF16)] * 2
        + [pltpu.VMEM((2, 8, 2 * length), F32), pltpu.VMEM((2, 2 * length), jnp.int32), pltpu.SMEM(order.shape, jnp.int32)]
        + [pltpu.SemaphoreType.DMA, pltpu.SemaphoreType.DMA((4,))]
        + line_sems(depth, CHUNKS) + line_sems(depth, 1)
        + sems(2 * n) + sems(n) + sems(total) + sems(total * depth) + sems(total * depth) + sems(total) + sems(3 + depth),
        compiler_params=pltpu.CompilerParams(collective_id=0, has_side_effects=True, vmem_limit_bytes=TAIL_VMEM),
    )(order, *operands)


def widen_kernel(first, last, small, *refs):
    ready, outs, gains_out, bias_out = refs[:3], refs[3:16], refs[16], refs[17]
    wide, sem, sem_ready = refs[18:]
    copies = [pltpu.make_async_copy(ready[i], outs[i], sem_ready.at[i]) for i in range(3)]
    for copy in copies:
        copy.start()
    outs = outs[3:]
    count = first.shape[0] + last.shape[0]
    quarter, width = first.shape[1], first.shape[2]
    for j in range(count):
        wide[j] = (first[j] if j < count - WAYS else last[j - (count - WAYS)]).astype(F32)
        if j < count - 2 * WAYS:
            dst = outs[j]
        elif j < count - WAYS:
            i = j - (count - 2 * WAYS)
            dst = outs[-2].at[:, i * width : (i + 1) * width]
        else:
            i = j - (count - WAYS)
            dst = outs[-1].at[i * quarter : (i + 1) * quarter]
        copies.append(pltpu.make_async_copy(wide.at[j], dst, sem.at[j]))
        copies[-1].start()
    f = lax.axis_index("fsdp")
    turned = pltpu.roll(small[0:8, :], lax.rem(WAYS - f, WAYS) * quarter, 1)
    gains_out[...] = turned[:, :quarter]
    eighth = bias_out.shape[0]
    sums = jnp.concatenate([small[8:, 0:LANES], jnp.zeros((LANES - STAT, LANES), F32)], 0)
    flipped = sums.T
    part = flipped[0:eighth, :]
    for i in range(1, WAYS):
        part = jnp.where(f == i, flipped[i * eighth : (i + 1) * eighth, :], part)
    bias_out[...] = part[:, :HEADS]
    for copy in copies:
        copy.wait()


def widen(first, last, small, ready):
    quarter, width = first.shape[1:]
    count = first.shape[0] + last.shape[0]
    each = [sds((quarter, width), F32)] * (count - 2 * WAYS)
    big = [sds(x.shape, x.dtype) for x in ready] + each
    big += [sds((quarter, WAYS * width), F32), sds((WAYS * quarter, width), F32)]
    return pl.pallas_call(
        widen_kernel,
        name="widen",
        out_shape=big + [sds((8, quarter), F32), sds((BUCKETS // WAYS, HEADS), F32)],
        in_specs=[full_spec()] * 6,
        out_specs=[any_spec()] * len(big) + [full_spec()] * 2,
        scratch_shapes=[
            pltpu.VMEM((count, quarter, width), F32),
            pltpu.SemaphoreType.DMA((count,)),
            pltpu.SemaphoreType.DMA((3,)),
        ],
        compiler_params=pltpu.CompilerParams(vmem_limit_bytes=VMEM_LIMIT),
    )(first, last, small, *ready)


def shards(
    tokens,
    memory,
    piece_order,
    bucket_table,
    passage_lengths,
    self_gain,
    cross_gain,
    hidden_gain,
    position_bias,
    self_query,
    self_attention_key,
    self_value,
    self_output,
    cross_query,
    cross_key,
    cross_value,
    cross_output,
    hidden_in,
    hidden_out,
    grad_output,
):
    tok, mem, grad = tokens[0], memory[0], grad_output[0]
    rows, slots = tok.shape[0], mem.shape[0]
    length = (bucket_table.shape[0] + 1) // 2
    peers = length // rows
    f = lax.axis_index("fsdp")
    quarter, eighth = self_query.shape[0], position_bias.shape[0]
    buckets = jnp.pad(bucket_table, (0, 1), constant_values=-1)[None]
    w_self, w_rest, gains, ahead, table_back, q1_nat, k1_nat, v1_nat, a1, o1, h1, a2, q2, lse1 = front(
        peers,
        piece_order,
        tok,
        jnp.concatenate([self_gain, cross_gain, hidden_gain])[None],
        position_bias,
        buckets,
        [self_query, self_attention_key, self_value, self_output, cross_query],
    )
    (
        o2,
        branch2,
        dq2,
        dk2,
        dv2,
        branch1,
        dh1,
        do1,
        stat1,
        in_all,
        out_sum,
        layer_output,
        grad_memory,
        small_mid,
    ) = middle(
        peers,
        passage_lengths,
        q2,
        h1,
        o1,
        lse1,
        w_rest,
        gains,
        mem,
        grad,
        cross_key,
        cross_value,
        cross_output,
        hidden_in,
        hidden_out,
    )
    total, small, grad_tokens = tail(
        peers,
        piece_order,
        do1,
        stat1,
        q1_nat,
        k1_nat,
        v1_nat,
        ahead,
        table_back,
        tok,
        w_self,
        gains,
        dh1,
        buckets,
        a1,
        o1,
        branch1,
        a2,
        dq2,
        mem,
        dk2,
        dv2,
        o2,
        branch2,
        in_all,
        small_mid,
    )
    ready = [layer_output, grad_tokens, grad_memory]
    *ready, e0, e1, e2, e3, e4, e5, e6, e7, sum_in, sum_out, gains_out, bias_out = widen(total, out_sum, small, ready)
    return (
        ready[0][None],
        ready[1][None],
        ready[2][None],
        gains_out[0],
        gains_out[1],
        gains_out[2],
        bias_out,
        e5,
        e6,
        e7,
        e4,
        e3,
        e1,
        e2,
        e0,
        sum_in,
        sum_out,
    )


def pick(*arrays):
    resident = (arrays[3].shape[0] + 1) // 2 <= RESIDENT_ROWS
    return (shards if resident else streamed_shards)(*arrays)


def solution(mesh):
    return jax.shard_map(
        pick,
        mesh=mesh,
        in_specs=(
            P("fsdp", "ctx", None),
            P("fsdp", "ctx", None),
            P(),
            P(),
            P("fsdp", None),
            P("fsdp"),
            P("fsdp"),
            P("fsdp"),
            P("fsdp", None),
            P("fsdp", None),
            P("fsdp", None),
            P("fsdp", None),
            P("fsdp", None),
            P("fsdp", None),
            P("fsdp", None),
            P("fsdp", None),
            P("fsdp", None),
            P("fsdp", None),
            P("fsdp", None),
            P("fsdp", "ctx", None),
        ),
        out_specs=(
            P("fsdp", "ctx", None),
            P("fsdp", "ctx", None),
            P("fsdp", "ctx", None),
            P("fsdp"),
            P("fsdp"),
            P("fsdp"),
            P("fsdp", None),
            P("fsdp", None),
            P("fsdp", None),
            P("fsdp", None),
            P("fsdp", None),
            P("fsdp", None),
            P("fsdp", None),
            P("fsdp", None),
            P("fsdp", None),
            P("fsdp", None),
            P("fsdp", None),
        ),
        check_vma=False,
    )
```
